32 devices in a mesh: tm: 8 (over y, x, core), dp: 4 (over z).
Axes of the slice: x: 2, y: 2, z: 4, core: 2. Of those that a mesh axis runs over, the one named last changes fastest.
Arguments:
- embedded_features: bfloat16 [32, 1024, 160], P('dp', 'tm'), may hold values from -6 to 6
- earliest_seen_moment: int32 [32], P('dp'), may hold values from 0 to 511
- reach_choice: int32 [32], P('dp'), may hold values from 0 to 2
- lstm_valve_coeffs: float32 [160, 640], P('dp'), may hold values from -0.5 to 0.5
- lstm_unit_coeffs: float32 [160, 320], P('dp'), may hold values from -0.5 to 0.5
- asker_lookup_coeffs: float32 [160, 360], P('dp'), may hold values from -0.5 to 0.5
- attend_exit_coeffs: float32 [40, 160], P('dp'), may hold values from -3 to 3
- attend_unit_coeffs: float32 [160, 320], P('dp'), may hold values from -0.5 to 0.5
- skipnet_entry_coeffs: float32 [160, 160], P('dp'), may hold values from -0.5 to 0.5
- skipnet_inner_coeffs: float32 [160, 160], P('dp'), may hold values from -0.5 to 0.5
- skipnet_unit_coeffs: float32 [160, 320], P('dp'), may hold values from -0.5 to 0.5
- level_map_coeffs: float32 [160, 3], P('dp'), may hold values from -0.5 to 0.5
- bias_gain_table: float32 [160, 18], P('dp')
- block_emit_adjoint: bfloat16 [32, 1024, 160], P('dp', 'tm'), may hold values from -6 to 6
- predicted_adjoint: bfloat16 [32, 3, 1024], P('dp', None, 'tm'), may hold values from -6 to 6
Outputs:
- second_block_emit: bfloat16 [32, 1024, 160], P('dp', 'tm')
- predicted_levels: float32 [32, 3, 1024], P('dp', None, 'tm')
- grad_inputs: bfloat16 [32, 1024, 160], P('dp', 'tm')
- grad_lstm_weight: float32 [160, 640], P('dp')
- grad_lstm_glu_weight: float32 [160, 320], P('dp')
- grad_qkv_weight: float32 [160, 360], P('dp')
- grad_attn_out_weight: float32 [40, 160], P('dp')
- grad_attn_glu_weight: float32 [160, 320], P('dp')
- grad_grn_in_weight: float32 [160, 160], P('dp')
- grad_grn_mid_weight: float32 [160, 160], P('dp')
- grad_grn_glu_weight: float32 [160, 320], P('dp')
- grad_quantile_weight: float32 [160, 3], P('dp')
- grad_vectors: float32 [160, 18], P('dp')
The draws below stay inside these ranges and needn't reach their ends.
All inputs are finite; a program needn't handle non-finite values.
Results may differ from the reference program's by a relative error of at most 0.018.
The reference program's roundings to bfloat16 on the way count: a program that leaves them out, or rounds other values in their place, can miss the bound.
Values may be sent and summed in bfloat16 or wider, within the bound.
A program may use at most 320 MiB of HBM per device.

```python
import math
import jax
import jax.numpy as jnp
from jax import lax

MODEL_BREADTH = 160
HEADS = 4
HEAD = 40
LEVEL_TALLY = 3
DEC = 24
NVEC = 18
SER_DEV = 8
WINDOW_SPAN = 1024
TOTAL_TRACKS = 32


def draw_earliest_seen_moment(key, part):
    key = jax.random.fold_in(key, 11)
    first_key, second_key = jax.random.split(key)
    block_count = TOTAL_TRACKS // SER_DEV
    raw_steps = jax.random.randint(first_key, (block_count, SER_DEV), 0, WINDOW_SPAN // 2, dtype=jnp.int32)
    block_keys = jax.random.split(second_key, block_count)
    orders = jax.vmap(lambda block_key: jax.random.permutation(block_key, SER_DEV))(block_keys)
    steps_out = jnp.where(orders == 0, 0, jnp.where(orders == 1, WINDOW_SPAN // 2 - 1, raw_steps))
    return steps_out.reshape(TOTAL_TRACKS).astype(jnp.int32)


def draw_bias_gain_table(key, part):
    key = jax.random.fold_in(key, 23)
    normal_key, spread_key, slow_key = jax.random.split(key, 3)
    column = jnp.arange(NVEC, dtype=jnp.int32)[None, :]
    normals = jax.random.normal(normal_key, (MODEL_BREADTH, NVEC), jnp.float32)
    spreads = jax.random.uniform(spread_key, (MODEL_BREADTH, NVEC), jnp.float32)
    slow_rows = jax.random.bernoulli(slow_key, 0.5, (MODEL_BREADTH, 1))
    forget_bias = jnp.where(slow_rows, jnp.log(WINDOW_SPAN * 1.0) + 1.5 * spreads, 2.5 + 1.5 * spreads)
    gains = 0.6 + 0.8 * spreads
    is_gain = (column == 6) | (column == 10) | (column == 16)
    table = jnp.where(column == 0, forget_bias, jnp.where(is_gain, gains, 0.5 * normals))
    return table.astype(jnp.float32)


def place_ends(values, key, low, largest):
    longest = values.shape.index(max(values.shape))
    spots = []
    for shift in (0, 1):
        where = [jax.random.randint(jax.random.fold_in(key, axis), (), 0, length) for axis, length in enumerate(values.shape)]
        where[longest] = (where[longest] + shift) % values.shape[longest]
        spots.append(tuple(where))
    return values.at[spots[0]].set(low).at[spots[1]].set(largest)


def steps_of(rng, shape, shards, least, high):
    gain = 1.0
    for dim, parts in shards:
        heights = jax.random.uniform(jax.random.fold_in(jax.random.fold_in(rng, 6), dim), (parts,), jnp.float32, least / len(shards), high / len(shards))
        gain = gain * jnp.repeat(jnp.exp(heights), shape[dim] // parts).reshape((-1,) + (1,) * (len(shape) - 1 - dim))
    return gain


def gaussian(own_key, shape, width, most, cuts=(), held_as=jnp.bfloat16):
    result = jax.random.normal(own_key, shape, jnp.float32) * width
    if len(cuts) > 0:
        result = steps_of(own_key, shape, cuts, -0.22, 0.18) * result
    return jnp.clip(result, min=-most, max=most).astype(held_as)


def setup_inputs(seed: int = 0) -> dict:
    streams_of = jax.random.split(jax.random.key(seed), 16)
    return {
        "embedded_features": gaussian(streams_of[0], (TOTAL_TRACKS, WINDOW_SPAN, MODEL_BREADTH), 1.0, 6.0, ((0, 4), (1, 8))),
        "earliest_seen_moment": draw_earliest_seen_moment(jax.random.fold_in(streams_of[15], 71), 0),
        "reach_choice": place_ends(jax.random.randint(streams_of[2], (TOTAL_TRACKS,), 0, 3), jax.random.fold_in(streams_of[2], 1), 0, 2).astype(jnp.int32),
        "lstm_valve_coeffs": gaussian(streams_of[3], (MODEL_BREADTH, 4 * MODEL_BREADTH), MODEL_BREADTH ** -0.5, 0.5, ((0, 4),), jnp.float32),
        "lstm_unit_coeffs": gaussian(streams_of[4], (MODEL_BREADTH, 2 * MODEL_BREADTH), MODEL_BREADTH ** -0.5, 0.5, ((0, 4),), jnp.float32),
        "asker_lookup_coeffs": gaussian(streams_of[5], (MODEL_BREADTH, 2 * MODEL_BREADTH + HEAD), MODEL_BREADTH ** -0.5, 0.5, ((0, 4),), jnp.float32),
        "attend_exit_coeffs": gaussian(streams_of[6], (HEAD, MODEL_BREADTH), 4 ** -0.5, 3.0, ((0, 4),), jnp.float32),
        "attend_unit_coeffs": gaussian(streams_of[7], (MODEL_BREADTH, 2 * MODEL_BREADTH), MODEL_BREADTH ** -0.5, 0.5, ((0, 4),), jnp.float32),
        "skipnet_entry_coeffs": gaussian(streams_of[8], (MODEL_BREADTH, MODEL_BREADTH), MODEL_BREADTH ** -0.5, 0.5, ((0, 4),), jnp.float32),
        "skipnet_inner_coeffs": gaussian(streams_of[9], (MODEL_BREADTH, MODEL_BREADTH), MODEL_BREADTH ** -0.5, 0.5, ((0, 4),), jnp.float32),
        "skipnet_unit_coeffs": gaussian(streams_of[10], (MODEL_BREADTH, 2 * MODEL_BREADTH), MODEL_BREADTH ** -0.5, 0.5, ((0, 4),), jnp.float32),
        "level_map_coeffs": gaussian(streams_of[11], (MODEL_BREADTH, LEVEL_TALLY), MODEL_BREADTH ** -0.5, 0.5, ((0, 4),), jnp.float32),
        "bias_gain_table": draw_bias_gain_table(jax.random.fold_in(streams_of[15], 71), 0),
        "block_emit_adjoint": gaussian(streams_of[13], (TOTAL_TRACKS, WINDOW_SPAN, MODEL_BREADTH), 1.0, 6.0, ((0, 4), (1, 8))),
        "predicted_adjoint": gaussian(streams_of[14], (TOTAL_TRACKS, LEVEL_TALLY, WINDOW_SPAN), 1.0, 6.0, ((0, 4), (2, 8))),
    }


@jax.custom_vjp
def narrow_format(v):
    return lax.optimization_barrier(v.astype(jnp.bfloat16)).astype(jnp.float32)

@jax.custom_vjp
def narrow_reverse(v):
    return v

def low_keep(v):
    return (narrow_format(v), None)

def low_pass(kept, grad):
    return (grad,)

def back_keep(v):
    return (v, None)

def back_low(kept, grad):
    return (narrow_format(grad),)
narrow_format.defvjp(low_keep, low_pass)
narrow_reverse.defvjp(back_keep, back_low)
HIGHEST = lax.Precision.HIGHEST
EPSILON = 1e-05
NEG_BIG = -1e+30

def dot_outcome(left, right):
    return jnp.dot(left, right, precision=HIGHEST, preferred_element_type=jnp.float32)

def affine_join(earlier, later):
    return (later[0] * earlier[0], later[0] * earlier[1] + later[1])

def layer_norm(values, gains, offsets):
    centred = values - lax.optimization_barrier(jnp.mean(values, axis=-1, keepdims=True))
    spread = lax.optimization_barrier(jnp.mean(centred * centred, axis=-1, keepdims=True))
    return centred * lax.rsqrt(spread + EPSILON) * gains + offsets

def gated_unit(pre_act):
    half_width = pre_act.shape[-1] // 2
    return pre_act[..., :half_width] * jax.nn.sigmoid(pre_act[..., half_width:])

def lstm_gates(pre_act, keep_mask):
    quarter = pre_act.shape[-1] // 4
    forget = jax.nn.sigmoid(pre_act[..., :quarter]) * keep_mask
    inflow = jax.nn.sigmoid(pre_act[..., quarter:2 * quarter]) * jnp.tanh(pre_act[..., 2 * quarter:3 * quarter])
    out_gate = jax.nn.sigmoid(pre_act[..., 3 * quarter:])
    return (forget, inflow, out_gate)

def attend_block(query_block, query_pos, keys, values, begin_one):
    raw = jnp.einsum('qhd,khd->hqk', query_block, keys, precision=HIGHEST)
    scores = narrow_reverse(raw) * HEAD ** (-0.5)
    key_pos = jnp.arange(WINDOW_SPAN, dtype=jnp.int32)
    lowest = jnp.minimum(begin_one, query_pos)
    allowed = (key_pos[None, :] <= query_pos[:, None]) & (key_pos[None, :] >= lowest[:, None])
    scores = jnp.where(allowed[None], scores, NEG_BIG)
    weights = jax.nn.softmax(scores, axis=-1)
    return jnp.einsum('hqk,kd->qd', narrow_format(weights), values, precision=HIGHEST) * (1.0 / HEADS)
checked_block = jax.checkpoint(attend_block)

def attend_series(series_args):
    queries, keys, values, begin_one = series_args
    block_rows = math.gcd(WINDOW_SPAN, 512)
    block_count = WINDOW_SPAN // block_rows
    query_blocks = queries.reshape(block_count, block_rows, HEADS, HEAD)
    pos_blocks = jnp.arange(WINDOW_SPAN, dtype=jnp.int32).reshape(block_count, block_rows)

    def one_block(block_pair):
        return checked_block(block_pair[0], block_pair[1], keys, values, begin_one)
    mixed = lax.map(one_block, (query_blocks, pos_blocks))
    return mixed.reshape(WINDOW_SPAN, HEAD)

def forward(embedded_features, lstm_valve_coeffs, lstm_unit_coeffs, asker_lookup_coeffs, attend_exit_coeffs, attend_unit_coeffs, skipnet_entry_coeffs, skipnet_inner_coeffs, skipnet_unit_coeffs, level_map_coeffs, bias_gain_table, earliest_seen_moment, reach_choice):
    table = narrow_format(bias_gain_table)
    count_of_rows = TOTAL_TRACKS * WINDOW_SPAN
    input_rows = embedded_features.reshape(count_of_rows, MODEL_BREADTH)
    times = jnp.arange(WINDOW_SPAN, dtype=jnp.int32)
    keep_mask = (times[None, :] != earliest_seen_moment[:, None]).astype(jnp.float32).reshape(count_of_rows, 1)
    horizon_len = jnp.where(reach_choice == 0, 1, jnp.where(reach_choice == 1, 5, 24))
    ahead_moment_filter = ((times[None, :] >= WINDOW_SPAN - DEC) & (times[None, :] < WINDOW_SPAN - DEC + horizon_len[:, None])).astype(jnp.float32).reshape(count_of_rows, 1)
    lstm_pre = narrow_reverse(dot_outcome(narrow_format(input_rows), narrow_format(lstm_valve_coeffs))) + table[:, 0:4].T.reshape(-1)
    forget, inflow, out_gate = lstm_gates(lstm_pre, keep_mask)
    _, cells = lax.associative_scan(affine_join, (forget.reshape(TOTAL_TRACKS, WINDOW_SPAN, MODEL_BREADTH), inflow.reshape(TOTAL_TRACKS, WINDOW_SPAN, MODEL_BREADTH)), axis=1)
    hidden = out_gate * jnp.tanh(cells.reshape(count_of_rows, MODEL_BREADTH))
    glu_one = narrow_reverse(dot_outcome(narrow_format(hidden), narrow_format(lstm_unit_coeffs))) + table[:, 4:6].T.reshape(-1)
    first = layer_norm(input_rows + gated_unit(glu_one), table[:, 6], table[:, 7])
    qkv = narrow_format(narrow_reverse(dot_outcome(narrow_format(first), narrow_format(asker_lookup_coeffs))))
    queries = qkv[:, :MODEL_BREADTH].reshape(TOTAL_TRACKS, WINDOW_SPAN, HEADS, HEAD)
    keys = qkv[:, MODEL_BREADTH:2 * MODEL_BREADTH].reshape(TOTAL_TRACKS, WINDOW_SPAN, HEADS, HEAD)
    values = qkv[:, 2 * MODEL_BREADTH:].reshape(TOTAL_TRACKS, WINDOW_SPAN, HEAD)
    mixed = lax.map(attend_series, (queries, keys, values, earliest_seen_moment))
    mixed = narrow_format(narrow_reverse(mixed.reshape(count_of_rows, HEAD)))
    attn = narrow_format(narrow_reverse(dot_outcome(mixed, narrow_format(attend_exit_coeffs))))
    glu_two = narrow_reverse(dot_outcome(attn, narrow_format(attend_unit_coeffs))) + table[:, 8:10].T.reshape(-1)
    second = layer_norm(first + gated_unit(glu_two), table[:, 10], table[:, 11])
    inner = jax.nn.elu(narrow_reverse(dot_outcome(narrow_format(second), narrow_format(skipnet_entry_coeffs))) + table[:, 12])
    middle = narrow_reverse(dot_outcome(narrow_format(inner), narrow_format(skipnet_inner_coeffs))) + table[:, 13]
    glu_three = narrow_reverse(dot_outcome(narrow_format(middle), narrow_format(skipnet_unit_coeffs))) + table[:, 14:16].T.reshape(-1)
    second_block_emit = layer_norm(second + gated_unit(glu_three), table[:, 16], table[:, 17])
    predicted_levels = narrow_reverse(dot_outcome(narrow_format(second_block_emit), narrow_format(level_map_coeffs))) * ahead_moment_filter
    return (second_block_emit.reshape(TOTAL_TRACKS, WINDOW_SPAN, MODEL_BREADTH), predicted_levels.reshape(TOTAL_TRACKS, WINDOW_SPAN, LEVEL_TALLY).transpose(0, 2, 1))

def reference(embedded_features, earliest_seen_moment, reach_choice, lstm_valve_coeffs, lstm_unit_coeffs, asker_lookup_coeffs, attend_exit_coeffs, attend_unit_coeffs, skipnet_entry_coeffs, skipnet_inner_coeffs, skipnet_unit_coeffs, level_map_coeffs, bias_gain_table, block_emit_adjoint, predicted_adjoint):

    def run(inputs_full, weight_a, weight_b, weight_c, weight_d, weight_e, weight_f, weight_g, weight_h, weight_i, table):
        return forward(inputs_full, weight_a, weight_b, weight_c, weight_d, weight_e, weight_f, weight_g, weight_h, weight_i, table, earliest_seen_moment, reach_choice)
    outputs, adjoint_mapping = jax.vjp(run, embedded_features.astype(jnp.float32), lstm_valve_coeffs, lstm_unit_coeffs, asker_lookup_coeffs, attend_exit_coeffs, attend_unit_coeffs, skipnet_entry_coeffs, skipnet_inner_coeffs, skipnet_unit_coeffs, level_map_coeffs, bias_gain_table)
    slope_collection = adjoint_mapping((block_emit_adjoint.astype(jnp.float32), predicted_adjoint.astype(jnp.float32)))
    return (outputs[0].astype(jnp.bfloat16), outputs[1], slope_collection[0].astype(jnp.bfloat16), slope_collection[1], slope_collection[2], slope_collection[3], slope_collection[4], slope_collection[5], slope_collection[6], slope_collection[7], slope_collection[8], slope_collection[9], slope_collection[10])
```

```python
import types

import jax
import jax.numpy as jnp
from jax import lax
from jax.experimental import pallas as pl
from jax.experimental.pallas import tpu as pltpu
from jax.sharding import PartitionSpec as P

HEADS = 4
LEVEL_TALLY = 3
DEC = 24
MICRO = 2


EPSILON = 1e-05
NEG_BIG = -1e30
attend_group = 2
LOG2_E = 1.4426950408889634
VMEM_BYTES = 60 * 2**20


def entering(value, axis, join, neutral, backward):
    count, mine = (lax.axis_size(axis), lax.axis_index(axis))
    pieces = jax.tree.map(lambda part: lax.all_gather(part, axis), value)
    if backward:
        pieces = jax.tree.map(lambda part: part[::-1], pieces)
        mine = count - 1 - mine
    so_far = jax.tree.map(
        lambda part, zero: jnp.full_like(part, 0) + jnp.asarray(zero, part.dtype), value, neutral
    )

    def turn(position, so_far):
        longer = join(so_far, jax.tree.map(lambda part: part[position], pieces))
        return jax.tree.map(lambda new, old: jnp.where(position < mine, new, old), longer, so_far)

    return lax.fori_loop(0, count - 1, turn, so_far)


def narrow_convert(values):
    return values.astype(jnp.bfloat16)


def tensor_dot_plain(left, right):
    return jnp.dot(left, right, preferred_element_type=jnp.float32)


def flipped_dot(left, right):
    return lax.dot_general(
        left, right, (((0,), (0,)), ((), ())), preferred_element_type=jnp.float32
    )


def dot_against_flipped(left, right):
    return lax.dot_general(
        left, right, (((1,), (1,)), ((), ())), preferred_element_type=jnp.float32
    )


def affine_join(earlier, later):
    return (later[0] * earlier[0], later[0] * earlier[1] + later[1])


def layer_norm(values, gains, offsets):
    centred = values - jnp.mean(values, axis=-1, keepdims=True)
    spread = jnp.mean(centred * centred, axis=-1, keepdims=True)
    return centred * lax.rsqrt(spread + EPSILON) * gains + offsets


def gated_unit(pre_act):
    half_width = pre_act.shape[-1] // 2
    return pre_act[..., :half_width] * jax.nn.sigmoid(pre_act[..., half_width:])


def lstm_gates(pre_act, keep_mask):
    quarter = pre_act.shape[-1] // 4
    forget = jax.nn.sigmoid(pre_act[..., :quarter]) * keep_mask
    inflow = jax.nn.sigmoid(pre_act[..., quarter : 2 * quarter]) * jnp.tanh(
        pre_act[..., 2 * quarter : 3 * quarter]
    )
    out_gate = jax.nn.sigmoid(pre_act[..., 3 * quarter :])
    return (forget, inflow, out_gate)


def masked_scores(query_block, key_block, query_pos, key_pos, begin_block, scale):
    raw = jnp.einsum("gqhd,gkhd->ghqk", query_block, key_block, preferred_element_type=jnp.float32)
    lowest = jnp.minimum(begin_block[:, None], query_pos[None, :])
    allowed = (key_pos[None, None, :] <= query_pos[None, :, None]) & (
        key_pos[None, None, :] >= lowest[:, :, None]
    )
    return jnp.where(allowed[:, None], raw * scale, NEG_BIG)


def score_grad(chances, dprob, row_delta, scale):
    return narrow_convert(chances * (dprob[:, None] - row_delta[..., None]) * scale)


def shards(
    embedded_features,
    earliest_seen_moment,
    reach_choice,
    lstm_valve_coeffs,
    lstm_unit_coeffs,
    asker_lookup_coeffs,
    attend_exit_coeffs,
    attend_unit_coeffs,
    skipnet_entry_coeffs,
    skipnet_inner_coeffs,
    skipnet_unit_coeffs,
    level_map_coeffs,
    bias_gain_table,
    block_emit_adjoint,
    predicted_adjoint,
):
    (
        mat_lstm,
        mat_glu_one,
        mat_qkv,
        mat_attn,
        mat_glu_two,
        mat_inner,
        mat_middle,
        mat_glu_three,
        level_dot,
        vec_table,
    ) = (
        lax.all_gather(narrow_convert(lstm_valve_coeffs), "dp", axis=0, tiled=True),
        lax.all_gather(narrow_convert(lstm_unit_coeffs), "dp", axis=0, tiled=True),
        lax.all_gather(narrow_convert(asker_lookup_coeffs), "dp", axis=0, tiled=True),
        lax.all_gather(narrow_convert(attend_exit_coeffs), "dp", axis=0, tiled=True),
        lax.all_gather(narrow_convert(attend_unit_coeffs), "dp", axis=0, tiled=True),
        lax.all_gather(narrow_convert(skipnet_entry_coeffs), "dp", axis=0, tiled=True),
        lax.all_gather(narrow_convert(skipnet_inner_coeffs), "dp", axis=0, tiled=True),
        lax.all_gather(narrow_convert(skipnet_unit_coeffs), "dp", axis=0, tiled=True),
        lax.all_gather(narrow_convert(level_map_coeffs), "dp", axis=0, tiled=True),
        lax.all_gather(narrow_convert(bias_gain_table), "dp", axis=0, tiled=True),
    )
    series_per_device, steps_per_device, model_width = embedded_features.shape
    seq_total = steps_per_device * lax.axis_size("tm")
    head_width = model_width // HEADS
    count_of_rows = series_per_device * steps_per_device
    scale = head_width ** (-0.5)
    vec_full = vec_table.astype(jnp.float32)
    time_local = lax.axis_index("tm") * steps_per_device + jnp.arange(
        steps_per_device, dtype=jnp.int32
    )
    time_all = jnp.arange(seq_total, dtype=jnp.int32)
    horizon_len = jnp.where(reach_choice == 0, 1, jnp.where(reach_choice == 1, 5, 24))
    ahead_moment_filter = (
        (
            (time_local[None, :] >= seq_total - DEC)
            & (time_local[None, :] < seq_total - DEC + horizon_len[:, None])
        )
        .astype(jnp.float32)
        .reshape(count_of_rows, 1)
    )
    keep_mask = (
        (time_local[None, :] != earliest_seen_moment[:, None])
        .astype(jnp.float32)
        .reshape(count_of_rows, 1)
    )
    group_size = series_per_device // MICRO
    group_total = series_per_device // attend_group
    state_ones = jnp.ones((group_size, model_width), jnp.float32)
    state_zeros = jnp.zeros((group_size, model_width), jnp.float32)

    def split_groups(array):
        return array.reshape((group_total, attend_group) + array.shape[1:])

    input_rows = embedded_features.reshape(count_of_rows, model_width)
    input_full = input_rows.astype(jnp.float32)
    lstm_pre = tensor_dot_plain(input_rows, mat_lstm) + vec_full[:, 0:4].T.reshape(-1)
    forget, inflow, out_gate = lstm_gates(lstm_pre, keep_mask)
    forget_seq = forget.reshape(series_per_device, steps_per_device, model_width)
    inflow_seq = inflow.reshape(series_per_device, steps_per_device, model_width)
    mult_seq, cell_local = lax.associative_scan(affine_join, (forget_seq, inflow_seq), axis=1)
    cell_parts = []
    for group in range(MICRO):
        lower_row = group * group_size
        upper_row = lower_row + group_size
        _, arriving = entering(
            (mult_seq[lower_row:upper_row, -1], cell_local[lower_row:upper_row, -1]),
            "tm",
            affine_join,
            (state_ones, state_zeros),
            False,
        )
        cell_parts.append(arriving)
    cell_in = jnp.concatenate(cell_parts, axis=0)
    cell_seq = cell_local + mult_seq * cell_in[:, None, :]
    cell_tanh = jnp.tanh(cell_seq.reshape(count_of_rows, model_width))
    hidden_low = narrow_convert(out_gate * cell_tanh)
    glu_one_pre = tensor_dot_plain(hidden_low, mat_glu_one) + vec_full[:, 4:6].T.reshape(-1)
    first_sum = input_full + gated_unit(glu_one_pre)
    first = layer_norm(first_sum, vec_full[:, 6], vec_full[:, 7])
    first_low = narrow_convert(first)
    qkv_low = narrow_convert(tensor_dot_plain(first_low, mat_qkv))
    query_low = qkv_low[:, :model_width].reshape(
        series_per_device, steps_per_device, HEADS, head_width
    )
    key_value = qkv_low[:, model_width:].reshape(
        series_per_device, steps_per_device, model_width + head_width
    )
    key_value_all = lax.all_gather(key_value, "tm", axis=1, tiled=True)
    keys_all = key_value_all[..., :model_width].reshape(
        series_per_device, seq_total, HEADS, head_width
    )
    values_all = key_value_all[..., model_width:]

    def attend_forward(block_args):
        query_block, key_block, value_block, begin_block = block_args
        scores = masked_scores(query_block, key_block, time_local, time_all, begin_block, scale)
        row_top = jnp.max(scores, axis=-1, keepdims=True)
        row_exp = jnp.exp(scores - row_top)
        row_total = jnp.sum(row_exp, axis=-1, keepdims=True)
        weights_low = narrow_convert(row_exp / row_total)
        mixed_block = jnp.einsum(
            "ghqk,gkd->gqd", weights_low, value_block, preferred_element_type=jnp.float32
        ) * (1.0 / HEADS)
        return (mixed_block, (row_top + jnp.log(row_total))[..., 0])

    mixed, log_total = lax.map(
        attend_forward,
        (
            split_groups(query_low),
            split_groups(keys_all),
            split_groups(values_all),
            split_groups(earliest_seen_moment),
        ),
    )
    mixed_low = narrow_convert(mixed.reshape(count_of_rows, head_width))
    attn_low = narrow_convert(tensor_dot_plain(mixed_low, mat_attn))
    glu_two_pre = tensor_dot_plain(attn_low, mat_glu_two) + vec_full[:, 8:10].T.reshape(-1)
    second_sum = first + gated_unit(glu_two_pre)
    second = layer_norm(second_sum, vec_full[:, 10], vec_full[:, 11])
    second_low = narrow_convert(second)
    inner_pre = tensor_dot_plain(second_low, mat_inner) + vec_full[:, 12]
    inner_low = narrow_convert(jax.nn.elu(inner_pre))
    middle_low = narrow_convert(tensor_dot_plain(inner_low, mat_middle) + vec_full[:, 13])
    glu_three_pre = tensor_dot_plain(middle_low, mat_glu_three) + vec_full[:, 14:16].T.reshape(-1)
    final_sum = second + gated_unit(glu_three_pre)
    second_block_emit = layer_norm(final_sum, vec_full[:, 16], vec_full[:, 17])
    closing_narrowed = narrow_convert(second_block_emit)
    predicted_entries = tensor_dot_plain(closing_narrowed, level_dot) * ahead_moment_filter
    predicted_levels = predicted_entries.reshape(
        series_per_device, steps_per_device, LEVEL_TALLY
    ).transpose(0, 2, 1)
    predicted_slope = narrow_convert(
        predicted_adjoint.astype(jnp.float32).transpose(0, 2, 1).reshape(count_of_rows, LEVEL_TALLY)
        * ahead_moment_filter
    )
    level_slope = flipped_dot(closing_narrowed, predicted_slope)
    final_grad = block_emit_adjoint.reshape(count_of_rows, model_width).astype(
        jnp.float32
    ) + dot_against_flipped(predicted_slope, level_dot)
    _, norm_pull = jax.vjp(layer_norm, final_sum, vec_full[:, 16], vec_full[:, 17])
    sum_three_grad, gain_three_grad, offset_three_grad = norm_pull(final_grad)
    _, glu_pull = jax.vjp(gated_unit, glu_three_pre)
    (glu_three_grad,) = glu_pull(sum_three_grad)
    glu_three_low = narrow_convert(glu_three_grad)
    grad_glu_three = flipped_dot(middle_low, glu_three_low)
    middle_grad = dot_against_flipped(glu_three_low, mat_glu_three)
    middle_grad_low = narrow_convert(middle_grad)
    grad_middle = flipped_dot(inner_low, middle_grad_low)
    inner_grad = dot_against_flipped(middle_grad_low, mat_middle)
    _, elu_pull = jax.vjp(jax.nn.elu, inner_pre)
    (inner_pre_grad,) = elu_pull(inner_grad)
    inner_pre_low = narrow_convert(inner_pre_grad)
    grad_inner = flipped_dot(second_low, inner_pre_low)
    second_grad = sum_three_grad + dot_against_flipped(inner_pre_low, mat_inner)
    _, norm_pull = jax.vjp(layer_norm, second_sum, vec_full[:, 10], vec_full[:, 11])
    sum_two_grad, gain_two_grad, offset_two_grad = norm_pull(second_grad)
    _, glu_pull = jax.vjp(gated_unit, glu_two_pre)
    (glu_two_grad,) = glu_pull(sum_two_grad)
    glu_two_low = narrow_convert(glu_two_grad)
    grad_glu_two = flipped_dot(attn_low, glu_two_low)
    attn_grad_low = narrow_convert(dot_against_flipped(glu_two_low, mat_glu_two))
    grad_attn = flipped_dot(mixed_low, attn_grad_low)
    mixed_grad_low = narrow_convert(dot_against_flipped(attn_grad_low, mat_attn))
    head_grad = (mixed_grad_low * (1.0 / HEADS)).reshape(
        series_per_device, steps_per_device, head_width
    )

    def attend_backward(block_args):
        query_block, key_block, value_block, begin_block, lse_block, dout_block = block_args
        scores = masked_scores(query_block, key_block, time_local, time_all, begin_block, scale)
        chances = jnp.exp(scores - lse_block[..., None])
        dprob = jnp.einsum(
            "gqd,gkd->gqk", dout_block, value_block, preferred_element_type=jnp.float32
        )
        row_delta = jnp.sum(chances * dprob[:, None], axis=-1)
        dscore = score_grad(chances, dprob, row_delta, scale)
        dquery = jnp.einsum(
            "ghqk,gkhd->gqhd", dscore, key_block, preferred_element_type=jnp.float32
        )
        dkey = jnp.einsum(
            "ghqk,gqhd->gkhd", dscore, query_block, preferred_element_type=jnp.float32
        )
        dvalue = jnp.einsum(
            "ghqk,gqd->gkd", narrow_convert(chances), dout_block, preferred_element_type=jnp.float32
        )
        key_terms = jnp.concatenate(
            [dkey.reshape(attend_group, seq_total, model_width), dvalue], axis=-1
        )
        return (dquery, key_terms)

    dquery, key_terms = lax.map(
        attend_backward,
        (
            split_groups(query_low),
            split_groups(keys_all),
            split_groups(values_all),
            split_groups(earliest_seen_moment),
            log_total,
            split_groups(head_grad),
        ),
    )
    own_keys = lax.psum_scatter(
        key_terms.reshape(series_per_device, seq_total, model_width + head_width),
        "tm",
        scatter_dimension=1,
        tiled=True,
    )
    qkv_grad = jnp.concatenate(
        [
            dquery.reshape(count_of_rows, model_width),
            own_keys.reshape(count_of_rows, model_width + head_width),
        ],
        axis=1,
    )
    qkv_grad_low = narrow_convert(qkv_grad)
    grad_qkv = flipped_dot(first_low, qkv_grad_low)
    first_grad = sum_two_grad + dot_against_flipped(qkv_grad_low, mat_qkv)
    _, norm_pull = jax.vjp(layer_norm, first_sum, vec_full[:, 6], vec_full[:, 7])
    sum_one_grad, gain_one_grad, offset_one_grad = norm_pull(first_grad)
    _, glu_pull = jax.vjp(gated_unit, glu_one_pre)
    (glu_one_grad,) = glu_pull(sum_one_grad)
    glu_one_low = narrow_convert(glu_one_grad)
    grad_glu_one = flipped_dot(hidden_low, glu_one_low)
    hidden_grad = dot_against_flipped(glu_one_low, mat_glu_one)
    out_gate_grad = hidden_grad * cell_tanh
    direct_grad = (hidden_grad * out_gate * (1.0 - cell_tanh * cell_tanh)).reshape(
        series_per_device, steps_per_device, model_width
    )
    next_forget = jnp.concatenate([forget_seq[:, 1:], jnp.ones_like(forget_seq[:, :1])], axis=1)
    rev_mult, rev_cell = lax.associative_scan(
        affine_join, (next_forget, direct_grad), axis=1, reverse=True
    )
    head_mult = forget_seq[:, 0] * rev_mult[:, 0]
    head_cell = forget_seq[:, 0] * rev_cell[:, 0]
    coming_parts = []
    for group in range(MICRO):
        lower_row = group * group_size
        upper_row = lower_row + group_size
        _, coming = entering(
            (head_mult[lower_row:upper_row], head_cell[lower_row:upper_row]),
            "tm",
            affine_join,
            (state_ones, state_zeros),
            True,
        )
        coming_parts.append(coming)
    coming_all = jnp.concatenate(coming_parts, axis=0)
    cell_grad = rev_cell + rev_mult * coming_all[:, None, :]
    cell_prev = jnp.concatenate([cell_in[:, None, :], cell_seq[:, :-1]], axis=1)
    forget_grad = (cell_grad * cell_prev).reshape(count_of_rows, model_width)
    _, gate_pull = jax.vjp(lambda pre_value: lstm_gates(pre_value, keep_mask), lstm_pre)
    (lstm_pre_grad,) = gate_pull(
        (forget_grad, cell_grad.reshape(count_of_rows, model_width), out_gate_grad)
    )
    lstm_low = narrow_convert(lstm_pre_grad)
    grad_lstm = flipped_dot(input_rows, lstm_low)
    input_grad = sum_one_grad + dot_against_flipped(lstm_low, mat_lstm)
    grad_table = jnp.concatenate(
        [
            jnp.sum(lstm_pre_grad, axis=0).reshape(4, model_width).T,
            jnp.sum(glu_one_grad, axis=0).reshape(2, model_width).T,
            gain_one_grad[:, None],
            offset_one_grad[:, None],
            jnp.sum(glu_two_grad, axis=0).reshape(2, model_width).T,
            gain_two_grad[:, None],
            offset_two_grad[:, None],
            jnp.sum(inner_pre_grad, axis=0)[:, None],
            jnp.sum(middle_grad, axis=0)[:, None],
            jnp.sum(glu_three_grad, axis=0).reshape(2, model_width).T,
            gain_three_grad[:, None],
            offset_three_grad[:, None],
        ],
        axis=1,
    )
    (
        whole_lstm,
        whole_glu_one,
        whole_qkv,
        whole_attn,
        whole_glu_two,
        whole_inner,
        whole_middle,
        whole_glu_three,
        whole_quant,
        whole_table,
    ) = lax.psum(
        (
            grad_lstm,
            grad_glu_one,
            grad_qkv,
            grad_attn,
            grad_glu_two,
            grad_inner,
            grad_middle,
            grad_glu_three,
            level_slope,
            grad_table,
        ),
        "tm",
    )
    summed = (
        lax.psum_scatter(
            whole_lstm.astype(jnp.bfloat16), "dp", scatter_dimension=0, tiled=True
        ).astype(jnp.float32),
        lax.psum_scatter(
            whole_glu_one.astype(jnp.bfloat16), "dp", scatter_dimension=0, tiled=True
        ).astype(jnp.float32),
        lax.psum_scatter(
            whole_qkv.astype(jnp.bfloat16), "dp", scatter_dimension=0, tiled=True
        ).astype(jnp.float32),
        lax.psum_scatter(
            whole_attn.astype(jnp.bfloat16), "dp", scatter_dimension=0, tiled=True
        ).astype(jnp.float32),
        lax.psum_scatter(
            whole_glu_two.astype(jnp.bfloat16), "dp", scatter_dimension=0, tiled=True
        ).astype(jnp.float32),
        lax.psum_scatter(
            whole_inner.astype(jnp.bfloat16), "dp", scatter_dimension=0, tiled=True
        ).astype(jnp.float32),
        lax.psum_scatter(
            whole_middle.astype(jnp.bfloat16), "dp", scatter_dimension=0, tiled=True
        ).astype(jnp.float32),
        lax.psum_scatter(
            whole_glu_three.astype(jnp.bfloat16), "dp", scatter_dimension=0, tiled=True
        ).astype(jnp.float32),
        lax.psum_scatter(
            whole_quant.astype(jnp.bfloat16), "dp", scatter_dimension=0, tiled=True
        ).astype(jnp.float32),
        lax.psum_scatter(
            whole_table.astype(jnp.bfloat16), "dp", scatter_dimension=0, tiled=True
        ).astype(jnp.float32),
    )
    final_out = second_block_emit.astype(jnp.bfloat16).reshape(
        series_per_device, steps_per_device, model_width
    )
    input_out = input_grad.astype(jnp.bfloat16).reshape(
        series_per_device, steps_per_device, model_width
    )
    return (
        final_out,
        predicted_levels,
        input_out,
        summed[0],
        summed[1],
        summed[2],
        summed[3],
        summed[4],
        summed[5],
        summed[6],
        summed[7],
        summed[8],
        summed[9],
    )


def lane_head(shape, head_width, head):
    lane = lax.broadcasted_iota(jnp.int32, shape, len(shape) - 1)
    return (lane >= head * head_width) & (lane < (head + 1) * head_width)


FORGET, ENTER, CANDIDATE, EXIT = 0, 256, 512, 768
GLU_ONE_A, GLU_ONE_B = 1024, 1280
QUERY, KEY, VALUE = 1536, 1792, 2048
GLU_TWO_A, GLU_TWO_B = 2176, 2432
INNER, MIDDLE = 2688, 2944
GLU_THREE_A, GLU_THREE_B = 3200, 3456
ATTN_OUT = 3712
PACKED = 3968
VECTORS = 24
LANES = 128
CHUNKS = 8
TILE = 256


def nn(left, right):
    return jnp.dot(left, right, preferred_element_type=jnp.float32)


def nt(left, right):
    return lax.dot_general(
        left, right, (((1,), (1,)), ((), ())), preferred_element_type=jnp.float32
    )


def tn(left, right):
    return lax.dot_general(
        left, right, (((0,), (0,)), ((), ())), preferred_element_type=jnp.float32
    )


def low(values):
    return values.astype(jnp.bfloat16)


def sigmoid(values):
    return 0.5 * jnp.tanh(0.5 * values) + 0.5


def normalise(values, gain, shift):
    centred = values - jnp.mean(values, axis=-1, keepdims=True)
    spread = jnp.mean(centred * centred, axis=-1, keepdims=True)
    inverse = lax.rsqrt(spread + EPSILON)
    unit = centred * inverse
    return unit * gain + shift, unit, inverse


def normalise_back(grad, unit, inverse, gain):
    scaled = grad * gain
    return inverse * (
        scaled
        - jnp.mean(scaled, axis=-1, keepdims=True)
        - unit * jnp.mean(scaled * unit, axis=-1, keepdims=True)
    )


def rows_of(tile, size=TILE):
    return pl.ds(pl.multiple_of(tile * size, size), size)


def put_halves(ref, rows, values):
    ref[0, rows, :] = values[:, :LANES]
    ref[1, rows, : values.shape[1] - LANES] = values[:, LANES:]


def get_halves(ref, rows, width):
    return jnp.concatenate([ref[0, rows, :], ref[1, rows, : width - LANES]], axis=1)


def row_sum(ref, column, values):
    ref[column : column + 1, :] += jnp.sum(values, axis=0, keepdims=True)


def series_scratch(span, width, head_width):
    full = pltpu.VMEM((span, width), jnp.float32)
    half = pltpu.VMEM((span, width), jnp.bfloat16)
    scan = pltpu.VMEM((2, span, LANES), jnp.float32)
    scan_more = pltpu.VMEM((2, span + 8, LANES), jnp.float32)
    narrow = pltpu.VMEM((span, head_width), jnp.bfloat16)
    column = pltpu.VMEM((span, 1), jnp.float32)
    return dict(
        forget=scan_more,
        local=scan,
        mult=scan,
        cell=scan_more,
        carry=pltpu.VMEM((2, CHUNKS, LANES), jnp.float32),
        enter_gate=full,
        candidate=full,
        exit_gate=full,
        cell_tanh=full,
        hidden=half,
        glu_one=full,
        gate_one=full,
        unit_one=full,
        inverse_one=column,
        first_low=half,
        queries=half,
        keys=half,
        values=narrow,
        head_queries=pltpu.VMEM((HEADS, span, width), jnp.bfloat16),
        head_keys=pltpu.VMEM((HEADS, span, width), jnp.bfloat16),
        chances=pltpu.VMEM((HEADS, span, span), jnp.float32),
        chance_sum=pltpu.VMEM((span, span), jnp.bfloat16),
        score_grads=pltpu.VMEM((HEADS, span, span), jnp.bfloat16),
        block=pltpu.VMEM((TILE, span), jnp.float32),
        mixed=narrow,
        mixed_grad=narrow,
        sum_two_grad=full,
        query_grad=half,
        key_grad=half,
        value_grad=narrow,
        exit_grad=half,
    )


def series_forward_lstm(r, w, vec, x_ref, begin):
    span, width = x_ref.shape

    def gates(tile, _):
        rows = rows_of(tile)
        x = x_ref[rows, :]

        def pre(block, column):
            return nn(x, w[:, block : block + width]) + vec[column : column + 1, :]

        time = tile * TILE + lax.broadcasted_iota(jnp.int32, (TILE, width), 0)
        forget = jnp.where(time != begin, sigmoid(pre(FORGET, 0)), 0.0)
        enter = sigmoid(pre(ENTER, 1))
        candidate = jnp.tanh(pre(CANDIDATE, 2))
        r.enter_gate[rows, :] = enter
        r.candidate[rows, :] = candidate
        r.exit_gate[rows, :] = sigmoid(pre(EXIT, 3))
        put_halves(r.forget, rows, forget)
        put_halves(r.local, rows, enter * candidate)
        return 0

    lax.fori_loop(0, span // TILE, gates, 0)
    steps = span // CHUNKS
    zeros = jnp.zeros((CHUNKS, LANES), jnp.float32)

    def step(t, state):
        out = []
        at = pl.ds(t, CHUNKS, stride=steps)
        for half in range(2):
            cell, mult = state[half]
            forget = r.forget[half, at, :]
            cell = forget * cell + r.local[half, at, :]
            mult = mult * forget
            r.local[half, at, :] = cell
            r.mult[half, at, :] = mult
            out.append((cell, mult))
        return tuple(out)

    ends = lax.fori_loop(0, steps, step, ((zeros, zeros + 1.0),) * 2, unroll=8)
    for half in range(2):
        cells, mults = ends[half]
        state = jnp.zeros((1, LANES), jnp.float32)
        r.carry[half, 0:1, :] = state
        for chunk in range(CHUNKS - 1):
            state = cells[chunk : chunk + 1] + mults[chunk : chunk + 1] * state
            r.carry[half, chunk + 1 : chunk + 2, :] = state
        r.cell[half, 0:8, :] = zeros


def series_forward_first(r, w, vec, x_ref):
    span, width = x_ref.shape
    head_width = width // HEADS
    steps = span // CHUNKS

    def cells(chunk, _):
        rows = rows_of(chunk, steps)
        later = pl.ds(pl.multiple_of(chunk * steps + 8, 8), steps)
        for half in range(2):
            r.cell[half, later, :] = r.local[half, rows, :] + r.mult[half, rows, :] * r.carry[
                half, pl.ds(chunk, 1), :
            ]
        tanh = jnp.tanh(get_halves(r.cell, later, width))
        r.cell_tanh[rows, :] = tanh
        r.hidden[rows, :] = low(r.exit_gate[rows, :] * tanh)
        return 0

    lax.fori_loop(0, CHUNKS, cells, 0)

    def first(tile, _):
        rows = rows_of(tile)
        hidden = r.hidden[rows, :]
        value = nn(hidden, w[:, GLU_ONE_A : GLU_ONE_A + width]) + vec[4:5, :]
        gate = sigmoid(nn(hidden, w[:, GLU_ONE_B : GLU_ONE_B + width]) + vec[5:6, :])
        r.glu_one[rows, :] = value
        r.gate_one[rows, :] = gate
        out, unit, inverse = normalise(
            x_ref[rows, :].astype(jnp.float32) + value * gate, vec[6:7, :], vec[7:8, :]
        )
        r.unit_one[rows, :] = unit
        r.inverse_one[rows, :] = inverse
        out = low(out)
        r.first_low[rows, :] = out
        query = low(nn(out, w[:, QUERY : QUERY + width]))
        key = low(nn(out, w[:, KEY : KEY + width]))
        r.keys[rows, :] = key
        r.values[rows, :] = low(nn(out, w[:, VALUE : VALUE + head_width]))
        for head in range(HEADS):
            mine = lane_head((TILE, width), head_width, head)
            r.head_queries[head, rows, :] = jnp.where(mine, query, jnp.zeros_like(query))
            r.head_keys[head, rows, :] = jnp.where(mine, key, jnp.zeros_like(key))
        return 0

    lax.fori_loop(0, span // TILE, first, 0)


def series_forward_attention(r, begin):
    span, head_width = r.values.shape
    scale = head_width ** (-0.5) * LOG2_E
    for tile in range(span // TILE):
        rows = slice(tile * TILE, (tile + 1) * TILE)
        seen = (tile + 1) * TILE
        row = tile * TILE + lax.broadcasted_iota(jnp.int32, (TILE, seen), 0)
        col = lax.broadcasted_iota(jnp.int32, (TILE, seen), 1)
        r.block[:, :seen] = jnp.where(
            (col <= row) & (col >= jnp.minimum(begin, row)), 0.0, NEG_BIG
        )

        def one_head(head, _):
            scores = (
                nt(r.head_queries[head, rows, :], r.keys[:seen, :]) * scale + r.block[:, :seen]
            )
            top = jnp.max(scores, axis=-1, keepdims=True)
            raised = jnp.exp2(scores - top)
            total = jnp.sum(raised, axis=-1, keepdims=True)
            r.chances[head, rows, :seen] = raised * (1.0 / total)
            return 0

        lax.fori_loop(0, HEADS, one_head, 0)
        weights = r.chances[0, rows, :seen]
        for head in range(1, HEADS):
            weights = weights + r.chances[head, rows, :seen]
        weights = low(weights)
        r.chance_sum[rows, :seen] = weights
        r.mixed[rows, :] = low(nn(weights, r.values[:seen, :]) * (1.0 / HEADS))


def series_middle(r, w, vec, level, adjoint_ref, slope_ref, horizon, out_ref, predicted_ref, g, gv):
    span, width = out_ref.shape
    head_width = width // HEADS

    def middle(tile, last):
        rows = rows_of(tile)
        first = r.unit_one[rows, :] * vec[6:7, :] + vec[7:8, :]
        mixed = r.mixed[rows, :]
        attn = low(nn(mixed, w[:head_width, ATTN_OUT : ATTN_OUT + width]))
        value_two = nn(attn, w[:, GLU_TWO_A : GLU_TWO_A + width]) + vec[8:9, :]
        gate_two = sigmoid(nn(attn, w[:, GLU_TWO_B : GLU_TWO_B + width]) + vec[9:10, :])
        second, unit_two, inverse_two = normalise(
            first + value_two * gate_two, vec[10:11, :], vec[11:12, :]
        )
        second_low = low(second)
        inner_pre = nn(second_low, w[:, INNER : INNER + width]) + vec[12:13, :]
        inner_exp = jnp.exp(jnp.minimum(inner_pre, 0.0))
        inner_low = low(jnp.where(inner_pre > 0, inner_pre, inner_exp - 1.0))
        middle_low = low(nn(inner_low, w[:, MIDDLE : MIDDLE + width]) + vec[13:14, :])
        value_three = nn(middle_low, w[:, GLU_THREE_A : GLU_THREE_A + width]) + vec[14:15, :]
        gate_three = sigmoid(
            nn(middle_low, w[:, GLU_THREE_B : GLU_THREE_B + width]) + vec[15:16, :]
        )
        final, unit_three, inverse_three = normalise(
            second + value_three * gate_three, vec[16:17, :], vec[17:18, :]
        )
        final_low = low(final)
        out_ref[rows, :] = final_low
        grad = adjoint_ref[rows, :].astype(jnp.float32)
        if last:
            start = span - TILE
            time = start + lax.broadcasted_iota(jnp.int32, (8, TILE), 1)
            ahead = jnp.where((time >= span - DEC) & (time < span - DEC + horizon), 1.0, 0.0)
            predicted_ref[:, :start] = jnp.zeros((8, start), jnp.float32)
            predicted_ref[:, start:] = nt(level[...], final_low) * ahead
            slope = low(slope_ref[:, start:].astype(jnp.float32) * ahead)
            gv[VECTORS:, :] = nn(slope, final_low)
            grad = grad + tn(slope, level[...])
        row_sum(gv, 16, grad * unit_three)
        row_sum(gv, 17, grad)
        sum_three = normalise_back(grad, unit_three, inverse_three, vec[16:17, :])
        grad_a = sum_three * gate_three
        grad_b = grad_a * value_three * (1.0 - gate_three)
        row_sum(gv, 14, grad_a)
        row_sum(gv, 15, grad_b)
        low_a, low_b = low(grad_a), low(grad_b)
        g[:, GLU_THREE_A : GLU_THREE_A + width] += tn(middle_low, low_a)
        g[:, GLU_THREE_B : GLU_THREE_B + width] += tn(middle_low, low_b)
        middle_grad = nt(low_a, w[:, GLU_THREE_A : GLU_THREE_A + width]) + nt(
            low_b, w[:, GLU_THREE_B : GLU_THREE_B + width]
        )
        row_sum(gv, 13, middle_grad)
        middle_grad = low(middle_grad)
        g[:, MIDDLE : MIDDLE + width] += tn(inner_low, middle_grad)
        inner_grad = nt(middle_grad, w[:, MIDDLE : MIDDLE + width]) * jnp.where(
            inner_pre > 0, 1.0, inner_exp
        )
        row_sum(gv, 12, inner_grad)
        inner_grad = low(inner_grad)
        g[:, INNER : INNER + width] += tn(second_low, inner_grad)
        grad = sum_three + nt(inner_grad, w[:, INNER : INNER + width])
        row_sum(gv, 10, grad * unit_two)
        row_sum(gv, 11, grad)
        sum_two = normalise_back(grad, unit_two, inverse_two, vec[10:11, :])
        r.sum_two_grad[rows, :] = sum_two
        grad_a = sum_two * gate_two
        grad_b = grad_a * value_two * (1.0 - gate_two)
        row_sum(gv, 8, grad_a)
        row_sum(gv, 9, grad_b)
        low_a, low_b = low(grad_a), low(grad_b)
        g[:, GLU_TWO_A : GLU_TWO_A + width] += tn(attn, low_a)
        g[:, GLU_TWO_B : GLU_TWO_B + width] += tn(attn, low_b)
        attn_grad = low(
            nt(low_a, w[:, GLU_TWO_A : GLU_TWO_A + width])
            + nt(low_b, w[:, GLU_TWO_B : GLU_TWO_B + width])
        )
        g[:head_width, ATTN_OUT : ATTN_OUT + width] += tn(mixed, attn_grad)
        r.mixed_grad[rows, :] = low(nt(attn_grad, w[:head_width, ATTN_OUT : ATTN_OUT + width]))
        return 0

    lax.fori_loop(0, span // TILE - 1, lambda tile, _: middle(tile, False), 0)
    middle(span // TILE - 1, True)


def series_backward_attention(r):
    span, head_width = r.values.shape
    width = head_width * HEADS
    scale = head_width ** (-0.5)
    for tile in range(span // TILE):
        rows = slice(tile * TILE, (tile + 1) * TILE)
        seen = (tile + 1) * TILE
        head_grad = r.mixed_grad[rows, :] * (1.0 / HEADS)
        r.block[:, :seen] = nt(head_grad, r.values[:seen, :]) * scale

        def one_head(head, total):
            chances = r.chances[head, rows, :seen]
            slope = r.block[:, :seen]
            delta = jnp.sum(chances * slope, axis=-1, keepdims=True)
            grads = low(chances * (slope - delta))
            r.score_grads[head, rows, :seen] = grads
            return total + nn(grads, r.head_keys[head, :seen, :])

        r.query_grad[rows, :] = low(
            lax.fori_loop(0, HEADS, one_head, jnp.zeros((TILE, width), jnp.float32))
        )
    for tile in range(span // TILE):
        cols = slice(tile * TILE, (tile + 1) * TILE)
        start = tile * TILE

        def one_key(head, total):
            return total + tn(
                r.score_grads[head, start:, cols], r.head_queries[head, start:, :]
            )

        r.key_grad[cols, :] = low(
            lax.fori_loop(0, HEADS, one_key, jnp.zeros((TILE, width), jnp.float32))
        )
        r.value_grad[cols, :] = low(
            tn(r.chance_sum[start:, cols], r.mixed_grad[start:, :] * (1.0 / HEADS))
        )


def series_backward_first(r, w, vec, g, gv):
    span, width = r.hidden.shape
    head_width = width // HEADS

    def back(tile, _):
        rows = rows_of(tile)
        query, key, value = r.query_grad[rows, :], r.key_grad[rows, :], r.value_grad[rows, :]
        grad = (
            r.sum_two_grad[rows, :]
            + nt(query, w[:, QUERY : QUERY + width])
            + nt(key, w[:, KEY : KEY + width])
            + nt(value, w[:, VALUE : VALUE + head_width])
        )
        first = r.first_low[rows, :]
        g[:, QUERY : QUERY + width] += tn(first, query)
        g[:, KEY : KEY + width] += tn(first, key)
        g[:, VALUE : VALUE + head_width] += tn(first, value)
        unit = r.unit_one[rows, :]
        row_sum(gv, 6, grad * unit)
        row_sum(gv, 7, grad)
        sum_one = normalise_back(grad, unit, r.inverse_one[rows, :], vec[6:7, :])
        r.sum_two_grad[rows, :] = sum_one
        gate = r.gate_one[rows, :]
        grad_a = sum_one * gate
        grad_b = grad_a * r.glu_one[rows, :] * (1.0 - gate)
        row_sum(gv, 4, grad_a)
        row_sum(gv, 5, grad_b)
        low_a, low_b = low(grad_a), low(grad_b)
        hidden = r.hidden[rows, :]
        g[:, GLU_ONE_A : GLU_ONE_A + width] += tn(hidden, low_a)
        g[:, GLU_ONE_B : GLU_ONE_B + width] += tn(hidden, low_b)
        hidden_grad = nt(low_a, w[:, GLU_ONE_A : GLU_ONE_A + width]) + nt(
            low_b, w[:, GLU_ONE_B : GLU_ONE_B + width]
        )
        tanh, gate = r.cell_tanh[rows, :], r.exit_gate[rows, :]
        put_halves(r.local, rows, hidden_grad * gate * (1.0 - tanh * tanh))
        exit_grad = hidden_grad * tanh * gate * (1.0 - gate)
        row_sum(gv, 3, exit_grad)
        r.exit_grad[rows, :] = low(exit_grad)
        return 0

    lax.fori_loop(0, span // TILE, back, 0)


def series_backward_lstm(r, w, x_ref, input_grad_ref, g, gv):
    span, width = x_ref.shape
    steps = span // CHUNKS
    zeros = jnp.zeros((CHUNKS, LANES), jnp.float32)
    for half in range(2):
        r.forget[half, span:, :] = zeros

    def step(count, state):
        t = steps - 1 - count
        out = []
        at, after = pl.ds(t, CHUNKS, stride=steps), pl.ds(t + 1, CHUNKS, stride=steps)
        for half in range(2):
            grad, mult = state[half]
            forget = r.forget[half, after, :]
            grad = forget * grad + r.local[half, at, :]
            mult = mult * forget
            r.local[half, at, :] = grad
            r.mult[half, at, :] = mult
            out.append((grad, mult))
        return tuple(out)

    ends = lax.fori_loop(0, steps, step, ((zeros, zeros + 1.0),) * 2, unroll=8)
    for half in range(2):
        grads, mults = ends[half]
        state = jnp.zeros((1, LANES), jnp.float32)
        r.carry[half, CHUNKS - 1 : CHUNKS, :] = state
        for chunk in range(CHUNKS - 1, 0, -1):
            state = grads[chunk : chunk + 1] + mults[chunk : chunk + 1] * state
            r.carry[half, chunk - 1 : chunk, :] = state

    def back(chunk, _):
        rows = rows_of(chunk, steps)
        before = pl.ds(chunk * steps + 7, steps)
        grad, grad_forget = [], []
        for half in range(2):
            one = r.local[half, rows, :] + r.mult[half, rows, :] * r.carry[
                half, pl.ds(chunk, 1), :
            ]
            forget = r.forget[half, rows, :]
            grad.append(one)
            grad_forget.append(one * r.cell[half, before, :] * forget * (1.0 - forget))
        grad = jnp.concatenate([grad[0], grad[1][:, : width - LANES]], axis=1)
        grad_forget = jnp.concatenate([grad_forget[0], grad_forget[1][:, : width - LANES]], axis=1)
        enter, candidate = r.enter_gate[rows, :], r.candidate[rows, :]
        grad_enter = grad * candidate * enter * (1.0 - enter)
        grad_candidate = grad * enter * (1.0 - candidate * candidate)
        row_sum(gv, 0, grad_forget)
        row_sum(gv, 1, grad_enter)
        row_sum(gv, 2, grad_candidate)
        x = x_ref[rows, :]
        out = r.sum_two_grad[rows, :]
        for block, one in (
            (FORGET, low(grad_forget)),
            (ENTER, low(grad_enter)),
            (CANDIDATE, low(grad_candidate)),
            (EXIT, r.exit_grad[rows, :]),
        ):
            g[:, block : block + width] += tn(x, one)
            out = out + nt(one, w[:, block : block + width])
        input_grad_ref[rows, :] = low(out)
        return 0

    lax.fori_loop(0, CHUNKS, back, 0)


def series_kernel(
    scalars,
    x_ref,
    adjoint_ref,
    slope_ref,
    w,
    vec,
    level,
    out_ref,
    predicted_ref,
    input_grad_ref,
    g,
    gv,
    *scratch,
):
    span, width = x_ref.shape
    names = series_scratch(span, width, width // HEADS)
    r = types.SimpleNamespace(**dict(zip(names, scratch)))
    begin, horizon = scalars[0], scalars[1]
    g[...] = jnp.zeros_like(g)
    gv[...] = jnp.zeros_like(gv)
    series_forward_lstm(r, w, vec, x_ref, begin)
    series_forward_first(r, w, vec, x_ref)
    series_forward_attention(r, begin)
    series_middle(
        r, w, vec, level, adjoint_ref, slope_ref, horizon, out_ref, predicted_ref, g, gv
    )
    series_backward_attention(r)
    series_backward_first(r, w, vec, g, gv)
    series_backward_lstm(r, w, x_ref, input_grad_ref, g, gv)


def pack_weights(parts, width):
    (lstm, glu_one, qkv, glu_two, inner, middle, glu_three) = parts
    half = 2 * LANES

    def spread(array, block):
        return [
            jnp.pad(array[:, at : at + block], ((0, 0), (0, half - block)))
            for at in range(0, array.shape[1], block)
        ]

    pieces = spread(lstm, width) + spread(glu_one, width) + spread(qkv[:, : 2 * width], width)
    pieces.append(jnp.pad(qkv[:, 2 * width :], ((0, 0), (0, LANES - (qkv.shape[1] - 2 * width)))))
    pieces += spread(glu_two, width) + spread(inner, width) + spread(middle, width)
    pieces += spread(glu_three, width)
    return jnp.concatenate(pieces, axis=1)


def whole_series(
    embedded_features,
    earliest_seen_moment,
    reach_choice,
    lstm_valve_coeffs,
    lstm_unit_coeffs,
    asker_lookup_coeffs,
    attend_exit_coeffs,
    attend_unit_coeffs,
    skipnet_entry_coeffs,
    skipnet_inner_coeffs,
    skipnet_unit_coeffs,
    level_map_coeffs,
    bias_gain_table,
    block_emit_adjoint,
    predicted_adjoint,
):
    count, steps, width = embedded_features.shape
    span = count * steps
    head_width = width // HEADS
    mine = lax.axis_index("tm")

    def to_series(array, axis):
        return lax.all_to_all(array, "tm", split_axis=0, concat_axis=axis, tiled=True)

    def to_time(array, axis):
        return lax.all_to_all(array, "tm", split_axis=axis, concat_axis=0, tiled=True)

    x = to_series(embedded_features, 1)[0]
    adjoint = to_series(block_emit_adjoint, 1)[0]
    slope = jnp.pad(to_series(predicted_adjoint, 2)[0], ((0, 8 - LEVEL_TALLY), (0, 0)))
    packed = pack_weights(
        [
            narrow_convert(array)
            for array in (
                lstm_valve_coeffs,
                lstm_unit_coeffs,
                asker_lookup_coeffs,
                attend_unit_coeffs,
                skipnet_entry_coeffs,
                skipnet_inner_coeffs,
                skipnet_unit_coeffs,
            )
        ],
        width,
    )
    packed = lax.all_gather(packed, "dp", axis=0, tiled=True)
    attn_out = lax.all_gather(narrow_convert(attend_exit_coeffs), "dp", axis=0, tiled=True)
    packed = jnp.concatenate(
        [
            packed,
            jnp.pad(attn_out, ((0, width - head_width), (0, PACKED - ATTN_OUT - width))),
        ],
        axis=1,
    )
    columns = lax.all_gather(
        narrow_convert(jnp.concatenate([bias_gain_table, level_map_coeffs], axis=1)),
        "dp",
        axis=0,
        tiled=True,
    )
    vectors = bias_gain_table.shape[1]
    vec = jnp.pad(columns[:, :vectors].astype(jnp.float32).T, ((0, VECTORS - vectors), (0, 0)))
    level = jnp.pad(columns[:, vectors:].T, ((0, 8 - LEVEL_TALLY), (0, 0)))
    begin = earliest_seen_moment[mine]
    choice = reach_choice[mine]
    horizon = jnp.where(choice == 0, 1, jnp.where(choice == 1, 5, 24))
    out, predicted, input_grad, g, gv = pl.pallas_call(
        series_kernel,
        out_shape=(
            jax.ShapeDtypeStruct((span, width), jnp.bfloat16),
            jax.ShapeDtypeStruct((8, span), jnp.float32),
            jax.ShapeDtypeStruct((span, width), jnp.bfloat16),
            jax.ShapeDtypeStruct((width, PACKED), jnp.float32),
            jax.ShapeDtypeStruct((VECTORS + 8, width), jnp.float32),
        ),
        in_specs=[pl.BlockSpec(memory_space=pltpu.SMEM)]
        + [pl.BlockSpec(memory_space=pltpu.VMEM)] * 6,
        out_specs=(pl.BlockSpec(memory_space=pltpu.VMEM),) * 5,
        scratch_shapes=list(series_scratch(span, width, head_width).values()),
        compiler_params=pltpu.CompilerParams(vmem_limit_bytes=VMEM_BYTES),
    )(jnp.stack([begin, horizon]), x, adjoint, slope, packed, vec, level)
    emitted = to_time(out[None], 1)
    input_out = to_time(input_grad[None], 1)
    levels = to_time(predicted[None, :LEVEL_TALLY], 2)
    vector_columns = gv.T
    whole = lax.psum(
        jnp.concatenate([g[:, :ATTN_OUT], vector_columns], axis=1), "tm"
    )
    whole = lax.psum_scatter(
        whole.astype(jnp.bfloat16), "dp", scatter_dimension=0, tiled=True
    ).astype(jnp.float32)
    attn_whole = lax.psum_scatter(
        lax.psum(g[:head_width, ATTN_OUT : ATTN_OUT + width], "tm").astype(jnp.bfloat16),
        "dp",
        scatter_dimension=0,
        tiled=True,
    ).astype(jnp.float32)

    def gather(*starts):
        return jnp.concatenate([whole[:, at : at + width] for at in starts], axis=1)

    return (
        emitted,
        levels,
        input_out,
        gather(FORGET, ENTER, CANDIDATE, EXIT),
        gather(GLU_ONE_A, GLU_ONE_B),
        jnp.concatenate([gather(QUERY, KEY), whole[:, VALUE : VALUE + head_width]], axis=1),
        attn_whole,
        gather(GLU_TWO_A, GLU_TWO_B),
        whole[:, INNER : INNER + width],
        whole[:, MIDDLE : MIDDLE + width],
        gather(GLU_THREE_A, GLU_THREE_B),
        whole[:, ATTN_OUT + VECTORS : ATTN_OUT + VECTORS + LEVEL_TALLY],
        whole[:, ATTN_OUT : ATTN_OUT + vectors],
    )


def on_device(embedded_features, *others):
    one_each = embedded_features.shape[0] == lax.axis_size("tm")
    return (whole_series if one_each else shards)(embedded_features, *others)


def solution(mesh):
    placed = (
        P("dp", "tm", None),
        P("dp"),
        P("dp"),
        P("dp", None),
        P("dp", None),
        P("dp", None),
        P("dp", None),
        P("dp", None),
        P("dp", None),
        P("dp", None),
        P("dp", None),
        P("dp", None),
        P("dp", None),
        P("dp", "tm", None),
        P("dp", None, "tm"),
    )
    return jax.shard_map(
        on_device,
        mesh=mesh,
        in_specs=placed,
        out_specs=(
            P("dp", "tm", None),
            P("dp", None, "tm"),
            P("dp", "tm", None),
            P("dp", None),
            P("dp", None),
            P("dp", None),
            P("dp", None),
            P("dp", None),
            P("dp", None),
            P("dp", None),
            P("dp", None),
            P("dp", None),
            P("dp", None),
        ),
        check_vma=False,
    )
```

```python
import types

import jax
import jax.numpy as jnp
from jax import lax
from jax.experimental import pallas as pl
from jax.experimental.pallas import tpu as pltpu
from jax.sharding import PartitionSpec as P

HEADS = 4
LEVEL_TALLY = 3
DEC = 24
MICRO = 2


EPSILON = 1e-05
NEG_BIG = -1e30
attend_group = 2
LOG2_E = 1.4426950408889634
VMEM_BYTES = 60 * 2**20


def entering(value, axis, join, neutral, backward):
    count, mine = (lax.axis_size(axis), lax.axis_index(axis))
    pieces = jax.tree.map(lambda part: lax.all_gather(part, axis), value)
    if backward:
        pieces = jax.tree.map(lambda part: part[::-1], pieces)
        mine = count - 1 - mine
    so_far = jax.tree.map(
        lambda part, zero: jnp.full_like(part, 0) + jnp.asarray(zero, part.dtype), value, neutral
    )

    def turn(position, so_far):
        longer = join(so_far, jax.tree.map(lambda part: part[position], pieces))
        return jax.tree.map(lambda new, old: jnp.where(position < mine, new, old), longer, so_far)

    return lax.fori_loop(0, count - 1, turn, so_far)


def narrow_convert(values):
    return values.astype(jnp.bfloat16)


def tensor_dot_plain(left, right):
    return jnp.dot(left, right, preferred_element_type=jnp.float32)


def flipped_dot(left, right):
    return lax.dot_general(
        left, right, (((0,), (0,)), ((), ())), preferred_element_type=jnp.float32
    )


def dot_against_flipped(left, right):
    return lax.dot_general(
        left, right, (((1,), (1,)), ((), ())), preferred_element_type=jnp.float32
    )


def affine_join(earlier, later):
    return (later[0] * earlier[0], later[0] * earlier[1] + later[1])


def layer_norm(values, gains, offsets):
    centred = values - jnp.mean(values, axis=-1, keepdims=True)
    spread = jnp.mean(centred * centred, axis=-1, keepdims=True)
    return centred * lax.rsqrt(spread + EPSILON) * gains + offsets


def gated_unit(pre_act):
    half_width = pre_act.shape[-1] // 2
    return pre_act[..., :half_width] * jax.nn.sigmoid(pre_act[..., half_width:])


def lstm_gates(pre_act, keep_mask):
    quarter = pre_act.shape[-1] // 4
    forget = jax.nn.sigmoid(pre_act[..., :quarter]) * keep_mask
    inflow = jax.nn.sigmoid(pre_act[..., quarter : 2 * quarter]) * jnp.tanh(
        pre_act[..., 2 * quarter : 3 * quarter]
    )
    out_gate = jax.nn.sigmoid(pre_act[..., 3 * quarter :])
    return (forget, inflow, out_gate)


def masked_scores(query_block, key_block, query_pos, key_pos, begin_block, scale):
    raw = jnp.einsum("gqhd,gkhd->ghqk", query_block, key_block, preferred_element_type=jnp.float32)
    lowest = jnp.minimum(begin_block[:, None], query_pos[None, :])
    allowed = (key_pos[None, None, :] <= query_pos[None, :, None]) & (
        key_pos[None, None, :] >= lowest[:, :, None]
    )
    return jnp.where(allowed[:, None], raw * scale, NEG_BIG)


def score_grad(chances, dprob, row_delta, scale):
    return narrow_convert(chances * (dprob[:, None] - row_delta[..., None]) * scale)


def shards(
    embedded_features,
    earliest_seen_moment,
    reach_choice,
    lstm_valve_coeffs,
    lstm_unit_coeffs,
    asker_lookup_coeffs,
    attend_exit_coeffs,
    attend_unit_coeffs,
    skipnet_entry_coeffs,
    skipnet_inner_coeffs,
    skipnet_unit_coeffs,
    level_map_coeffs,
    bias_gain_table,
    block_emit_adjoint,
    predicted_adjoint,
):
    (
        mat_lstm,
        mat_glu_one,
        mat_qkv,
        mat_attn,
        mat_glu_two,
        mat_inner,
        mat_middle,
        mat_glu_three,
        level_dot,
        vec_table,
    ) = (
        lax.all_gather(narrow_convert(lstm_valve_coeffs), "dp", axis=0, tiled=True),
        lax.all_gather(narrow_convert(lstm_unit_coeffs), "dp", axis=0, tiled=True),
        lax.all_gather(narrow_convert(asker_lookup_coeffs), "dp", axis=0, tiled=True),
        lax.all_gather(narrow_convert(attend_exit_coeffs), "dp", axis=0, tiled=True),
        lax.all_gather(narrow_convert(attend_unit_coeffs), "dp", axis=0, tiled=True),
        lax.all_gather(narrow_convert(skipnet_entry_coeffs), "dp", axis=0, tiled=True),
        lax.all_gather(narrow_convert(skipnet_inner_coeffs), "dp", axis=0, tiled=True),
        lax.all_gather(narrow_convert(skipnet_unit_coeffs), "dp", axis=0, tiled=True),
        lax.all_gather(narrow_convert(level_map_coeffs), "dp", axis=0, tiled=True),
        lax.all_gather(narrow_convert(bias_gain_table), "dp", axis=0, tiled=True),
    )
    series_per_device, steps_per_device, model_width = embedded_features.shape
    seq_total = steps_per_device * lax.axis_size("tm")
    head_width = model_width // HEADS
    count_of_rows = series_per_device * steps_per_device
    scale = head_width ** (-0.5)
    vec_full = vec_table.astype(jnp.float32)
    time_local = lax.axis_index("tm") * steps_per_device + jnp.arange(
        steps_per_device, dtype=jnp.int32
    )
    time_all = jnp.arange(seq_total, dtype=jnp.int32)
    horizon_len = jnp.where(reach_choice == 0, 1, jnp.where(reach_choice == 1, 5, 24))
    ahead_moment_filter = (
        (
            (time_local[None, :] >= seq_total - DEC)
            & (time_local[None, :] < seq_total - DEC + horizon_len[:, None])
        )
        .astype(jnp.float32)
        .reshape(count_of_rows, 1)
    )
    keep_mask = (
        (time_local[None, :] != earliest_seen_moment[:, None])
        .astype(jnp.float32)
        .reshape(count_of_rows, 1)
    )
    group_size = series_per_device // MICRO
    group_total = series_per_device // attend_group
    state_ones = jnp.ones((group_size, model_width), jnp.float32)
    state_zeros = jnp.zeros((group_size, model_width), jnp.float32)

    def split_groups(array):
        return array.reshape((group_total, attend_group) + array.shape[1:])

    input_rows = embedded_features.reshape(count_of_rows, model_width)
    input_full = input_rows.astype(jnp.float32)
    lstm_pre = tensor_dot_plain(input_rows, mat_lstm) + vec_full[:, 0:4].T.reshape(-1)
    forget, inflow, out_gate = lstm_gates(lstm_pre, keep_mask)
    forget_seq = forget.reshape(series_per_device, steps_per_device, model_width)
    inflow_seq = inflow.reshape(series_per_device, steps_per_device, model_width)
    mult_seq, cell_local = lax.associative_scan(affine_join, (forget_seq, inflow_seq), axis=1)
    cell_parts = []
    for group in range(MICRO):
        lower_row = group * group_size
        upper_row = lower_row + group_size
        _, arriving = entering(
            (mult_seq[lower_row:upper_row, -1], cell_local[lower_row:upper_row, -1]),
            "tm",
            affine_join,
            (state_ones, state_zeros),
            False,
        )
        cell_parts.append(arriving)
    cell_in = jnp.concatenate(cell_parts, axis=0)
    cell_seq = cell_local + mult_seq * cell_in[:, None, :]
    cell_tanh = jnp.tanh(cell_seq.reshape(count_of_rows, model_width))
    hidden_low = narrow_convert(out_gate * cell_tanh)
    glu_one_pre = tensor_dot_plain(hidden_low, mat_glu_one) + vec_full[:, 4:6].T.reshape(-1)
    first_sum = input_full + gated_unit(glu_one_pre)
    first = layer_norm(first_sum, vec_full[:, 6], vec_full[:, 7])
    first_low = narrow_convert(first)
    qkv_low = narrow_convert(tensor_dot_plain(first_low, mat_qkv))
    query_low = qkv_low[:, :model_width].reshape(
        series_per_device, steps_per_device, HEADS, head_width
    )
    key_value = qkv_low[:, model_width:].reshape(
        series_per_device, steps_per_device, model_width + head_width
    )
    key_value_all = lax.all_gather(key_value, "tm", axis=1, tiled=True)
    keys_all = key_value_all[..., :model_width].reshape(
        series_per_device, seq_total, HEADS, head_width
    )
    values_all = key_value_all[..., model_width:]

    def attend_forward(block_args):
        query_block, key_block, value_block, begin_block = block_args
        scores = masked_scores(query_block, key_block, time_local, time_all, begin_block, scale)
        row_top = jnp.max(scores, axis=-1, keepdims=True)
        row_exp = jnp.exp(scores - row_top)
        row_total = jnp.sum(row_exp, axis=-1, keepdims=True)
        weights_low = narrow_convert(row_exp / row_total)
        mixed_block = jnp.einsum(
            "ghqk,gkd->gqd", weights_low, value_block, preferred_element_type=jnp.float32
        ) * (1.0 / HEADS)
        return (mixed_block, (row_top + jnp.log(row_total))[..., 0])

    mixed, log_total = lax.map(
        attend_forward,
        (
            split_groups(query_low),
            split_groups(keys_all),
            split_groups(values_all),
            split_groups(earliest_seen_moment),
        ),
    )
    mixed_low = narrow_convert(mixed.reshape(count_of_rows, head_width))
    attn_low = narrow_convert(tensor_dot_plain(mixed_low, mat_attn))
    glu_two_pre = tensor_dot_plain(attn_low, mat_glu_two) + vec_full[:, 8:10].T.reshape(-1)
    second_sum = first + gated_unit(glu_two_pre)
    second = layer_norm(second_sum, vec_full[:, 10], vec_full[:, 11])
    second_low = narrow_convert(second)
    inner_pre = tensor_dot_plain(second_low, mat_inner) + vec_full[:, 12]
    inner_low = narrow_convert(jax.nn.elu(inner_pre))
    middle_low = narrow_convert(tensor_dot_plain(inner_low, mat_middle) + vec_full[:, 13])
    glu_three_pre = tensor_dot_plain(middle_low, mat_glu_three) + vec_full[:, 14:16].T.reshape(-1)
    final_sum = second + gated_unit(glu_three_pre)
    second_block_emit = layer_norm(final_sum, vec_full[:, 16], vec_full[:, 17])
    closing_narrowed = narrow_convert(second_block_emit)
    predicted_entries = tensor_dot_plain(closing_narrowed, level_dot) * ahead_moment_filter
    predicted_levels = predicted_entries.reshape(
        series_per_device, steps_per_device, LEVEL_TALLY
    ).transpose(0, 2, 1)
    predicted_slope = narrow_convert(
        predicted_adjoint.astype(jnp.float32).transpose(0, 2, 1).reshape(count_of_rows, LEVEL_TALLY)
        * ahead_moment_filter
    )
    level_slope = flipped_dot(closing_narrowed, predicted_slope)
    final_grad = block_emit_adjoint.reshape(count_of_rows, model_width).astype(
        jnp.float32
    ) + dot_against_flipped(predicted_slope, level_dot)
    _, norm_pull = jax.vjp(layer_norm, final_sum, vec_full[:, 16], vec_full[:, 17])
    sum_three_grad, gain_three_grad, offset_three_grad = norm_pull(final_grad)
    _, glu_pull = jax.vjp(gated_unit, glu_three_pre)
    (glu_three_grad,) = glu_pull(sum_three_grad)
    glu_three_low = narrow_convert(glu_three_grad)
    grad_glu_three = flipped_dot(middle_low, glu_three_low)
    middle_grad = dot_against_flipped(glu_three_low, mat_glu_three)
    middle_grad_low = narrow_convert(middle_grad)
    grad_middle = flipped_dot(inner_low, middle_grad_low)
    inner_grad = dot_against_flipped(middle_grad_low, mat_middle)
    _, elu_pull = jax.vjp(jax.nn.elu, inner_pre)
    (inner_pre_grad,) = elu_pull(inner_grad)
    inner_pre_low = narrow_convert(inner_pre_grad)
    grad_inner = flipped_dot(second_low, inner_pre_low)
    second_grad = sum_three_grad + dot_against_flipped(inner_pre_low, mat_inner)
    _, norm_pull = jax.vjp(layer_norm, second_sum, vec_full[:, 10], vec_full[:, 11])
    sum_two_grad, gain_two_grad, offset_two_grad = norm_pull(second_grad)
    _, glu_pull = jax.vjp(gated_unit, glu_two_pre)
    (glu_two_grad,) = glu_pull(sum_two_grad)
    glu_two_low = narrow_convert(glu_two_grad)
    grad_glu_two = flipped_dot(attn_low, glu_two_low)
    attn_grad_low = narrow_convert(dot_against_flipped(glu_two_low, mat_glu_two))
    grad_attn = flipped_dot(mixed_low, attn_grad_low)
    mixed_grad_low = narrow_convert(dot_against_flipped(attn_grad_low, mat_attn))
    head_grad = (mixed_grad_low * (1.0 / HEADS)).reshape(
        series_per_device, steps_per_device, head_width
    )

    def attend_backward(block_args):
        query_block, key_block, value_block, begin_block, lse_block, dout_block = block_args
        scores = masked_scores(query_block, key_block, time_local, time_all, begin_block, scale)
        chances = jnp.exp(scores - lse_block[..., None])
        dprob = jnp.einsum(
            "gqd,gkd->gqk", dout_block, value_block, preferred_element_type=jnp.float32
        )
        row_delta = jnp.sum(chances * dprob[:, None], axis=-1)
        dscore = score_grad(chances, dprob, row_delta, scale)
        dquery = jnp.einsum(
            "ghqk,gkhd->gqhd", dscore, key_block, preferred_element_type=jnp.float32
        )
        dkey = jnp.einsum(
            "ghqk,gqhd->gkhd", dscore, query_block, preferred_element_type=jnp.float32
        )
        dvalue = jnp.einsum(
            "ghqk,gqd->gkd", narrow_convert(chances), dout_block, preferred_element_type=jnp.float32
        )
        key_terms = jnp.concatenate(
            [dkey.reshape(attend_group, seq_total, model_width), dvalue], axis=-1
        )
        return (dquery, key_terms)

    dquery, key_terms = lax.map(
        attend_backward,
        (
            split_groups(query_low),
            split_groups(keys_all),
            split_groups(values_all),
            split_groups(earliest_seen_moment),
            log_total,
            split_groups(head_grad),
        ),
    )
    own_keys = lax.psum_scatter(
        key_terms.reshape(series_per_device, seq_total, model_width + head_width),
        "tm",
        scatter_dimension=1,
        tiled=True,
    )
    qkv_grad = jnp.concatenate(
        [
            dquery.reshape(count_of_rows, model_width),
            own_keys.reshape(count_of_rows, model_width + head_width),
        ],
        axis=1,
    )
    qkv_grad_low = narrow_convert(qkv_grad)
    grad_qkv = flipped_dot(first_low, qkv_grad_low)
    first_grad = sum_two_grad + dot_against_flipped(qkv_grad_low, mat_qkv)
    _, norm_pull = jax.vjp(layer_norm, first_sum, vec_full[:, 6], vec_full[:, 7])
    sum_one_grad, gain_one_grad, offset_one_grad = norm_pull(first_grad)
    _, glu_pull = jax.vjp(gated_unit, glu_one_pre)
    (glu_one_grad,) = glu_pull(sum_one_grad)
    glu_one_low = narrow_convert(glu_one_grad)
    grad_glu_one = flipped_dot(hidden_low, glu_one_low)
    hidden_grad = dot_against_flipped(glu_one_low, mat_glu_one)
    out_gate_grad = hidden_grad * cell_tanh
    direct_grad = (hidden_grad * out_gate * (1.0 - cell_tanh * cell_tanh)).reshape(
        series_per_device, steps_per_device, model_width
    )
    next_forget = jnp.concatenate([forget_seq[:, 1:], jnp.ones_like(forget_seq[:, :1])], axis=1)
    rev_mult, rev_cell = lax.associative_scan(
        affine_join, (next_forget, direct_grad), axis=1, reverse=True
    )
    head_mult = forget_seq[:, 0] * rev_mult[:, 0]
    head_cell = forget_seq[:, 0] * rev_cell[:, 0]
    coming_parts = []
    for group in range(MICRO):
        lower_row = group * group_size
        upper_row = lower_row + group_size
        _, coming = entering(
            (head_mult[lower_row:upper_row], head_cell[lower_row:upper_row]),
            "tm",
            affine_join,
            (state_ones, state_zeros),
            True,
        )
        coming_parts.append(coming)
    coming_all = jnp.concatenate(coming_parts, axis=0)
    cell_grad = rev_cell + rev_mult * coming_all[:, None, :]
    cell_prev = jnp.concatenate([cell_in[:, None, :], cell_seq[:, :-1]], axis=1)
    forget_grad = (cell_grad * cell_prev).reshape(count_of_rows, model_width)
    _, gate_pull = jax.vjp(lambda pre_value: lstm_gates(pre_value, keep_mask), lstm_pre)
    (lstm_pre_grad,) = gate_pull(
        (forget_grad, cell_grad.reshape(count_of_rows, model_width), out_gate_grad)
    )
    lstm_low = narrow_convert(lstm_pre_grad)
    grad_lstm = flipped_dot(input_rows, lstm_low)
    input_grad = sum_one_grad + dot_against_flipped(lstm_low, mat_lstm)
    grad_table = jnp.concatenate(
        [
            jnp.sum(lstm_pre_grad, axis=0).reshape(4, model_width).T,
            jnp.sum(glu_one_grad, axis=0).reshape(2, model_width).T,
            gain_one_grad[:, None],
            offset_one_grad[:, None],
            jnp.sum(glu_two_grad, axis=0).reshape(2, model_width).T,
            gain_two_grad[:, None],
            offset_two_grad[:, None],
            jnp.sum(inner_pre_grad, axis=0)[:, None],
            jnp.sum(middle_grad, axis=0)[:, None],
            jnp.sum(glu_three_grad, axis=0).reshape(2, model_width).T,
            gain_three_grad[:, None],
            offset_three_grad[:, None],
        ],
        axis=1,
    )
    (
        whole_lstm,
        whole_glu_one,
        whole_qkv,
        whole_attn,
        whole_glu_two,
        whole_inner,
        whole_middle,
        whole_glu_three,
        whole_quant,
        whole_table,
    ) = lax.psum(
        (
            grad_lstm,
            grad_glu_one,
            grad_qkv,
            grad_attn,
            grad_glu_two,
            grad_inner,
            grad_middle,
            grad_glu_three,
            level_slope,
            grad_table,
        ),
        "tm",
    )
    summed = (
        lax.psum_scatter(
            whole_lstm.astype(jnp.bfloat16), "dp", scatter_dimension=0, tiled=True
        ).astype(jnp.float32),
        lax.psum_scatter(
            whole_glu_one.astype(jnp.bfloat16), "dp", scatter_dimension=0, tiled=True
        ).astype(jnp.float32),
        lax.psum_scatter(
            whole_qkv.astype(jnp.bfloat16), "dp", scatter_dimension=0, tiled=True
        ).astype(jnp.float32),
        lax.psum_scatter(
            whole_attn.astype(jnp.bfloat16), "dp", scatter_dimension=0, tiled=True
        ).astype(jnp.float32),
        lax.psum_scatter(
            whole_glu_two.astype(jnp.bfloat16), "dp", scatter_dimension=0, tiled=True
        ).astype(jnp.float32),
        lax.psum_scatter(
            whole_inner.astype(jnp.bfloat16), "dp", scatter_dimension=0, tiled=True
        ).astype(jnp.float32),
        lax.psum_scatter(
            whole_middle.astype(jnp.bfloat16), "dp", scatter_dimension=0, tiled=True
        ).astype(jnp.float32),
        lax.psum_scatter(
            whole_glu_three.astype(jnp.bfloat16), "dp", scatter_dimension=0, tiled=True
        ).astype(jnp.float32),
        lax.psum_scatter(
            whole_quant.astype(jnp.bfloat16), "dp", scatter_dimension=0, tiled=True
        ).astype(jnp.float32),
        lax.psum_scatter(
            whole_table.astype(jnp.bfloat16), "dp", scatter_dimension=0, tiled=True
        ).astype(jnp.float32),
    )
    final_out = second_block_emit.astype(jnp.bfloat16).reshape(
        series_per_device, steps_per_device, model_width
    )
    input_out = input_grad.astype(jnp.bfloat16).reshape(
        series_per_device, steps_per_device, model_width
    )
    return (
        final_out,
        predicted_levels,
        input_out,
        summed[0],
        summed[1],
        summed[2],
        summed[3],
        summed[4],
        summed[5],
        summed[6],
        summed[7],
        summed[8],
        summed[9],
    )


def lane_head(shape, head_width, head):
    lane = lax.broadcasted_iota(jnp.int32, shape, len(shape) - 1)
    return (lane >= head * head_width) & (lane < (head + 1) * head_width)


FORGET, ENTER, CANDIDATE, EXIT = 0, 256, 512, 768
GLU_ONE_A, GLU_ONE_B = 1024, 1280
QUERY, KEY, VALUE = 1536, 1792, 2048
GLU_TWO_A, GLU_TWO_B = 2176, 2432
INNER, MIDDLE = 2688, 2944
GLU_THREE_A, GLU_THREE_B = 3200, 3456
ATTN_OUT = 3712
PACKED = 3968
VECTORS = 24
LANES = 128
CHUNKS = 8
TILE = 256


def nn(left, right):
    return jnp.dot(left, right, preferred_element_type=jnp.float32)


def nt(left, right):
    return lax.dot_general(
        left, right, (((1,), (1,)), ((), ())), preferred_element_type=jnp.float32
    )


def tn(left, right):
    return lax.dot_general(
        left, right, (((0,), (0,)), ((), ())), preferred_element_type=jnp.float32
    )


def low(values):
    return values.astype(jnp.bfloat16)


def sigmoid(values):
    return 0.5 * jnp.tanh(0.5 * values) + 0.5


def normalise(values, gain, shift):
    centred = values - jnp.mean(values, axis=-1, keepdims=True)
    spread = jnp.mean(centred * centred, axis=-1, keepdims=True)
    inverse = lax.rsqrt(spread + EPSILON)
    unit = centred * inverse
    return unit * gain + shift, unit, inverse


def normalise_back(grad, unit, inverse, gain):
    scaled = grad * gain
    return inverse * (
        scaled
        - jnp.mean(scaled, axis=-1, keepdims=True)
        - unit * jnp.mean(scaled * unit, axis=-1, keepdims=True)
    )


def rows_of(tile, size=TILE):
    return pl.ds(pl.multiple_of(tile * size, size), size)


def put_halves(ref, rows, values):
    ref[0, rows, :] = values[:, :LANES]
    ref[1, rows, : values.shape[1] - LANES] = values[:, LANES:]


def get_halves(ref, rows, width):
    return jnp.concatenate([ref[0, rows, :], ref[1, rows, : width - LANES]], axis=1)


def row_sum(ref, column, values):
    ref[column : column + 1, :] += jnp.sum(values, axis=0, keepdims=True)


def series_scratch(span, width, head_width):
    full = pltpu.VMEM((span, width), jnp.float32)
    half = pltpu.VMEM((span, width), jnp.bfloat16)
    flat = pltpu.VMEM((width, span), jnp.bfloat16)
    scan = pltpu.VMEM((2, span, LANES), jnp.float32)
    scan_more = pltpu.VMEM((2, span + 8, LANES), jnp.float32)
    narrow = pltpu.VMEM((span, head_width), jnp.bfloat16)
    column = pltpu.VMEM((span, 1), jnp.float32)
    return dict(
        forget=scan_more,
        local=scan,
        mult=scan,
        cell=scan_more,
        carry=pltpu.VMEM((2, CHUNKS, LANES), jnp.float32),
        enter_gate=full,
        candidate=full,
        exit_gate=full,
        cell_tanh=full,
        hidden=half,
        glu_one=full,
        gate_one=full,
        unit_one=full,
        inverse_one=column,
        first_low=half,
        queries=half,
        keys=half,
        values=narrow,
        head_queries=pltpu.VMEM((HEADS, span, width), jnp.bfloat16),
        head_keys=pltpu.VMEM((HEADS, span, width), jnp.bfloat16),
        **{
            "chances%d" % tile: pltpu.VMEM((HEADS, TILE, (tile + 1) * TILE), jnp.float32)
            for tile in range(span // TILE)
        },
        chance_sum=pltpu.VMEM((span, span), jnp.bfloat16),
        **{
            "score_grads%d" % tile: pltpu.VMEM((HEADS, span - tile * TILE, TILE), jnp.bfloat16)
            for tile in range(span // TILE)
        },
        block=pltpu.VMEM((TILE, span), jnp.float32),
        mixed=narrow,
        mixed_grad=narrow,
        sum_two_grad=full,
        query_grad=half,
        key_grad=half,
        value_grad=narrow,
        gate_grads=pltpu.VMEM((4, span, width), jnp.bfloat16),
        x=half,
        x_flat=flat,
        adjoint=flat,
        out=flat,
        input_grad=flat,
        w=pltpu.VMEM((width, PACKED), jnp.bfloat16),
        g=pltpu.VMEM((width, PACKED), jnp.float32),
        gv=pltpu.VMEM((VECTORS + 8, width), jnp.float32),
        vec=pltpu.VMEM((VECTORS, width), jnp.float32),
        level=pltpu.VMEM((8, width), jnp.bfloat16),
    )


def series_gates(r, begin, chunk, steps):
    w, vec = r.w, r.vec
    width = r.x.shape[1]
    rows = rows_of(chunk, steps)
    x = r.x_flat[:, rows].T
    r.x[rows, :] = x

    def pre(block, column):
        return nn(x, w[:, block : block + width]) + vec[column : column + 1, :]

    time = chunk * steps + lax.broadcasted_iota(jnp.int32, (steps, width), 0)
    forget = jnp.where(time != begin, sigmoid(pre(FORGET, 0)), 0.0)
    enter = sigmoid(pre(ENTER, 1))
    candidate = jnp.tanh(pre(CANDIDATE, 2))
    r.enter_gate[rows, :] = enter
    r.candidate[rows, :] = candidate
    r.exit_gate[rows, :] = sigmoid(pre(EXIT, 3))
    put_halves(r.forget, rows, forget)
    put_halves(r.local, rows, enter * candidate)


def series_forward_scan(r):
    span = r.x.shape[0]
    steps = span // CHUNKS
    zeros = jnp.zeros((CHUNKS, LANES), jnp.float32)

    def step(t, state):
        out = []
        at = pl.ds(t, CHUNKS, stride=steps)
        for half in range(2):
            cell, mult = state[half]
            forget = r.forget[half, at, :]
            cell = forget * cell + r.local[half, at, :]
            mult = mult * forget
            r.local[half, at, :] = cell
            r.mult[half, at, :] = mult
            out.append((cell, mult))
        return tuple(out)

    ends = lax.fori_loop(0, steps, step, ((zeros, zeros + 1.0),) * 2, unroll=8)
    for half in range(2):
        cells, mults = ends[half]
        state = jnp.zeros((1, LANES), jnp.float32)
        r.carry[half, 0:1, :] = state
        for chunk in range(CHUNKS - 1):
            state = cells[chunk : chunk + 1] + mults[chunk : chunk + 1] * state
            r.carry[half, chunk + 1 : chunk + 2, :] = state
        r.cell[half, 0:8, :] = zeros


def series_forward_first(r):
    w, vec = r.w, r.vec
    span, width = r.x.shape
    head_width = width // HEADS
    steps = span // CHUNKS

    def cells(chunk, _):
        rows = rows_of(chunk, steps)
        later = pl.ds(pl.multiple_of(chunk * steps + 8, 8), steps)
        for half in range(2):
            r.cell[half, later, :] = r.local[half, rows, :] + r.mult[half, rows, :] * r.carry[
                half, pl.ds(chunk, 1), :
            ]
        tanh = jnp.tanh(get_halves(r.cell, later, width))
        r.cell_tanh[rows, :] = tanh
        r.hidden[rows, :] = low(r.exit_gate[rows, :] * tanh)
        return 0

    lax.fori_loop(0, CHUNKS, cells, 0)

    def first(tile, _):
        rows = rows_of(tile)
        hidden = r.hidden[rows, :]
        value = nn(hidden, w[:, GLU_ONE_A : GLU_ONE_A + width]) + vec[4:5, :]
        gate = sigmoid(nn(hidden, w[:, GLU_ONE_B : GLU_ONE_B + width]) + vec[5:6, :])
        r.glu_one[rows, :] = value
        r.gate_one[rows, :] = gate
        out, unit, inverse = normalise(
            r.x[rows, :].astype(jnp.float32) + value * gate, vec[6:7, :], vec[7:8, :]
        )
        r.unit_one[rows, :] = unit
        r.inverse_one[rows, :] = inverse
        out = low(out)
        r.first_low[rows, :] = out
        query = low(nn(out, w[:, QUERY : QUERY + width]))
        key = low(nn(out, w[:, KEY : KEY + width]))
        r.keys[rows, :] = key
        r.values[rows, :] = low(nn(out, w[:, VALUE : VALUE + head_width]))
        for head in range(HEADS):
            mine = lane_head((TILE, width), head_width, head)
            r.head_queries[head, rows, :] = jnp.where(mine, query, jnp.zeros_like(query))
            r.head_keys[head, rows, :] = jnp.where(mine, key, jnp.zeros_like(key))
        return 0

    lax.fori_loop(0, span // TILE, first, 0)


def series_forward_attention(r, begin):
    span, head_width = r.values.shape
    scale = head_width ** (-0.5) * LOG2_E
    for tile in range(span // TILE):
        rows = slice(tile * TILE, (tile + 1) * TILE)
        seen = (tile + 1) * TILE
        row = tile * TILE + lax.broadcasted_iota(jnp.int32, (TILE, seen), 0)
        col = lax.broadcasted_iota(jnp.int32, (TILE, seen), 1)
        chances = getattr(r, "chances%d" % tile)
        r.block[:, :seen] = jnp.where(
            (col <= row) & (col >= jnp.minimum(begin, row)), 0.0, NEG_BIG
        )

        def one_head(head, _):
            scores = (
                nt(r.head_queries[head, rows, :], r.keys[:seen, :]) * scale + r.block[:, :seen]
            )
            top = jnp.max(scores, axis=-1, keepdims=True)
            raised = jnp.exp2(scores - top)
            total = jnp.sum(raised, axis=-1, keepdims=True)
            chances[head] = raised * (1.0 / total)
            return 0

        lax.fori_loop(0, HEADS, one_head, 0)
        weights = chances[0]
        for head in range(1, HEADS):
            weights = weights + chances[head]
        weights = low(weights)
        r.chance_sum[rows, :seen] = weights
        r.mixed[rows, :] = low(nn(weights, r.values[:seen, :]) * (1.0 / HEADS))


def series_middle(r, horizon):
    w, vec, g, gv = r.w, r.vec, r.g, r.gv
    span, width = r.x.shape
    head_width = width // HEADS

    def middle(tile, last):
        rows = rows_of(tile)
        first = r.unit_one[rows, :] * vec[6:7, :] + vec[7:8, :]
        mixed = r.mixed[rows, :]
        attn = low(nn(mixed, w[:head_width, ATTN_OUT : ATTN_OUT + width]))
        value_two = nn(attn, w[:, GLU_TWO_A : GLU_TWO_A + width]) + vec[8:9, :]
        gate_two = sigmoid(nn(attn, w[:, GLU_TWO_B : GLU_TWO_B + width]) + vec[9:10, :])
        second, unit_two, inverse_two = normalise(
            first + value_two * gate_two, vec[10:11, :], vec[11:12, :]
        )
        second_low = low(second)
        inner_pre = nn(second_low, w[:, INNER : INNER + width]) + vec[12:13, :]
        inner_exp = jnp.exp(jnp.minimum(inner_pre, 0.0))
        inner_low = low(jnp.where(inner_pre > 0, inner_pre, inner_exp - 1.0))
        middle_low = low(nn(inner_low, w[:, MIDDLE : MIDDLE + width]) + vec[13:14, :])
        value_three = nn(middle_low, w[:, GLU_THREE_A : GLU_THREE_A + width]) + vec[14:15, :]
        gate_three = sigmoid(
            nn(middle_low, w[:, GLU_THREE_B : GLU_THREE_B + width]) + vec[15:16, :]
        )
        final, unit_three, inverse_three = normalise(
            second + value_three * gate_three, vec[16:17, :], vec[17:18, :]
        )
        final_low = low(final)
        r.out[:, rows] = final_low.T
        grad = r.adjoint[:, rows].T.astype(jnp.float32)
        if last:
            start = span - TILE
            time = start + lax.broadcasted_iota(jnp.int32, (8, TILE), 1)
            ahead = jnp.where((time >= span - DEC) & (time < span - DEC + horizon), 1.0, 0.0)
            steps = r.slope.shape[1]
            r.predicted[...] = (nt(r.level[...], final_low) * ahead)[:, TILE - steps :]
            slope = jnp.concatenate(
                [jnp.zeros((8, TILE - steps), jnp.float32), r.slope[...]], axis=1
            )
            slope = low(slope * ahead)
            gv[VECTORS : VECTORS + 8, :] = nn(slope, final_low)
            grad = grad + tn(slope, r.level[...])
        row_sum(gv, 16, grad * unit_three)
        row_sum(gv, 17, grad)
        sum_three = normalise_back(grad, unit_three, inverse_three, vec[16:17, :])
        grad_a = sum_three * gate_three
        grad_b = grad_a * value_three * (1.0 - gate_three)
        row_sum(gv, 14, grad_a)
        row_sum(gv, 15, grad_b)
        low_a, low_b = low(grad_a), low(grad_b)
        g[:, GLU_THREE_A : GLU_THREE_A + width] += tn(middle_low, low_a)
        g[:, GLU_THREE_B : GLU_THREE_B + width] += tn(middle_low, low_b)
        middle_grad = nt(low_a, w[:, GLU_THREE_A : GLU_THREE_A + width]) + nt(
            low_b, w[:, GLU_THREE_B : GLU_THREE_B + width]
        )
        row_sum(gv, 13, middle_grad)
        middle_grad = low(middle_grad)
        g[:, MIDDLE : MIDDLE + width] += tn(inner_low, middle_grad)
        inner_grad = nt(middle_grad, w[:, MIDDLE : MIDDLE + width]) * jnp.where(
            inner_pre > 0, 1.0, inner_exp
        )
        row_sum(gv, 12, inner_grad)
        inner_grad = low(inner_grad)
        g[:, INNER : INNER + width] += tn(second_low, inner_grad)
        grad = sum_three + nt(inner_grad, w[:, INNER : INNER + width])
        row_sum(gv, 10, grad * unit_two)
        row_sum(gv, 11, grad)
        sum_two = normalise_back(grad, unit_two, inverse_two, vec[10:11, :])
        r.sum_two_grad[rows, :] = sum_two
        grad_a = sum_two * gate_two
        grad_b = grad_a * value_two * (1.0 - gate_two)
        row_sum(gv, 8, grad_a)
        row_sum(gv, 9, grad_b)
        low_a, low_b = low(grad_a), low(grad_b)
        g[:, GLU_TWO_A : GLU_TWO_A + width] += tn(attn, low_a)
        g[:, GLU_TWO_B : GLU_TWO_B + width] += tn(attn, low_b)
        attn_grad = low(
            nt(low_a, w[:, GLU_TWO_A : GLU_TWO_A + width])
            + nt(low_b, w[:, GLU_TWO_B : GLU_TWO_B + width])
        )
        g[:head_width, ATTN_OUT : ATTN_OUT + width] += tn(mixed, attn_grad)
        r.mixed_grad[rows, :] = low(nt(attn_grad, w[:head_width, ATTN_OUT : ATTN_OUT + width]))
        return 0

    lax.fori_loop(0, span // TILE - 1, lambda tile, _: middle(tile, False), 0)
    middle(span // TILE - 1, True)


def series_backward_attention(r):
    span, head_width = r.values.shape
    width = head_width * HEADS
    scale = head_width ** (-0.5)
    for tile in range(span // TILE):
        rows = slice(tile * TILE, (tile + 1) * TILE)
        seen = (tile + 1) * TILE
        held = getattr(r, "chances%d" % tile)
        head_grad = r.mixed_grad[rows, :] * (1.0 / HEADS)
        r.block[:, :seen] = nt(head_grad, r.values[:seen, :]) * scale

        def one_head(head, total):
            chances = held[head]
            slope = r.block[:, :seen]
            delta = jnp.sum(chances * slope, axis=-1, keepdims=True)
            grads = low(chances * (slope - delta))
            for part in range(tile + 1):
                getattr(r, "score_grads%d" % part)[
                    head, (tile - part) * TILE : (tile - part + 1) * TILE, :
                ] = grads[:, part * TILE : (part + 1) * TILE]
            return total + nn(grads, r.head_keys[head, :seen, :])

        r.query_grad[rows, :] = low(
            lax.fori_loop(0, HEADS, one_head, jnp.zeros((TILE, width), jnp.float32))
        )
    for tile in range(span // TILE):
        cols = slice(tile * TILE, (tile + 1) * TILE)
        start = tile * TILE

        def one_key(head, total):
            return total + tn(
                getattr(r, "score_grads%d" % tile)[head], r.head_queries[head, start:, :]
            )

        r.key_grad[cols, :] = low(
            lax.fori_loop(0, HEADS, one_key, jnp.zeros((TILE, width), jnp.float32))
        )
        r.value_grad[cols, :] = low(
            tn(r.chance_sum[start:, cols], r.mixed_grad[start:, :] * (1.0 / HEADS))
        )


def series_backward_first(r):
    w, vec, g, gv = r.w, r.vec, r.g, r.gv
    span, width = r.hidden.shape
    head_width = width // HEADS

    def back(tile, _):
        rows = rows_of(tile)
        query, key, value = r.query_grad[rows, :], r.key_grad[rows, :], r.value_grad[rows, :]
        grad = (
            r.sum_two_grad[rows, :]
            + nt(query, w[:, QUERY : QUERY + width])
            + nt(key, w[:, KEY : KEY + width])
            + nt(value, w[:, VALUE : VALUE + head_width])
        )
        first = r.first_low[rows, :]
        g[:, QUERY : QUERY + width] += tn(first, query)
        g[:, KEY : KEY + width] += tn(first, key)
        g[:, VALUE : VALUE + head_width] += tn(first, value)
        unit = r.unit_one[rows, :]
        row_sum(gv, 6, grad * unit)
        row_sum(gv, 7, grad)
        sum_one = normalise_back(grad, unit, r.inverse_one[rows, :], vec[6:7, :])
        r.sum_two_grad[rows, :] = sum_one
        gate = r.gate_one[rows, :]
        grad_a = sum_one * gate
        grad_b = grad_a * r.glu_one[rows, :] * (1.0 - gate)
        row_sum(gv, 4, grad_a)
        row_sum(gv, 5, grad_b)
        low_a, low_b = low(grad_a), low(grad_b)
        hidden = r.hidden[rows, :]
        g[:, GLU_ONE_A : GLU_ONE_A + width] += tn(hidden, low_a)
        g[:, GLU_ONE_B : GLU_ONE_B + width] += tn(hidden, low_b)
        hidden_grad = nt(low_a, w[:, GLU_ONE_A : GLU_ONE_A + width]) + nt(
            low_b, w[:, GLU_ONE_B : GLU_ONE_B + width]
        )
        tanh, gate = r.cell_tanh[rows, :], r.exit_gate[rows, :]
        put_halves(r.local, rows, hidden_grad * gate * (1.0 - tanh * tanh))
        exit_grad = hidden_grad * tanh * gate * (1.0 - gate)
        row_sum(gv, 3, exit_grad)
        r.gate_grads[3, rows, :] = low(exit_grad)
        return 0

    lax.fori_loop(0, span // TILE, back, 0)


def series_backward_scan(r):
    span = r.x.shape[0]
    steps = span // CHUNKS
    zeros = jnp.zeros((CHUNKS, LANES), jnp.float32)
    for half in range(2):
        r.forget[half, span:, :] = zeros

    def step(count, state):
        t = steps - 1 - count
        out = []
        at, after = pl.ds(t, CHUNKS, stride=steps), pl.ds(t + 1, CHUNKS, stride=steps)
        for half in range(2):
            grad, mult = state[half]
            forget = r.forget[half, after, :]
            grad = forget * grad + r.local[half, at, :]
            mult = mult * forget
            r.local[half, at, :] = grad
            r.mult[half, at, :] = mult
            out.append((grad, mult))
        return tuple(out)

    ends = lax.fori_loop(0, steps, step, ((zeros, zeros + 1.0),) * 2, unroll=8)
    for half in range(2):
        grads, mults = ends[half]
        state = jnp.zeros((1, LANES), jnp.float32)
        r.carry[half, CHUNKS - 1 : CHUNKS, :] = state
        for chunk in range(CHUNKS - 1, 0, -1):
            state = grads[chunk : chunk + 1] + mults[chunk : chunk + 1] * state
            r.carry[half, chunk - 1 : chunk, :] = state


def series_gate_grads(r):
    gv = r.gv
    span, width = r.x.shape
    steps = span // CHUNKS

    def back(chunk, _):
        rows = rows_of(chunk, steps)
        before = pl.ds(chunk * steps + 7, steps)
        grad, grad_forget = [], []
        for half in range(2):
            one = r.local[half, rows, :] + r.mult[half, rows, :] * r.carry[
                half, pl.ds(chunk, 1), :
            ]
            forget = r.forget[half, rows, :]
            grad.append(one)
            grad_forget.append(one * r.cell[half, before, :] * forget * (1.0 - forget))
        grad = jnp.concatenate([grad[0], grad[1][:, : width - LANES]], axis=1)
        grad_forget = jnp.concatenate([grad_forget[0], grad_forget[1][:, : width - LANES]], axis=1)
        enter, candidate = r.enter_gate[rows, :], r.candidate[rows, :]
        grad_enter = grad * candidate * enter * (1.0 - enter)
        grad_candidate = grad * enter * (1.0 - candidate * candidate)
        row_sum(gv, 0, grad_forget)
        row_sum(gv, 1, grad_enter)
        row_sum(gv, 2, grad_candidate)
        r.gate_grads[0, rows, :] = low(grad_forget)
        r.gate_grads[1, rows, :] = low(grad_enter)
        r.gate_grads[2, rows, :] = low(grad_candidate)
        return 0

    lax.fori_loop(0, CHUNKS, back, 0)


def series_input_grad(r, chunk, steps):
    width = r.x.shape[1]
    rows = rows_of(chunk, steps)
    out = r.sum_two_grad[rows, :].T
    for gate, block in enumerate((FORGET, ENTER, CANDIDATE, EXIT)):
        out = out + nt(r.w[:, block : block + width], r.gate_grads[gate, rows, :])
    r.input_grad[:, rows] = low(out)


class Exchange:
    def __init__(self, sems, axis, source, target):
        self.sems, self.axis, self.source, self.target = sems, axis, source, target
        self.count, self.me = lax.axis_size(axis), lax.axis_index(axis)

    def other(self, step):
        return lax.rem(self.me + step, self.count)

    def copy(self, to, origin):
        return pltpu.make_async_remote_copy(
            src_ref=self.source(to),
            dst_ref=self.target(origin),
            send_sem=self.sems.at[0, to],
            recv_sem=self.sems.at[1, origin],
            device_id={self.axis: to},
            device_id_type=pl.DeviceIdType.MESH,
        )

    def send(self, to):
        self.copy(to, self.me).start()

    def arrive(self, origin):
        self.copy(origin, origin).wait_recv()

    def start(self):
        for step in range(1, self.count):
            self.send(self.other(step))

    def arrive_all(self):
        for step in range(1, self.count):
            self.arrive(self.other(step))

    def sent(self):
        for step in range(1, self.count):
            to = self.other(step)
            self.copy(to, self.me).wait_send()


PAD_ROWS = 48
GROUP_COLUMNS = (384, 384, 768)
BLOCKS_MIDDLE = (GLU_TWO_A, GLU_TWO_B, INNER, MIDDLE, GLU_THREE_A, GLU_THREE_B, ATTN_OUT)
BLOCKS_FIRST = (GLU_ONE_A, GLU_ONE_B, QUERY, KEY)
BLOCKS_LSTM = (FORGET, ENTER, CANDIDATE, EXIT)


def travel_scratch(count, groups, steps, width, rows):
    half, wide = LANES, 2 * LANES

    def pieces(lanes):
        return dict(
            send=pltpu.VMEM((count, width, lanes), jnp.bfloat16),
            land=pltpu.VMEM((count, width, lanes), jnp.bfloat16),
            part=pltpu.VMEM((groups, rows, lanes), jnp.float32),
            parts=pltpu.VMEM((groups, rows, lanes), jnp.float32),
        )

    out = dict(
        slope=pltpu.VMEM((8, steps), jnp.float32),
        slopes=pltpu.VMEM((count, 8, steps), jnp.float32),
        levels=pltpu.VMEM((count, 8, steps), jnp.float32),
        predicted=pltpu.VMEM((8, steps), jnp.float32),
        stage=pltpu.VMEM((width, 2 * GROUP_COLUMNS[2]), jnp.float32),
        attn_stage=pltpu.VMEM((width, wide), jnp.float32),
        table_stage=pltpu.VMEM((PAD_ROWS, LANES), jnp.float32),
    )
    for group, columns in enumerate(GROUP_COLUMNS):
        out["params%d" % group] = pltpu.VMEM((2, groups, PAD_ROWS, columns), jnp.bfloat16)
        out["params%d_dp" % group] = pltpu.SemaphoreType.DMA((2, groups))
        out["params%d_core" % group] = pltpu.SemaphoreType.DMA((2, groups))
    for name, lanes in (("middle", wide), ("first", half), ("lstm", half)):
        for what, shape in pieces(lanes).items():
            out[name + "_" + what] = shape
        out[name + "_tm"] = pltpu.SemaphoreType.DMA((2, count))
        out[name + "_dp"] = pltpu.SemaphoreType.DMA((2, groups))
        out[name + "_all"] = pltpu.SemaphoreType.DMA((2, count))
    for name in ("x", "adjoint", "out", "input", "slope", "predicted"):
        out[name + "_sems"] = pltpu.SemaphoreType.DMA((2, count))
    out["own_sems"] = pltpu.SemaphoreType.DMA((4,))
    return out


class Parameters:
    def __init__(self, r, group):
        self.buffer = getattr(r, "params%d" % group)
        self.mine, self.core = lax.axis_index("dp"), lax.rem(lax.axis_index("tm"), 2)
        self.count = lax.axis_size("dp")
        buffer, core, mine = self.buffer, self.core, self.mine
        self.over = Exchange(
            getattr(r, "params%d_dp" % group),
            "dp",
            lambda to: buffer.at[core, mine],
            lambda origin: buffer.at[core, origin],
        )
        self.sems = getattr(r, "params%d_core" % group)
        self.sibling = lax.axis_index("tm") + 1 - 2 * core

    def hand(self, origin, core):
        return pltpu.make_async_remote_copy(
            src_ref=self.buffer.at[core, origin],
            dst_ref=self.buffer.at[core, origin],
            send_sem=self.sems.at[0, origin],
            recv_sem=self.sems.at[1, origin],
            device_id={"tm": self.sibling},
            device_id_type=pl.DeviceIdType.MESH,
        )

    def pass_on(self):
        for step in range(1, self.count):
            origin = self.over.other(step)
            self.over.arrive(origin)
            self.hand(origin, self.core).start()

    def arrive(self):
        for step in range(1, self.count):
            self.hand(self.over.other(step), 1 - self.core).wait_recv()

    def sent(self):
        self.over.sent()
        for step in range(1, self.count):
            self.hand(self.over.other(step), self.core).wait_send()


class Reduction:
    def __init__(self, r, name, final, owners):
        self.send, self.land = getattr(r, name + "_send"), getattr(r, name + "_land")
        self.part, self.parts = getattr(r, name + "_part"), getattr(r, name + "_parts")
        self.final, self.owners = final, owners
        self.me, self.mine = lax.axis_index("tm"), lax.axis_index("dp")
        self.count, self.groups = lax.axis_size("tm"), lax.axis_size("dp")
        send, land, part, parts, me, mine = (
            self.send, self.land, self.part, self.parts, self.me, self.mine
        )
        self.over_time = Exchange(
            getattr(r, name + "_tm"), "tm", lambda to: send.at[to], lambda origin: land.at[origin]
        )
        self.over_series = Exchange(
            getattr(r, name + "_dp"), "dp", lambda to: part.at[to], lambda origin: parts.at[origin]
        )
        self.to_all = Exchange(
            getattr(r, name + "_all"), "tm", lambda to: final.at[me], lambda origin: final.at[origin]
        )

    def owned(self, index, action):
        if self.owners == self.count:
            action()
        else:
            pl.when(index < self.owners)(action)

    def start(self):
        for step in range(1, self.count):
            to = self.over_time.other(step)
            self.owned(to, lambda: self.over_time.send(to))

    def sum_time(self):
        def action():
            self.over_time.arrive_all()
            self.land[self.me] = self.send[self.me]
            total = self.land[0].astype(jnp.float32)
            for origin in range(1, self.count):
                total = total + self.land[origin].astype(jnp.float32)
            rows = self.part.shape[1]
            for group in range(self.groups):
                self.part[group] = total[group * rows : (group + 1) * rows]
            self.over_series.start()

        self.owned(self.me, action)

    def sum_series(self):
        def action():
            self.over_series.arrive_all()
            self.parts[self.mine] = self.part[self.mine]
            total = self.parts[0]
            for origin in range(1, self.groups):
                total = total + self.parts[origin]
            self.final[self.me] = total
            self.to_all.start()

        self.owned(self.me, action)

    def finish(self):
        for step in range(1, self.count):
            origin = self.to_all.other(step)
            self.owned(origin, lambda: self.to_all.arrive(origin))
        for step in range(1, self.count):
            to = self.over_time.other(step)
            self.owned(to, lambda: self.over_time.copy(to, self.me).wait_send())

        def action():
            self.over_series.sent()
            self.to_all.sent()

        self.owned(self.me, action)


def greet():
    barrier = pltpu.get_barrier_semaphore()
    total = 0
    for axis in ("tm", "dp"):
        me, count = lax.axis_index(axis), lax.axis_size(axis)
        for step in range(1, count):
            pl.semaphore_signal(
                barrier,
                inc=1,
                device_id={axis: lax.rem(me + step, count)},
                device_id_type=pl.DeviceIdType.MESH,
            )
            total += 1
    return lambda: pl.semaphore_wait(barrier, total)


def pack_params(r, group, params):
    mine = lax.axis_index("dp")
    buffer = getattr(r, "params%d" % group)

    def put(half, column, array, rows):
        buffer[half, mine, :rows, column : column + array.shape[1]] = low(array)

    if group == 0:
        lstm, table, level = params
        rows = lstm.shape[0]
        split = GROUP_COLUMNS[0]
        put(0, 0, lstm[:, :split], rows)
        put(1, 0, lstm[:, split:], rows)
        r.table_stage[...] = jnp.zeros_like(r.table_stage)
        r.table_stage[: table.shape[0], :rows] = table[...]
        r.table_stage[VECTORS : VECTORS + LEVEL_TALLY, :rows] = level[...]
        put(1, lstm.shape[1] - split, r.table_stage[...], PAD_ROWS)
    elif group == 1:
        glu_one, qkv = params
        put(0, 0, glu_one[...], glu_one.shape[0])
        put(1, 0, qkv[...], qkv.shape[0])
    else:
        glu_two, glu_three, inner, middle, attn = params
        rows = glu_two.shape[0]
        put(0, 0, glu_two[...], rows)
        put(0, 3 * LANES, glu_three[...], rows)
        put(1, 0, inner[...], rows)
        put(1, 2 * LANES, middle[...], rows)
        put(1, 4 * LANES, attn[...], attn.shape[0])


def unpack_params(r, group, rows, attn_rows):
    width = r.w.shape[0]
    head_width = width // HEADS
    buffer, stage = getattr(r, "params%d" % group), r.stage
    columns = GROUP_COLUMNS[group]
    for half in range(2):
        for origin in range(buffer.shape[1]):
            stage[origin * rows : (origin + 1) * rows, half * columns : (half + 1) * columns] = (
                buffer[half, origin].astype(jnp.float32)[:rows]
            )

    def place(block, column, size):
        r.w[:, block : block + size] = low(stage[:, column : column + size])

    if group == 0:
        for gate, block in enumerate(BLOCKS_LSTM):
            place(block, gate * width, width)
        vectors = jnp.concatenate(
            [
                buffer[1, origin][:, columns - LANES :].astype(jnp.float32)[: VECTORS + 8, :rows]
                for origin in range(buffer.shape[1])
            ],
            axis=1,
        )
        r.vec[...] = vectors[:VECTORS]
        r.level[...] = low(vectors[VECTORS:])
    elif group == 1:
        place(GLU_ONE_A, 0, width)
        place(GLU_ONE_B, width, width)
        place(QUERY, columns, width)
        place(KEY, columns + width, width)
        place(VALUE, columns + 2 * width, head_width)
    else:
        place(GLU_TWO_A, 0, width)
        place(GLU_TWO_B, width, width)
        place(GLU_THREE_A, 3 * LANES, width)
        place(GLU_THREE_B, 3 * LANES + width, width)
        place(INNER, columns, width)
        place(MIDDLE, columns + 2 * LANES, width)
        for origin in range(buffer.shape[1]):
            r.attn_stage[origin * attn_rows : (origin + 1) * attn_rows, :] = stage[
                origin * rows : origin * rows + attn_rows, columns + 4 * LANES :
            ]
        r.w[:head_width, ATTN_OUT : ATTN_OUT + width] = low(r.attn_stage[:head_width, :width])


def series_kernel(
    begins,
    reaches,
    x_hbm,
    adjoint_hbm,
    slopes,
    lstm,
    glu_one,
    qkv,
    attn,
    glu_two,
    inner,
    middle,
    glu_three,
    level,
    table,
    out_hbm,
    predicted_out,
    input_hbm,
    final_middle,
    final_first,
    final_lstm,
    *scratch,
):
    count, width, steps = x_hbm.shape
    span = count * steps
    head_width = width // HEADS
    groups = lax.axis_size("dp")
    rows = lstm.shape[0]
    names = series_scratch(span, width, head_width)
    names.update(travel_scratch(count, groups, steps, width, rows))
    r = types.SimpleNamespace(**dict(zip(names, scratch)))
    me = lax.axis_index("tm")
    last = count - 1

    def block(ref, index):
        return ref.at[:, rows_of(index, steps)]

    x_over = Exchange(r.x_sems, "tm", lambda to: x_hbm.at[to], lambda origin: block(r.x_flat, origin))
    adjoint_over = Exchange(
        r.adjoint_sems, "tm", lambda to: adjoint_hbm.at[to], lambda origin: block(r.adjoint, origin)
    )
    out_over = Exchange(
        r.out_sems, "tm", lambda to: block(r.out, to), lambda origin: out_hbm.at[origin]
    )
    input_over = Exchange(
        r.input_sems, "tm", lambda to: block(r.input_grad, to), lambda origin: input_hbm.at[origin]
    )
    slope_over = Exchange(
        r.slope_sems, "tm", lambda to: r.slopes.at[to], lambda origin: r.slope
    )
    predicted_over = Exchange(
        r.predicted_sems, "tm", lambda to: r.predicted, lambda origin: r.levels.at[origin]
    )
    params = [Parameters(r, group) for group in range(3)]
    middle_sum = Reduction(r, "middle", final_middle, len(BLOCKS_MIDDLE))
    first_sum = Reduction(r, "first", final_first, count)
    lstm_sum = Reduction(r, "lstm", final_lstm, count)

    own_x = pltpu.make_async_copy(x_hbm.at[me], block(r.x_flat, me), r.own_sems.at[0])
    own_adjoint = pltpu.make_async_copy(adjoint_hbm.at[me], block(r.adjoint, me), r.own_sems.at[1])
    own_out = pltpu.make_async_copy(block(r.out, me), out_hbm.at[me], r.own_sems.at[2])
    own_input = pltpu.make_async_copy(block(r.input_grad, me), input_hbm.at[me], r.own_sems.at[3])

    everyone_here = greet()
    own_x.start()
    own_adjoint.start()
    pack_params(r, 0, (lstm, table, level))
    everyone_here()
    x_over.start()
    params[0].over.start()
    pack_params(r, 1, (glu_one, qkv))
    params[1].over.start()
    pack_params(r, 2, (glu_two, glu_three, inner, middle, attn))
    params[2].over.start()
    for track in range(count):
        r.slopes[track] = jnp.concatenate(
            [
                slopes[level_at].astype(jnp.float32)[track : track + 1]
                for level_at in range(LEVEL_TALLY)
            ]
            + [jnp.zeros((8 - LEVEL_TALLY, steps), jnp.float32)],
            axis=0,
        )

    @pl.when(me == last)
    def _():
        slope_over.start()
        r.slope[...] = r.slopes[last]

    r.g[...] = jnp.zeros_like(r.g)
    r.gv[...] = jnp.zeros_like(r.gv)
    begin = begins[me]
    choice = reaches[me]
    horizon = jnp.where(choice == 0, 1, jnp.where(choice == 1, 5, 24))

    params[0].pass_on()
    params[0].arrive()
    unpack_params(r, 0, rows, attn.shape[0])
    own_x.wait()
    series_gates(r, begin, me, steps)

    def arriving(step, _):
        origin = x_over.other(step)
        x_over.arrive(origin)
        series_gates(r, begin, origin, steps)
        return 0

    lax.fori_loop(1, count, arriving, 0)
    adjoint_over.start()
    params[1].pass_on()
    series_forward_scan(r)
    params[1].arrive()
    unpack_params(r, 1, rows, attn.shape[0])
    series_forward_first(r)
    params[2].pass_on()
    series_forward_attention(r, begin)
    params[2].arrive()
    unpack_params(r, 2, rows, attn.shape[0])
    own_adjoint.wait()
    adjoint_over.arrive_all()

    @pl.when(me != last)
    def _():
        slope_over.arrive(last)

    series_middle(r, horizon)
    own_out.start()
    out_over.start()

    @pl.when(me != last)
    def _():
        predicted_over.send(last)

    for index, column in enumerate(BLOCKS_MIDDLE[:-1]):
        middle_sum.send[index] = low(r.g[:, column : column + 2 * LANES])
    r.attn_stage[...] = jnp.zeros_like(r.attn_stage)
    small = attn.shape[0]
    for group in range(groups):
        r.attn_stage[group * rows : group * rows + small, :] = r.g[
            group * small : (group + 1) * small, ATTN_OUT : ATTN_OUT + 2 * LANES
        ]
    middle_sum.send[len(BLOCKS_MIDDLE) - 1] = low(r.attn_stage[...])
    middle_sum.start()
    series_backward_attention(r)
    middle_sum.sum_time()
    series_backward_first(r)
    for index, column in enumerate(BLOCKS_FIRST):
        for part in range(2):
            at = column + part * LANES
            piece = r.g[:, at : at + LANES]
            if column == QUERY and part == 1:
                spare = width - LANES
                piece = jnp.concatenate(
                    [
                        piece[:, :spare],
                        r.g[:, VALUE : VALUE + head_width],
                        jnp.zeros((width, LANES - spare - head_width), jnp.float32),
                    ],
                    axis=1,
                )
            first_sum.send[2 * index + part] = low(piece)
    first_sum.start()
    middle_sum.sum_series()
    series_backward_scan(r)
    series_gate_grads(r)
    first_sum.sum_time()
    spare = width - LANES
    r.attn_stage[...] = jnp.zeros_like(r.attn_stage)
    for group in range(groups):
        r.attn_stage[group * rows : group * rows + VECTORS + 8, spare : spare + rows] = r.gv[
            :, group * rows : (group + 1) * rows
        ]
    for gate in range(4):
        grad = nn(r.x_flat[...], r.gate_grads[gate])
        lstm_sum.send[2 * gate] = low(grad[:, :LANES])
        rest = [grad[:, LANES:], jnp.zeros((width, LANES - spare), jnp.float32)]
        if gate == 0:
            rest = [grad[:, LANES:], r.attn_stage[:, spare:LANES]]
        lstm_sum.send[2 * gate + 1] = low(jnp.concatenate(rest, axis=1))
    lstm_sum.start()
    first_sum.sum_series()
    for step in range(1, count):
        to = input_over.other(step)
        series_input_grad(r, to, steps)
        input_over.send(to)
    series_input_grad(r, me, steps)
    own_input.start()
    lstm_sum.sum_time()

    @pl.when(me != last)
    def _():
        predicted_over.copy(last, me).wait_send()
        predicted_out[...] = jnp.zeros_like(predicted_out)

    @pl.when(me == last)
    def _():
        slope_over.sent()
        predicted_over.arrive_all()
        r.levels[last] = r.predicted[...]
        for level_at in range(LEVEL_TALLY):
            predicted_out[level_at] = jnp.concatenate(
                [r.levels[track][level_at : level_at + 1] for track in range(count)], axis=0
            )

    lstm_sum.sum_series()
    x_over.sent()
    adjoint_over.sent()
    for group in params:
        group.sent()
    own_out.wait()
    out_over.arrive_all()
    out_over.sent()
    middle_sum.finish()
    first_sum.finish()
    own_input.wait()
    input_over.arrive_all()
    input_over.sent()
    lstm_sum.finish()


def unpack_kernel(
    final_middle,
    final_first,
    final_lstm,
    lstm,
    glu_one,
    qkv,
    attn,
    glu_two,
    inner,
    middle,
    glu_three,
    level,
    table,
):
    width = inner.shape[1]
    spare = width - LANES

    def halves(out, column, final, index):
        out[:, column : column + LANES] = final[index]
        out[:, column + LANES : column + width] = final[index + 1][:, :spare]

    for gate in range(4):
        halves(lstm, gate * width, final_lstm, 2 * gate)
    vectors = final_lstm[1][:, spare : spare + table.shape[1]]
    table[...] = vectors[: table.shape[0]]
    level[...] = vectors[VECTORS : VECTORS + LEVEL_TALLY]
    for index in range(2):
        halves(glu_one, index * width, final_first, 2 * index)
        halves(qkv, index * width, final_first, 4 + 2 * index)
        glu_two[:, index * width : (index + 1) * width] = final_middle[index][:, :width]
        glu_three[:, index * width : (index + 1) * width] = final_middle[4 + index][:, :width]
    qkv[:, 2 * width :] = final_first[5][:, spare : spare + qkv.shape[1] - 2 * width]
    inner[...] = final_middle[2][:, :width]
    middle[...] = final_middle[3][:, :width]
    attn[...] = final_middle[6][: attn.shape[0], :width]


def whole_series(embedded_features, earliest_seen_moment, reach_choice, *others):
    count, steps, width = embedded_features.shape
    features = embedded_features.swapaxes(1, 2)
    adjoint = others[-2].swapaxes(1, 2)
    slopes = others[-1].swapaxes(0, 1)
    params = others[:-4] + (others[-4].T, others[-3].T)
    head_width = width // HEADS
    groups = lax.axis_size("dp")
    rows = params[0].shape[0]
    names = series_scratch(count * steps, width, head_width)
    names.update(travel_scratch(count, groups, steps, width, rows))
    smem, vmem, anywhere = (
        pl.BlockSpec(memory_space=space) for space in (pltpu.SMEM, pltpu.VMEM, pl.ANY)
    )
    out, predicted, input_grad, *finals = pl.pallas_call(
        series_kernel,
        out_shape=(
            jax.ShapeDtypeStruct(features.shape, jnp.bfloat16),
            jax.ShapeDtypeStruct(slopes.shape, jnp.float32),
            jax.ShapeDtypeStruct(features.shape, jnp.bfloat16),
            jax.ShapeDtypeStruct((count, rows, 2 * LANES), jnp.float32),
            jax.ShapeDtypeStruct((count, rows, LANES), jnp.float32),
            jax.ShapeDtypeStruct((count, rows, LANES), jnp.float32),
        ),
        in_specs=[smem, smem, anywhere, anywhere] + [vmem] * 11,
        out_specs=(anywhere, vmem, anywhere) + (vmem,) * 3,
        scratch_shapes=list(names.values()),
        compiler_params=pltpu.CompilerParams(
            vmem_limit_bytes=VMEM_BYTES, collective_id=0, has_side_effects=True
        ),
    )(
        earliest_seen_moment,
        reach_choice,
        features,
        adjoint,
        slopes,
        *params,
    )
    *grads, level_grad, table_grad = pl.pallas_call(
        unpack_kernel,
        out_shape=tuple(jax.ShapeDtypeStruct(param.shape, jnp.float32) for param in params),
        in_specs=[vmem] * 3,
        out_specs=(vmem,) * len(params),
    )(*finals)
    return (
        out.swapaxes(1, 2),
        predicted.swapaxes(0, 1),
        input_grad.swapaxes(1, 2),
        *grads,
        level_grad.T,
        table_grad.T,
    )


def on_device(embedded_features, *others):
    count, steps, _ = embedded_features.shape
    one_each = count == lax.axis_size("tm") == CHUNKS and steps == LANES
    return (whole_series if one_each else shards)(embedded_features, *others)


def solution(mesh):
    placed = (
        P("dp", "tm", None),
        P("dp"),
        P("dp"),
        P("dp", None),
        P("dp", None),
        P("dp", None),
        P("dp", None),
        P("dp", None),
        P("dp", None),
        P("dp", None),
        P("dp", None),
        P("dp", None),
        P("dp", None),
        P("dp", "tm", None),
        P("dp", None, "tm"),
    )
    return jax.shard_map(
        on_device,
        mesh=mesh,
        in_specs=placed,
        out_specs=(
            P("dp", "tm", None),
            P("dp", None, "tm"),
            P("dp", "tm", None),
            P("dp", None),
            P("dp", None),
            P("dp", None),
            P("dp", None),
            P("dp", None),
            P("dp", None),
            P("dp", None),
            P("dp", None),
            P("dp", None),
            P("dp", None),
        ),
        check_vma=False,
    )
```

```python
import types

import jax
import jax.numpy as jnp
from jax import lax
from jax.experimental import pallas as pl
from jax.experimental.pallas import tpu as pltpu
from jax.sharding import PartitionSpec as P

HEADS = 4
LEVEL_TALLY = 3
DEC = 24
MICRO = 2


EPSILON = 1e-05
NEG_BIG = -1e30
attend_group = 2
LOG2_E = 1.4426950408889634
VMEM_BYTES = 60 * 2**20


def entering(value, axis, join, neutral, backward):
    count, mine = (lax.axis_size(axis), lax.axis_index(axis))
    pieces = jax.tree.map(lambda part: lax.all_gather(part, axis), value)
    if backward:
        pieces = jax.tree.map(lambda part: part[::-1], pieces)
        mine = count - 1 - mine
    so_far = jax.tree.map(
        lambda part, zero: jnp.full_like(part, 0) + jnp.asarray(zero, part.dtype), value, neutral
    )

    def turn(position, so_far):
        longer = join(so_far, jax.tree.map(lambda part: part[position], pieces))
        return jax.tree.map(lambda new, old: jnp.where(position < mine, new, old), longer, so_far)

    return lax.fori_loop(0, count - 1, turn, so_far)


def narrow_convert(values):
    return values.astype(jnp.bfloat16)


def tensor_dot_plain(left, right):
    return jnp.dot(left, right, preferred_element_type=jnp.float32)


def flipped_dot(left, right):
    return lax.dot_general(
        left, right, (((0,), (0,)), ((), ())), preferred_element_type=jnp.float32
    )


def dot_against_flipped(left, right):
    return lax.dot_general(
        left, right, (((1,), (1,)), ((), ())), preferred_element_type=jnp.float32
    )


def affine_join(earlier, later):
    return (later[0] * earlier[0], later[0] * earlier[1] + later[1])


def layer_norm(values, gains, offsets):
    centred = values - jnp.mean(values, axis=-1, keepdims=True)
    spread = jnp.mean(centred * centred, axis=-1, keepdims=True)
    return centred * lax.rsqrt(spread + EPSILON) * gains + offsets


def gated_unit(pre_act):
    half_width = pre_act.shape[-1] // 2
    return pre_act[..., :half_width] * jax.nn.sigmoid(pre_act[..., half_width:])


def lstm_gates(pre_act, keep_mask):
    quarter = pre_act.shape[-1] // 4
    forget = jax.nn.sigmoid(pre_act[..., :quarter]) * keep_mask
    inflow = jax.nn.sigmoid(pre_act[..., quarter : 2 * quarter]) * jnp.tanh(
        pre_act[..., 2 * quarter : 3 * quarter]
    )
    out_gate = jax.nn.sigmoid(pre_act[..., 3 * quarter :])
    return (forget, inflow, out_gate)


def masked_scores(query_block, key_block, query_pos, key_pos, begin_block, scale):
    raw = jnp.einsum("gqhd,gkhd->ghqk", query_block, key_block, preferred_element_type=jnp.float32)
    lowest = jnp.minimum(begin_block[:, None], query_pos[None, :])
    allowed = (key_pos[None, None, :] <= query_pos[None, :, None]) & (
        key_pos[None, None, :] >= lowest[:, :, None]
    )
    return jnp.where(allowed[:, None], raw * scale, NEG_BIG)


def score_grad(chances, dprob, row_delta, scale):
    return narrow_convert(chances * (dprob[:, None] - row_delta[..., None]) * scale)


def shards(
    embedded_features,
    earliest_seen_moment,
    reach_choice,
    lstm_valve_coeffs,
    lstm_unit_coeffs,
    asker_lookup_coeffs,
    attend_exit_coeffs,
    attend_unit_coeffs,
    skipnet_entry_coeffs,
    skipnet_inner_coeffs,
    skipnet_unit_coeffs,
    level_map_coeffs,
    bias_gain_table,
    block_emit_adjoint,
    predicted_adjoint,
):
    (
        mat_lstm,
        mat_glu_one,
        mat_qkv,
        mat_attn,
        mat_glu_two,
        mat_inner,
        mat_middle,
        mat_glu_three,
        level_dot,
        vec_table,
    ) = (
        lax.all_gather(narrow_convert(lstm_valve_coeffs), "dp", axis=0, tiled=True),
        lax.all_gather(narrow_convert(lstm_unit_coeffs), "dp", axis=0, tiled=True),
        lax.all_gather(narrow_convert(asker_lookup_coeffs), "dp", axis=0, tiled=True),
        lax.all_gather(narrow_convert(attend_exit_coeffs), "dp", axis=0, tiled=True),
        lax.all_gather(narrow_convert(attend_unit_coeffs), "dp", axis=0, tiled=True),
        lax.all_gather(narrow_convert(skipnet_entry_coeffs), "dp", axis=0, tiled=True),
        lax.all_gather(narrow_convert(skipnet_inner_coeffs), "dp", axis=0, tiled=True),
        lax.all_gather(narrow_convert(skipnet_unit_coeffs), "dp", axis=0, tiled=True),
        lax.all_gather(narrow_convert(level_map_coeffs), "dp", axis=0, tiled=True),
        lax.all_gather(narrow_convert(bias_gain_table), "dp", axis=0, tiled=True),
    )
    series_per_device, steps_per_device, model_width = embedded_features.shape
    seq_total = steps_per_device * lax.axis_size("tm")
    head_width = model_width // HEADS
    count_of_rows = series_per_device * steps_per_device
    scale = head_width ** (-0.5)
    vec_full = vec_table.astype(jnp.float32)
    time_local = lax.axis_index("tm") * steps_per_device + jnp.arange(
        steps_per_device, dtype=jnp.int32
    )
    time_all = jnp.arange(seq_total, dtype=jnp.int32)
    horizon_len = jnp.where(reach_choice == 0, 1, jnp.where(reach_choice == 1, 5, 24))
    ahead_moment_filter = (
        (
            (time_local[None, :] >= seq_total - DEC)
            & (time_local[None, :] < seq_total - DEC + horizon_len[:, None])
        )
        .astype(jnp.float32)
        .reshape(count_of_rows, 1)
    )
    keep_mask = (
        (time_local[None, :] != earliest_seen_moment[:, None])
        .astype(jnp.float32)
        .reshape(count_of_rows, 1)
    )
    group_size = series_per_device // MICRO
    group_total = series_per_device // attend_group
    state_ones = jnp.ones((group_size, model_width), jnp.float32)
    state_zeros = jnp.zeros((group_size, model_width), jnp.float32)

    def split_groups(array):
        return array.reshape((group_total, attend_group) + array.shape[1:])

    input_rows = embedded_features.reshape(count_of_rows, model_width)
    input_full = input_rows.astype(jnp.float32)
    lstm_pre = tensor_dot_plain(input_rows, mat_lstm) + vec_full[:, 0:4].T.reshape(-1)
    forget, inflow, out_gate = lstm_gates(lstm_pre, keep_mask)
    forget_seq = forget.reshape(series_per_device, steps_per_device, model_width)
    inflow_seq = inflow.reshape(series_per_device, steps_per_device, model_width)
    mult_seq, cell_local = lax.associative_scan(affine_join, (forget_seq, inflow_seq), axis=1)
    cell_parts = []
    for group in range(MICRO):
        lower_row = group * group_size
        upper_row = lower_row + group_size
        _, arriving = entering(
            (mult_seq[lower_row:upper_row, -1], cell_local[lower_row:upper_row, -1]),
            "tm",
            affine_join,
            (state_ones, state_zeros),
            False,
        )
        cell_parts.append(arriving)
    cell_in = jnp.concatenate(cell_parts, axis=0)
    cell_seq = cell_local + mult_seq * cell_in[:, None, :]
    cell_tanh = jnp.tanh(cell_seq.reshape(count_of_rows, model_width))
    hidden_low = narrow_convert(out_gate * cell_tanh)
    glu_one_pre = tensor_dot_plain(hidden_low, mat_glu_one) + vec_full[:, 4:6].T.reshape(-1)
    first_sum = input_full + gated_unit(glu_one_pre)
    first = layer_norm(first_sum, vec_full[:, 6], vec_full[:, 7])
    first_low = narrow_convert(first)
    qkv_low = narrow_convert(tensor_dot_plain(first_low, mat_qkv))
    query_low = qkv_low[:, :model_width].reshape(
        series_per_device, steps_per_device, HEADS, head_width
    )
    key_value = qkv_low[:, model_width:].reshape(
        series_per_device, steps_per_device, model_width + head_width
    )
    key_value_all = lax.all_gather(key_value, "tm", axis=1, tiled=True)
    keys_all = key_value_all[..., :model_width].reshape(
        series_per_device, seq_total, HEADS, head_width
    )
    values_all = key_value_all[..., model_width:]

    def attend_forward(block_args):
        query_block, key_block, value_block, begin_block = block_args
        scores = masked_scores(query_block, key_block, time_local, time_all, begin_block, scale)
        row_top = jnp.max(scores, axis=-1, keepdims=True)
        row_exp = jnp.exp(scores - row_top)
        row_total = jnp.sum(row_exp, axis=-1, keepdims=True)
        weights_low = narrow_convert(row_exp / row_total)
        mixed_block = jnp.einsum(
            "ghqk,gkd->gqd", weights_low, value_block, preferred_element_type=jnp.float32
        ) * (1.0 / HEADS)
        return (mixed_block, (row_top + jnp.log(row_total))[..., 0])

    mixed, log_total = lax.map(
        attend_forward,
        (
            split_groups(query_low),
            split_groups(keys_all),
            split_groups(values_all),
            split_groups(earliest_seen_moment),
        ),
    )
    mixed_low = narrow_convert(mixed.reshape(count_of_rows, head_width))
    attn_low = narrow_convert(tensor_dot_plain(mixed_low, mat_attn))
    glu_two_pre = tensor_dot_plain(attn_low, mat_glu_two) + vec_full[:, 8:10].T.reshape(-1)
    second_sum = first + gated_unit(glu_two_pre)
    second = layer_norm(second_sum, vec_full[:, 10], vec_full[:, 11])
    second_low = narrow_convert(second)
    inner_pre = tensor_dot_plain(second_low, mat_inner) + vec_full[:, 12]
    inner_low = narrow_convert(jax.nn.elu(inner_pre))
    middle_low = narrow_convert(tensor_dot_plain(inner_low, mat_middle) + vec_full[:, 13])
    glu_three_pre = tensor_dot_plain(middle_low, mat_glu_three) + vec_full[:, 14:16].T.reshape(-1)
    final_sum = second + gated_unit(glu_three_pre)
    second_block_emit = layer_norm(final_sum, vec_full[:, 16], vec_full[:, 17])
    closing_narrowed = narrow_convert(second_block_emit)
    predicted_entries = tensor_dot_plain(closing_narrowed, level_dot) * ahead_moment_filter
    predicted_levels = predicted_entries.reshape(
        series_per_device, steps_per_device, LEVEL_TALLY
    ).transpose(0, 2, 1)
    predicted_slope = narrow_convert(
        predicted_adjoint.astype(jnp.float32).transpose(0, 2, 1).reshape(count_of_rows, LEVEL_TALLY)
        * ahead_moment_filter
    )
    level_slope = flipped_dot(closing_narrowed, predicted_slope)
    final_grad = block_emit_adjoint.reshape(count_of_rows, model_width).astype(
        jnp.float32
    ) + dot_against_flipped(predicted_slope, level_dot)
    _, norm_pull = jax.vjp(layer_norm, final_sum, vec_full[:, 16], vec_full[:, 17])
    sum_three_grad, gain_three_grad, offset_three_grad = norm_pull(final_grad)
    _, glu_pull = jax.vjp(gated_unit, glu_three_pre)
    (glu_three_grad,) = glu_pull(sum_three_grad)
    glu_three_low = narrow_convert(glu_three_grad)
    grad_glu_three = flipped_dot(middle_low, glu_three_low)
    middle_grad = dot_against_flipped(glu_three_low, mat_glu_three)
    middle_grad_low = narrow_convert(middle_grad)
    grad_middle = flipped_dot(inner_low, middle_grad_low)
    inner_grad = dot_against_flipped(middle_grad_low, mat_middle)
    _, elu_pull = jax.vjp(jax.nn.elu, inner_pre)
    (inner_pre_grad,) = elu_pull(inner_grad)
    inner_pre_low = narrow_convert(inner_pre_grad)
    grad_inner = flipped_dot(second_low, inner_pre_low)
    second_grad = sum_three_grad + dot_against_flipped(inner_pre_low, mat_inner)
    _, norm_pull = jax.vjp(layer_norm, second_sum, vec_full[:, 10], vec_full[:, 11])
    sum_two_grad, gain_two_grad, offset_two_grad = norm_pull(second_grad)
    _, glu_pull = jax.vjp(gated_unit, glu_two_pre)
    (glu_two_grad,) = glu_pull(sum_two_grad)
    glu_two_low = narrow_convert(glu_two_grad)
    grad_glu_two = flipped_dot(attn_low, glu_two_low)
    attn_grad_low = narrow_convert(dot_against_flipped(glu_two_low, mat_glu_two))
    grad_attn = flipped_dot(mixed_low, attn_grad_low)
    mixed_grad_low = narrow_convert(dot_against_flipped(attn_grad_low, mat_attn))
    head_grad = (mixed_grad_low * (1.0 / HEADS)).reshape(
        series_per_device, steps_per_device, head_width
    )

    def attend_backward(block_args):
        query_block, key_block, value_block, begin_block, lse_block, dout_block = block_args
        scores = masked_scores(query_block, key_block, time_local, time_all, begin_block, scale)
        chances = jnp.exp(scores - lse_block[..., None])
        dprob = jnp.einsum(
            "gqd,gkd->gqk", dout_block, value_block, preferred_element_type=jnp.float32
        )
        row_delta = jnp.sum(chances * dprob[:, None], axis=-1)
        dscore = score_grad(chances, dprob, row_delta, scale)
        dquery = jnp.einsum(
            "ghqk,gkhd->gqhd", dscore, key_block, preferred_element_type=jnp.float32
        )
        dkey = jnp.einsum(
            "ghqk,gqhd->gkhd", dscore, query_block, preferred_element_type=jnp.float32
        )
        dvalue = jnp.einsum(
            "ghqk,gqd->gkd", narrow_convert(chances), dout_block, preferred_element_type=jnp.float32
        )
        key_terms = jnp.concatenate(
            [dkey.reshape(attend_group, seq_total, model_width), dvalue], axis=-1
        )
        return (dquery, key_terms)

    dquery, key_terms = lax.map(
        attend_backward,
        (
            split_groups(query_low),
            split_groups(keys_all),
            split_groups(values_all),
            split_groups(earliest_seen_moment),
            log_total,
            split_groups(head_grad),
        ),
    )
    own_keys = lax.psum_scatter(
        key_terms.reshape(series_per_device, seq_total, model_width + head_width),
        "tm",
        scatter_dimension=1,
        tiled=True,
    )
    qkv_grad = jnp.concatenate(
        [
            dquery.reshape(count_of_rows, model_width),
            own_keys.reshape(count_of_rows, model_width + head_width),
        ],
        axis=1,
    )
    qkv_grad_low = narrow_convert(qkv_grad)
    grad_qkv = flipped_dot(first_low, qkv_grad_low)
    first_grad = sum_two_grad + dot_against_flipped(qkv_grad_low, mat_qkv)
    _, norm_pull = jax.vjp(layer_norm, first_sum, vec_full[:, 6], vec_full[:, 7])
    sum_one_grad, gain_one_grad, offset_one_grad = norm_pull(first_grad)
    _, glu_pull = jax.vjp(gated_unit, glu_one_pre)
    (glu_one_grad,) = glu_pull(sum_one_grad)
    glu_one_low = narrow_convert(glu_one_grad)
    grad_glu_one = flipped_dot(hidden_low, glu_one_low)
    hidden_grad = dot_against_flipped(glu_one_low, mat_glu_one)
    out_gate_grad = hidden_grad * cell_tanh
    direct_grad = (hidden_grad * out_gate * (1.0 - cell_tanh * cell_tanh)).reshape(
        series_per_device, steps_per_device, model_width
    )
    next_forget = jnp.concatenate([forget_seq[:, 1:], jnp.ones_like(forget_seq[:, :1])], axis=1)
    rev_mult, rev_cell = lax.associative_scan(
        affine_join, (next_forget, direct_grad), axis=1, reverse=True
    )
    head_mult = forget_seq[:, 0] * rev_mult[:, 0]
    head_cell = forget_seq[:, 0] * rev_cell[:, 0]
    coming_parts = []
    for group in range(MICRO):
        lower_row = group * group_size
        upper_row = lower_row + group_size
        _, coming = entering(
            (head_mult[lower_row:upper_row], head_cell[lower_row:upper_row]),
            "tm",
            affine_join,
            (state_ones, state_zeros),
            True,
        )
        coming_parts.append(coming)
    coming_all = jnp.concatenate(coming_parts, axis=0)
    cell_grad = rev_cell + rev_mult * coming_all[:, None, :]
    cell_prev = jnp.concatenate([cell_in[:, None, :], cell_seq[:, :-1]], axis=1)
    forget_grad = (cell_grad * cell_prev).reshape(count_of_rows, model_width)
    _, gate_pull = jax.vjp(lambda pre_value: lstm_gates(pre_value, keep_mask), lstm_pre)
    (lstm_pre_grad,) = gate_pull(
        (forget_grad, cell_grad.reshape(count_of_rows, model_width), out_gate_grad)
    )
    lstm_low = narrow_convert(lstm_pre_grad)
    grad_lstm = flipped_dot(input_rows, lstm_low)
    input_grad = sum_one_grad + dot_against_flipped(lstm_low, mat_lstm)
    grad_table = jnp.concatenate(
        [
            jnp.sum(lstm_pre_grad, axis=0).reshape(4, model_width).T,
            jnp.sum(glu_one_grad, axis=0).reshape(2, model_width).T,
            gain_one_grad[:, None],
            offset_one_grad[:, None],
            jnp.sum(glu_two_grad, axis=0).reshape(2, model_width).T,
            gain_two_grad[:, None],
            offset_two_grad[:, None],
            jnp.sum(inner_pre_grad, axis=0)[:, None],
            jnp.sum(middle_grad, axis=0)[:, None],
            jnp.sum(glu_three_grad, axis=0).reshape(2, model_width).T,
            gain_three_grad[:, None],
            offset_three_grad[:, None],
        ],
        axis=1,
    )
    (
        whole_lstm,
        whole_glu_one,
        whole_qkv,
        whole_attn,
        whole_glu_two,
        whole_inner,
        whole_middle,
        whole_glu_three,
        whole_quant,
        whole_table,
    ) = lax.psum(
        (
            grad_lstm,
            grad_glu_one,
            grad_qkv,
            grad_attn,
            grad_glu_two,
            grad_inner,
            grad_middle,
            grad_glu_three,
            level_slope,
            grad_table,
        ),
        "tm",
    )
    summed = (
        lax.psum_scatter(
            whole_lstm.astype(jnp.bfloat16), "dp", scatter_dimension=0, tiled=True
        ).astype(jnp.float32),
        lax.psum_scatter(
            whole_glu_one.astype(jnp.bfloat16), "dp", scatter_dimension=0, tiled=True
        ).astype(jnp.float32),
        lax.psum_scatter(
            whole_qkv.astype(jnp.bfloat16), "dp", scatter_dimension=0, tiled=True
        ).astype(jnp.float32),
        lax.psum_scatter(
            whole_attn.astype(jnp.bfloat16), "dp", scatter_dimension=0, tiled=True
        ).astype(jnp.float32),
        lax.psum_scatter(
            whole_glu_two.astype(jnp.bfloat16), "dp", scatter_dimension=0, tiled=True
        ).astype(jnp.float32),
        lax.psum_scatter(
            whole_inner.astype(jnp.bfloat16), "dp", scatter_dimension=0, tiled=True
        ).astype(jnp.float32),
        lax.psum_scatter(
            whole_middle.astype(jnp.bfloat16), "dp", scatter_dimension=0, tiled=True
        ).astype(jnp.float32),
        lax.psum_scatter(
            whole_glu_three.astype(jnp.bfloat16), "dp", scatter_dimension=0, tiled=True
        ).astype(jnp.float32),
        lax.psum_scatter(
            whole_quant.astype(jnp.bfloat16), "dp", scatter_dimension=0, tiled=True
        ).astype(jnp.float32),
        lax.psum_scatter(
            whole_table.astype(jnp.bfloat16), "dp", scatter_dimension=0, tiled=True
        ).astype(jnp.float32),
    )
    final_out = second_block_emit.astype(jnp.bfloat16).reshape(
        series_per_device, steps_per_device, model_width
    )
    input_out = input_grad.astype(jnp.bfloat16).reshape(
        series_per_device, steps_per_device, model_width
    )
    return (
        final_out,
        predicted_levels,
        input_out,
        summed[0],
        summed[1],
        summed[2],
        summed[3],
        summed[4],
        summed[5],
        summed[6],
        summed[7],
        summed[8],
        summed[9],
    )


def lane_head(shape, head_width, head):
    lane = lax.broadcasted_iota(jnp.int32, shape, len(shape) - 1)
    return (lane >= head * head_width) & (lane < (head + 1) * head_width)


FORGET, ENTER, CANDIDATE, EXIT = 0, 256, 512, 768
GLU_ONE_A, GLU_ONE_B = 1024, 1280
QUERY, KEY, VALUE = 1536, 1792, 2048
GLU_TWO_A, GLU_TWO_B = 2176, 2432
INNER, MIDDLE = 2688, 2944
GLU_THREE_A, GLU_THREE_B = 3200, 3456
ATTN_OUT = 3712
PACKED = 3968
VECTORS = 24
LANES = 128
CHUNKS = 8
TILE = 256
DENSE = 1024


def nn(left, right):
    return jnp.dot(left, right, preferred_element_type=jnp.float32)


def nt(left, right):
    return lax.dot_general(
        left, right, (((1,), (1,)), ((), ())), preferred_element_type=jnp.float32
    )


def tn(left, right):
    return lax.dot_general(
        left, right, (((0,), (0,)), ((), ())), preferred_element_type=jnp.float32
    )


def low(values):
    return values.astype(jnp.bfloat16)


def sigmoid(values):
    return 0.5 * jnp.tanh(0.5 * values) + 0.5


def normalise(values, gain, shift):
    centred = values - jnp.mean(values, axis=-1, keepdims=True)
    spread = jnp.mean(centred * centred, axis=-1, keepdims=True)
    inverse = lax.rsqrt(spread + EPSILON)
    unit = centred * inverse
    return unit * gain + shift, unit, inverse


def normalise_back(grad, unit, inverse, gain):
    scaled = grad * gain
    return inverse * (
        scaled
        - jnp.mean(scaled, axis=-1, keepdims=True)
        - unit * jnp.mean(scaled * unit, axis=-1, keepdims=True)
    )


def rows_of(tile, size=TILE):
    return pl.ds(pl.multiple_of(tile * size, size), size)


def put_halves(ref, rows, values):
    ref[0, rows, :] = values[:, :LANES]
    ref[1, rows, : values.shape[1] - LANES] = values[:, LANES:]


def get_halves(ref, rows, width):
    return jnp.concatenate([ref[0, rows, :], ref[1, rows, : width - LANES]], axis=1)


def row_sum(ref, column, values):
    ref[column : column + 1, :] += jnp.sum(values, axis=0, keepdims=True)


def series_scratch(span, width, head_width):
    full = pltpu.VMEM((span, width), jnp.float32)
    half = pltpu.VMEM((span, width), jnp.bfloat16)
    flat = pltpu.VMEM((width, span), jnp.bfloat16)
    scan = pltpu.VMEM((2, span, LANES), jnp.float32)
    scan_more = pltpu.VMEM((2, span + 8, LANES), jnp.float32)
    narrow = pltpu.VMEM((span, head_width), jnp.bfloat16)
    column = pltpu.VMEM((span, 1), jnp.float32)
    return dict(
        forget=scan_more,
        local=scan,
        mult=scan,
        cell=scan_more,
        carry=pltpu.VMEM((2, CHUNKS, LANES), jnp.float32),
        enter_gate=full,
        candidate=full,
        exit_gate=full,
        cell_tanh=full,
        hidden=half,
        glu_one=full,
        gate_one=full,
        unit_one=full,
        inverse_one=column,
        first_low=half,
        queries=half,
        keys=half,
        values=narrow,
        head_queries=pltpu.VMEM((HEADS, span, width), jnp.bfloat16),
        head_keys=pltpu.VMEM((HEADS, span, width), jnp.bfloat16),
        **{
            "chances%d" % tile: pltpu.VMEM((HEADS, TILE, (tile + 1) * TILE), jnp.float32)
            for tile in range(span // TILE)
        },
        chance_sum=pltpu.VMEM((span, span), jnp.bfloat16),
        **{
            "score_grads%d" % tile: pltpu.VMEM((HEADS, span - tile * TILE, TILE), jnp.bfloat16)
            for tile in range(span // TILE)
        },
        block=pltpu.VMEM((TILE, span), jnp.float32),
        mixed=narrow,
        mixed_grad=narrow,
        sum_two_grad=full,
        query_grad=half,
        key_grad=half,
        value_grad=narrow,
        gate_grads=pltpu.VMEM((4, span, width), jnp.bfloat16),
        x=half,
        x_flat=flat,
        adjoint=flat,
        out=flat,
        input_grad=flat,
        w=pltpu.VMEM((width, PACKED), jnp.bfloat16),
        g=pltpu.VMEM((width, PACKED), jnp.float32),
        gv=pltpu.VMEM((VECTORS + 8, width), jnp.float32),
        vec=pltpu.VMEM((VECTORS, width), jnp.float32),
        level=pltpu.VMEM((8, width), jnp.bfloat16),
    )


def series_gates(r, begin, chunk, steps):
    w, vec = r.w, r.vec
    width = r.x.shape[1]
    rows = rows_of(chunk, steps)
    x = r.x_flat[:, rows].T
    r.x[rows, :] = x

    def pre(block, column):
        return nn(x, w[:, block : block + width]) + vec[column : column + 1, :]

    time = chunk * steps + lax.broadcasted_iota(jnp.int32, (steps, width), 0)
    forget = jnp.where(time != begin, sigmoid(pre(FORGET, 0)), 0.0)
    enter = sigmoid(pre(ENTER, 1))
    candidate = jnp.tanh(pre(CANDIDATE, 2))
    r.enter_gate[rows, :] = enter
    r.candidate[rows, :] = candidate
    r.exit_gate[rows, :] = sigmoid(pre(EXIT, 3))
    put_halves(r.forget, rows, forget)
    put_halves(r.local, rows, enter * candidate)


def series_forward_scan(r):
    span = r.x.shape[0]
    steps = span // CHUNKS
    zeros = jnp.zeros((CHUNKS, LANES), jnp.float32)

    def step(t, state):
        out = []
        at = pl.ds(t, CHUNKS, stride=steps)
        for half in range(2):
            cell, mult = state[half]
            forget = r.forget[half, at, :]
            cell = forget * cell + r.local[half, at, :]
            mult = mult * forget
            r.local[half, at, :] = cell
            r.mult[half, at, :] = mult
            out.append((cell, mult))
        return tuple(out)

    ends = lax.fori_loop(0, steps, step, ((zeros, zeros + 1.0),) * 2, unroll=8)
    for half in range(2):
        cells, mults = ends[half]
        state = jnp.zeros((1, LANES), jnp.float32)
        r.carry[half, 0:1, :] = state
        for chunk in range(CHUNKS - 1):
            state = cells[chunk : chunk + 1] + mults[chunk : chunk + 1] * state
            r.carry[half, chunk + 1 : chunk + 2, :] = state
        r.cell[half, 0:8, :] = zeros


def series_forward_first(r):
    w, vec = r.w, r.vec
    span, width = r.x.shape
    head_width = width // HEADS
    steps = span // CHUNKS

    def cells(chunk, _):
        rows = rows_of(chunk, steps)
        later = pl.ds(pl.multiple_of(chunk * steps + 8, 8), steps)
        for half in range(2):
            r.cell[half, later, :] = r.local[half, rows, :] + r.mult[half, rows, :] * r.carry[
                half, pl.ds(chunk, 1), :
            ]
        tanh = jnp.tanh(get_halves(r.cell, later, width))
        r.cell_tanh[rows, :] = tanh
        r.hidden[rows, :] = low(r.exit_gate[rows, :] * tanh)
        return 0

    lax.fori_loop(0, CHUNKS, cells, 0)

    def first(tile, _):
        rows = rows_of(tile, DENSE)
        hidden = r.hidden[rows, :]
        value = nn(hidden, w[:, GLU_ONE_A : GLU_ONE_A + width]) + vec[4:5, :]
        gate = sigmoid(nn(hidden, w[:, GLU_ONE_B : GLU_ONE_B + width]) + vec[5:6, :])
        r.glu_one[rows, :] = value
        r.gate_one[rows, :] = gate
        out, unit, inverse = normalise(
            r.x[rows, :].astype(jnp.float32) + value * gate, vec[6:7, :], vec[7:8, :]
        )
        r.unit_one[rows, :] = unit
        r.inverse_one[rows, :] = inverse
        out = low(out)
        r.first_low[rows, :] = out
        query = low(nn(out, w[:, QUERY : QUERY + width]))
        key = low(nn(out, w[:, KEY : KEY + width]))
        r.keys[rows, :] = key
        r.values[rows, :] = low(nn(out, w[:, VALUE : VALUE + head_width]))
        for head in range(HEADS):
            mine = lane_head((DENSE, width), head_width, head)
            r.head_queries[head, rows, :] = jnp.where(mine, query, jnp.zeros_like(query))
            r.head_keys[head, rows, :] = jnp.where(mine, key, jnp.zeros_like(key))
        return 0

    lax.fori_loop(0, span // DENSE, first, 0)


def series_forward_attention(r, begin):
    span, head_width = r.values.shape
    scale = head_width ** (-0.5) * LOG2_E
    for tile in range(span // TILE):
        rows = slice(tile * TILE, (tile + 1) * TILE)
        seen = (tile + 1) * TILE
        row = tile * TILE + lax.broadcasted_iota(jnp.int32, (TILE, seen), 0)
        col = lax.broadcasted_iota(jnp.int32, (TILE, seen), 1)
        chances = getattr(r, "chances%d" % tile)
        r.block[:, :seen] = jnp.where(
            (col <= row) & (col >= jnp.minimum(begin, row)), 0.0, NEG_BIG
        )

        def one_head(head, _):
            scores = (
                nt(r.head_queries[head, rows, :], r.keys[:seen, :]) * scale + r.block[:, :seen]
            )
            top = jnp.max(scores, axis=-1, keepdims=True)
            raised = jnp.exp2(scores - top)
            total = jnp.sum(raised, axis=-1, keepdims=True)
            chances[head] = raised * (1.0 / total)
            return 0

        lax.fori_loop(0, HEADS, one_head, 0, unroll=True)
        weights = chances[0]
        for head in range(1, HEADS):
            weights = weights + chances[head]
        weights = low(weights)
        r.chance_sum[rows, :seen] = weights
        r.mixed[rows, :] = low(nn(weights, r.values[:seen, :]) * (1.0 / HEADS))


def series_middle(r, horizon):
    w, vec, g, gv = r.w, r.vec, r.g, r.gv
    span, width = r.x.shape
    head_width = width // HEADS

    def middle(tile, last):
        rows = rows_of(tile, DENSE)
        first = r.unit_one[rows, :] * vec[6:7, :] + vec[7:8, :]
        mixed = r.mixed[rows, :]
        attn = low(nn(mixed, w[:head_width, ATTN_OUT : ATTN_OUT + width]))
        value_two = nn(attn, w[:, GLU_TWO_A : GLU_TWO_A + width]) + vec[8:9, :]
        gate_two = sigmoid(nn(attn, w[:, GLU_TWO_B : GLU_TWO_B + width]) + vec[9:10, :])
        second, unit_two, inverse_two = normalise(
            first + value_two * gate_two, vec[10:11, :], vec[11:12, :]
        )
        second_low = low(second)
        inner_pre = nn(second_low, w[:, INNER : INNER + width]) + vec[12:13, :]
        inner_exp = jnp.exp(jnp.minimum(inner_pre, 0.0))
        inner_low = low(jnp.where(inner_pre > 0, inner_pre, inner_exp - 1.0))
        middle_low = low(nn(inner_low, w[:, MIDDLE : MIDDLE + width]) + vec[13:14, :])
        value_three = nn(middle_low, w[:, GLU_THREE_A : GLU_THREE_A + width]) + vec[14:15, :]
        gate_three = sigmoid(
            nn(middle_low, w[:, GLU_THREE_B : GLU_THREE_B + width]) + vec[15:16, :]
        )
        final, unit_three, inverse_three = normalise(
            second + value_three * gate_three, vec[16:17, :], vec[17:18, :]
        )
        final_low = low(final)
        r.out[:, rows] = final_low.T
        grad = r.adjoint[:, rows].T.astype(jnp.float32)
        if last:
            start = span - DENSE
            time = start + lax.broadcasted_iota(jnp.int32, (8, DENSE), 1)
            ahead = jnp.where((time >= span - DEC) & (time < span - DEC + horizon), 1.0, 0.0)
            steps = r.slope.shape[1]
            r.predicted[...] = (nt(r.level[...], final_low) * ahead)[:, DENSE - steps :]
            slope = jnp.concatenate(
                [jnp.zeros((8, DENSE - steps), jnp.float32), r.slope[...]], axis=1
            )
            slope = low(slope * ahead)
            gv[VECTORS : VECTORS + 8, :] = nn(slope, final_low)
            grad = grad + tn(slope, r.level[...])
        row_sum(gv, 16, grad * unit_three)
        row_sum(gv, 17, grad)
        sum_three = normalise_back(grad, unit_three, inverse_three, vec[16:17, :])
        grad_a = sum_three * gate_three
        grad_b = grad_a * value_three * (1.0 - gate_three)
        row_sum(gv, 14, grad_a)
        row_sum(gv, 15, grad_b)
        low_a, low_b = low(grad_a), low(grad_b)
        g[:, GLU_THREE_A : GLU_THREE_A + width] += tn(middle_low, low_a)
        g[:, GLU_THREE_B : GLU_THREE_B + width] += tn(middle_low, low_b)
        middle_grad = nt(low_a, w[:, GLU_THREE_A : GLU_THREE_A + width]) + nt(
            low_b, w[:, GLU_THREE_B : GLU_THREE_B + width]
        )
        row_sum(gv, 13, middle_grad)
        middle_grad = low(middle_grad)
        g[:, MIDDLE : MIDDLE + width] += tn(inner_low, middle_grad)
        inner_grad = nt(middle_grad, w[:, MIDDLE : MIDDLE + width]) * jnp.where(
            inner_pre > 0, 1.0, inner_exp
        )
        row_sum(gv, 12, inner_grad)
        inner_grad = low(inner_grad)
        g[:, INNER : INNER + width] += tn(second_low, inner_grad)
        grad = sum_three + nt(inner_grad, w[:, INNER : INNER + width])
        row_sum(gv, 10, grad * unit_two)
        row_sum(gv, 11, grad)
        sum_two = normalise_back(grad, unit_two, inverse_two, vec[10:11, :])
        r.sum_two_grad[rows, :] = sum_two
        grad_a = sum_two * gate_two
        grad_b = grad_a * value_two * (1.0 - gate_two)
        row_sum(gv, 8, grad_a)
        row_sum(gv, 9, grad_b)
        low_a, low_b = low(grad_a), low(grad_b)
        g[:, GLU_TWO_A : GLU_TWO_A + width] += tn(attn, low_a)
        g[:, GLU_TWO_B : GLU_TWO_B + width] += tn(attn, low_b)
        attn_grad = low(
            nt(low_a, w[:, GLU_TWO_A : GLU_TWO_A + width])
            + nt(low_b, w[:, GLU_TWO_B : GLU_TWO_B + width])
        )
        g[:head_width, ATTN_OUT : ATTN_OUT + width] += tn(mixed, attn_grad)
        r.mixed_grad[rows, :] = low(nt(attn_grad, w[:head_width, ATTN_OUT : ATTN_OUT + width]))
        return 0

    lax.fori_loop(0, span // DENSE - 1, lambda tile, _: middle(tile, False), 0)
    middle(span // DENSE - 1, True)


def series_backward_attention(r):
    span, head_width = r.values.shape
    width = head_width * HEADS
    scale = head_width ** (-0.5)
    for tile in range(span // TILE):
        rows = slice(tile * TILE, (tile + 1) * TILE)
        seen = (tile + 1) * TILE
        held = getattr(r, "chances%d" % tile)
        head_grad = r.mixed_grad[rows, :] * (1.0 / HEADS)
        r.block[:, :seen] = nt(head_grad, r.values[:seen, :]) * scale

        def one_head(head, total):
            chances = held[head]
            slope = r.block[:, :seen]
            delta = jnp.sum(chances * slope, axis=-1, keepdims=True)
            grads = low(chances * (slope - delta))
            for part in range(tile + 1):
                getattr(r, "score_grads%d" % part)[
                    head, (tile - part) * TILE : (tile - part + 1) * TILE, :
                ] = grads[:, part * TILE : (part + 1) * TILE]
            return total + nn(grads, r.head_keys[head, :seen, :])

        r.query_grad[rows, :] = low(
            lax.fori_loop(0, HEADS, one_head, jnp.zeros((TILE, width), jnp.float32), unroll=True)
        )
    for tile in range(span // TILE):
        cols = slice(tile * TILE, (tile + 1) * TILE)
        start = tile * TILE

        def one_key(head, total):
            return total + tn(
                getattr(r, "score_grads%d" % tile)[head], r.head_queries[head, start:, :]
            )

        r.key_grad[cols, :] = low(
            lax.fori_loop(0, HEADS, one_key, jnp.zeros((TILE, width), jnp.float32), unroll=True)
        )
        r.value_grad[cols, :] = low(
            tn(r.chance_sum[start:, cols], r.mixed_grad[start:, :] * (1.0 / HEADS))
        )


def series_backward_first(r):
    w, vec, g, gv = r.w, r.vec, r.g, r.gv
    span, width = r.hidden.shape
    head_width = width // HEADS

    def back(tile, _):
        rows = rows_of(tile, DENSE)
        query, key, value = r.query_grad[rows, :], r.key_grad[rows, :], r.value_grad[rows, :]
        grad = (
            r.sum_two_grad[rows, :]
            + nt(query, w[:, QUERY : QUERY + width])
            + nt(key, w[:, KEY : KEY + width])
            + nt(value, w[:, VALUE : VALUE + head_width])
        )
        first = r.first_low[rows, :]
        g[:, QUERY : QUERY + width] += tn(first, query)
        g[:, KEY : KEY + width] += tn(first, key)
        g[:, VALUE : VALUE + head_width] += tn(first, value)
        unit = r.unit_one[rows, :]
        row_sum(gv, 6, grad * unit)
        row_sum(gv, 7, grad)
        sum_one = normalise_back(grad, unit, r.inverse_one[rows, :], vec[6:7, :])
        r.sum_two_grad[rows, :] = sum_one
        gate = r.gate_one[rows, :]
        grad_a = sum_one * gate
        grad_b = grad_a * r.glu_one[rows, :] * (1.0 - gate)
        row_sum(gv, 4, grad_a)
        row_sum(gv, 5, grad_b)
        low_a, low_b = low(grad_a), low(grad_b)
        hidden = r.hidden[rows, :]
        g[:, GLU_ONE_A : GLU_ONE_A + width] += tn(hidden, low_a)
        g[:, GLU_ONE_B : GLU_ONE_B + width] += tn(hidden, low_b)
        hidden_grad = nt(low_a, w[:, GLU_ONE_A : GLU_ONE_A + width]) + nt(
            low_b, w[:, GLU_ONE_B : GLU_ONE_B + width]
        )
        tanh, gate = r.cell_tanh[rows, :], r.exit_gate[rows, :]
        put_halves(r.local, rows, hidden_grad * gate * (1.0 - tanh * tanh))
        exit_grad = hidden_grad * tanh * gate * (1.0 - gate)
        row_sum(gv, 3, exit_grad)
        r.gate_grads[3, rows, :] = low(exit_grad)
        return 0

    lax.fori_loop(0, span // DENSE, back, 0)


def series_backward_scan(r):
    span = r.x.shape[0]
    steps = span // CHUNKS
    zeros = jnp.zeros((CHUNKS, LANES), jnp.float32)
    for half in range(2):
        r.forget[half, span:, :] = zeros

    def step(count, state):
        t = steps - 1 - count
        out = []
        at, after = pl.ds(t, CHUNKS, stride=steps), pl.ds(t + 1, CHUNKS, stride=steps)
        for half in range(2):
            grad, mult = state[half]
            forget = r.forget[half, after, :]
            grad = forget * grad + r.local[half, at, :]
            mult = mult * forget
            r.local[half, at, :] = grad
            r.mult[half, at, :] = mult
            out.append((grad, mult))
        return tuple(out)

    ends = lax.fori_loop(0, steps, step, ((zeros, zeros + 1.0),) * 2, unroll=8)
    for half in range(2):
        grads, mults = ends[half]
        state = jnp.zeros((1, LANES), jnp.float32)
        r.carry[half, CHUNKS - 1 : CHUNKS, :] = state
        for chunk in range(CHUNKS - 1, 0, -1):
            state = grads[chunk : chunk + 1] + mults[chunk : chunk + 1] * state
            r.carry[half, chunk - 1 : chunk, :] = state


def series_gate_grads(r):
    gv = r.gv
    span, width = r.x.shape
    steps = span // CHUNKS

    def back(chunk, _):
        rows = rows_of(chunk, steps)
        before = pl.ds(chunk * steps + 7, steps)
        grad, grad_forget = [], []
        for half in range(2):
            one = r.local[half, rows, :] + r.mult[half, rows, :] * r.carry[
                half, pl.ds(chunk, 1), :
            ]
            forget = r.forget[half, rows, :]
            grad.append(one)
            grad_forget.append(one * r.cell[half, before, :] * forget * (1.0 - forget))
        grad = jnp.concatenate([grad[0], grad[1][:, : width - LANES]], axis=1)
        grad_forget = jnp.concatenate([grad_forget[0], grad_forget[1][:, : width - LANES]], axis=1)
        enter, candidate = r.enter_gate[rows, :], r.candidate[rows, :]
        grad_enter = grad * candidate * enter * (1.0 - enter)
        grad_candidate = grad * enter * (1.0 - candidate * candidate)
        row_sum(gv, 0, grad_forget)
        row_sum(gv, 1, grad_enter)
        row_sum(gv, 2, grad_candidate)
        r.gate_grads[0, rows, :] = low(grad_forget)
        r.gate_grads[1, rows, :] = low(grad_enter)
        r.gate_grads[2, rows, :] = low(grad_candidate)
        return 0

    lax.fori_loop(0, CHUNKS, back, 0)


def series_input_grad(r, chunk, steps):
    width = r.x.shape[1]
    rows = rows_of(chunk, steps)
    out = r.sum_two_grad[rows, :].T
    for gate, block in enumerate((FORGET, ENTER, CANDIDATE, EXIT)):
        out = out + nt(r.w[:, block : block + width], r.gate_grads[gate, rows, :])
    r.input_grad[:, rows] = low(out)


class Exchange:
    def __init__(self, sems, axis, source, target):
        self.sems, self.axis, self.source, self.target = sems, axis, source, target
        self.count, self.me = lax.axis_size(axis), lax.axis_index(axis)

    def other(self, step):
        return lax.rem(self.me + step, self.count)

    def copy(self, to, origin):
        return pltpu.make_async_remote_copy(
            src_ref=self.source(to),
            dst_ref=self.target(origin),
            send_sem=self.sems.at[0, to],
            recv_sem=self.sems.at[1, origin],
            device_id={self.axis: to},
            device_id_type=pl.DeviceIdType.MESH,
        )

    def send(self, to):
        self.copy(to, self.me).start()

    def arrive(self, origin):
        self.copy(origin, origin).wait_recv()

    def start(self):
        for step in range(1, self.count):
            self.send(self.other(step))

    def arrive_all(self):
        for step in range(1, self.count):
            self.arrive(self.other(step))

    def sent(self):
        for step in range(1, self.count):
            to = self.other(step)
            self.copy(to, self.me).wait_send()


PAD_ROWS = 48
GROUP_COLUMNS = (384, 384, 768)
BLOCKS_MIDDLE = (GLU_TWO_A, GLU_TWO_B, INNER, MIDDLE, GLU_THREE_A, GLU_THREE_B, ATTN_OUT)
BLOCKS_FIRST = (GLU_ONE_A, GLU_ONE_B, QUERY, KEY)
BLOCKS_LSTM = (FORGET, ENTER, CANDIDATE, EXIT)


def travel_scratch(count, groups, steps, width, rows):
    half, wide = LANES, 2 * LANES

    def pieces(lanes):
        return dict(
            send=pltpu.VMEM((count, width, lanes), jnp.bfloat16),
            land=pltpu.VMEM((count, width, lanes), jnp.bfloat16),
            part=pltpu.VMEM((groups, rows, lanes), jnp.float32),
            parts=pltpu.VMEM((groups, rows, lanes), jnp.float32),
        )

    out = dict(
        slope=pltpu.VMEM((8, steps), jnp.float32),
        slopes=pltpu.VMEM((count, 8, steps), jnp.float32),
        levels=pltpu.VMEM((count, 8, steps), jnp.float32),
        predicted=pltpu.VMEM((8, steps), jnp.float32),
        stage=pltpu.VMEM((width, 2 * GROUP_COLUMNS[2]), jnp.float32),
        attn_stage=pltpu.VMEM((width, wide), jnp.float32),
        table_stage=pltpu.VMEM((PAD_ROWS, LANES), jnp.float32),
    )
    for group, columns in enumerate(GROUP_COLUMNS):
        out["params%d" % group] = pltpu.VMEM((2, groups, PAD_ROWS, columns), jnp.bfloat16)
        out["params%d_dp" % group] = pltpu.SemaphoreType.DMA((2, groups))
        out["params%d_core" % group] = pltpu.SemaphoreType.DMA((2, groups))
    for name, lanes in (("middle", wide), ("first", half), ("lstm", half)):
        for what, shape in pieces(lanes).items():
            out[name + "_" + what] = shape
        out[name + "_tm"] = pltpu.SemaphoreType.DMA((2, count))
        out[name + "_dp"] = pltpu.SemaphoreType.DMA((2, groups))
        out[name + "_all"] = pltpu.SemaphoreType.DMA((2, count))
    for name in ("x", "adjoint", "out", "input", "slope", "predicted"):
        out[name + "_sems"] = pltpu.SemaphoreType.DMA((2, count))
    out["own_sems"] = pltpu.SemaphoreType.DMA((4,))
    return out


class Parameters:
    def __init__(self, r, group):
        self.buffer = getattr(r, "params%d" % group)
        self.mine, self.core = lax.axis_index("dp"), lax.rem(lax.axis_index("tm"), 2)
        self.count = lax.axis_size("dp")
        buffer, core, mine = self.buffer, self.core, self.mine
        self.over = Exchange(
            getattr(r, "params%d_dp" % group),
            "dp",
            lambda to: buffer.at[core, mine],
            lambda origin: buffer.at[core, origin],
        )
        self.sems = getattr(r, "params%d_core" % group)
        self.sibling = lax.axis_index("tm") + 1 - 2 * core

    def hand(self, origin, core):
        return pltpu.make_async_remote_copy(
            src_ref=self.buffer.at[core, origin],
            dst_ref=self.buffer.at[core, origin],
            send_sem=self.sems.at[0, origin],
            recv_sem=self.sems.at[1, origin],
            device_id={"tm": self.sibling},
            device_id_type=pl.DeviceIdType.MESH,
        )

    def pass_on(self):
        for step in range(1, self.count):
            origin = self.over.other(step)
            self.over.arrive(origin)
            self.hand(origin, self.core).start()

    def arrive(self):
        for step in range(1, self.count):
            self.hand(self.over.other(step), 1 - self.core).wait_recv()

    def sent(self):
        self.over.sent()
        for step in range(1, self.count):
            self.hand(self.over.other(step), self.core).wait_send()


class Reduction:
    def __init__(self, r, name, final, owners):
        self.send, self.land = getattr(r, name + "_send"), getattr(r, name + "_land")
        self.part, self.parts = getattr(r, name + "_part"), getattr(r, name + "_parts")
        self.final, self.owners = final, owners
        self.me, self.mine = lax.axis_index("tm"), lax.axis_index("dp")
        self.count, self.groups = lax.axis_size("tm"), lax.axis_size("dp")
        send, land, part, parts, me, mine = (
            self.send, self.land, self.part, self.parts, self.me, self.mine
        )
        self.over_time = Exchange(
            getattr(r, name + "_tm"), "tm", lambda to: send.at[to], lambda origin: land.at[origin]
        )
        self.over_series = Exchange(
            getattr(r, name + "_dp"), "dp", lambda to: part.at[to], lambda origin: parts.at[origin]
        )
        self.to_all = Exchange(
            getattr(r, name + "_all"), "tm", lambda to: final.at[me], lambda origin: final.at[origin]
        )

    def owned(self, index, action):
        if self.owners == self.count:
            action()
        else:
            pl.when(index < self.owners)(action)

    def start(self):
        for step in range(1, self.count):
            to = self.over_time.other(step)
            self.owned(to, lambda: self.over_time.send(to))

    def sum_time(self):
        def action():
            self.over_time.arrive_all()
            self.land[self.me] = self.send[self.me]
            total = self.land[0].astype(jnp.float32)
            for origin in range(1, self.count):
                total = total + self.land[origin].astype(jnp.float32)
            rows = self.part.shape[1]
            for group in range(self.groups):
                self.part[group] = total[group * rows : (group + 1) * rows]
            self.over_series.start()

        self.owned(self.me, action)

    def sum_series(self):
        def action():
            self.over_series.arrive_all()
            self.parts[self.mine] = self.part[self.mine]
            total = self.parts[0]
            for origin in range(1, self.groups):
                total = total + self.parts[origin]
            self.final[self.me] = total
            self.to_all.start()

        self.owned(self.me, action)

    def finish(self):
        for step in range(1, self.count):
            origin = self.to_all.other(step)
            self.owned(origin, lambda: self.to_all.arrive(origin))
        for step in range(1, self.count):
            to = self.over_time.other(step)
            self.owned(to, lambda: self.over_time.copy(to, self.me).wait_send())

        def action():
            self.over_series.sent()
            self.to_all.sent()

        self.owned(self.me, action)


def greet():
    barrier = pltpu.get_barrier_semaphore()
    total = 0
    for axis in ("tm", "dp"):
        me, count = lax.axis_index(axis), lax.axis_size(axis)
        for step in range(1, count):
            pl.semaphore_signal(
                barrier,
                inc=1,
                device_id={axis: lax.rem(me + step, count)},
                device_id_type=pl.DeviceIdType.MESH,
            )
            total += 1
    return lambda: pl.semaphore_wait(barrier, total)


def pack_params(r, group, params):
    mine = lax.axis_index("dp")
    buffer = getattr(r, "params%d" % group)

    def put(half, column, array, rows):
        buffer[half, mine, :rows, column : column + array.shape[1]] = low(array)

    if group == 0:
        lstm, table, level = params
        rows = lstm.shape[0]
        split = GROUP_COLUMNS[0]
        put(0, 0, lstm[:, :split], rows)
        put(1, 0, lstm[:, split:], rows)
        r.table_stage[...] = jnp.zeros_like(r.table_stage)
        r.table_stage[: table.shape[0], :rows] = table[...]
        r.table_stage[VECTORS : VECTORS + LEVEL_TALLY, :rows] = level[...]
        put(1, lstm.shape[1] - split, r.table_stage[...], PAD_ROWS)
    elif group == 1:
        glu_one, qkv = params
        put(0, 0, glu_one[...], glu_one.shape[0])
        put(1, 0, qkv[...], qkv.shape[0])
    else:
        glu_two, glu_three, inner, middle, attn = params
        rows = glu_two.shape[0]
        put(0, 0, glu_two[...], rows)
        put(0, 3 * LANES, glu_three[...], rows)
        put(1, 0, inner[...], rows)
        put(1, 2 * LANES, middle[...], rows)
        put(1, 4 * LANES, attn[...], attn.shape[0])


def unpack_params(r, group, rows, attn_rows):
    width = r.w.shape[0]
    head_width = width // HEADS
    buffer, stage = getattr(r, "params%d" % group), r.stage
    columns = GROUP_COLUMNS[group]
    for half in range(2):
        for origin in range(buffer.shape[1]):
            stage[origin * rows : (origin + 1) * rows, half * columns : (half + 1) * columns] = (
                buffer[half, origin].astype(jnp.float32)[:rows]
            )

    def place(block, column, size):
        r.w[:, block : block + size] = low(stage[:, column : column + size])

    if group == 0:
        for gate, block in enumerate(BLOCKS_LSTM):
            place(block, gate * width, width)
        vectors = jnp.concatenate(
            [
                buffer[1, origin][:, columns - LANES :].astype(jnp.float32)[: VECTORS + 8, :rows]
                for origin in range(buffer.shape[1])
            ],
            axis=1,
        )
        r.vec[...] = vectors[:VECTORS]
        r.level[...] = low(vectors[VECTORS:])
    elif group == 1:
        place(GLU_ONE_A, 0, width)
        place(GLU_ONE_B, width, width)
        place(QUERY, columns, width)
        place(KEY, columns + width, width)
        place(VALUE, columns + 2 * width, head_width)
    else:
        place(GLU_TWO_A, 0, width)
        place(GLU_TWO_B, width, width)
        place(GLU_THREE_A, 3 * LANES, width)
        place(GLU_THREE_B, 3 * LANES + width, width)
        place(INNER, columns, width)
        place(MIDDLE, columns + 2 * LANES, width)
        for origin in range(buffer.shape[1]):
            r.attn_stage[origin * attn_rows : (origin + 1) * attn_rows, :] = stage[
                origin * rows : origin * rows + attn_rows, columns + 4 * LANES :
            ]
        r.w[:head_width, ATTN_OUT : ATTN_OUT + width] = low(r.attn_stage[:head_width, :width])


def series_kernel(
    begins,
    reaches,
    x_hbm,
    adjoint_hbm,
    slopes,
    lstm,
    glu_one,
    qkv,
    attn,
    glu_two,
    inner,
    middle,
    glu_three,
    level,
    table,
    out_hbm,
    predicted_out,
    input_hbm,
    final_middle,
    final_first,
    final_lstm,
    *scratch,
):
    count, width, steps = x_hbm.shape
    span = count * steps
    head_width = width // HEADS
    groups = lax.axis_size("dp")
    rows = lstm.shape[0]
    names = series_scratch(span, width, head_width)
    names.update(travel_scratch(count, groups, steps, width, rows))
    r = types.SimpleNamespace(**dict(zip(names, scratch)))
    me = lax.axis_index("tm")
    last = count - 1

    def block(ref, index):
        return ref.at[:, rows_of(index, steps)]

    x_over = Exchange(r.x_sems, "tm", lambda to: x_hbm.at[to], lambda origin: block(r.x_flat, origin))
    adjoint_over = Exchange(
        r.adjoint_sems, "tm", lambda to: adjoint_hbm.at[to], lambda origin: block(r.adjoint, origin)
    )
    out_over = Exchange(
        r.out_sems, "tm", lambda to: block(r.out, to), lambda origin: out_hbm.at[origin]
    )
    input_over = Exchange(
        r.input_sems, "tm", lambda to: block(r.input_grad, to), lambda origin: input_hbm.at[origin]
    )
    slope_over = Exchange(
        r.slope_sems, "tm", lambda to: r.slopes.at[to], lambda origin: r.slope
    )
    predicted_over = Exchange(
        r.predicted_sems, "tm", lambda to: r.predicted, lambda origin: r.levels.at[origin]
    )
    params = [Parameters(r, group) for group in range(3)]
    middle_sum = Reduction(r, "middle", final_middle, len(BLOCKS_MIDDLE))
    first_sum = Reduction(r, "first", final_first, count)
    lstm_sum = Reduction(r, "lstm", final_lstm, count)

    own_x = pltpu.make_async_copy(x_hbm.at[me], block(r.x_flat, me), r.own_sems.at[0])
    own_adjoint = pltpu.make_async_copy(adjoint_hbm.at[me], block(r.adjoint, me), r.own_sems.at[1])
    own_out = pltpu.make_async_copy(block(r.out, me), out_hbm.at[me], r.own_sems.at[2])
    own_input = pltpu.make_async_copy(block(r.input_grad, me), input_hbm.at[me], r.own_sems.at[3])

    everyone_here = greet()
    own_x.start()
    own_adjoint.start()
    pack_params(r, 0, (lstm, table, level))
    everyone_here()
    x_over.start()
    params[0].over.start()
    pack_params(r, 1, (glu_one, qkv))
    params[1].over.start()
    pack_params(r, 2, (glu_two, glu_three, inner, middle, attn))
    params[2].over.start()
    for track in range(count):
        r.slopes[track] = jnp.concatenate(
            [
                slopes[level_at].astype(jnp.float32)[track : track + 1]
                for level_at in range(LEVEL_TALLY)
            ]
            + [jnp.zeros((8 - LEVEL_TALLY, steps), jnp.float32)],
            axis=0,
        )

    @pl.when(me == last)
    def _():
        slope_over.start()
        r.slope[...] = r.slopes[last]

    r.g[...] = jnp.zeros_like(r.g)
    r.gv[...] = jnp.zeros_like(r.gv)
    begin = begins[me]
    choice = reaches[me]
    horizon = jnp.where(choice == 0, 1, jnp.where(choice == 1, 5, 24))

    params[0].pass_on()
    params[0].arrive()
    unpack_params(r, 0, rows, attn.shape[0])
    own_x.wait()
    series_gates(r, begin, me, steps)

    def arriving(step, _):
        origin = x_over.other(step)
        x_over.arrive(origin)
        series_gates(r, begin, origin, steps)
        return 0

    lax.fori_loop(1, count, arriving, 0)
    adjoint_over.start()
    params[1].pass_on()
    series_forward_scan(r)
    params[1].arrive()
    unpack_params(r, 1, rows, attn.shape[0])
    series_forward_first(r)
    params[2].pass_on()
    series_forward_attention(r, begin)
    params[2].arrive()
    unpack_params(r, 2, rows, attn.shape[0])
    own_adjoint.wait()
    adjoint_over.arrive_all()

    @pl.when(me != last)
    def _():
        slope_over.arrive(last)

    series_middle(r, horizon)
    own_out.start()
    out_over.start()

    @pl.when(me != last)
    def _():
        predicted_over.send(last)

    for index, column in enumerate(BLOCKS_MIDDLE[:-1]):
        middle_sum.send[index] = low(r.g[:, column : column + 2 * LANES])
    r.attn_stage[...] = jnp.zeros_like(r.attn_stage)
    small = attn.shape[0]
    for group in range(groups):
        r.attn_stage[group * rows : group * rows + small, :] = r.g[
            group * small : (group + 1) * small, ATTN_OUT : ATTN_OUT + 2 * LANES
        ]
    middle_sum.send[len(BLOCKS_MIDDLE) - 1] = low(r.attn_stage[...])
    middle_sum.start()
    series_backward_attention(r)
    middle_sum.sum_time()
    series_backward_first(r)
    for index, column in enumerate(BLOCKS_FIRST):
        for part in range(2):
            at = column + part * LANES
            piece = r.g[:, at : at + LANES]
            if column == QUERY and part == 1:
                spare = width - LANES
                piece = jnp.concatenate(
                    [
                        piece[:, :spare],
                        r.g[:, VALUE : VALUE + head_width],
                        jnp.zeros((width, LANES - spare - head_width), jnp.float32),
                    ],
                    axis=1,
                )
            first_sum.send[2 * index + part] = low(piece)
    first_sum.start()
    middle_sum.sum_series()
    series_backward_scan(r)
    series_gate_grads(r)
    first_sum.sum_time()
    spare = width - LANES
    r.attn_stage[...] = jnp.zeros_like(r.attn_stage)
    for group in range(groups):
        r.attn_stage[group * rows : group * rows + VECTORS + 8, spare : spare + rows] = r.gv[
            :, group * rows : (group + 1) * rows
        ]
    for gate in range(4):
        grad = nn(r.x_flat[...], r.gate_grads[gate])
        lstm_sum.send[2 * gate] = low(grad[:, :LANES])
        rest = [grad[:, LANES:], jnp.zeros((width, LANES - spare), jnp.float32)]
        if gate == 0:
            rest = [grad[:, LANES:], r.attn_stage[:, spare:LANES]]
        lstm_sum.send[2 * gate + 1] = low(jnp.concatenate(rest, axis=1))
    lstm_sum.start()
    first_sum.sum_series()
    for step in range(1, count):
        to = input_over.other(step)
        series_input_grad(r, to, steps)
        input_over.send(to)
    series_input_grad(r, me, steps)
    own_input.start()
    lstm_sum.sum_time()

    @pl.when(me != last)
    def _():
        predicted_over.copy(last, me).wait_send()
        predicted_out[...] = jnp.zeros_like(predicted_out)

    @pl.when(me == last)
    def _():
        slope_over.sent()
        predicted_over.arrive_all()
        r.levels[last] = r.predicted[...]
        for level_at in range(LEVEL_TALLY):
            predicted_out[level_at] = jnp.concatenate(
                [r.levels[track][level_at : level_at + 1] for track in range(count)], axis=0
            )

    lstm_sum.sum_series()
    x_over.sent()
    adjoint_over.sent()
    for group in params:
        group.sent()
    own_out.wait()
    out_over.arrive_all()
    out_over.sent()
    middle_sum.finish()
    first_sum.finish()
    own_input.wait()
    input_over.arrive_all()
    input_over.sent()
    lstm_sum.finish()


def unpack_kernel(
    final_middle,
    final_first,
    final_lstm,
    lstm,
    glu_one,
    qkv,
    attn,
    glu_two,
    inner,
    middle,
    glu_three,
    level,
    table,
):
    width = inner.shape[1]
    spare = width - LANES

    def halves(out, column, final, index):
        out[:, column : column + LANES] = final[index]
        out[:, column + LANES : column + width] = final[index + 1][:, :spare]

    for gate in range(4):
        halves(lstm, gate * width, final_lstm, 2 * gate)
    vectors = final_lstm[1][:, spare : spare + table.shape[1]]
    table[...] = vectors[: table.shape[0]]
    level[...] = vectors[VECTORS : VECTORS + LEVEL_TALLY]
    for index in range(2):
        halves(glu_one, index * width, final_first, 2 * index)
        halves(qkv, index * width, final_first, 4 + 2 * index)
        glu_two[:, index * width : (index + 1) * width] = final_middle[index][:, :width]
        glu_three[:, index * width : (index + 1) * width] = final_middle[4 + index][:, :width]
    qkv[:, 2 * width :] = final_first[5][:, spare : spare + qkv.shape[1] - 2 * width]
    inner[...] = final_middle[2][:, :width]
    middle[...] = final_middle[3][:, :width]
    attn[...] = final_middle[6][: attn.shape[0], :width]


def whole_series(embedded_features, earliest_seen_moment, reach_choice, *others):
    count, steps, width = embedded_features.shape
    features = embedded_features.swapaxes(1, 2)
    adjoint = others[-2].swapaxes(1, 2)
    slopes = others[-1].swapaxes(0, 1)
    params = others[:-4] + (others[-4].T, others[-3].T)
    head_width = width // HEADS
    groups = lax.axis_size("dp")
    rows = params[0].shape[0]
    names = series_scratch(count * steps, width, head_width)
    names.update(travel_scratch(count, groups, steps, width, rows))
    smem, vmem, anywhere = (
        pl.BlockSpec(memory_space=space) for space in (pltpu.SMEM, pltpu.VMEM, pl.ANY)
    )
    out, predicted, input_grad, *finals = pl.pallas_call(
        series_kernel,
        out_shape=(
            jax.ShapeDtypeStruct(features.shape, jnp.bfloat16),
            jax.ShapeDtypeStruct(slopes.shape, jnp.float32),
            jax.ShapeDtypeStruct(features.shape, jnp.bfloat16),
            jax.ShapeDtypeStruct((count, rows, 2 * LANES), jnp.float32),
            jax.ShapeDtypeStruct((count, rows, LANES), jnp.float32),
            jax.ShapeDtypeStruct((count, rows, LANES), jnp.float32),
        ),
        in_specs=[smem, smem, anywhere, anywhere] + [vmem] * 11,
        out_specs=(anywhere, vmem, anywhere) + (vmem,) * 3,
        scratch_shapes=list(names.values()),
        compiler_params=pltpu.CompilerParams(
            vmem_limit_bytes=VMEM_BYTES, collective_id=0, has_side_effects=True
        ),
    )(
        earliest_seen_moment,
        reach_choice,
        features,
        adjoint,
        slopes,
        *params,
    )
    *grads, level_grad, table_grad = pl.pallas_call(
        unpack_kernel,
        out_shape=tuple(jax.ShapeDtypeStruct(param.shape, jnp.float32) for param in params),
        in_specs=[vmem] * 3,
        out_specs=(vmem,) * len(params),
    )(*finals)
    return (
        out.swapaxes(1, 2),
        predicted.swapaxes(0, 1),
        input_grad.swapaxes(1, 2),
        *grads,
        level_grad.T,
        table_grad.T,
    )


def on_device(embedded_features, *others):
    count, steps, _ = embedded_features.shape
    one_each = count == lax.axis_size("tm") == CHUNKS and steps == LANES
    return (whole_series if one_each else shards)(embedded_features, *others)


def solution(mesh):
    placed = (
        P("dp", "tm", None),
        P("dp"),
        P("dp"),
        P("dp", None),
        P("dp", None),
        P("dp", None),
        P("dp", None),
        P("dp", None),
        P("dp", None),
        P("dp", None),
        P("dp", None),
        P("dp", None),
        P("dp", None),
        P("dp", "tm", None),
        P("dp", None, "tm"),
    )
    return jax.shard_map(
        on_device,
        mesh=mesh,
        in_specs=placed,
        out_specs=(
            P("dp", "tm", None),
            P("dp", None, "tm"),
            P("dp", "tm", None),
            P("dp", None),
            P("dp", None),
            P("dp", None),
            P("dp", None),
            P("dp", None),
            P("dp", None),
            P("dp", None),
            P("dp", None),
            P("dp", None),
            P("dp", None),
        ),
        check_vma=False,
    )
```

```python
import types

import jax
import jax.numpy as jnp
from jax import lax
from jax.experimental import pallas as pl
from jax.experimental.pallas import tpu as pltpu
from jax.sharding import PartitionSpec as P

HEADS = 4
LEVEL_TALLY = 3
DEC = 24
MICRO = 2


EPSILON = 1e-05
NEG_BIG = -1e30
attend_group = 2
LOG2_E = 1.4426950408889634
VMEM_BYTES = 60 * 2**20


def entering(value, axis, join, neutral, backward):
    count, mine = (lax.axis_size(axis), lax.axis_index(axis))
    pieces = jax.tree.map(lambda part: lax.all_gather(part, axis), value)
    if backward:
        pieces = jax.tree.map(lambda part: part[::-1], pieces)
        mine = count - 1 - mine
    so_far = jax.tree.map(
        lambda part, zero: jnp.full_like(part, 0) + jnp.asarray(zero, part.dtype), value, neutral
    )

    def turn(position, so_far):
        longer = join(so_far, jax.tree.map(lambda part: part[position], pieces))
        return jax.tree.map(lambda new, old: jnp.where(position < mine, new, old), longer, so_far)

    return lax.fori_loop(0, count - 1, turn, so_far)


def narrow_convert(values):
    return values.astype(jnp.bfloat16)


def tensor_dot_plain(left, right):
    return jnp.dot(left, right, preferred_element_type=jnp.float32)


def flipped_dot(left, right):
    return lax.dot_general(
        left, right, (((0,), (0,)), ((), ())), preferred_element_type=jnp.float32
    )


def dot_against_flipped(left, right):
    return lax.dot_general(
        left, right, (((1,), (1,)), ((), ())), preferred_element_type=jnp.float32
    )


def affine_join(earlier, later):
    return (later[0] * earlier[0], later[0] * earlier[1] + later[1])


def layer_norm(values, gains, offsets):
    centred = values - jnp.mean(values, axis=-1, keepdims=True)
    spread = jnp.mean(centred * centred, axis=-1, keepdims=True)
    return centred * lax.rsqrt(spread + EPSILON) * gains + offsets


def gated_unit(pre_act):
    half_width = pre_act.shape[-1] // 2
    return pre_act[..., :half_width] * jax.nn.sigmoid(pre_act[..., half_width:])


def lstm_gates(pre_act, keep_mask):
    quarter = pre_act.shape[-1] // 4
    forget = jax.nn.sigmoid(pre_act[..., :quarter]) * keep_mask
    inflow = jax.nn.sigmoid(pre_act[..., quarter : 2 * quarter]) * jnp.tanh(
        pre_act[..., 2 * quarter : 3 * quarter]
    )
    out_gate = jax.nn.sigmoid(pre_act[..., 3 * quarter :])
    return (forget, inflow, out_gate)


def masked_scores(query_block, key_block, query_pos, key_pos, begin_block, scale):
    raw = jnp.einsum("gqhd,gkhd->ghqk", query_block, key_block, preferred_element_type=jnp.float32)
    lowest = jnp.minimum(begin_block[:, None], query_pos[None, :])
    allowed = (key_pos[None, None, :] <= query_pos[None, :, None]) & (
        key_pos[None, None, :] >= lowest[:, :, None]
    )
    return jnp.where(allowed[:, None], raw * scale, NEG_BIG)


def score_grad(chances, dprob, row_delta, scale):
    return narrow_convert(chances * (dprob[:, None] - row_delta[..., None]) * scale)


def shards(
    embedded_features,
    earliest_seen_moment,
    reach_choice,
    lstm_valve_coeffs,
    lstm_unit_coeffs,
    asker_lookup_coeffs,
    attend_exit_coeffs,
    attend_unit_coeffs,
    skipnet_entry_coeffs,
    skipnet_inner_coeffs,
    skipnet_unit_coeffs,
    level_map_coeffs,
    bias_gain_table,
    block_emit_adjoint,
    predicted_adjoint,
):
    (
        mat_lstm,
        mat_glu_one,
        mat_qkv,
        mat_attn,
        mat_glu_two,
        mat_inner,
        mat_middle,
        mat_glu_three,
        level_dot,
        vec_table,
    ) = (
        lax.all_gather(narrow_convert(lstm_valve_coeffs), "dp", axis=0, tiled=True),
        lax.all_gather(narrow_convert(lstm_unit_coeffs), "dp", axis=0, tiled=True),
        lax.all_gather(narrow_convert(asker_lookup_coeffs), "dp", axis=0, tiled=True),
        lax.all_gather(narrow_convert(attend_exit_coeffs), "dp", axis=0, tiled=True),
        lax.all_gather(narrow_convert(attend_unit_coeffs), "dp", axis=0, tiled=True),
        lax.all_gather(narrow_convert(skipnet_entry_coeffs), "dp", axis=0, tiled=True),
        lax.all_gather(narrow_convert(skipnet_inner_coeffs), "dp", axis=0, tiled=True),
        lax.all_gather(narrow_convert(skipnet_unit_coeffs), "dp", axis=0, tiled=True),
        lax.all_gather(narrow_convert(level_map_coeffs), "dp", axis=0, tiled=True),
        lax.all_gather(narrow_convert(bias_gain_table), "dp", axis=0, tiled=True),
    )
    series_per_device, steps_per_device, model_width = embedded_features.shape
    seq_total = steps_per_device * lax.axis_size("tm")
    head_width = model_width // HEADS
    count_of_rows = series_per_device * steps_per_device
    scale = head_width ** (-0.5)
    vec_full = vec_table.astype(jnp.float32)
    time_local = lax.axis_index("tm") * steps_per_device + jnp.arange(
        steps_per_device, dtype=jnp.int32
    )
    time_all = jnp.arange(seq_total, dtype=jnp.int32)
    horizon_len = jnp.where(reach_choice == 0, 1, jnp.where(reach_choice == 1, 5, 24))
    ahead_moment_filter = (
        (
            (time_local[None, :] >= seq_total - DEC)
            & (time_local[None, :] < seq_total - DEC + horizon_len[:, None])
        )
        .astype(jnp.float32)
        .reshape(count_of_rows, 1)
    )
    keep_mask = (
        (time_local[None, :] != earliest_seen_moment[:, None])
        .astype(jnp.float32)
        .reshape(count_of_rows, 1)
    )
    group_size = series_per_device // MICRO
    group_total = series_per_device // attend_group
    state_ones = jnp.ones((group_size, model_width), jnp.float32)
    state_zeros = jnp.zeros((group_size, model_width), jnp.float32)

    def split_groups(array):
        return array.reshape((group_total, attend_group) + array.shape[1:])

    input_rows = embedded_features.reshape(count_of_rows, model_width)
    input_full = input_rows.astype(jnp.float32)
    lstm_pre = tensor_dot_plain(input_rows, mat_lstm) + vec_full[:, 0:4].T.reshape(-1)
    forget, inflow, out_gate = lstm_gates(lstm_pre, keep_mask)
    forget_seq = forget.reshape(series_per_device, steps_per_device, model_width)
    inflow_seq = inflow.reshape(series_per_device, steps_per_device, model_width)
    mult_seq, cell_local = lax.associative_scan(affine_join, (forget_seq, inflow_seq), axis=1)
    cell_parts = []
    for group in range(MICRO):
        lower_row = group * group_size
        upper_row = lower_row + group_size
        _, arriving = entering(
            (mult_seq[lower_row:upper_row, -1], cell_local[lower_row:upper_row, -1]),
            "tm",
            affine_join,
            (state_ones, state_zeros),
            False,
        )
        cell_parts.append(arriving)
    cell_in = jnp.concatenate(cell_parts, axis=0)
    cell_seq = cell_local + mult_seq * cell_in[:, None, :]
    cell_tanh = jnp.tanh(cell_seq.reshape(count_of_rows, model_width))
    hidden_low = narrow_convert(out_gate * cell_tanh)
    glu_one_pre = tensor_dot_plain(hidden_low, mat_glu_one) + vec_full[:, 4:6].T.reshape(-1)
    first_sum = input_full + gated_unit(glu_one_pre)
    first = layer_norm(first_sum, vec_full[:, 6], vec_full[:, 7])
    first_low = narrow_convert(first)
    qkv_low = narrow_convert(tensor_dot_plain(first_low, mat_qkv))
    query_low = qkv_low[:, :model_width].reshape(
        series_per_device, steps_per_device, HEADS, head_width
    )
    key_value = qkv_low[:, model_width:].reshape(
        series_per_device, steps_per_device, model_width + head_width
    )
    key_value_all = lax.all_gather(key_value, "tm", axis=1, tiled=True)
    keys_all = key_value_all[..., :model_width].reshape(
        series_per_device, seq_total, HEADS, head_width
    )
    values_all = key_value_all[..., model_width:]

    def attend_forward(block_args):
        query_block, key_block, value_block, begin_block = block_args
        scores = masked_scores(query_block, key_block, time_local, time_all, begin_block, scale)
        row_top = jnp.max(scores, axis=-1, keepdims=True)
        row_exp = jnp.exp(scores - row_top)
        row_total = jnp.sum(row_exp, axis=-1, keepdims=True)
        weights_low = narrow_convert(row_exp / row_total)
        mixed_block = jnp.einsum(
            "ghqk,gkd->gqd", weights_low, value_block, preferred_element_type=jnp.float32
        ) * (1.0 / HEADS)
        return (mixed_block, (row_top + jnp.log(row_total))[..., 0])

    mixed, log_total = lax.map(
        attend_forward,
        (
            split_groups(query_low),
            split_groups(keys_all),
            split_groups(values_all),
            split_groups(earliest_seen_moment),
        ),
    )
    mixed_low = narrow_convert(mixed.reshape(count_of_rows, head_width))
    attn_low = narrow_convert(tensor_dot_plain(mixed_low, mat_attn))
    glu_two_pre = tensor_dot_plain(attn_low, mat_glu_two) + vec_full[:, 8:10].T.reshape(-1)
    second_sum = first + gated_unit(glu_two_pre)
    second = layer_norm(second_sum, vec_full[:, 10], vec_full[:, 11])
    second_low = narrow_convert(second)
    inner_pre = tensor_dot_plain(second_low, mat_inner) + vec_full[:, 12]
    inner_low = narrow_convert(jax.nn.elu(inner_pre))
    middle_low = narrow_convert(tensor_dot_plain(inner_low, mat_middle) + vec_full[:, 13])
    glu_three_pre = tensor_dot_plain(middle_low, mat_glu_three) + vec_full[:, 14:16].T.reshape(-1)
    final_sum = second + gated_unit(glu_three_pre)
    second_block_emit = layer_norm(final_sum, vec_full[:, 16], vec_full[:, 17])
    closing_narrowed = narrow_convert(second_block_emit)
    predicted_entries = tensor_dot_plain(closing_narrowed, level_dot) * ahead_moment_filter
    predicted_levels = predicted_entries.reshape(
        series_per_device, steps_per_device, LEVEL_TALLY
    ).transpose(0, 2, 1)
    predicted_slope = narrow_convert(
        predicted_adjoint.astype(jnp.float32).transpose(0, 2, 1).reshape(count_of_rows, LEVEL_TALLY)
        * ahead_moment_filter
    )
    level_slope = flipped_dot(closing_narrowed, predicted_slope)
    final_grad = block_emit_adjoint.reshape(count_of_rows, model_width).astype(
        jnp.float32
    ) + dot_against_flipped(predicted_slope, level_dot)
    _, norm_pull = jax.vjp(layer_norm, final_sum, vec_full[:, 16], vec_full[:, 17])
    sum_three_grad, gain_three_grad, offset_three_grad = norm_pull(final_grad)
    _, glu_pull = jax.vjp(gated_unit, glu_three_pre)
    (glu_three_grad,) = glu_pull(sum_three_grad)
    glu_three_low = narrow_convert(glu_three_grad)
    grad_glu_three = flipped_dot(middle_low, glu_three_low)
    middle_grad = dot_against_flipped(glu_three_low, mat_glu_three)
    middle_grad_low = narrow_convert(middle_grad)
    grad_middle = flipped_dot(inner_low, middle_grad_low)
    inner_grad = dot_against_flipped(middle_grad_low, mat_middle)
    _, elu_pull = jax.vjp(jax.nn.elu, inner_pre)
    (inner_pre_grad,) = elu_pull(inner_grad)
    inner_pre_low = narrow_convert(inner_pre_grad)
    grad_inner = flipped_dot(second_low, inner_pre_low)
    second_grad = sum_three_grad + dot_against_flipped(inner_pre_low, mat_inner)
    _, norm_pull = jax.vjp(layer_norm, second_sum, vec_full[:, 10], vec_full[:, 11])
    sum_two_grad, gain_two_grad, offset_two_grad = norm_pull(second_grad)
    _, glu_pull = jax.vjp(gated_unit, glu_two_pre)
    (glu_two_grad,) = glu_pull(sum_two_grad)
    glu_two_low = narrow_convert(glu_two_grad)
    grad_glu_two = flipped_dot(attn_low, glu_two_low)
    attn_grad_low = narrow_convert(dot_against_flipped(glu_two_low, mat_glu_two))
    grad_attn = flipped_dot(mixed_low, attn_grad_low)
    mixed_grad_low = narrow_convert(dot_against_flipped(attn_grad_low, mat_attn))
    head_grad = (mixed_grad_low * (1.0 / HEADS)).reshape(
        series_per_device, steps_per_device, head_width
    )

    def attend_backward(block_args):
        query_block, key_block, value_block, begin_block, lse_block, dout_block = block_args
        scores = masked_scores(query_block, key_block, time_local, time_all, begin_block, scale)
        chances = jnp.exp(scores - lse_block[..., None])
        dprob = jnp.einsum(
            "gqd,gkd->gqk", dout_block, value_block, preferred_element_type=jnp.float32
        )
        row_delta = jnp.sum(chances * dprob[:, None], axis=-1)
        dscore = score_grad(chances, dprob, row_delta, scale)
        dquery = jnp.einsum(
            "ghqk,gkhd->gqhd", dscore, key_block, preferred_element_type=jnp.float32
        )
        dkey = jnp.einsum(
            "ghqk,gqhd->gkhd", dscore, query_block, preferred_element_type=jnp.float32
        )
        dvalue = jnp.einsum(
            "ghqk,gqd->gkd", narrow_convert(chances), dout_block, preferred_element_type=jnp.float32
        )
        key_terms = jnp.concatenate(
            [dkey.reshape(attend_group, seq_total, model_width), dvalue], axis=-1
        )
        return (dquery, key_terms)

    dquery, key_terms = lax.map(
        attend_backward,
        (
            split_groups(query_low),
            split_groups(keys_all),
            split_groups(values_all),
            split_groups(earliest_seen_moment),
            log_total,
            split_groups(head_grad),
        ),
    )
    own_keys = lax.psum_scatter(
        key_terms.reshape(series_per_device, seq_total, model_width + head_width),
        "tm",
        scatter_dimension=1,
        tiled=True,
    )
    qkv_grad = jnp.concatenate(
        [
            dquery.reshape(count_of_rows, model_width),
            own_keys.reshape(count_of_rows, model_width + head_width),
        ],
        axis=1,
    )
    qkv_grad_low = narrow_convert(qkv_grad)
    grad_qkv = flipped_dot(first_low, qkv_grad_low)
    first_grad = sum_two_grad + dot_against_flipped(qkv_grad_low, mat_qkv)
    _, norm_pull = jax.vjp(layer_norm, first_sum, vec_full[:, 6], vec_full[:, 7])
    sum_one_grad, gain_one_grad, offset_one_grad = norm_pull(first_grad)
    _, glu_pull = jax.vjp(gated_unit, glu_one_pre)
    (glu_one_grad,) = glu_pull(sum_one_grad)
    glu_one_low = narrow_convert(glu_one_grad)
    grad_glu_one = flipped_dot(hidden_low, glu_one_low)
    hidden_grad = dot_against_flipped(glu_one_low, mat_glu_one)
    out_gate_grad = hidden_grad * cell_tanh
    direct_grad = (hidden_grad * out_gate * (1.0 - cell_tanh * cell_tanh)).reshape(
        series_per_device, steps_per_device, model_width
    )
    next_forget = jnp.concatenate([forget_seq[:, 1:], jnp.ones_like(forget_seq[:, :1])], axis=1)
    rev_mult, rev_cell = lax.associative_scan(
        affine_join, (next_forget, direct_grad), axis=1, reverse=True
    )
    head_mult = forget_seq[:, 0] * rev_mult[:, 0]
    head_cell = forget_seq[:, 0] * rev_cell[:, 0]
    coming_parts = []
    for group in range(MICRO):
        lower_row = group * group_size
        upper_row = lower_row + group_size
        _, coming = entering(
            (head_mult[lower_row:upper_row], head_cell[lower_row:upper_row]),
            "tm",
            affine_join,
            (state_ones, state_zeros),
            True,
        )
        coming_parts.append(coming)
    coming_all = jnp.concatenate(coming_parts, axis=0)
    cell_grad = rev_cell + rev_mult * coming_all[:, None, :]
    cell_prev = jnp.concatenate([cell_in[:, None, :], cell_seq[:, :-1]], axis=1)
    forget_grad = (cell_grad * cell_prev).reshape(count_of_rows, model_width)
    _, gate_pull = jax.vjp(lambda pre_value: lstm_gates(pre_value, keep_mask), lstm_pre)
    (lstm_pre_grad,) = gate_pull(
        (forget_grad, cell_grad.reshape(count_of_rows, model_width), out_gate_grad)
    )
    lstm_low = narrow_convert(lstm_pre_grad)
    grad_lstm = flipped_dot(input_rows, lstm_low)
    input_grad = sum_one_grad + dot_against_flipped(lstm_low, mat_lstm)
    grad_table = jnp.concatenate(
        [
            jnp.sum(lstm_pre_grad, axis=0).reshape(4, model_width).T,
            jnp.sum(glu_one_grad, axis=0).reshape(2, model_width).T,
            gain_one_grad[:, None],
            offset_one_grad[:, None],
            jnp.sum(glu_two_grad, axis=0).reshape(2, model_width).T,
            gain_two_grad[:, None],
            offset_two_grad[:, None],
            jnp.sum(inner_pre_grad, axis=0)[:, None],
            jnp.sum(middle_grad, axis=0)[:, None],
            jnp.sum(glu_three_grad, axis=0).reshape(2, model_width).T,
            gain_three_grad[:, None],
            offset_three_grad[:, None],
        ],
        axis=1,
    )
    (
        whole_lstm,
        whole_glu_one,
        whole_qkv,
        whole_attn,
        whole_glu_two,
        whole_inner,
        whole_middle,
        whole_glu_three,
        whole_quant,
        whole_table,
    ) = lax.psum(
        (
            grad_lstm,
            grad_glu_one,
            grad_qkv,
            grad_attn,
            grad_glu_two,
            grad_inner,
            grad_middle,
            grad_glu_three,
            level_slope,
            grad_table,
        ),
        "tm",
    )
    summed = (
        lax.psum_scatter(
            whole_lstm.astype(jnp.bfloat16), "dp", scatter_dimension=0, tiled=True
        ).astype(jnp.float32),
        lax.psum_scatter(
            whole_glu_one.astype(jnp.bfloat16), "dp", scatter_dimension=0, tiled=True
        ).astype(jnp.float32),
        lax.psum_scatter(
            whole_qkv.astype(jnp.bfloat16), "dp", scatter_dimension=0, tiled=True
        ).astype(jnp.float32),
        lax.psum_scatter(
            whole_attn.astype(jnp.bfloat16), "dp", scatter_dimension=0, tiled=True
        ).astype(jnp.float32),
        lax.psum_scatter(
            whole_glu_two.astype(jnp.bfloat16), "dp", scatter_dimension=0, tiled=True
        ).astype(jnp.float32),
        lax.psum_scatter(
            whole_inner.astype(jnp.bfloat16), "dp", scatter_dimension=0, tiled=True
        ).astype(jnp.float32),
        lax.psum_scatter(
            whole_middle.astype(jnp.bfloat16), "dp", scatter_dimension=0, tiled=True
        ).astype(jnp.float32),
        lax.psum_scatter(
            whole_glu_three.astype(jnp.bfloat16), "dp", scatter_dimension=0, tiled=True
        ).astype(jnp.float32),
        lax.psum_scatter(
            whole_quant.astype(jnp.bfloat16), "dp", scatter_dimension=0, tiled=True
        ).astype(jnp.float32),
        lax.psum_scatter(
            whole_table.astype(jnp.bfloat16), "dp", scatter_dimension=0, tiled=True
        ).astype(jnp.float32),
    )
    final_out = second_block_emit.astype(jnp.bfloat16).reshape(
        series_per_device, steps_per_device, model_width
    )
    input_out = input_grad.astype(jnp.bfloat16).reshape(
        series_per_device, steps_per_device, model_width
    )
    return (
        final_out,
        predicted_levels,
        input_out,
        summed[0],
        summed[1],
        summed[2],
        summed[3],
        summed[4],
        summed[5],
        summed[6],
        summed[7],
        summed[8],
        summed[9],
    )


def lane_head(shape, head_width, head):
    lane = lax.broadcasted_iota(jnp.int32, shape, len(shape) - 1)
    return (lane >= head * head_width) & (lane < (head + 1) * head_width)


FORGET, ENTER, CANDIDATE, EXIT = 0, 256, 512, 768
GLU_ONE_A, GLU_ONE_B = 1024, 1280
QUERY, KEY, VALUE = 1536, 1792, 2048
GLU_TWO_A, GLU_TWO_B = 2176, 2432
INNER, MIDDLE = 2688, 2944
GLU_THREE_A, GLU_THREE_B = 3200, 3456
ATTN_OUT = 3712
PACKED = 3968
VECTORS = 24
LANES = 128
CHUNKS = 8
TILE = 256


def nn(left, right):
    return jnp.dot(left, right, preferred_element_type=jnp.float32)


def nt(left, right):
    return lax.dot_general(
        left, right, (((1,), (1,)), ((), ())), preferred_element_type=jnp.float32
    )


def tn(left, right):
    return lax.dot_general(
        left, right, (((0,), (0,)), ((), ())), preferred_element_type=jnp.float32
    )


def low(values):
    return values.astype(jnp.bfloat16)


def sigmoid(values):
    return 0.5 * jnp.tanh(0.5 * values) + 0.5


def normalise(values, gain, shift):
    centred = values - jnp.mean(values, axis=-1, keepdims=True)
    spread = jnp.mean(centred * centred, axis=-1, keepdims=True)
    inverse = lax.rsqrt(spread + EPSILON)
    unit = centred * inverse
    return unit * gain + shift, unit, inverse


def normalise_back(grad, unit, inverse, gain):
    scaled = grad * gain
    return inverse * (
        scaled
        - jnp.mean(scaled, axis=-1, keepdims=True)
        - unit * jnp.mean(scaled * unit, axis=-1, keepdims=True)
    )


def rows_of(tile, size):
    return pl.ds(pl.multiple_of(tile * size, size), size)


def put_halves(ref, rows, values):
    ref[0, rows, :] = values[:, :LANES]
    ref[1, rows, : values.shape[1] - LANES] = values[:, LANES:]


def get_halves(ref, rows, width):
    return jnp.concatenate([ref[0, rows, :], ref[1, rows, : width - LANES]], axis=1)


def row_sum(ref, column, values):
    ref[column : column + 1, :] = jnp.sum(values, axis=0, keepdims=True)


def series_scratch(span, width, head_width):
    full = pltpu.VMEM((span, width), jnp.float32)
    half = pltpu.VMEM((span, width), jnp.bfloat16)
    flat = pltpu.VMEM((width, span), jnp.bfloat16)
    scan = pltpu.VMEM((2, span, LANES), jnp.float32)
    scan_more = pltpu.VMEM((2, span + 8, LANES), jnp.float32)
    narrow = pltpu.VMEM((span, head_width), jnp.bfloat16)
    column = pltpu.VMEM((span, 1), jnp.float32)
    tiles = span // TILE
    return dict(
        forget=scan_more,
        local=scan,
        mult=scan,
        cell=scan_more,
        carry=pltpu.VMEM((2, CHUNKS, LANES), jnp.float32),
        enter_gate=full,
        candidate=full,
        exit_gate=full,
        cell_tanh=full,
        hidden=half,
        glu_one=full,
        gate_one=full,
        unit_one=full,
        inverse_one=column,
        first_low=half,
        keys=half,
        values=narrow,
        head_queries=pltpu.VMEM((HEADS, span, width), jnp.bfloat16),
        head_keys=pltpu.VMEM((HEADS, span, width), jnp.bfloat16),
        **{
            "chances%d" % tile: pltpu.VMEM((HEADS, TILE, (tile + 1) * TILE), jnp.float32)
            for tile in range(tiles)
        },
        chance_sum=pltpu.VMEM((span, span), jnp.bfloat16),
        **{
            "score_grads%d" % tile: pltpu.VMEM((HEADS, span - tile * TILE, TILE), jnp.bfloat16)
            for tile in range(tiles)
        },
        block=pltpu.VMEM((TILE, span), jnp.float32),
        mixed=narrow,
        mixed_grad=narrow,
        sum_two_grad=full,
        query_grad=half,
        key_grad=half,
        value_grad=narrow,
        gate_grads=pltpu.VMEM((4, span, width), jnp.bfloat16),
        x=half,
        x_flat=flat,
        adjoint=flat,
        out=flat,
        input_grad=flat,
        w=pltpu.VMEM((width, PACKED), jnp.bfloat16),
        vec=pltpu.VMEM((VECTORS, width), jnp.float32),
        level=pltpu.VMEM((8, width), jnp.bfloat16),
        gv=pltpu.VMEM((VECTORS + 8, width), jnp.float32),
        slope=pltpu.VMEM((8, LANES), jnp.float32),
        predicted=pltpu.VMEM((8, LANES), jnp.float32),
        attn_flat=pltpu.VMEM((width, 2 * width // 5), jnp.float32),
        lstm_flat=pltpu.VMEM((width, 4 * LANES), jnp.float32),
        middle_send=pltpu.VMEM((2, width, GROUP_LANES["middle"]), jnp.bfloat16),
        first_send=pltpu.VMEM((2, width, GROUP_LANES["first"]), jnp.bfloat16),
        lstm_send=pltpu.VMEM((2, width, GROUP_LANES["lstm"]), jnp.bfloat16),
    )


def series_turn(r, chunk, steps):
    rows = rows_of(chunk, steps)
    r.x[rows, :] = r.x_flat[:, rows].T


def series_gates(r, begin):
    w, vec = r.w, r.vec
    span, width = r.x.shape
    rows = slice(0, span)
    x = r.x[...]

    def pre(block, column):
        return nn(x, w[:, block : block + width]) + vec[column : column + 1, :]

    time = lax.broadcasted_iota(jnp.int32, (span, width), 0)
    put_halves(r.forget, rows, jnp.where(time != begin, sigmoid(pre(FORGET, 0)), 0.0))
    enter = sigmoid(pre(ENTER, 1))
    candidate = jnp.tanh(pre(CANDIDATE, 2))
    r.enter_gate[...] = enter
    r.candidate[...] = candidate
    put_halves(r.local, rows, enter * candidate)
    r.exit_gate[...] = sigmoid(pre(EXIT, 3))


def series_forward_scan(r):
    span = r.x.shape[0]
    steps = span // CHUNKS
    zeros = jnp.zeros((CHUNKS, LANES), jnp.float32)

    def step(t, state):
        out = []
        at = pl.ds(t, CHUNKS, stride=steps)
        for half in range(2):
            cell, mult = state[half]
            forget = r.forget[half, at, :]
            cell = forget * cell + r.local[half, at, :]
            mult = mult * forget
            r.local[half, at, :] = cell
            r.mult[half, at, :] = mult
            out.append((cell, mult))
        return tuple(out)

    ends = lax.fori_loop(0, steps, step, ((zeros, zeros + 1.0),) * 2, unroll=8)
    for half in range(2):
        cells, mults = ends[half]
        state = jnp.zeros((1, LANES), jnp.float32)
        r.carry[half, 0:1, :] = state
        for chunk in range(CHUNKS - 1):
            state = cells[chunk : chunk + 1] + mults[chunk : chunk + 1] * state
            r.carry[half, chunk + 1 : chunk + 2, :] = state
        r.cell[half, 0:8, :] = zeros


def series_forward_first(r):
    w, vec = r.w, r.vec
    span, width = r.x.shape
    head_width = width // HEADS
    steps = span // CHUNKS
    for chunk in range(CHUNKS):
        rows = slice(chunk * steps, (chunk + 1) * steps)
        later = slice(chunk * steps + 8, (chunk + 1) * steps + 8)
        for half in range(2):
            r.cell[half, later, :] = (
                r.local[half, rows, :]
                + r.mult[half, rows, :] * r.carry[half, chunk : chunk + 1, :]
            )
    tanh = jnp.tanh(get_halves(r.cell, slice(8, 8 + span), width))
    r.cell_tanh[...] = tanh
    hidden = low(r.exit_gate[...] * tanh)
    r.hidden[...] = hidden
    value = nn(hidden, w[:, GLU_ONE_A : GLU_ONE_A + width]) + vec[4:5, :]
    gate = sigmoid(nn(hidden, w[:, GLU_ONE_B : GLU_ONE_B + width]) + vec[5:6, :])
    r.glu_one[...] = value
    r.gate_one[...] = gate
    out, unit, inverse = normalise(
        r.x[...].astype(jnp.float32) + value * gate, vec[6:7, :], vec[7:8, :]
    )
    r.unit_one[...] = unit
    r.inverse_one[...] = inverse
    out = low(out)
    r.first_low[...] = out
    query = low(nn(out, w[:, QUERY : QUERY + width]))
    key = low(nn(out, w[:, KEY : KEY + width]))
    r.keys[...] = key
    r.values[...] = low(nn(out, w[:, VALUE : VALUE + head_width]))
    for head in range(HEADS):
        mine = lane_head((span, width), head_width, head)
        r.head_queries[head] = jnp.where(mine, query, jnp.zeros_like(query))
        r.head_keys[head] = jnp.where(mine, key, jnp.zeros_like(key))


def series_forward_attention(r, begin):
    span, head_width = r.values.shape
    scale = head_width ** (-0.5) * LOG2_E
    for tile in range(span // TILE):
        rows = slice(tile * TILE, (tile + 1) * TILE)
        seen = (tile + 1) * TILE
        row = tile * TILE + lax.broadcasted_iota(jnp.int32, (TILE, seen), 0)
        col = lax.broadcasted_iota(jnp.int32, (TILE, seen), 1)
        chances = getattr(r, "chances%d" % tile)
        r.block[:, :seen] = jnp.where(
            (col <= row) & (col >= jnp.minimum(begin, row)), 0.0, NEG_BIG
        )
        for head in range(HEADS):
            scores = (
                nt(r.head_queries[head, rows, :], r.keys[:seen, :]) * scale + r.block[:, :seen]
            )
            top = jnp.max(scores, axis=-1, keepdims=True)
            raised = jnp.exp2(scores - top)
            total = jnp.sum(raised, axis=-1, keepdims=True)
            chances[head] = raised * (1.0 / total)
        weights = chances[0]
        for head in range(1, HEADS):
            weights = weights + chances[head]
        weights = low(weights)
        r.chance_sum[rows, :seen] = weights
        r.mixed[rows, :] = low(nn(weights, r.values[:seen, :]) * (1.0 / HEADS))


def series_middle(r, horizon, after_forward):
    w, vec, gv = r.w, r.vec, r.gv
    span, width = r.x.shape
    head_width = width // HEADS
    first = r.unit_one[...] * vec[6:7, :] + vec[7:8, :]
    mixed = r.mixed[...]
    attn = low(nn(mixed, w[:head_width, ATTN_OUT : ATTN_OUT + width]))
    value_two = nn(attn, w[:, GLU_TWO_A : GLU_TWO_A + width]) + vec[8:9, :]
    gate_two = sigmoid(nn(attn, w[:, GLU_TWO_B : GLU_TWO_B + width]) + vec[9:10, :])
    second, unit_two, inverse_two = normalise(
        first + value_two * gate_two, vec[10:11, :], vec[11:12, :]
    )
    second_low = low(second)
    inner_pre = nn(second_low, w[:, INNER : INNER + width]) + vec[12:13, :]
    inner_exp = jnp.exp(jnp.minimum(inner_pre, 0.0))
    inner_low = low(jnp.where(inner_pre > 0, inner_pre, inner_exp - 1.0))
    middle_low = low(nn(inner_low, w[:, MIDDLE : MIDDLE + width]) + vec[13:14, :])
    value_three = nn(middle_low, w[:, GLU_THREE_A : GLU_THREE_A + width]) + vec[14:15, :]
    gate_three = sigmoid(nn(middle_low, w[:, GLU_THREE_B : GLU_THREE_B + width]) + vec[15:16, :])
    final, unit_three, inverse_three = normalise(
        second + value_three * gate_three, vec[16:17, :], vec[17:18, :]
    )
    final_low = low(final)
    r.out[...] = final_low.T
    steps = r.slope.shape[1]
    time = span - steps + lax.broadcasted_iota(jnp.int32, (8, steps), 1)
    ahead = jnp.where((time >= span - DEC) & (time < span - DEC + horizon), 1.0, 0.0)
    r.predicted[...] = nt(r.level[...], final_low[span - steps :]) * ahead
    after_forward()
    slope = low(r.slope[...] * ahead)
    gv[VECTORS : VECTORS + 8, :] = nn(slope, final_low[span - steps :])
    grad = r.adjoint[...].T.astype(jnp.float32)
    grad = jnp.concatenate(
        [grad[: span - steps], grad[span - steps :] + tn(slope, r.level[...])], axis=0
    )
    row_sum(gv, 16, grad * unit_three)
    row_sum(gv, 17, grad)
    sum_three = normalise_back(grad, unit_three, inverse_three, vec[16:17, :])
    grad_a = sum_three * gate_three
    grad_b = grad_a * value_three * (1.0 - gate_three)
    row_sum(gv, 14, grad_a)
    row_sum(gv, 15, grad_b)
    low_a, low_b = low(grad_a), low(grad_b)
    send = r.middle_send
    send[1, :, :width] = low(tn(middle_low, low_a))
    send[1, :, width : 2 * width] = low(tn(middle_low, low_b))
    middle_grad = nt(low_a, w[:, GLU_THREE_A : GLU_THREE_A + width]) + nt(
        low_b, w[:, GLU_THREE_B : GLU_THREE_B + width]
    )
    row_sum(gv, 13, middle_grad)
    middle_grad = low(middle_grad)
    send[1, :, 2 * width : 3 * width] = low(tn(inner_low, middle_grad))
    inner_grad = nt(middle_grad, w[:, MIDDLE : MIDDLE + width]) * jnp.where(
        inner_pre > 0, 1.0, inner_exp
    )
    row_sum(gv, 12, inner_grad)
    inner_grad = low(inner_grad)
    send[0, :, 2 * width : 3 * width] = low(tn(second_low, inner_grad))
    grad = sum_three + nt(inner_grad, w[:, INNER : INNER + width])
    row_sum(gv, 10, grad * unit_two)
    row_sum(gv, 11, grad)
    sum_two = normalise_back(grad, unit_two, inverse_two, vec[10:11, :])
    r.sum_two_grad[...] = sum_two
    grad_a = sum_two * gate_two
    grad_b = grad_a * value_two * (1.0 - gate_two)
    row_sum(gv, 8, grad_a)
    row_sum(gv, 9, grad_b)
    low_a, low_b = low(grad_a), low(grad_b)
    attn_grad = low(
        nt(low_a, w[:, GLU_TWO_A : GLU_TWO_A + width])
        + nt(low_b, w[:, GLU_TWO_B : GLU_TWO_B + width])
    )
    r.mixed_grad[...] = low(nt(attn_grad, w[:head_width, ATTN_OUT : ATTN_OUT + width]))
    send[0, :, :width] = low(tn(attn, low_a))
    send[0, :, width : 2 * width] = low(tn(attn, low_b))
    attn_weight = tn(mixed, attn_grad)
    rows, small = head_width, head_width // HEADS
    spare = width // 5
    r.attn_flat[...] = jnp.zeros_like(r.attn_flat)
    for group in range(HEADS):
        for piece in range(5):
            at = group * rows + small * (piece % 4)
            half = piece // 4
            r.attn_flat[at : at + small, half * spare : (half + 1) * spare] = attn_weight[
                group * small : (group + 1) * small, piece * spare : (piece + 1) * spare
            ]
    for half in range(2):
        send[half, :, 3 * width :] = low(r.attn_flat[:, half * spare : (half + 1) * spare])


def series_backward_attention(r, between):
    span, head_width = r.values.shape
    width = head_width * HEADS
    scale = head_width ** (-0.5)
    for tile in range(span // TILE):
        rows = slice(tile * TILE, (tile + 1) * TILE)
        seen = (tile + 1) * TILE
        held = getattr(r, "chances%d" % tile)
        head_grad = r.mixed_grad[rows, :] * (1.0 / HEADS)
        r.block[:, :seen] = nt(head_grad, r.values[:seen, :]) * scale
        total = jnp.zeros((TILE, width), jnp.float32)
        for head in range(HEADS):
            chances = held[head]
            slope = r.block[:, :seen]
            delta = jnp.sum(chances * slope, axis=-1, keepdims=True)
            grads = low(chances * (slope - delta))
            for part in range(tile + 1):
                getattr(r, "score_grads%d" % part)[
                    head, (tile - part) * TILE : (tile - part + 1) * TILE, :
                ] = grads[:, part * TILE : (part + 1) * TILE]
            total = total + nn(grads, r.head_keys[head, :seen, :])
        r.query_grad[rows, :] = low(total)
        between(tile)
    for tile in range(span // TILE):
        cols = slice(tile * TILE, (tile + 1) * TILE)
        start = tile * TILE
        total = jnp.zeros((TILE, width), jnp.float32)
        for head in range(HEADS):
            total = total + tn(
                getattr(r, "score_grads%d" % tile)[head], r.head_queries[head, start:, :]
            )
        r.key_grad[cols, :] = low(total)
        r.value_grad[cols, :] = low(
            tn(r.chance_sum[start:, cols], r.mixed_grad[start:, :] * (1.0 / HEADS))
        )


def series_backward_first(r):
    w, vec, gv = r.w, r.vec, r.gv
    span, width = r.hidden.shape
    head_width = width // HEADS
    rows = slice(0, span)
    send = r.first_send
    query, key, value = r.query_grad[...], r.key_grad[...], r.value_grad[...]
    grad = (
        r.sum_two_grad[...]
        + nt(query, w[:, QUERY : QUERY + width])
        + nt(key, w[:, KEY : KEY + width])
        + nt(value, w[:, VALUE : VALUE + head_width])
    )
    first = r.first_low[...]
    send[1, :, :width] = low(tn(first, query))
    send[1, :, width : 2 * width] = low(tn(first, key))
    send[1, :, 2 * width : 2 * width + head_width] = low(tn(first, value))
    unit = r.unit_one[...]
    row_sum(gv, 6, grad * unit)
    row_sum(gv, 7, grad)
    sum_one = normalise_back(grad, unit, r.inverse_one[...], vec[6:7, :])
    r.sum_two_grad[...] = sum_one
    gate = r.gate_one[...]
    grad_a = sum_one * gate
    grad_b = grad_a * r.glu_one[...] * (1.0 - gate)
    row_sum(gv, 4, grad_a)
    row_sum(gv, 5, grad_b)
    low_a, low_b = low(grad_a), low(grad_b)
    hidden_grad = nt(low_a, w[:, GLU_ONE_A : GLU_ONE_A + width]) + nt(
        low_b, w[:, GLU_ONE_B : GLU_ONE_B + width]
    )
    tanh, gate = r.cell_tanh[...], r.exit_gate[...]
    put_halves(r.local, rows, hidden_grad * gate * (1.0 - tanh * tanh))
    exit_grad = hidden_grad * tanh * gate * (1.0 - gate)
    row_sum(gv, 3, exit_grad)
    exit_grad = low(exit_grad)
    r.gate_grads[3] = exit_grad
    hidden = r.hidden[...]
    send[0, :, :width] = low(tn(hidden, low_a))
    send[0, :, width : 2 * width] = low(tn(hidden, low_b))
    send[0, :, 2 * width : 3 * width] = low(nn(r.x_flat[...], exit_grad))


def series_backward_scan(r):
    span = r.x.shape[0]
    steps = span // CHUNKS
    zeros = jnp.zeros((CHUNKS, LANES), jnp.float32)
    for half in range(2):
        r.forget[half, span:, :] = zeros

    def step(count, state):
        t = steps - 1 - count
        out = []
        at, after = pl.ds(t, CHUNKS, stride=steps), pl.ds(t + 1, CHUNKS, stride=steps)
        for half in range(2):
            grad, mult = state[half]
            forget = r.forget[half, after, :]
            grad = forget * grad + r.local[half, at, :]
            mult = mult * forget
            r.local[half, at, :] = grad
            r.mult[half, at, :] = mult
            out.append((grad, mult))
        return tuple(out)

    ends = lax.fori_loop(0, steps, step, ((zeros, zeros + 1.0),) * 2, unroll=8)
    for half in range(2):
        grads, mults = ends[half]
        state = jnp.zeros((1, LANES), jnp.float32)
        r.carry[half, CHUNKS - 1 : CHUNKS, :] = state
        for chunk in range(CHUNKS - 1, 0, -1):
            state = grads[chunk : chunk + 1] + mults[chunk : chunk + 1] * state
            r.carry[half, chunk - 1 : chunk, :] = state


def series_gate_grads(r):
    gv = r.gv
    span, width = r.x.shape
    steps = span // CHUNKS
    for half in range(2):
        for chunk in range(CHUNKS):
            rows = slice(chunk * steps, (chunk + 1) * steps)
            r.local[half, rows, :] += r.mult[half, rows, :] * r.carry[half, chunk : chunk + 1, :]
    grad = get_halves(r.local, slice(0, span), width)
    forget = get_halves(r.forget, slice(0, span), width)
    before = get_halves(r.cell, slice(7, 7 + span), width)
    enter, candidate = r.enter_gate[...], r.candidate[...]
    for gate, one in enumerate(
        (
            grad * before * forget * (1.0 - forget),
            grad * candidate * enter * (1.0 - enter),
            grad * enter * (1.0 - candidate * candidate),
        )
    ):
        row_sum(gv, gate, one)
        one = low(one)
        r.gate_grads[gate] = one
        r.lstm_flat[:, gate * width : (gate + 1) * width] = nn(r.x_flat[...], one)
    r.lstm_flat[:, 3 * width :] = gv[...].T
    lanes = r.lstm_send.shape[2]
    for half in range(2):
        r.lstm_send[half] = low(r.lstm_flat[:, half * lanes : (half + 1) * lanes])


def series_input_grad(r):
    width = r.x.shape[1]
    out = r.sum_two_grad[...].T
    for gate, block in enumerate((FORGET, ENTER, CANDIDATE, EXIT)):
        out = out + nt(r.w[:, block : block + width], r.gate_grads[gate])
    r.input_grad[...] = low(out)


class Exchange:
    def __init__(self, sems, devices, source, target):
        self.sems, self.source, self.target = sems, source, target
        self.count, self.me, self.device = devices

    def other(self, step):
        return lax.rem(self.me + step, self.count)

    def copy(self, to, origin):
        return pltpu.make_async_remote_copy(
            src_ref=self.source(to),
            dst_ref=self.target(origin),
            send_sem=self.sems.at[0, to],
            recv_sem=self.sems.at[1, origin],
            device_id=self.device(to),
            device_id_type=pl.DeviceIdType.MESH,
        )

    def send(self, to):
        self.copy(to, self.me).start()

    def arrive(self, origin):
        self.copy(origin, origin).wait_recv()

    def start(self):
        for step in range(1, self.count):
            self.send(self.other(step))

    def arrive_all(self):
        for step in range(1, self.count):
            self.arrive(self.other(step))

    def sent(self):
        for step in range(1, self.count):
            self.copy(self.other(step), self.me).wait_send()


def over_time():
    return lax.axis_size("tm"), lax.axis_index("tm"), lambda to: {"tm": to}


def over_series():
    return lax.axis_size("dp"), lax.axis_index("dp"), lambda to: {"dp": to}


def over_chips():
    core = my_core()
    return (
        lax.axis_size("tm") // 2,
        lax.div(lax.axis_index("tm"), 2),
        lambda to: {"tm": 2 * to + core},
    )


def my_core():
    return lax.rem(lax.axis_index("tm"), 2)


def to_other_core(source, target, sems, index):
    return pltpu.make_async_remote_copy(
        src_ref=source,
        dst_ref=target,
        send_sem=sems.at[0, index],
        recv_sem=sems.at[1, index],
        device_id={"tm": lax.axis_index("tm") + 1 - 2 * my_core()},
        device_id_type=pl.DeviceIdType.MESH,
    )


PAD_ROWS = 48
GROUP_COLUMNS = (384, 384, 640)
GROUP_LANES = {"middle": 512, "first": 512, "lstm": 256}


def travel_scratch(count, groups, steps, width, params):
    rows = params[0].shape[0]
    out = dict(
        slopes=pltpu.VMEM((count, 8, steps), jnp.float32),
        levels=pltpu.VMEM((count, 8, steps), jnp.float32),
        stage=pltpu.VMEM((width, 2 * GROUP_COLUMNS[2]), jnp.float32),
        attn_stage=pltpu.VMEM((width, width), jnp.float32),
        table_stage=pltpu.VMEM((PAD_ROWS, LANES), jnp.float32),
    )
    for index, param in enumerate(params):
        out["param%d" % index] = pltpu.VMEM(param.shape, jnp.float32)
    out["load_sems"] = pltpu.SemaphoreType.DMA((len(params),))
    for group, columns in enumerate(GROUP_COLUMNS):
        out["params%d" % group] = pltpu.VMEM((2, groups, PAD_ROWS, columns), jnp.bfloat16)
        out["params%d_dp" % group] = pltpu.SemaphoreType.DMA((2, groups))
        out["params%d_core" % group] = pltpu.SemaphoreType.DMA((2, groups))
    for name, lanes in GROUP_LANES.items():
        out[name + "_near"] = pltpu.VMEM((width, lanes), jnp.bfloat16)
        out[name + "_part"] = pltpu.VMEM((groups, PAD_ROWS, lanes), jnp.bfloat16)
        out[name + "_parts"] = pltpu.VMEM((groups, PAD_ROWS, lanes), jnp.bfloat16)
        out[name + "_chips"] = pltpu.VMEM((count // 2, PAD_ROWS, lanes), jnp.bfloat16)
        out[name + "_core_sems"] = pltpu.SemaphoreType.DMA((2, 2))
        out[name + "_dp_sems"] = pltpu.SemaphoreType.DMA((2, groups))
        out[name + "_chip_sems"] = pltpu.SemaphoreType.DMA((2, count // 2))
    for name in ("x", "adjoint", "out", "input", "slope", "predicted"):
        out[name + "_sems"] = pltpu.SemaphoreType.DMA((2, count))
    out["own_sems"] = pltpu.SemaphoreType.DMA((4,))
    return out


class Parameters:
    def __init__(self, r, group):
        self.buffer = buffer = getattr(r, "params%d" % group)
        self.core = core = my_core()
        self.over = Exchange(
            getattr(r, "params%d_dp" % group),
            over_series(),
            lambda to: buffer.at[core, lax.axis_index("dp")],
            lambda origin: buffer.at[core, origin],
        )
        self.sems = getattr(r, "params%d_core" % group)

    def hand(self, origin, core):
        block = self.buffer.at[core, origin]
        return to_other_core(block, block, self.sems, origin)

    def pass_on(self):
        for step in range(1, self.over.count):
            origin = self.over.other(step)
            self.over.arrive(origin)
            self.hand(origin, self.core).start()

    def arrive(self):
        for step in range(1, self.over.count):
            self.hand(self.over.other(step), 1 - self.core).wait_recv()

    def sent(self):
        self.over.sent()
        for step in range(1, self.over.count):
            self.hand(self.over.other(step), self.core).wait_send()


class Reduction:
    def __init__(self, r, name, final):
        self.send, self.near = getattr(r, name + "_send"), getattr(r, name + "_near")
        self.part, self.parts = getattr(r, name + "_part"), getattr(r, name + "_parts")
        self.chips, self.final = getattr(r, name + "_chips"), final
        self.core, self.rows = my_core(), final.shape[1]
        self.core_sems = getattr(r, name + "_core_sems")
        part, parts, chips = self.part, self.parts, self.chips
        self.to_series = Exchange(
            getattr(r, name + "_dp_sems"),
            over_series(),
            lambda to: part.at[to],
            lambda origin: parts.at[origin],
        )
        chip = over_chips()[1]
        self.to_chips = Exchange(
            getattr(r, name + "_chip_sems"),
            over_chips(),
            lambda to: chips.at[chip],
            lambda origin: chips.at[origin],
        )

    def out(self):
        return to_other_core(self.send.at[1 - self.core], self.near, self.core_sems, 0)

    def back(self, core):
        return to_other_core(self.final.at[core], self.final.at[core], self.core_sems, 1)

    def sum_of(self, ref):
        total = ref[0, : self.rows].astype(jnp.float32)
        for index in range(1, ref.shape[0]):
            total = total + ref[index, : self.rows].astype(jnp.float32)
        return total

    def start(self):
        self.out().start()

    def across_series(self):
        self.out().wait_recv()
        total = self.send[self.core].astype(jnp.float32) + self.near[...].astype(jnp.float32)
        for group in range(self.to_series.count):
            self.part[group, : self.rows] = low(total[group * self.rows : (group + 1) * self.rows])
        self.to_series.start()

    def across_chips(self):
        self.to_series.arrive_all()
        self.parts[self.to_series.me] = self.part[self.to_series.me]
        self.chips[self.to_chips.me, : self.rows] = low(self.sum_of(self.parts))
        self.to_chips.start()

    def to_both(self):
        self.to_chips.arrive_all()
        self.final[self.core] = self.sum_of(self.chips)
        self.back(self.core).start()

    def finish(self):
        self.back(1 - self.core).wait_recv()
        self.out().wait_send()
        self.to_series.sent()
        self.to_chips.sent()
        self.back(self.core).wait_send()


def greet():
    barrier = pltpu.get_barrier_semaphore()
    total = 0
    for count, me, device in (over_time(), over_series()):
        for step in range(1, count):
            pl.semaphore_signal(
                barrier,
                inc=1,
                device_id=device(lax.rem(me + step, count)),
                device_id_type=pl.DeviceIdType.MESH,
            )
            total += 1
    return lambda: pl.semaphore_wait(barrier, total)


def pack_params(r, group, params):
    mine = lax.axis_index("dp")
    buffer = getattr(r, "params%d" % group)

    def put(half, column, array):
        rows, columns = array.shape
        buffer[half, mine, :rows, column : column + columns] = low(array[...])

    if group == 0:
        lstm, table, level = params
        rows, columns = lstm.shape
        split = GROUP_COLUMNS[0]
        buffer[0, mine, :rows, :] = low(lstm[:, :split])
        buffer[1, mine, :rows, : columns - split] = low(lstm[:, split:])
        r.table_stage[...] = jnp.zeros_like(r.table_stage)
        r.table_stage[: table.shape[0], :rows] = table[...]
        r.table_stage[VECTORS : VECTORS + LEVEL_TALLY, :rows] = level[...]
        put(1, columns - split, r.table_stage)
    elif group == 1:
        glu_one, qkv = params
        put(0, 0, glu_one)
        put(1, 0, qkv)
    else:
        glu_two, glu_three, inner, middle, attn = params
        put(0, 0, glu_two)
        put(0, glu_two.shape[1], glu_three)
        put(1, 0, inner)
        put(1, inner.shape[1], middle)
        put(1, 2 * inner.shape[1], attn)


def unpack_params(r, group, rows, attn_rows):
    width = r.w.shape[0]
    head_width = width // HEADS
    buffer, stage = getattr(r, "params%d" % group), r.stage
    columns = GROUP_COLUMNS[group]
    for half in range(2):
        for origin in range(buffer.shape[1]):
            stage[origin * rows : (origin + 1) * rows, half * columns : (half + 1) * columns] = (
                buffer[half, origin].astype(jnp.float32)[:rows]
            )

    def place(block, column, size):
        r.w[:, block : block + size] = low(stage[:, column : column + size])

    if group == 0:
        for gate, block in enumerate((FORGET, ENTER, CANDIDATE, EXIT)):
            place(block, gate * width, width)
        vectors = jnp.concatenate(
            [
                buffer[1, origin][:, columns - LANES :].astype(jnp.float32)[: VECTORS + 8, :rows]
                for origin in range(buffer.shape[1])
            ],
            axis=1,
        )
        r.vec[...] = vectors[:VECTORS]
        r.level[...] = low(vectors[VECTORS:])
    elif group == 1:
        place(GLU_ONE_A, 0, width)
        place(GLU_ONE_B, width, width)
        place(QUERY, columns, width)
        place(KEY, columns + width, width)
        place(VALUE, columns + 2 * width, head_width)
    else:
        place(GLU_TWO_A, 0, width)
        place(GLU_TWO_B, width, width)
        place(GLU_THREE_A, 2 * width, width)
        place(GLU_THREE_B, 3 * width, width)
        place(INNER, columns, width)
        place(MIDDLE, columns + width, width)
        for origin in range(buffer.shape[1]):
            r.attn_stage[origin * attn_rows : (origin + 1) * attn_rows, :] = stage[
                origin * rows : origin * rows + attn_rows,
                columns + 2 * width : columns + 3 * width,
            ]
        r.w[:head_width, ATTN_OUT : ATTN_OUT + width] = low(r.attn_stage[:head_width, :])


def series_kernel(begins, reaches, x_hbm, adjoint_hbm, slopes, *others):
    params, others = others[:10], others[10:]
    (out_hbm, predicted_out, input_hbm, final_middle, final_first, final_lstm), scratch = (
        others[:6],
        others[6:],
    )
    count, width, steps = x_hbm.shape
    span = count * steps
    groups = lax.axis_size("dp")
    names = series_scratch(span, width, width // HEADS)
    names.update(travel_scratch(count, groups, steps, width, params))
    r = types.SimpleNamespace(**dict(zip(names, scratch)))
    me = lax.axis_index("tm")
    last = count - 1

    def block(ref, index):
        return ref.at[:, rows_of(index, steps)]

    x_over = Exchange(
        r.x_sems, over_time(), lambda to: x_hbm.at[to], lambda origin: block(r.x_flat, origin)
    )
    adjoint_over = Exchange(
        r.adjoint_sems,
        over_time(),
        lambda to: adjoint_hbm.at[to],
        lambda origin: block(r.adjoint, origin),
    )
    out_over = Exchange(
        r.out_sems, over_time(), lambda to: block(r.out, to), lambda origin: out_hbm.at[origin]
    )
    input_over = Exchange(
        r.input_sems,
        over_time(),
        lambda to: block(r.input_grad, to),
        lambda origin: input_hbm.at[origin],
    )
    slope_over = Exchange(
        r.slope_sems, over_time(), lambda to: r.slopes.at[to], lambda origin: r.slope
    )
    predicted_over = Exchange(
        r.predicted_sems, over_time(), lambda to: r.predicted, lambda origin: r.levels.at[origin]
    )
    travelling = [Parameters(r, group) for group in range(3)]
    middle_sum = Reduction(r, "middle", final_middle)
    first_sum = Reduction(r, "first", final_first)
    lstm_sum = Reduction(r, "lstm", final_lstm)
    own_x = pltpu.make_async_copy(x_hbm.at[me], block(r.x_flat, me), r.own_sems.at[0])
    own_adjoint = pltpu.make_async_copy(adjoint_hbm.at[me], block(r.adjoint, me), r.own_sems.at[1])
    own_out = pltpu.make_async_copy(block(r.out, me), out_hbm.at[me], r.own_sems.at[2])
    own_input = pltpu.make_async_copy(block(r.input_grad, me), input_hbm.at[me], r.own_sems.at[3])
    held = [getattr(r, "param%d" % index) for index in range(len(params))]
    loads = [
        pltpu.make_async_copy(param, here, r.load_sems.at[index])
        for index, (param, here) in enumerate(zip(params, held))
    ]

    def pack(group, *indices):
        for index in indices:
            loads[index].wait()
        pack_params(r, group, [held[index] for index in indices])

    everyone_here = greet()
    for load in loads:
        load.start()
    own_x.start()
    own_adjoint.start()
    pack(0, 0, 9, 8)
    everyone_here()
    travelling[0].over.start()
    x_over.start()
    pack(1, 1, 2)
    pack(2, 4, 7, 5, 6, 3)
    for track in range(count):
        r.slopes[track] = jnp.concatenate(
            [
                slopes[level_at].astype(jnp.float32)[track : track + 1]
                for level_at in range(LEVEL_TALLY)
            ]
            + [jnp.zeros((8 - LEVEL_TALLY, steps), jnp.float32)],
            axis=0,
        )
    begin = begins[me]
    choice = reaches[me]
    horizon = jnp.where(choice == 0, 1, jnp.where(choice == 1, 5, 24))
    rows, attn_rows = params[0].shape[0], params[3].shape[0]
    r.gv[...] = jnp.zeros_like(r.gv)
    own_x.wait()
    series_turn(r, me, steps)
    travelling[0].pass_on()
    travelling[1].over.start()

    def arriving(step, _):
        origin = x_over.other(step)
        x_over.arrive(origin)
        series_turn(r, origin, steps)
        return 0

    lax.fori_loop(1, count, arriving, 0)
    travelling[0].arrive()
    unpack_params(r, 0, rows, attn_rows)
    series_gates(r, begin)
    adjoint_over.start()

    @pl.when(me == last)
    def _():
        slope_over.start()
        r.slope[...] = r.slopes[last]

    series_forward_scan(r)
    travelling[1].pass_on()
    travelling[2].over.start()
    travelling[1].arrive()
    unpack_params(r, 1, rows, attn_rows)
    series_forward_first(r)
    series_forward_attention(r, begin)
    travelling[2].pass_on()
    travelling[2].arrive()
    unpack_params(r, 2, rows, attn_rows)
    own_adjoint.wait()
    adjoint_over.arrive_all()

    @pl.when(me != last)
    def _():
        slope_over.arrive(last)

    def forward_done():
        own_out.start()
        out_over.start()

        @pl.when(me != last)
        def _():
            predicted_over.send(last)

    series_middle(r, horizon, forward_done)
    middle_sum.start()

    def between(tile):
        if tile == 2:
            middle_sum.across_series()

    series_backward_attention(r, between)
    series_backward_first(r)
    first_sum.start()
    series_backward_scan(r)
    first_sum.across_series()
    series_gate_grads(r)
    lstm_sum.start()
    middle_sum.across_chips()
    series_input_grad(r)
    own_input.start()
    input_over.start()
    lstm_sum.across_series()
    middle_sum.to_both()
    first_sum.across_chips()

    @pl.when(me != last)
    def _():
        predicted_over.copy(last, me).wait_send()
        predicted_out[...] = jnp.zeros_like(predicted_out)

    @pl.when(me == last)
    def _():
        slope_over.sent()
        predicted_over.arrive_all()
        r.levels[last] = r.predicted[...]
        for level_at in range(LEVEL_TALLY):
            predicted_out[level_at] = jnp.concatenate(
                [r.levels[track][level_at : level_at + 1] for track in range(count)], axis=0
            )

    lstm_sum.across_chips()
    first_sum.to_both()
    x_over.sent()
    adjoint_over.sent()
    for group in travelling:
        group.sent()
    own_out.wait()
    out_over.arrive_all()
    out_over.sent()
    middle_sum.finish()
    first_sum.finish()
    lstm_sum.to_both()
    own_input.wait()
    input_over.arrive_all()
    input_over.sent()
    lstm_sum.finish()


def unpack_kernel(final_middle, final_first, final_lstm, out_in, predicted_in, input_in, *others):
    (lstm, glu_one, qkv, attn, glu_two, inner, middle, glu_three, level, table) = others[:10]
    out, predicted, input_grad = others[10:]
    predicted[...] = predicted_in[...]
    rows, width = inner.shape
    lanes = final_lstm.shape[2]
    for ref, at in ((glu_two, 0), (glu_three, 1)):
        ref[...] = final_middle[at, :, : 2 * width]
    for ref, at in ((inner, 0), (middle, 1)):
        ref[...] = final_middle[at, :, 2 * width : 3 * width]
    small, spare = attn.shape[0], width // 5
    for piece in range(5):
        at = small * (piece % 4)
        attn[:, piece * spare : (piece + 1) * spare] = final_middle[
            piece // 4, at : at + small, 3 * width : 3 * width + spare
        ]
    glu_one[...] = final_first[0, :, : 2 * width]
    qkv[...] = final_first[1, :, : qkv.shape[1]]
    lstm[:, :lanes] = final_lstm[0]
    lstm[:, lanes : 3 * width] = final_lstm[1, :, : 3 * width - lanes]
    lstm[:, 3 * width :] = final_first[0, :, 2 * width : 3 * width]
    vectors = final_lstm[1, :, 3 * width - lanes :].T
    table[...] = vectors[: table.shape[0]]
    level[...] = vectors[VECTORS : VECTORS + LEVEL_TALLY]
    out[...] = out_in[...]
    input_grad[...] = input_in[...]


def whole_series(embedded_features, earliest_seen_moment, reach_choice, *others):
    count, steps, width = embedded_features.shape
    features = embedded_features.swapaxes(1, 2)
    adjoint = others[-2].swapaxes(1, 2)
    slopes = others[-1].swapaxes(0, 1)
    params = others[:-4] + (others[-4].T, others[-3].T)
    groups = lax.axis_size("dp")
    rows = params[0].shape[0]
    names = series_scratch(count * steps, width, width // HEADS)
    names.update(travel_scratch(count, groups, steps, width, params))
    smem, vmem, anywhere = (
        pl.BlockSpec(memory_space=space) for space in (pltpu.SMEM, pltpu.VMEM, pl.ANY)
    )
    moved = (
        jax.ShapeDtypeStruct(features.shape, jnp.bfloat16),
        jax.ShapeDtypeStruct(slopes.shape, jnp.float32),
        jax.ShapeDtypeStruct(features.shape, jnp.bfloat16),
    )
    out, predicted, input_grad, *finals = pl.pallas_call(
        series_kernel,
        out_shape=moved
        + tuple(
            jax.ShapeDtypeStruct((2, rows, lanes), jnp.float32) for lanes in GROUP_LANES.values()
        ),
        in_specs=[smem, smem, anywhere, anywhere, vmem] + [anywhere] * len(params),
        out_specs=(anywhere, vmem, anywhere) + (vmem,) * 3,
        scratch_shapes=list(names.values()),
        compiler_params=pltpu.CompilerParams(
            vmem_limit_bytes=VMEM_BYTES, collective_id=0, has_side_effects=True
        ),
    )(
        earliest_seen_moment,
        reach_choice,
        features,
        adjoint,
        slopes,
        *params,
    )
    *grads, level_grad, table_grad, out, predicted, input_grad = pl.pallas_call(
        unpack_kernel,
        out_shape=tuple(jax.ShapeDtypeStruct(param.shape, jnp.float32) for param in params) + moved,
        in_specs=[vmem] * 6,
        out_specs=(vmem,) * (len(params) + 3),
    )(*finals, out, predicted, input_grad)
    return (
        out.swapaxes(1, 2),
        predicted.swapaxes(0, 1),
        input_grad.swapaxes(1, 2),
        *grads,
        level_grad.T,
        table_grad.T,
    )


def on_device(embedded_features, *others):
    count, steps, _ = embedded_features.shape
    one_each = count == lax.axis_size("tm") == CHUNKS and steps == LANES
    return (whole_series if one_each else shards)(embedded_features, *others)


def solution(mesh):
    placed = (
        P("dp", "tm", None),
        P("dp"),
        P("dp"),
        P("dp", None),
        P("dp", None),
        P("dp", None),
        P("dp", None),
        P("dp", None),
        P("dp", None),
        P("dp", None),
        P("dp", None),
        P("dp", None),
        P("dp", None),
        P("dp", "tm", None),
        P("dp", None, "tm"),
    )
    return jax.shard_map(
        on_device,
        mesh=mesh,
        in_specs=placed,
        out_specs=(
            P("dp", "tm", None),
            P("dp", None, "tm"),
            P("dp", "tm", None),
            P("dp", None),
            P("dp", None),
            P("dp", None),
            P("dp", None),
            P("dp", None),
            P("dp", None),
            P("dp", None),
            P("dp", None),
            P("dp", None),
            P("dp", None),
        ),
        check_vma=False,
    )
```

```python
import types

import jax
import jax.numpy as jnp
from jax import lax
from jax.experimental import pallas as pl
from jax.experimental.pallas import tpu as pltpu
from jax.sharding import PartitionSpec as P

HEADS = 4
LEVEL_TALLY = 3
DEC = 24
MICRO = 2


EPSILON = 1e-05
NEG_BIG = -1e30
attend_group = 2
LOG2_E = 1.4426950408889634
VMEM_BYTES = 60 * 2**20


def entering(value, axis, join, neutral, backward):
    count, mine = (lax.axis_size(axis), lax.axis_index(axis))
    pieces = jax.tree.map(lambda part: lax.all_gather(part, axis), value)
    if backward:
        pieces = jax.tree.map(lambda part: part[::-1], pieces)
        mine = count - 1 - mine
    so_far = jax.tree.map(
        lambda part, zero: jnp.full_like(part, 0) + jnp.asarray(zero, part.dtype), value, neutral
    )

    def turn(position, so_far):
        longer = join(so_far, jax.tree.map(lambda part: part[position], pieces))
        return jax.tree.map(lambda new, old: jnp.where(position < mine, new, old), longer, so_far)

    return lax.fori_loop(0, count - 1, turn, so_far)


def narrow_convert(values):
    return values.astype(jnp.bfloat16)


def tensor_dot_plain(left, right):
    return jnp.dot(left, right, preferred_element_type=jnp.float32)


def flipped_dot(left, right):
    return lax.dot_general(
        left, right, (((0,), (0,)), ((), ())), preferred_element_type=jnp.float32
    )


def dot_against_flipped(left, right):
    return lax.dot_general(
        left, right, (((1,), (1,)), ((), ())), preferred_element_type=jnp.float32
    )


def affine_join(earlier, later):
    return (later[0] * earlier[0], later[0] * earlier[1] + later[1])


def layer_norm(values, gains, offsets):
    centred = values - jnp.mean(values, axis=-1, keepdims=True)
    spread = jnp.mean(centred * centred, axis=-1, keepdims=True)
    return centred * lax.rsqrt(spread + EPSILON) * gains + offsets


def gated_unit(pre_act):
    half_width = pre_act.shape[-1] // 2
    return pre_act[..., :half_width] * jax.nn.sigmoid(pre_act[..., half_width:])


def lstm_gates(pre_act, keep_mask):
    quarter = pre_act.shape[-1] // 4
    forget = jax.nn.sigmoid(pre_act[..., :quarter]) * keep_mask
    inflow = jax.nn.sigmoid(pre_act[..., quarter : 2 * quarter]) * jnp.tanh(
        pre_act[..., 2 * quarter : 3 * quarter]
    )
    out_gate = jax.nn.sigmoid(pre_act[..., 3 * quarter :])
    return (forget, inflow, out_gate)


def masked_scores(query_block, key_block, query_pos, key_pos, begin_block, scale):
    raw = jnp.einsum("gqhd,gkhd->ghqk", query_block, key_block, preferred_element_type=jnp.float32)
    lowest = jnp.minimum(begin_block[:, None], query_pos[None, :])
    allowed = (key_pos[None, None, :] <= query_pos[None, :, None]) & (
        key_pos[None, None, :] >= lowest[:, :, None]
    )
    return jnp.where(allowed[:, None], raw * scale, NEG_BIG)


def score_grad(chances, dprob, row_delta, scale):
    return narrow_convert(chances * (dprob[:, None] - row_delta[..., None]) * scale)


def shards(
    embedded_features,
    earliest_seen_moment,
    reach_choice,
    lstm_valve_coeffs,
    lstm_unit_coeffs,
    asker_lookup_coeffs,
    attend_exit_coeffs,
    attend_unit_coeffs,
    skipnet_entry_coeffs,
    skipnet_inner_coeffs,
    skipnet_unit_coeffs,
    level_map_coeffs,
    bias_gain_table,
    block_emit_adjoint,
    predicted_adjoint,
):
    (
        mat_lstm,
        mat_glu_one,
        mat_qkv,
        mat_attn,
        mat_glu_two,
        mat_inner,
        mat_middle,
        mat_glu_three,
        level_dot,
        vec_table,
    ) = (
        lax.all_gather(narrow_convert(lstm_valve_coeffs), "dp", axis=0, tiled=True),
        lax.all_gather(narrow_convert(lstm_unit_coeffs), "dp", axis=0, tiled=True),
        lax.all_gather(narrow_convert(asker_lookup_coeffs), "dp", axis=0, tiled=True),
        lax.all_gather(narrow_convert(attend_exit_coeffs), "dp", axis=0, tiled=True),
        lax.all_gather(narrow_convert(attend_unit_coeffs), "dp", axis=0, tiled=True),
        lax.all_gather(narrow_convert(skipnet_entry_coeffs), "dp", axis=0, tiled=True),
        lax.all_gather(narrow_convert(skipnet_inner_coeffs), "dp", axis=0, tiled=True),
        lax.all_gather(narrow_convert(skipnet_unit_coeffs), "dp", axis=0, tiled=True),
        lax.all_gather(narrow_convert(level_map_coeffs), "dp", axis=0, tiled=True),
        lax.all_gather(narrow_convert(bias_gain_table), "dp", axis=0, tiled=True),
    )
    series_per_device, steps_per_device, model_width = embedded_features.shape
    seq_total = steps_per_device * lax.axis_size("tm")
    head_width = model_width // HEADS
    count_of_rows = series_per_device * steps_per_device
    scale = head_width ** (-0.5)
    vec_full = vec_table.astype(jnp.float32)
    time_local = lax.axis_index("tm") * steps_per_device + jnp.arange(
        steps_per_device, dtype=jnp.int32
    )
    time_all = jnp.arange(seq_total, dtype=jnp.int32)
    horizon_len = jnp.where(reach_choice == 0, 1, jnp.where(reach_choice == 1, 5, 24))
    ahead_moment_filter = (
        (
            (time_local[None, :] >= seq_total - DEC)
            & (time_local[None, :] < seq_total - DEC + horizon_len[:, None])
        )
        .astype(jnp.float32)
        .reshape(count_of_rows, 1)
    )
    keep_mask = (
        (time_local[None, :] != earliest_seen_moment[:, None])
        .astype(jnp.float32)
        .reshape(count_of_rows, 1)
    )
    group_size = series_per_device // MICRO
    group_total = series_per_device // attend_group
    state_ones = jnp.ones((group_size, model_width), jnp.float32)
    state_zeros = jnp.zeros((group_size, model_width), jnp.float32)

    def split_groups(array):
        return array.reshape((group_total, attend_group) + array.shape[1:])

    input_rows = embedded_features.reshape(count_of_rows, model_width)
    input_full = input_rows.astype(jnp.float32)
    lstm_pre = tensor_dot_plain(input_rows, mat_lstm) + vec_full[:, 0:4].T.reshape(-1)
    forget, inflow, out_gate = lstm_gates(lstm_pre, keep_mask)
    forget_seq = forget.reshape(series_per_device, steps_per_device, model_width)
    inflow_seq = inflow.reshape(series_per_device, steps_per_device, model_width)
    mult_seq, cell_local = lax.associative_scan(affine_join, (forget_seq, inflow_seq), axis=1)
    cell_parts = []
    for group in range(MICRO):
        lower_row = group * group_size
        upper_row = lower_row + group_size
        _, arriving = entering(
            (mult_seq[lower_row:upper_row, -1], cell_local[lower_row:upper_row, -1]),
            "tm",
            affine_join,
            (state_ones, state_zeros),
            False,
        )
        cell_parts.append(arriving)
    cell_in = jnp.concatenate(cell_parts, axis=0)
    cell_seq = cell_local + mult_seq * cell_in[:, None, :]
    cell_tanh = jnp.tanh(cell_seq.reshape(count_of_rows, model_width))
    hidden_low = narrow_convert(out_gate * cell_tanh)
    glu_one_pre = tensor_dot_plain(hidden_low, mat_glu_one) + vec_full[:, 4:6].T.reshape(-1)
    first_sum = input_full + gated_unit(glu_one_pre)
    first = layer_norm(first_sum, vec_full[:, 6], vec_full[:, 7])
    first_low = narrow_convert(first)
    qkv_low = narrow_convert(tensor_dot_plain(first_low, mat_qkv))
    query_low = qkv_low[:, :model_width].reshape(
        series_per_device, steps_per_device, HEADS, head_width
    )
    key_value = qkv_low[:, model_width:].reshape(
        series_per_device, steps_per_device, model_width + head_width
    )
    key_value_all = lax.all_gather(key_value, "tm", axis=1, tiled=True)
    keys_all = key_value_all[..., :model_width].reshape(
        series_per_device, seq_total, HEADS, head_width
    )
    values_all = key_value_all[..., model_width:]

    def attend_forward(block_args):
        query_block, key_block, value_block, begin_block = block_args
        scores = masked_scores(query_block, key_block, time_local, time_all, begin_block, scale)
        row_top = jnp.max(scores, axis=-1, keepdims=True)
        row_exp = jnp.exp(scores - row_top)
        row_total = jnp.sum(row_exp, axis=-1, keepdims=True)
        weights_low = narrow_convert(row_exp / row_total)
        mixed_block = jnp.einsum(
            "ghqk,gkd->gqd", weights_low, value_block, preferred_element_type=jnp.float32
        ) * (1.0 / HEADS)
        return (mixed_block, (row_top + jnp.log(row_total))[..., 0])

    mixed, log_total = lax.map(
        attend_forward,
        (
            split_groups(query_low),
            split_groups(keys_all),
            split_groups(values_all),
            split_groups(earliest_seen_moment),
        ),
    )
    mixed_low = narrow_convert(mixed.reshape(count_of_rows, head_width))
    attn_low = narrow_convert(tensor_dot_plain(mixed_low, mat_attn))
    glu_two_pre = tensor_dot_plain(attn_low, mat_glu_two) + vec_full[:, 8:10].T.reshape(-1)
    second_sum = first + gated_unit(glu_two_pre)
    second = layer_norm(second_sum, vec_full[:, 10], vec_full[:, 11])
    second_low = narrow_convert(second)
    inner_pre = tensor_dot_plain(second_low, mat_inner) + vec_full[:, 12]
    inner_low = narrow_convert(jax.nn.elu(inner_pre))
    middle_low = narrow_convert(tensor_dot_plain(inner_low, mat_middle) + vec_full[:, 13])
    glu_three_pre = tensor_dot_plain(middle_low, mat_glu_three) + vec_full[:, 14:16].T.reshape(-1)
    final_sum = second + gated_unit(glu_three_pre)
    second_block_emit = layer_norm(final_sum, vec_full[:, 16], vec_full[:, 17])
    closing_narrowed = narrow_convert(second_block_emit)
    predicted_entries = tensor_dot_plain(closing_narrowed, level_dot) * ahead_moment_filter
    predicted_levels = predicted_entries.reshape(
        series_per_device, steps_per_device, LEVEL_TALLY
    ).transpose(0, 2, 1)
    predicted_slope = narrow_convert(
        predicted_adjoint.astype(jnp.float32).transpose(0, 2, 1).reshape(count_of_rows, LEVEL_TALLY)
        * ahead_moment_filter
    )
    level_slope = flipped_dot(closing_narrowed, predicted_slope)
    final_grad = block_emit_adjoint.reshape(count_of_rows, model_width).astype(
        jnp.float32
    ) + dot_against_flipped(predicted_slope, level_dot)
    _, norm_pull = jax.vjp(layer_norm, final_sum, vec_full[:, 16], vec_full[:, 17])
    sum_three_grad, gain_three_grad, offset_three_grad = norm_pull(final_grad)
    _, glu_pull = jax.vjp(gated_unit, glu_three_pre)
    (glu_three_grad,) = glu_pull(sum_three_grad)
    glu_three_low = narrow_convert(glu_three_grad)
    grad_glu_three = flipped_dot(middle_low, glu_three_low)
    middle_grad = dot_against_flipped(glu_three_low, mat_glu_three)
    middle_grad_low = narrow_convert(middle_grad)
    grad_middle = flipped_dot(inner_low, middle_grad_low)
    inner_grad = dot_against_flipped(middle_grad_low, mat_middle)
    _, elu_pull = jax.vjp(jax.nn.elu, inner_pre)
    (inner_pre_grad,) = elu_pull(inner_grad)
    inner_pre_low = narrow_convert(inner_pre_grad)
    grad_inner = flipped_dot(second_low, inner_pre_low)
    second_grad = sum_three_grad + dot_against_flipped(inner_pre_low, mat_inner)
    _, norm_pull = jax.vjp(layer_norm, second_sum, vec_full[:, 10], vec_full[:, 11])
    sum_two_grad, gain_two_grad, offset_two_grad = norm_pull(second_grad)
    _, glu_pull = jax.vjp(gated_unit, glu_two_pre)
    (glu_two_grad,) = glu_pull(sum_two_grad)
    glu_two_low = narrow_convert(glu_two_grad)
    grad_glu_two = flipped_dot(attn_low, glu_two_low)
    attn_grad_low = narrow_convert(dot_against_flipped(glu_two_low, mat_glu_two))
    grad_attn = flipped_dot(mixed_low, attn_grad_low)
    mixed_grad_low = narrow_convert(dot_against_flipped(attn_grad_low, mat_attn))
    head_grad = (mixed_grad_low * (1.0 / HEADS)).reshape(
        series_per_device, steps_per_device, head_width
    )

    def attend_backward(block_args):
        query_block, key_block, value_block, begin_block, lse_block, dout_block = block_args
        scores = masked_scores(query_block, key_block, time_local, time_all, begin_block, scale)
        chances = jnp.exp(scores - lse_block[..., None])
        dprob = jnp.einsum(
            "gqd,gkd->gqk", dout_block, value_block, preferred_element_type=jnp.float32
        )
        row_delta = jnp.sum(chances * dprob[:, None], axis=-1)
        dscore = score_grad(chances, dprob, row_delta, scale)
        dquery = jnp.einsum(
            "ghqk,gkhd->gqhd", dscore, key_block, preferred_element_type=jnp.float32
        )
        dkey = jnp.einsum(
            "ghqk,gqhd->gkhd", dscore, query_block, preferred_element_type=jnp.float32
        )
        dvalue = jnp.einsum(
            "ghqk,gqd->gkd", narrow_convert(chances), dout_block, preferred_element_type=jnp.float32
        )
        key_terms = jnp.concatenate(
            [dkey.reshape(attend_group, seq_total, model_width), dvalue], axis=-1
        )
        return (dquery, key_terms)

    dquery, key_terms = lax.map(
        attend_backward,
        (
            split_groups(query_low),
            split_groups(keys_all),
            split_groups(values_all),
            split_groups(earliest_seen_moment),
            log_total,
            split_groups(head_grad),
        ),
    )
    own_keys = lax.psum_scatter(
        key_terms.reshape(series_per_device, seq_total, model_width + head_width),
        "tm",
        scatter_dimension=1,
        tiled=True,
    )
    qkv_grad = jnp.concatenate(
        [
            dquery.reshape(count_of_rows, model_width),
            own_keys.reshape(count_of_rows, model_width + head_width),
        ],
        axis=1,
    )
    qkv_grad_low = narrow_convert(qkv_grad)
    grad_qkv = flipped_dot(first_low, qkv_grad_low)
    first_grad = sum_two_grad + dot_against_flipped(qkv_grad_low, mat_qkv)
    _, norm_pull = jax.vjp(layer_norm, first_sum, vec_full[:, 6], vec_full[:, 7])
    sum_one_grad, gain_one_grad, offset_one_grad = norm_pull(first_grad)
    _, glu_pull = jax.vjp(gated_unit, glu_one_pre)
    (glu_one_grad,) = glu_pull(sum_one_grad)
    glu_one_low = narrow_convert(glu_one_grad)
    grad_glu_one = flipped_dot(hidden_low, glu_one_low)
    hidden_grad = dot_against_flipped(glu_one_low, mat_glu_one)
    out_gate_grad = hidden_grad * cell_tanh
    direct_grad = (hidden_grad * out_gate * (1.0 - cell_tanh * cell_tanh)).reshape(
        series_per_device, steps_per_device, model_width
    )
    next_forget = jnp.concatenate([forget_seq[:, 1:], jnp.ones_like(forget_seq[:, :1])], axis=1)
    rev_mult, rev_cell = lax.associative_scan(
        affine_join, (next_forget, direct_grad), axis=1, reverse=True
    )
    head_mult = forget_seq[:, 0] * rev_mult[:, 0]
    head_cell = forget_seq[:, 0] * rev_cell[:, 0]
    coming_parts = []
    for group in range(MICRO):
        lower_row = group * group_size
        upper_row = lower_row + group_size
        _, coming = entering(
            (head_mult[lower_row:upper_row], head_cell[lower_row:upper_row]),
            "tm",
            affine_join,
            (state_ones, state_zeros),
            True,
        )
        coming_parts.append(coming)
    coming_all = jnp.concatenate(coming_parts, axis=0)
    cell_grad = rev_cell + rev_mult * coming_all[:, None, :]
    cell_prev = jnp.concatenate([cell_in[:, None, :], cell_seq[:, :-1]], axis=1)
    forget_grad = (cell_grad * cell_prev).reshape(count_of_rows, model_width)
    _, gate_pull = jax.vjp(lambda pre_value: lstm_gates(pre_value, keep_mask), lstm_pre)
    (lstm_pre_grad,) = gate_pull(
        (forget_grad, cell_grad.reshape(count_of_rows, model_width), out_gate_grad)
    )
    lstm_low = narrow_convert(lstm_pre_grad)
    grad_lstm = flipped_dot(input_rows, lstm_low)
    input_grad = sum_one_grad + dot_against_flipped(lstm_low, mat_lstm)
    grad_table = jnp.concatenate(
        [
            jnp.sum(lstm_pre_grad, axis=0).reshape(4, model_width).T,
            jnp.sum(glu_one_grad, axis=0).reshape(2, model_width).T,
            gain_one_grad[:, None],
            offset_one_grad[:, None],
            jnp.sum(glu_two_grad, axis=0).reshape(2, model_width).T,
            gain_two_grad[:, None],
            offset_two_grad[:, None],
            jnp.sum(inner_pre_grad, axis=0)[:, None],
            jnp.sum(middle_grad, axis=0)[:, None],
            jnp.sum(glu_three_grad, axis=0).reshape(2, model_width).T,
            gain_three_grad[:, None],
            offset_three_grad[:, None],
        ],
        axis=1,
    )
    (
        whole_lstm,
        whole_glu_one,
        whole_qkv,
        whole_attn,
        whole_glu_two,
        whole_inner,
        whole_middle,
        whole_glu_three,
        whole_quant,
        whole_table,
    ) = lax.psum(
        (
            grad_lstm,
            grad_glu_one,
            grad_qkv,
            grad_attn,
            grad_glu_two,
            grad_inner,
            grad_middle,
            grad_glu_three,
            level_slope,
            grad_table,
        ),
        "tm",
    )
    summed = (
        lax.psum_scatter(
            whole_lstm.astype(jnp.bfloat16), "dp", scatter_dimension=0, tiled=True
        ).astype(jnp.float32),
        lax.psum_scatter(
            whole_glu_one.astype(jnp.bfloat16), "dp", scatter_dimension=0, tiled=True
        ).astype(jnp.float32),
        lax.psum_scatter(
            whole_qkv.astype(jnp.bfloat16), "dp", scatter_dimension=0, tiled=True
        ).astype(jnp.float32),
        lax.psum_scatter(
            whole_attn.astype(jnp.bfloat16), "dp", scatter_dimension=0, tiled=True
        ).astype(jnp.float32),
        lax.psum_scatter(
            whole_glu_two.astype(jnp.bfloat16), "dp", scatter_dimension=0, tiled=True
        ).astype(jnp.float32),
        lax.psum_scatter(
            whole_inner.astype(jnp.bfloat16), "dp", scatter_dimension=0, tiled=True
        ).astype(jnp.float32),
        lax.psum_scatter(
            whole_middle.astype(jnp.bfloat16), "dp", scatter_dimension=0, tiled=True
        ).astype(jnp.float32),
        lax.psum_scatter(
            whole_glu_three.astype(jnp.bfloat16), "dp", scatter_dimension=0, tiled=True
        ).astype(jnp.float32),
        lax.psum_scatter(
            whole_quant.astype(jnp.bfloat16), "dp", scatter_dimension=0, tiled=True
        ).astype(jnp.float32),
        lax.psum_scatter(
            whole_table.astype(jnp.bfloat16), "dp", scatter_dimension=0, tiled=True
        ).astype(jnp.float32),
    )
    final_out = second_block_emit.astype(jnp.bfloat16).reshape(
        series_per_device, steps_per_device, model_width
    )
    input_out = input_grad.astype(jnp.bfloat16).reshape(
        series_per_device, steps_per_device, model_width
    )
    return (
        final_out,
        predicted_levels,
        input_out,
        summed[0],
        summed[1],
        summed[2],
        summed[3],
        summed[4],
        summed[5],
        summed[6],
        summed[7],
        summed[8],
        summed[9],
    )


def lane_head(shape, head_width, head):
    lane = lax.broadcasted_iota(jnp.int32, shape, len(shape) - 1)
    return (lane >= head * head_width) & (lane < (head + 1) * head_width)


FORGET, ENTER, CANDIDATE, EXIT = 0, 256, 512, 768
GLU_ONE_A, GLU_ONE_B = 1024, 1280
QUERY, KEY, VALUE = 1536, 1792, 2048
GLU_TWO_A, GLU_TWO_B = 2176, 2432
INNER, MIDDLE = 2688, 2944
GLU_THREE_A, GLU_THREE_B = 3200, 3456
ATTN_OUT = 3712
PACKED = 3968
VECTORS = 24
LANES = 128
CHUNKS = 8
TILE = 256


def nn(left, right):
    return jnp.dot(left, right, preferred_element_type=jnp.float32)


def nt(left, right):
    return lax.dot_general(
        left, right, (((1,), (1,)), ((), ())), preferred_element_type=jnp.float32
    )


def tn(left, right):
    return lax.dot_general(
        left, right, (((0,), (0,)), ((), ())), preferred_element_type=jnp.float32
    )


def low(values):
    return values.astype(jnp.bfloat16)


def sigmoid(values):
    return 0.5 * jnp.tanh(0.5 * values) + 0.5


def normalise(values, gain, shift):
    centred = values - jnp.mean(values, axis=-1, keepdims=True)
    spread = jnp.mean(centred * centred, axis=-1, keepdims=True)
    inverse = lax.rsqrt(spread + EPSILON)
    unit = centred * inverse
    return unit * gain + shift, unit, inverse


def normalise_back(grad, unit, inverse, gain):
    scaled = grad * gain
    return inverse * (
        scaled
        - jnp.mean(scaled, axis=-1, keepdims=True)
        - unit * jnp.mean(scaled * unit, axis=-1, keepdims=True)
    )


def rows_of(tile, size):
    return pl.ds(pl.multiple_of(tile * size, size), size)


def put_halves(ref, rows, values):
    ref[0, rows, :] = values[:, :LANES]
    ref[1, rows, : values.shape[1] - LANES] = values[:, LANES:]


def get_halves(ref, rows, width):
    return jnp.concatenate([ref[0, rows, :], ref[1, rows, : width - LANES]], axis=1)


def row_sum(ref, column, values):
    ref[column : column + 1, :] = jnp.sum(values, axis=0, keepdims=True)


def series_scratch(span, width, head_width):
    full = pltpu.VMEM((span, width), jnp.float32)
    half = pltpu.VMEM((span, width), jnp.bfloat16)
    flat = pltpu.VMEM((width, span), jnp.bfloat16)
    scan = pltpu.VMEM((2, span, LANES), jnp.float32)
    scan_more = pltpu.VMEM((2, span + 8, LANES), jnp.float32)
    narrow = pltpu.VMEM((span, head_width), jnp.bfloat16)
    column = pltpu.VMEM((span, 1), jnp.float32)
    tiles = span // TILE
    return dict(
        forget=scan_more,
        local=scan,
        mult=scan,
        cell=scan_more,
        carry=pltpu.VMEM((2, CHUNKS, LANES), jnp.float32),
        enter_gate=full,
        candidate=full,
        exit_gate=full,
        cell_tanh=full,
        hidden=half,
        glu_one=full,
        gate_one=full,
        unit_one=full,
        inverse_one=column,
        first_low=half,
        keys=half,
        values=narrow,
        head_queries=pltpu.VMEM((HEADS, span, width), jnp.bfloat16),
        head_keys=pltpu.VMEM((HEADS, span, width), jnp.bfloat16),
        **{
            "chances%d" % tile: pltpu.VMEM((HEADS, TILE, (tile + 1) * TILE), jnp.float32)
            for tile in range(tiles)
        },
        chance_sum=pltpu.VMEM((span, span), jnp.bfloat16),
        **{
            "score_grads%d" % tile: pltpu.VMEM((HEADS, span - tile * TILE, TILE), jnp.bfloat16)
            for tile in range(tiles)
        },
        block=pltpu.VMEM((TILE, span), jnp.float32),
        mixed=narrow,
        mixed_grad=narrow,
        sum_two_grad=full,
        query_grad=half,
        key_grad=half,
        value_grad=narrow,
        gate_grads=pltpu.VMEM((4, span, width), jnp.bfloat16),
        x=half,
        x_flat=flat,
        adjoint=flat,
        out=flat,
        input_grad=flat,
        w=pltpu.VMEM((width, PACKED), jnp.bfloat16),
        vec=pltpu.VMEM((VECTORS, width), jnp.float32),
        level=pltpu.VMEM((8, width), jnp.bfloat16),
        gv=pltpu.VMEM((VECTORS + 8, width), jnp.float32),
        slope=pltpu.VMEM((8, LANES), jnp.float32),
        predicted=pltpu.VMEM((8, LANES), jnp.float32),
        attn_flat=pltpu.VMEM((width, 2 * width // 5), jnp.float32),
        lstm_flat=pltpu.VMEM((width, 4 * LANES), jnp.float32),
        middle_send=pltpu.VMEM((2, width, GROUP_LANES["middle"]), jnp.bfloat16),
        first_send=pltpu.VMEM((2, width, GROUP_LANES["first"]), jnp.bfloat16),
        lstm_send=pltpu.VMEM((2, width, GROUP_LANES["lstm"]), jnp.bfloat16),
    )


def series_turn(r, chunk, steps):
    rows = rows_of(chunk, steps)
    r.x[rows, :] = r.x_flat[:, rows].T


def series_gates(r, begin):
    w, vec = r.w, r.vec
    span, width = r.x.shape
    rows = slice(0, span)
    x = r.x[...]

    def pre(block, column):
        return nn(x, w[:, block : block + width]) + vec[column : column + 1, :]

    time = lax.broadcasted_iota(jnp.int32, (span, width), 0)
    put_halves(r.forget, rows, jnp.where(time != begin, sigmoid(pre(FORGET, 0)), 0.0))
    enter = sigmoid(pre(ENTER, 1))
    candidate = jnp.tanh(pre(CANDIDATE, 2))
    r.enter_gate[...] = enter
    r.candidate[...] = candidate
    put_halves(r.local, rows, enter * candidate)
    r.exit_gate[...] = sigmoid(pre(EXIT, 3))


def series_forward_scan(r):
    span = r.x.shape[0]
    steps = span // CHUNKS
    zeros = jnp.zeros((CHUNKS, LANES), jnp.float32)

    def step(t, state):
        out = []
        at = pl.ds(t, CHUNKS, stride=steps)
        for half in range(2):
            cell, mult = state[half]
            forget = r.forget[half, at, :]
            cell = forget * cell + r.local[half, at, :]
            mult = mult * forget
            r.local[half, at, :] = cell
            r.mult[half, at, :] = mult
            out.append((cell, mult))
        return tuple(out)

    ends = lax.fori_loop(0, steps, step, ((zeros, zeros + 1.0),) * 2, unroll=8)
    for half in range(2):
        cells, mults = ends[half]
        state = jnp.zeros((1, LANES), jnp.float32)
        r.carry[half, 0:1, :] = state
        for chunk in range(CHUNKS - 1):
            state = cells[chunk : chunk + 1] + mults[chunk : chunk + 1] * state
            r.carry[half, chunk + 1 : chunk + 2, :] = state
        r.cell[half, 0:8, :] = zeros


def series_forward_first(r):
    w, vec = r.w, r.vec
    span, width = r.x.shape
    head_width = width // HEADS
    steps = span // CHUNKS
    for chunk in range(CHUNKS):
        rows = slice(chunk * steps, (chunk + 1) * steps)
        later = slice(chunk * steps + 8, (chunk + 1) * steps + 8)
        for half in range(2):
            r.cell[half, later, :] = (
                r.local[half, rows, :]
                + r.mult[half, rows, :] * r.carry[half, chunk : chunk + 1, :]
            )
    tanh = jnp.tanh(get_halves(r.cell, slice(8, 8 + span), width))
    r.cell_tanh[...] = tanh
    hidden = low(r.exit_gate[...] * tanh)
    r.hidden[...] = hidden
    value = nn(hidden, w[:, GLU_ONE_A : GLU_ONE_A + width]) + vec[4:5, :]
    gate = sigmoid(nn(hidden, w[:, GLU_ONE_B : GLU_ONE_B + width]) + vec[5:6, :])
    r.glu_one[...] = value
    r.gate_one[...] = gate
    out, unit, inverse = normalise(
        r.x[...].astype(jnp.float32) + value * gate, vec[6:7, :], vec[7:8, :]
    )
    r.unit_one[...] = unit
    r.inverse_one[...] = inverse
    out = low(out)
    r.first_low[...] = out
    query = low(nn(out, w[:, QUERY : QUERY + width]))
    key = low(nn(out, w[:, KEY : KEY + width]))
    r.keys[...] = key
    r.values[...] = low(nn(out, w[:, VALUE : VALUE + head_width]))
    for head in range(HEADS):
        mine = lane_head((span, width), head_width, head)
        r.head_queries[head] = jnp.where(mine, query, jnp.zeros_like(query))
        r.head_keys[head] = jnp.where(mine, key, jnp.zeros_like(key))


def series_forward_attention(r, begin):
    span, head_width = r.values.shape
    scale = head_width ** (-0.5) * LOG2_E
    for tile in range(span // TILE):
        rows = slice(tile * TILE, (tile + 1) * TILE)
        seen = (tile + 1) * TILE
        row = tile * TILE + lax.broadcasted_iota(jnp.int32, (TILE, seen), 0)
        col = lax.broadcasted_iota(jnp.int32, (TILE, seen), 1)
        chances = getattr(r, "chances%d" % tile)
        r.block[:, :seen] = jnp.where(
            (col <= row) & (col >= jnp.minimum(begin, row)), 0.0, NEG_BIG
        )
        for head in range(HEADS):
            scores = (
                nt(r.head_queries[head, rows, :], r.keys[:seen, :]) * scale + r.block[:, :seen]
            )
            top = jnp.max(scores, axis=-1, keepdims=True)
            raised = jnp.exp2(scores - top)
            total = jnp.sum(raised, axis=-1, keepdims=True)
            chances[head] = raised * (1.0 / total)
        weights = chances[0]
        for head in range(1, HEADS):
            weights = weights + chances[head]
        weights = low(weights)
        r.chance_sum[rows, :seen] = weights
        r.mixed[rows, :] = low(nn(weights, r.values[:seen, :]) * (1.0 / HEADS))


def series_middle(r, horizon, after_forward):
    w, vec, gv = r.w, r.vec, r.gv
    span, width = r.x.shape
    head_width = width // HEADS
    first = r.unit_one[...] * vec[6:7, :] + vec[7:8, :]
    mixed = r.mixed[...]
    attn = low(nn(mixed, w[:head_width, ATTN_OUT : ATTN_OUT + width]))
    value_two = nn(attn, w[:, GLU_TWO_A : GLU_TWO_A + width]) + vec[8:9, :]
    gate_two = sigmoid(nn(attn, w[:, GLU_TWO_B : GLU_TWO_B + width]) + vec[9:10, :])
    second, unit_two, inverse_two = normalise(
        first + value_two * gate_two, vec[10:11, :], vec[11:12, :]
    )
    second_low = low(second)
    inner_pre = nn(second_low, w[:, INNER : INNER + width]) + vec[12:13, :]
    inner_exp = jnp.exp(jnp.minimum(inner_pre, 0.0))
    inner_low = low(jnp.where(inner_pre > 0, inner_pre, inner_exp - 1.0))
    middle_low = low(nn(inner_low, w[:, MIDDLE : MIDDLE + width]) + vec[13:14, :])
    value_three = nn(middle_low, w[:, GLU_THREE_A : GLU_THREE_A + width]) + vec[14:15, :]
    gate_three = sigmoid(nn(middle_low, w[:, GLU_THREE_B : GLU_THREE_B + width]) + vec[15:16, :])
    final, unit_three, inverse_three = normalise(
        second + value_three * gate_three, vec[16:17, :], vec[17:18, :]
    )
    final_low = low(final)
    r.out[...] = final_low.T
    steps = r.slope.shape[1]
    time = span - steps + lax.broadcasted_iota(jnp.int32, (8, steps), 1)
    ahead = jnp.where((time >= span - DEC) & (time < span - DEC + horizon), 1.0, 0.0)
    r.predicted[...] = nt(r.level[...], final_low[span - steps :]) * ahead
    after_forward()
    slope = low(r.slope[...] * ahead)
    gv[VECTORS : VECTORS + 8, :] = nn(slope, final_low[span - steps :])
    grad = r.adjoint[...].T.astype(jnp.float32)
    grad = jnp.concatenate(
        [grad[: span - steps], grad[span - steps :] + tn(slope, r.level[...])], axis=0
    )
    row_sum(gv, 16, grad * unit_three)
    row_sum(gv, 17, grad)
    sum_three = normalise_back(grad, unit_three, inverse_three, vec[16:17, :])
    grad_a = sum_three * gate_three
    grad_b = grad_a * value_three * (1.0 - gate_three)
    row_sum(gv, 14, grad_a)
    row_sum(gv, 15, grad_b)
    low_a, low_b = low(grad_a), low(grad_b)
    send = r.middle_send
    send[1, :, :width] = low(tn(middle_low, low_a))
    send[1, :, width : 2 * width] = low(tn(middle_low, low_b))
    middle_grad = nt(low_a, w[:, GLU_THREE_A : GLU_THREE_A + width]) + nt(
        low_b, w[:, GLU_THREE_B : GLU_THREE_B + width]
    )
    row_sum(gv, 13, middle_grad)
    middle_grad = low(middle_grad)
    send[1, :, 2 * width : 3 * width] = low(tn(inner_low, middle_grad))
    inner_grad = nt(middle_grad, w[:, MIDDLE : MIDDLE + width]) * jnp.where(
        inner_pre > 0, 1.0, inner_exp
    )
    row_sum(gv, 12, inner_grad)
    inner_grad = low(inner_grad)
    send[0, :, 2 * width : 3 * width] = low(tn(second_low, inner_grad))
    grad = sum_three + nt(inner_grad, w[:, INNER : INNER + width])
    row_sum(gv, 10, grad * unit_two)
    row_sum(gv, 11, grad)
    sum_two = normalise_back(grad, unit_two, inverse_two, vec[10:11, :])
    r.sum_two_grad[...] = sum_two
    grad_a = sum_two * gate_two
    grad_b = grad_a * value_two * (1.0 - gate_two)
    row_sum(gv, 8, grad_a)
    row_sum(gv, 9, grad_b)
    low_a, low_b = low(grad_a), low(grad_b)
    attn_grad = low(
        nt(low_a, w[:, GLU_TWO_A : GLU_TWO_A + width])
        + nt(low_b, w[:, GLU_TWO_B : GLU_TWO_B + width])
    )
    r.mixed_grad[...] = low(nt(attn_grad, w[:head_width, ATTN_OUT : ATTN_OUT + width]))
    send[0, :, :width] = low(tn(attn, low_a))
    send[0, :, width : 2 * width] = low(tn(attn, low_b))
    attn_weight = tn(mixed, attn_grad)
    rows, small = head_width, head_width // HEADS
    spare = width // 5
    r.attn_flat[...] = jnp.zeros_like(r.attn_flat)
    for group in range(HEADS):
        for piece in range(5):
            at = group * rows + small * (piece % 4)
            half = piece // 4
            r.attn_flat[at : at + small, half * spare : (half + 1) * spare] = attn_weight[
                group * small : (group + 1) * small, piece * spare : (piece + 1) * spare
            ]
    for half in range(2):
        send[half, :, 3 * width :] = low(r.attn_flat[:, half * spare : (half + 1) * spare])


def series_backward_attention(r, between):
    span, head_width = r.values.shape
    width = head_width * HEADS
    scale = head_width ** (-0.5)
    for tile in range(span // TILE):
        rows = slice(tile * TILE, (tile + 1) * TILE)
        seen = (tile + 1) * TILE
        held = getattr(r, "chances%d" % tile)
        head_grad = r.mixed_grad[rows, :] * (1.0 / HEADS)
        r.block[:, :seen] = nt(head_grad, r.values[:seen, :]) * scale
        total = jnp.zeros((TILE, width), jnp.float32)
        for head in range(HEADS):
            chances = held[head]
            slope = r.block[:, :seen]
            delta = jnp.sum(chances * slope, axis=-1, keepdims=True)
            grads = low(chances * (slope - delta))
            for part in range(tile + 1):
                getattr(r, "score_grads%d" % part)[
                    head, (tile - part) * TILE : (tile - part + 1) * TILE, :
                ] = grads[:, part * TILE : (part + 1) * TILE]
            total = total + nn(grads, r.head_keys[head, :seen, :])
        r.query_grad[rows, :] = low(total)
        between(tile)
    for tile in range(span // TILE):
        cols = slice(tile * TILE, (tile + 1) * TILE)
        start = tile * TILE
        total = jnp.zeros((TILE, width), jnp.float32)
        for head in range(HEADS):
            total = total + tn(
                getattr(r, "score_grads%d" % tile)[head], r.head_queries[head, start:, :]
            )
        r.key_grad[cols, :] = low(total)
        r.value_grad[cols, :] = low(
            tn(r.chance_sum[start:, cols], r.mixed_grad[start:, :] * (1.0 / HEADS))
        )


def series_backward_first(r):
    w, vec, gv = r.w, r.vec, r.gv
    span, width = r.hidden.shape
    head_width = width // HEADS
    rows = slice(0, span)
    send = r.first_send
    query, key, value = r.query_grad[...], r.key_grad[...], r.value_grad[...]
    grad = (
        r.sum_two_grad[...]
        + nt(query, w[:, QUERY : QUERY + width])
        + nt(key, w[:, KEY : KEY + width])
        + nt(value, w[:, VALUE : VALUE + head_width])
    )
    first = r.first_low[...]
    send[1, :, :width] = low(tn(first, query))
    send[1, :, width : 2 * width] = low(tn(first, key))
    send[1, :, 2 * width : 2 * width + head_width] = low(tn(first, value))
    unit = r.unit_one[...]
    row_sum(gv, 6, grad * unit)
    row_sum(gv, 7, grad)
    sum_one = normalise_back(grad, unit, r.inverse_one[...], vec[6:7, :])
    r.sum_two_grad[...] = sum_one
    gate = r.gate_one[...]
    grad_a = sum_one * gate
    grad_b = grad_a * r.glu_one[...] * (1.0 - gate)
    row_sum(gv, 4, grad_a)
    row_sum(gv, 5, grad_b)
    low_a, low_b = low(grad_a), low(grad_b)
    hidden_grad = nt(low_a, w[:, GLU_ONE_A : GLU_ONE_A + width]) + nt(
        low_b, w[:, GLU_ONE_B : GLU_ONE_B + width]
    )
    tanh, gate = r.cell_tanh[...], r.exit_gate[...]
    put_halves(r.local, rows, hidden_grad * gate * (1.0 - tanh * tanh))
    exit_grad = hidden_grad * tanh * gate * (1.0 - gate)
    row_sum(gv, 3, exit_grad)
    exit_grad = low(exit_grad)
    r.gate_grads[3] = exit_grad
    hidden = r.hidden[...]
    send[0, :, :width] = low(tn(hidden, low_a))
    send[0, :, width : 2 * width] = low(tn(hidden, low_b))
    send[0, :, 2 * width : 3 * width] = low(nn(r.x_flat[...], exit_grad))


def series_backward_scan(r, between):
    span = r.x.shape[0]
    steps = span // CHUNKS
    zeros = jnp.zeros((CHUNKS, LANES), jnp.float32)
    for half in range(2):
        r.forget[half, span:, :] = zeros

    def step(count, state):
        t = steps - 1 - count
        out = []
        at, after = pl.ds(t, CHUNKS, stride=steps), pl.ds(t + 1, CHUNKS, stride=steps)
        for half in range(2):
            grad, mult = state[half]
            forget = r.forget[half, after, :]
            grad = forget * grad + r.local[half, at, :]
            mult = mult * forget
            r.local[half, at, :] = grad
            r.mult[half, at, :] = mult
            out.append((grad, mult))
        return tuple(out)

    ends = lax.fori_loop(0, steps // 2, step, ((zeros, zeros + 1.0),) * 2, unroll=8)
    between()
    ends = lax.fori_loop(steps // 2, steps, step, ends, unroll=8)
    for half in range(2):
        grads, mults = ends[half]
        state = jnp.zeros((1, LANES), jnp.float32)
        r.carry[half, CHUNKS - 1 : CHUNKS, :] = state
        for chunk in range(CHUNKS - 1, 0, -1):
            state = grads[chunk : chunk + 1] + mults[chunk : chunk + 1] * state
            r.carry[half, chunk - 1 : chunk, :] = state


def series_gate_grads(r):
    gv = r.gv
    span, width = r.x.shape
    steps = span // CHUNKS
    for half in range(2):
        for chunk in range(CHUNKS):
            rows = slice(chunk * steps, (chunk + 1) * steps)
            r.local[half, rows, :] += r.mult[half, rows, :] * r.carry[half, chunk : chunk + 1, :]
    grad = get_halves(r.local, slice(0, span), width)
    forget = get_halves(r.forget, slice(0, span), width)
    before = get_halves(r.cell, slice(7, 7 + span), width)
    enter, candidate = r.enter_gate[...], r.candidate[...]
    for gate, one in enumerate(
        (
            grad * before * forget * (1.0 - forget),
            grad * candidate * enter * (1.0 - enter),
            grad * enter * (1.0 - candidate * candidate),
        )
    ):
        row_sum(gv, gate, one)
        one = low(one)
        r.gate_grads[gate] = one
        r.lstm_flat[:, gate * width : (gate + 1) * width] = nn(r.x_flat[...], one)
    r.lstm_flat[:, 3 * width :] = gv[...].T
    lanes = r.lstm_send.shape[2]
    for half in range(2):
        r.lstm_send[half] = low(r.lstm_flat[:, half * lanes : (half + 1) * lanes])


def series_input_grad(r):
    width = r.x.shape[1]
    out = r.sum_two_grad[...].T
    for gate, block in enumerate((FORGET, ENTER, CANDIDATE, EXIT)):
        out = out + nt(r.w[:, block : block + width], r.gate_grads[gate])
    r.input_grad[...] = low(out)


class Exchange:
    def __init__(self, sems, devices, source, target):
        self.sems, self.source, self.target = sems, source, target
        self.count, self.me, self.device = devices

    def other(self, step):
        return lax.rem(self.me + step, self.count)

    def copy(self, to, origin):
        return pltpu.make_async_remote_copy(
            src_ref=self.source(to),
            dst_ref=self.target(origin),
            send_sem=self.sems.at[0, to],
            recv_sem=self.sems.at[1, origin],
            device_id=self.device(to),
            device_id_type=pl.DeviceIdType.MESH,
        )

    def send(self, to):
        self.copy(to, self.me).start()

    def arrive(self, origin):
        self.copy(origin, origin).wait_recv()

    def start(self):
        for step in range(1, self.count):
            self.send(self.other(step))

    def arrive_all(self):
        for step in range(1, self.count):
            self.arrive(self.other(step))

    def sent(self):
        for step in range(1, self.count):
            self.copy(self.other(step), self.me).wait_send()


def over_time():
    return lax.axis_size("tm"), lax.axis_index("tm"), lambda to: {"tm": to}


def over_series():
    return lax.axis_size("dp"), lax.axis_index("dp"), lambda to: {"dp": to}


def over_chips():
    core = my_core()
    return (
        lax.axis_size("tm") // 2,
        lax.div(lax.axis_index("tm"), 2),
        lambda to: {"tm": 2 * to + core},
    )


def my_core():
    return lax.rem(lax.axis_index("tm"), 2)


def to_other_core(source, target, sems, index):
    return pltpu.make_async_remote_copy(
        src_ref=source,
        dst_ref=target,
        send_sem=sems.at[0, index],
        recv_sem=sems.at[1, index],
        device_id={"tm": lax.axis_index("tm") + 1 - 2 * my_core()},
        device_id_type=pl.DeviceIdType.MESH,
    )


GROUP_COLUMNS = (384, 384, 640)
GROUP_LANES = {"middle": 512, "first": 512, "lstm": 256}
DIRECT = ("lstm",)


def fold(values):
    lanes = values.shape[1] // 2
    return low(jnp.concatenate([values[:, :lanes], values[:, lanes:]], axis=0))


def unfold(values):
    rows = values.shape[0] // 2
    return jnp.concatenate([values[:rows], values[rows:]], axis=1)


def travel_scratch(count, groups, steps, width, params):
    rows = params[0].shape[0]
    out = dict(
        slopes=pltpu.VMEM((count, 8, steps), jnp.float32),
        levels=pltpu.VMEM((count, 8, steps), jnp.float32),
        stage=pltpu.VMEM((width, 2 * GROUP_COLUMNS[2]), jnp.float32),
        attn_stage=pltpu.VMEM((width, width), jnp.float32),
        table_stage=pltpu.VMEM((rows, LANES), jnp.float32),
        pack_stage=pltpu.VMEM((rows, GROUP_COLUMNS[2]), jnp.float32),
    )
    for index, param in enumerate(params):
        out["param%d" % index] = pltpu.VMEM(param.shape, jnp.float32)
    out["load_sems"] = pltpu.SemaphoreType.DMA((len(params),))
    for group, columns in enumerate(GROUP_COLUMNS):
        slab = -(-rows * columns // LANES // 16) * 16
        out["params%d" % group] = pltpu.VMEM((2, groups, slab, LANES), jnp.bfloat16)
        out["params%d_dp" % group] = pltpu.SemaphoreType.DMA((2, groups))
        out["params%d_core" % group] = pltpu.SemaphoreType.DMA((2, groups))
    for name, lanes in GROUP_LANES.items():
        out[name + "_near"] = pltpu.VMEM((width, lanes), jnp.bfloat16)
        folded = (2 * rows, lanes // 2)
        out[name + "_part"] = pltpu.VMEM((groups,) + folded, jnp.bfloat16)
        out[name + "_parts"] = pltpu.VMEM((groups,) + folded, jnp.bfloat16)
        places = count if name in DIRECT else count // 2
        out[name + "_chips"] = pltpu.VMEM((places,) + folded, jnp.bfloat16)
        out[name + "_core_sems"] = pltpu.SemaphoreType.DMA((2, 2))
        out[name + "_dp_sems"] = pltpu.SemaphoreType.DMA((2, groups))
        out[name + "_chip_sems"] = pltpu.SemaphoreType.DMA((2, places))
    for name in ("x", "adjoint", "out", "input", "slope", "predicted"):
        out[name + "_sems"] = pltpu.SemaphoreType.DMA((2, count))
    out["own_sems"] = pltpu.SemaphoreType.DMA((4,))
    return out


class Parameters:
    def __init__(self, r, group):
        self.buffer = buffer = getattr(r, "params%d" % group)
        self.core = core = my_core()
        self.over = Exchange(
            getattr(r, "params%d_dp" % group),
            over_series(),
            lambda to: buffer.at[core, lax.axis_index("dp")],
            lambda origin: buffer.at[core, origin],
        )
        self.sems = getattr(r, "params%d_core" % group)

    def hand(self, origin, core):
        block = self.buffer.at[core, origin]
        return to_other_core(block, block, self.sems, origin)

    def pass_on(self):
        for step in range(1, self.over.count):
            origin = self.over.other(step)
            self.over.arrive(origin)
            self.hand(origin, self.core).start()

    def arrive(self):
        for step in range(1, self.over.count):
            self.hand(self.over.other(step), 1 - self.core).wait_recv()

    def sent(self):
        self.over.sent()
        for step in range(1, self.over.count):
            self.hand(self.over.other(step), self.core).wait_send()


class Reduction:
    def __init__(self, r, name, final):
        self.send, self.near = getattr(r, name + "_send"), getattr(r, name + "_near")
        self.part, self.parts = getattr(r, name + "_part"), getattr(r, name + "_parts")
        self.chips, self.final = getattr(r, name + "_chips"), final
        self.core, self.rows = my_core(), final.shape[1]
        self.core_sems = getattr(r, name + "_core_sems")
        part, parts, chips = self.part, self.parts, self.chips
        self.to_series = Exchange(
            getattr(r, name + "_dp_sems"),
            over_series(),
            lambda to: part.at[to],
            lambda origin: parts.at[origin],
        )
        self.direct = name in DIRECT
        devices = over_time() if self.direct else over_chips()
        place = devices[1]
        self.to_chips = Exchange(
            getattr(r, name + "_chip_sems"),
            devices,
            lambda to: chips.at[place],
            lambda origin: chips.at[origin],
        )

    def out(self):
        return to_other_core(self.send.at[1 - self.core], self.near, self.core_sems, 0)

    def back(self, core):
        return to_other_core(self.final.at[core], self.final.at[core], self.core_sems, 1)

    def sum_of(self, ref, first=0, stride=1):
        total = ref[first].astype(jnp.float32)
        for index in range(first + stride, ref.shape[0], stride):
            total = total + ref[index].astype(jnp.float32)
        return total

    def start(self):
        self.out().start()

    def across_series(self):
        self.out().wait_recv()
        total = self.send[self.core].astype(jnp.float32) + self.near[...].astype(jnp.float32)
        for group in range(self.to_series.count):
            self.part[group] = fold(total[group * self.rows : (group + 1) * self.rows])
        self.to_series.start()

    def across_chips(self):
        self.to_series.arrive_all()
        self.parts[self.to_series.me] = self.part[self.to_series.me]
        self.chips[self.to_chips.me] = low(self.sum_of(self.parts))
        self.to_chips.start()

    def to_both(self):
        self.to_chips.arrive_all()
        if self.direct:
            for core in range(2):
                self.final[core] = unfold(self.sum_of(self.chips, core, 2))
        else:
            self.final[self.core] = unfold(self.sum_of(self.chips))
            self.back(self.core).start()

    def finish(self):
        if not self.direct:
            self.back(1 - self.core).wait_recv()
            self.back(self.core).wait_send()
        self.out().wait_send()
        self.to_series.sent()
        self.to_chips.sent()


def greet():
    barrier = pltpu.get_barrier_semaphore()
    total = 0
    for count, me, device in (over_time(), over_series()):
        for step in range(1, count):
            pl.semaphore_signal(
                barrier,
                inc=1,
                device_id=device(lax.rem(me + step, count)),
                device_id_type=pl.DeviceIdType.MESH,
            )
            total += 1
    return lambda: pl.semaphore_wait(barrier, total)


def pack_params(r, group, params):
    mine = lax.axis_index("dp")
    buffer, stage = getattr(r, "params%d" % group), r.pack_stage
    columns = GROUP_COLUMNS[group]

    def put(half, *arrays):
        at = 0
        for array in arrays:
            rows, width = array.shape
            stage[:rows, at : at + width] = array[...]
            at += width
        tiles = [stage[:, tile : tile + LANES] for tile in range(0, columns, LANES)]
        spare = buffer.shape[2] - stage.shape[0] * len(tiles)
        tiles.append(jnp.zeros((spare, LANES), jnp.float32))
        buffer[half, mine] = low(jnp.concatenate(tiles, axis=0))

    if group == 0:
        lstm, table, level = params
        rows = lstm.shape[0]
        r.table_stage[...] = jnp.zeros_like(r.table_stage)
        r.table_stage[: table.shape[0], :rows] = table[...]
        r.table_stage[VECTORS : VECTORS + LEVEL_TALLY, :rows] = level[...]
        put(0, lstm[:, :columns])
        put(1, lstm[:, columns:], r.table_stage)
    elif group == 1:
        for half, array in enumerate(params):
            put(half, array)
    else:
        glu_two, glu_three, inner, middle, attn = params
        put(0, glu_two, glu_three)
        put(1, inner, middle, attn)


def unpack_params(r, group, rows, attn_rows):
    width = r.w.shape[0]
    head_width = width // HEADS
    buffer, stage = getattr(r, "params%d" % group), r.stage
    columns = GROUP_COLUMNS[group]
    for half in range(2):
        for origin in range(buffer.shape[1]):
            tiles = buffer[half, origin].astype(jnp.float32)
            for tile in range(columns // LANES):
                at = half * columns + tile * LANES
                stage[origin * rows : (origin + 1) * rows, at : at + LANES] = tiles[
                    tile * rows : (tile + 1) * rows
                ]

    def place(block, column, size):
        r.w[:, block : block + size] = low(stage[:, column : column + size])

    if group == 0:
        for gate, block in enumerate((FORGET, ENTER, CANDIDATE, EXIT)):
            place(block, gate * width, width)
        vectors = jnp.concatenate(
            [
                stage[origin * rows : origin * rows + VECTORS + 8, 4 * width : 4 * width + rows]
                for origin in range(buffer.shape[1])
            ],
            axis=1,
        )
        r.vec[...] = vectors[:VECTORS]
        r.level[...] = low(vectors[VECTORS:])
    elif group == 1:
        place(GLU_ONE_A, 0, width)
        place(GLU_ONE_B, width, width)
        place(QUERY, columns, width)
        place(KEY, columns + width, width)
        place(VALUE, columns + 2 * width, head_width)
    else:
        place(GLU_TWO_A, 0, width)
        place(GLU_TWO_B, width, width)
        place(GLU_THREE_A, 2 * width, width)
        place(GLU_THREE_B, 3 * width, width)
        place(INNER, columns, width)
        place(MIDDLE, columns + width, width)
        for origin in range(buffer.shape[1]):
            r.attn_stage[origin * attn_rows : (origin + 1) * attn_rows, :] = stage[
                origin * rows : origin * rows + attn_rows,
                columns + 2 * width : columns + 3 * width,
            ]
        r.w[:head_width, ATTN_OUT : ATTN_OUT + width] = low(r.attn_stage[:head_width, :])


def series_kernel(begins, reaches, x_hbm, adjoint_hbm, slopes, *others):
    params, others = others[:10], others[10:]
    (out_hbm, predicted_out, input_hbm, final_middle, final_first, final_lstm), scratch = (
        others[:6],
        others[6:],
    )
    count, width, steps = x_hbm.shape
    span = count * steps
    groups = lax.axis_size("dp")
    names = series_scratch(span, width, width // HEADS)
    names.update(travel_scratch(count, groups, steps, width, params))
    r = types.SimpleNamespace(**dict(zip(names, scratch)))
    me = lax.axis_index("tm")
    last = count - 1

    def block(ref, index):
        return ref.at[:, rows_of(index, steps)]

    x_over = Exchange(
        r.x_sems, over_time(), lambda to: x_hbm.at[to], lambda origin: block(r.x_flat, origin)
    )
    adjoint_over = Exchange(
        r.adjoint_sems,
        over_time(),
        lambda to: adjoint_hbm.at[to],
        lambda origin: block(r.adjoint, origin),
    )
    out_over = Exchange(
        r.out_sems, over_time(), lambda to: block(r.out, to), lambda origin: out_hbm.at[origin]
    )
    input_over = Exchange(
        r.input_sems,
        over_time(),
        lambda to: block(r.input_grad, to),
        lambda origin: input_hbm.at[origin],
    )
    slope_over = Exchange(
        r.slope_sems, over_time(), lambda to: r.slopes.at[to], lambda origin: r.slope
    )
    predicted_over = Exchange(
        r.predicted_sems, over_time(), lambda to: r.predicted, lambda origin: r.levels.at[origin]
    )
    travelling = [Parameters(r, group) for group in range(3)]
    middle_sum = Reduction(r, "middle", final_middle)
    first_sum = Reduction(r, "first", final_first)
    lstm_sum = Reduction(r, "lstm", final_lstm)
    own_x = pltpu.make_async_copy(x_hbm.at[me], block(r.x_flat, me), r.own_sems.at[0])
    own_adjoint = pltpu.make_async_copy(adjoint_hbm.at[me], block(r.adjoint, me), r.own_sems.at[1])
    own_out = pltpu.make_async_copy(block(r.out, me), out_hbm.at[me], r.own_sems.at[2])
    own_input = pltpu.make_async_copy(block(r.input_grad, me), input_hbm.at[me], r.own_sems.at[3])
    held = [getattr(r, "param%d" % index) for index in range(len(params))]
    loads = [
        pltpu.make_async_copy(param, here, r.load_sems.at[index])
        for index, (param, here) in enumerate(zip(params, held))
    ]

    def pack(group, *indices):
        for index in indices:
            loads[index].wait()
        pack_params(r, group, [held[index] for index in indices])

    everyone_here = greet()
    for load in loads:
        load.start()
    own_x.start()
    own_adjoint.start()
    pack(0, 0, 9, 8)
    everyone_here()
    travelling[0].over.start()
    x_over.start()
    pack(1, 1, 2)
    pack(2, 4, 7, 5, 6, 3)
    for track in range(count):
        r.slopes[track] = jnp.concatenate(
            [
                slopes[level_at].astype(jnp.float32)[track : track + 1]
                for level_at in range(LEVEL_TALLY)
            ]
            + [jnp.zeros((8 - LEVEL_TALLY, steps), jnp.float32)],
            axis=0,
        )
    begin = begins[me]
    choice = reaches[me]
    horizon = jnp.where(choice == 0, 1, jnp.where(choice == 1, 5, 24))
    rows, attn_rows = params[0].shape[0], params[3].shape[0]
    r.gv[...] = jnp.zeros_like(r.gv)
    own_x.wait()
    series_turn(r, me, steps)
    travelling[0].pass_on()
    travelling[1].over.start()

    def arriving(step, _):
        origin = x_over.other(step)
        x_over.arrive(origin)
        series_turn(r, origin, steps)
        return 0

    lax.fori_loop(1, count, arriving, 0)
    travelling[0].arrive()
    unpack_params(r, 0, rows, attn_rows)
    series_gates(r, begin)
    adjoint_over.start()

    @pl.when(me == last)
    def _():
        slope_over.start()
        r.slope[...] = r.slopes[last]

    series_forward_scan(r)
    travelling[1].pass_on()
    travelling[2].over.start()
    travelling[1].arrive()
    unpack_params(r, 1, rows, attn_rows)
    series_forward_first(r)
    series_forward_attention(r, begin)
    travelling[2].pass_on()
    travelling[2].arrive()
    unpack_params(r, 2, rows, attn_rows)
    own_adjoint.wait()
    adjoint_over.arrive_all()

    @pl.when(me != last)
    def _():
        slope_over.arrive(last)

    def forward_done():
        own_out.start()
        out_over.start()

        @pl.when(me != last)
        def _():
            predicted_over.send(last)

    series_middle(r, horizon, forward_done)
    middle_sum.start()

    def between(tile):
        if tile == 2:
            middle_sum.across_series()

    series_backward_attention(r, between)
    series_backward_first(r)
    first_sum.start()
    series_backward_scan(r, first_sum.across_series)
    series_gate_grads(r)
    lstm_sum.start()
    middle_sum.across_chips()
    series_input_grad(r)
    own_input.start()
    input_over.start()
    lstm_sum.across_series()
    middle_sum.to_both()
    first_sum.across_chips()

    @pl.when(me != last)
    def _():
        predicted_over.copy(last, me).wait_send()
        predicted_out[...] = jnp.zeros_like(predicted_out)

    @pl.when(me == last)
    def _():
        slope_over.sent()
        predicted_over.arrive_all()
        r.levels[last] = r.predicted[...]
        for level_at in range(LEVEL_TALLY):
            predicted_out[level_at] = jnp.concatenate(
                [r.levels[track][level_at : level_at + 1] for track in range(count)], axis=0
            )

    lstm_sum.across_chips()
    first_sum.to_both()
    x_over.sent()
    adjoint_over.sent()
    for group in travelling:
        group.sent()
    own_out.wait()
    out_over.arrive_all()
    out_over.sent()
    middle_sum.finish()
    first_sum.finish()
    lstm_sum.to_both()
    own_input.wait()
    input_over.arrive_all()
    input_over.sent()
    lstm_sum.finish()


def unpack_kernel(final_middle, final_first, final_lstm, out_in, predicted_in, input_in, *others):
    (lstm, glu_one, qkv, attn, glu_two, inner, middle, glu_three, level, table) = others[:10]
    out, predicted, input_grad = others[10:]
    predicted[...] = predicted_in[...]
    rows, width = inner.shape
    lanes = final_lstm.shape[2]
    for ref, at in ((glu_two, 0), (glu_three, 1)):
        ref[...] = final_middle[at, :, : 2 * width]
    for ref, at in ((inner, 0), (middle, 1)):
        ref[...] = final_middle[at, :, 2 * width : 3 * width]
    small, spare = attn.shape[0], width // 5
    for piece in range(5):
        at = small * (piece % 4)
        attn[:, piece * spare : (piece + 1) * spare] = final_middle[
            piece // 4, at : at + small, 3 * width : 3 * width + spare
        ]
    glu_one[...] = final_first[0, :, : 2 * width]
    qkv[...] = final_first[1, :, : qkv.shape[1]]
    lstm[:, :lanes] = final_lstm[0]
    lstm[:, lanes : 3 * width] = final_lstm[1, :, : 3 * width - lanes]
    lstm[:, 3 * width :] = final_first[0, :, 2 * width : 3 * width]
    vectors = final_lstm[1, :, 3 * width - lanes :].T
    table[...] = vectors[: table.shape[0]]
    level[...] = vectors[VECTORS : VECTORS + LEVEL_TALLY]
    out[...] = out_in[...]
    input_grad[...] = input_in[...]


def whole_series(embedded_features, earliest_seen_moment, reach_choice, *others):
    count, steps, width = embedded_features.shape
    features = embedded_features.swapaxes(1, 2)
    adjoint = others[-2].swapaxes(1, 2)
    slopes = others[-1].swapaxes(0, 1)
    params = others[:-4] + (others[-4].T, others[-3].T)
    groups = lax.axis_size("dp")
    rows = params[0].shape[0]
    names = series_scratch(count * steps, width, width // HEADS)
    names.update(travel_scratch(count, groups, steps, width, params))
    smem, vmem, anywhere = (
        pl.BlockSpec(memory_space=space) for space in (pltpu.SMEM, pltpu.VMEM, pl.ANY)
    )
    moved = ((features.shape, jnp.bfloat16), (slopes.shape, jnp.float32))
    moved += moved[:1]
    out, predicted, input_grad, *finals = pl.pallas_call(
        series_kernel,
        out_shape=tuple(pltpu.VMEM(*one) for one in moved)
        + tuple(pltpu.VMEM((2, rows, lanes), jnp.float32) for lanes in GROUP_LANES.values()),
        in_specs=[smem, smem, anywhere, anywhere, vmem] + [anywhere] * len(params),
        out_specs=(vmem,) * 6,
        scratch_shapes=list(names.values()),
        compiler_params=pltpu.CompilerParams(
            vmem_limit_bytes=VMEM_BYTES, collective_id=0, has_side_effects=True
        ),
    )(
        earliest_seen_moment,
        reach_choice,
        features,
        adjoint,
        slopes,
        *params,
    )
    *grads, level_grad, table_grad, out, predicted, input_grad = pl.pallas_call(
        unpack_kernel,
        out_shape=tuple(jax.ShapeDtypeStruct(param.shape, jnp.float32) for param in params)
        + tuple(jax.ShapeDtypeStruct(*one) for one in moved),
        in_specs=[vmem] * 6,
        out_specs=(vmem,) * (len(params) + 3),
        compiler_params=pltpu.CompilerParams(vmem_limit_bytes=VMEM_BYTES // 6),
    )(*finals, out, predicted, input_grad)
    return (
        out.swapaxes(1, 2),
        predicted.swapaxes(0, 1),
        input_grad.swapaxes(1, 2),
        *grads,
        level_grad.T,
        table_grad.T,
    )


def on_device(embedded_features, *others):
    count, steps, _ = embedded_features.shape
    one_each = count == lax.axis_size("tm") == CHUNKS and steps == LANES
    return (whole_series if one_each else shards)(embedded_features, *others)


def solution(mesh):
    placed = (
        P("dp", "tm", None),
        P("dp"),
        P("dp"),
        P("dp", None),
        P("dp", None),
        P("dp", None),
        P("dp", None),
        P("dp", None),
        P("dp", None),
        P("dp", None),
        P("dp", None),
        P("dp", None),
        P("dp", None),
        P("dp", "tm", None),
        P("dp", None, "tm"),
    )
    return jax.shard_map(
        on_device,
        mesh=mesh,
        in_specs=placed,
        out_specs=(
            P("dp", "tm", None),
            P("dp", None, "tm"),
            P("dp", "tm", None),
            P("dp", None),
            P("dp", None),
            P("dp", None),
            P("dp", None),
            P("dp", None),
            P("dp", None),
            P("dp", None),
            P("dp", None),
            P("dp", None),
            P("dp", None),
        ),
        check_vma=False,
    )
```

```python
import types

import jax
import jax.numpy as jnp
from jax import lax
from jax.experimental import pallas as pl
from jax.experimental.pallas import tpu as pltpu
from jax.sharding import PartitionSpec as P

HEADS = 4
LEVEL_TALLY = 3
DEC = 24
MICRO = 2


EPSILON = 1e-05
NEG_BIG = -1e30
attend_group = 2
LOG2_E = 1.4426950408889634
VMEM_BYTES = 60 * 2**20


def entering(value, axis, join, neutral, backward):
    count, mine = (lax.axis_size(axis), lax.axis_index(axis))
    pieces = jax.tree.map(lambda part: lax.all_gather(part, axis), value)
    if backward:
        pieces = jax.tree.map(lambda part: part[::-1], pieces)
        mine = count - 1 - mine
    so_far = jax.tree.map(
        lambda part, zero: jnp.full_like(part, 0) + jnp.asarray(zero, part.dtype), value, neutral
    )

    def turn(position, so_far):
        longer = join(so_far, jax.tree.map(lambda part: part[position], pieces))
        return jax.tree.map(lambda new, old: jnp.where(position < mine, new, old), longer, so_far)

    return lax.fori_loop(0, count - 1, turn, so_far)


def narrow_convert(values):
    return values.astype(jnp.bfloat16)


def tensor_dot_plain(left, right):
    return jnp.dot(left, right, preferred_element_type=jnp.float32)


def flipped_dot(left, right):
    return lax.dot_general(
        left, right, (((0,), (0,)), ((), ())), preferred_element_type=jnp.float32
    )


def dot_against_flipped(left, right):
    return lax.dot_general(
        left, right, (((1,), (1,)), ((), ())), preferred_element_type=jnp.float32
    )


def affine_join(earlier, later):
    return (later[0] * earlier[0], later[0] * earlier[1] + later[1])


def layer_norm(values, gains, offsets):
    centred = values - jnp.mean(values, axis=-1, keepdims=True)
    spread = jnp.mean(centred * centred, axis=-1, keepdims=True)
    return centred * lax.rsqrt(spread + EPSILON) * gains + offsets


def gated_unit(pre_act):
    half_width = pre_act.shape[-1] // 2
    return pre_act[..., :half_width] * jax.nn.sigmoid(pre_act[..., half_width:])


def lstm_gates(pre_act, keep_mask):
    quarter = pre_act.shape[-1] // 4
    forget = jax.nn.sigmoid(pre_act[..., :quarter]) * keep_mask
    inflow = jax.nn.sigmoid(pre_act[..., quarter : 2 * quarter]) * jnp.tanh(
        pre_act[..., 2 * quarter : 3 * quarter]
    )
    out_gate = jax.nn.sigmoid(pre_act[..., 3 * quarter :])
    return (forget, inflow, out_gate)


def masked_scores(query_block, key_block, query_pos, key_pos, begin_block, scale):
    raw = jnp.einsum("gqhd,gkhd->ghqk", query_block, key_block, preferred_element_type=jnp.float32)
    lowest = jnp.minimum(begin_block[:, None], query_pos[None, :])
    allowed = (key_pos[None, None, :] <= query_pos[None, :, None]) & (
        key_pos[None, None, :] >= lowest[:, :, None]
    )
    return jnp.where(allowed[:, None], raw * scale, NEG_BIG)


def score_grad(chances, dprob, row_delta, scale):
    return narrow_convert(chances * (dprob[:, None] - row_delta[..., None]) * scale)


def shards(
    embedded_features,
    earliest_seen_moment,
    reach_choice,
    lstm_valve_coeffs,
    lstm_unit_coeffs,
    asker_lookup_coeffs,
    attend_exit_coeffs,
    attend_unit_coeffs,
    skipnet_entry_coeffs,
    skipnet_inner_coeffs,
    skipnet_unit_coeffs,
    level_map_coeffs,
    bias_gain_table,
    block_emit_adjoint,
    predicted_adjoint,
):
    (
        mat_lstm,
        mat_glu_one,
        mat_qkv,
        mat_attn,
        mat_glu_two,
        mat_inner,
        mat_middle,
        mat_glu_three,
        level_dot,
        vec_table,
    ) = (
        lax.all_gather(narrow_convert(lstm_valve_coeffs), "dp", axis=0, tiled=True),
        lax.all_gather(narrow_convert(lstm_unit_coeffs), "dp", axis=0, tiled=True),
        lax.all_gather(narrow_convert(asker_lookup_coeffs), "dp", axis=0, tiled=True),
        lax.all_gather(narrow_convert(attend_exit_coeffs), "dp", axis=0, tiled=True),
        lax.all_gather(narrow_convert(attend_unit_coeffs), "dp", axis=0, tiled=True),
        lax.all_gather(narrow_convert(skipnet_entry_coeffs), "dp", axis=0, tiled=True),
        lax.all_gather(narrow_convert(skipnet_inner_coeffs), "dp", axis=0, tiled=True),
        lax.all_gather(narrow_convert(skipnet_unit_coeffs), "dp", axis=0, tiled=True),
        lax.all_gather(narrow_convert(level_map_coeffs), "dp", axis=0, tiled=True),
        lax.all_gather(narrow_convert(bias_gain_table), "dp", axis=0, tiled=True),
    )
    series_per_device, steps_per_device, model_width = embedded_features.shape
    seq_total = steps_per_device * lax.axis_size("tm")
    head_width = model_width // HEADS
    count_of_rows = series_per_device * steps_per_device
    scale = head_width ** (-0.5)
    vec_full = vec_table.astype(jnp.float32)
    time_local = lax.axis_index("tm") * steps_per_device + jnp.arange(
        steps_per_device, dtype=jnp.int32
    )
    time_all = jnp.arange(seq_total, dtype=jnp.int32)
    horizon_len = jnp.where(reach_choice == 0, 1, jnp.where(reach_choice == 1, 5, 24))
    ahead_moment_filter = (
        (
            (time_local[None, :] >= seq_total - DEC)
            & (time_local[None, :] < seq_total - DEC + horizon_len[:, None])
        )
        .astype(jnp.float32)
        .reshape(count_of_rows, 1)
    )
    keep_mask = (
        (time_local[None, :] != earliest_seen_moment[:, None])
        .astype(jnp.float32)
        .reshape(count_of_rows, 1)
    )
    group_size = series_per_device // MICRO
    group_total = series_per_device // attend_group
    state_ones = jnp.ones((group_size, model_width), jnp.float32)
    state_zeros = jnp.zeros((group_size, model_width), jnp.float32)

    def split_groups(array):
        return array.reshape((group_total, attend_group) + array.shape[1:])

    input_rows = embedded_features.reshape(count_of_rows, model_width)
    input_full = input_rows.astype(jnp.float32)
    lstm_pre = tensor_dot_plain(input_rows, mat_lstm) + vec_full[:, 0:4].T.reshape(-1)
    forget, inflow, out_gate = lstm_gates(lstm_pre, keep_mask)
    forget_seq = forget.reshape(series_per_device, steps_per_device, model_width)
    inflow_seq = inflow.reshape(series_per_device, steps_per_device, model_width)
    mult_seq, cell_local = lax.associative_scan(affine_join, (forget_seq, inflow_seq), axis=1)
    cell_parts = []
    for group in range(MICRO):
        lower_row = group * group_size
        upper_row = lower_row + group_size
        _, arriving = entering(
            (mult_seq[lower_row:upper_row, -1], cell_local[lower_row:upper_row, -1]),
            "tm",
            affine_join,
            (state_ones, state_zeros),
            False,
        )
        cell_parts.append(arriving)
    cell_in = jnp.concatenate(cell_parts, axis=0)
    cell_seq = cell_local + mult_seq * cell_in[:, None, :]
    cell_tanh = jnp.tanh(cell_seq.reshape(count_of_rows, model_width))
    hidden_low = narrow_convert(out_gate * cell_tanh)
    glu_one_pre = tensor_dot_plain(hidden_low, mat_glu_one) + vec_full[:, 4:6].T.reshape(-1)
    first_sum = input_full + gated_unit(glu_one_pre)
    first = layer_norm(first_sum, vec_full[:, 6], vec_full[:, 7])
    first_low = narrow_convert(first)
    qkv_low = narrow_convert(tensor_dot_plain(first_low, mat_qkv))
    query_low = qkv_low[:, :model_width].reshape(
        series_per_device, steps_per_device, HEADS, head_width
    )
    key_value = qkv_low[:, model_width:].reshape(
        series_per_device, steps_per_device, model_width + head_width
    )
    key_value_all = lax.all_gather(key_value, "tm", axis=1, tiled=True)
    keys_all = key_value_all[..., :model_width].reshape(
        series_per_device, seq_total, HEADS, head_width
    )
    values_all = key_value_all[..., model_width:]

    def attend_forward(block_args):
        query_block, key_block, value_block, begin_block = block_args
        scores = masked_scores(query_block, key_block, time_local, time_all, begin_block, scale)
        row_top = jnp.max(scores, axis=-1, keepdims=True)
        row_exp = jnp.exp(scores - row_top)
        row_total = jnp.sum(row_exp, axis=-1, keepdims=True)
        weights_low = narrow_convert(row_exp / row_total)
        mixed_block = jnp.einsum(
            "ghqk,gkd->gqd", weights_low, value_block, preferred_element_type=jnp.float32
        ) * (1.0 / HEADS)
        return (mixed_block, (row_top + jnp.log(row_total))[..., 0])

    mixed, log_total = lax.map(
        attend_forward,
        (
            split_groups(query_low),
            split_groups(keys_all),
            split_groups(values_all),
            split_groups(earliest_seen_moment),
        ),
    )
    mixed_low = narrow_convert(mixed.reshape(count_of_rows, head_width))
    attn_low = narrow_convert(tensor_dot_plain(mixed_low, mat_attn))
    glu_two_pre = tensor_dot_plain(attn_low, mat_glu_two) + vec_full[:, 8:10].T.reshape(-1)
    second_sum = first + gated_unit(glu_two_pre)
    second = layer_norm(second_sum, vec_full[:, 10], vec_full[:, 11])
    second_low = narrow_convert(second)
    inner_pre = tensor_dot_plain(second_low, mat_inner) + vec_full[:, 12]
    inner_low = narrow_convert(jax.nn.elu(inner_pre))
    middle_low = narrow_convert(tensor_dot_plain(inner_low, mat_middle) + vec_full[:, 13])
    glu_three_pre = tensor_dot_plain(middle_low, mat_glu_three) + vec_full[:, 14:16].T.reshape(-1)
    final_sum = second + gated_unit(glu_three_pre)
    second_block_emit = layer_norm(final_sum, vec_full[:, 16], vec_full[:, 17])
    closing_narrowed = narrow_convert(second_block_emit)
    predicted_entries = tensor_dot_plain(closing_narrowed, level_dot) * ahead_moment_filter
    predicted_levels = predicted_entries.reshape(
        series_per_device, steps_per_device, LEVEL_TALLY
    ).transpose(0, 2, 1)
    predicted_slope = narrow_convert(
        predicted_adjoint.astype(jnp.float32).transpose(0, 2, 1).reshape(count_of_rows, LEVEL_TALLY)
        * ahead_moment_filter
    )
    level_slope = flipped_dot(closing_narrowed, predicted_slope)
    final_grad = block_emit_adjoint.reshape(count_of_rows, model_width).astype(
        jnp.float32
    ) + dot_against_flipped(predicted_slope, level_dot)
    _, norm_pull = jax.vjp(layer_norm, final_sum, vec_full[:, 16], vec_full[:, 17])
    sum_three_grad, gain_three_grad, offset_three_grad = norm_pull(final_grad)
    _, glu_pull = jax.vjp(gated_unit, glu_three_pre)
    (glu_three_grad,) = glu_pull(sum_three_grad)
    glu_three_low = narrow_convert(glu_three_grad)
    grad_glu_three = flipped_dot(middle_low, glu_three_low)
    middle_grad = dot_against_flipped(glu_three_low, mat_glu_three)
    middle_grad_low = narrow_convert(middle_grad)
    grad_middle = flipped_dot(inner_low, middle_grad_low)
    inner_grad = dot_against_flipped(middle_grad_low, mat_middle)
    _, elu_pull = jax.vjp(jax.nn.elu, inner_pre)
    (inner_pre_grad,) = elu_pull(inner_grad)
    inner_pre_low = narrow_convert(inner_pre_grad)
    grad_inner = flipped_dot(second_low, inner_pre_low)
    second_grad = sum_three_grad + dot_against_flipped(inner_pre_low, mat_inner)
    _, norm_pull = jax.vjp(layer_norm, second_sum, vec_full[:, 10], vec_full[:, 11])
    sum_two_grad, gain_two_grad, offset_two_grad = norm_pull(second_grad)
    _, glu_pull = jax.vjp(gated_unit, glu_two_pre)
    (glu_two_grad,) = glu_pull(sum_two_grad)
    glu_two_low = narrow_convert(glu_two_grad)
    grad_glu_two = flipped_dot(attn_low, glu_two_low)
    attn_grad_low = narrow_convert(dot_against_flipped(glu_two_low, mat_glu_two))
    grad_attn = flipped_dot(mixed_low, attn_grad_low)
    mixed_grad_low = narrow_convert(dot_against_flipped(attn_grad_low, mat_attn))
    head_grad = (mixed_grad_low * (1.0 / HEADS)).reshape(
        series_per_device, steps_per_device, head_width
    )

    def attend_backward(block_args):
        query_block, key_block, value_block, begin_block, lse_block, dout_block = block_args
        scores = masked_scores(query_block, key_block, time_local, time_all, begin_block, scale)
        chances = jnp.exp(scores - lse_block[..., None])
        dprob = jnp.einsum(
            "gqd,gkd->gqk", dout_block, value_block, preferred_element_type=jnp.float32
        )
        row_delta = jnp.sum(chances * dprob[:, None], axis=-1)
        dscore = score_grad(chances, dprob, row_delta, scale)
        dquery = jnp.einsum(
            "ghqk,gkhd->gqhd", dscore, key_block, preferred_element_type=jnp.float32
        )
        dkey = jnp.einsum(
            "ghqk,gqhd->gkhd", dscore, query_block, preferred_element_type=jnp.float32
        )
        dvalue = jnp.einsum(
            "ghqk,gqd->gkd", narrow_convert(chances), dout_block, preferred_element_type=jnp.float32
        )
        key_terms = jnp.concatenate(
            [dkey.reshape(attend_group, seq_total, model_width), dvalue], axis=-1
        )
        return (dquery, key_terms)

    dquery, key_terms = lax.map(
        attend_backward,
        (
            split_groups(query_low),
            split_groups(keys_all),
            split_groups(values_all),
            split_groups(earliest_seen_moment),
            log_total,
            split_groups(head_grad),
        ),
    )
    own_keys = lax.psum_scatter(
        key_terms.reshape(series_per_device, seq_total, model_width + head_width),
        "tm",
        scatter_dimension=1,
        tiled=True,
    )
    qkv_grad = jnp.concatenate(
        [
            dquery.reshape(count_of_rows, model_width),
            own_keys.reshape(count_of_rows, model_width + head_width),
        ],
        axis=1,
    )
    qkv_grad_low = narrow_convert(qkv_grad)
    grad_qkv = flipped_dot(first_low, qkv_grad_low)
    first_grad = sum_two_grad + dot_against_flipped(qkv_grad_low, mat_qkv)
    _, norm_pull = jax.vjp(layer_norm, first_sum, vec_full[:, 6], vec_full[:, 7])
    sum_one_grad, gain_one_grad, offset_one_grad = norm_pull(first_grad)
    _, glu_pull = jax.vjp(gated_unit, glu_one_pre)
    (glu_one_grad,) = glu_pull(sum_one_grad)
    glu_one_low = narrow_convert(glu_one_grad)
    grad_glu_one = flipped_dot(hidden_low, glu_one_low)
    hidden_grad = dot_against_flipped(glu_one_low, mat_glu_one)
    out_gate_grad = hidden_grad * cell_tanh
    direct_grad = (hidden_grad * out_gate * (1.0 - cell_tanh * cell_tanh)).reshape(
        series_per_device, steps_per_device, model_width
    )
    next_forget = jnp.concatenate([forget_seq[:, 1:], jnp.ones_like(forget_seq[:, :1])], axis=1)
    rev_mult, rev_cell = lax.associative_scan(
        affine_join, (next_forget, direct_grad), axis=1, reverse=True
    )
    head_mult = forget_seq[:, 0] * rev_mult[:, 0]
    head_cell = forget_seq[:, 0] * rev_cell[:, 0]
    coming_parts = []
    for group in range(MICRO):
        lower_row = group * group_size
        upper_row = lower_row + group_size
        _, coming = entering(
            (head_mult[lower_row:upper_row], head_cell[lower_row:upper_row]),
            "tm",
            affine_join,
            (state_ones, state_zeros),
            True,
        )
        coming_parts.append(coming)
    coming_all = jnp.concatenate(coming_parts, axis=0)
    cell_grad = rev_cell + rev_mult * coming_all[:, None, :]
    cell_prev = jnp.concatenate([cell_in[:, None, :], cell_seq[:, :-1]], axis=1)
    forget_grad = (cell_grad * cell_prev).reshape(count_of_rows, model_width)
    _, gate_pull = jax.vjp(lambda pre_value: lstm_gates(pre_value, keep_mask), lstm_pre)
    (lstm_pre_grad,) = gate_pull(
        (forget_grad, cell_grad.reshape(count_of_rows, model_width), out_gate_grad)
    )
    lstm_low = narrow_convert(lstm_pre_grad)
    grad_lstm = flipped_dot(input_rows, lstm_low)
    input_grad = sum_one_grad + dot_against_flipped(lstm_low, mat_lstm)
    grad_table = jnp.concatenate(
        [
            jnp.sum(lstm_pre_grad, axis=0).reshape(4, model_width).T,
            jnp.sum(glu_one_grad, axis=0).reshape(2, model_width).T,
            gain_one_grad[:, None],
            offset_one_grad[:, None],
            jnp.sum(glu_two_grad, axis=0).reshape(2, model_width).T,
            gain_two_grad[:, None],
            offset_two_grad[:, None],
            jnp.sum(inner_pre_grad, axis=0)[:, None],
            jnp.sum(middle_grad, axis=0)[:, None],
            jnp.sum(glu_three_grad, axis=0).reshape(2, model_width).T,
            gain_three_grad[:, None],
            offset_three_grad[:, None],
        ],
        axis=1,
    )
    (
        whole_lstm,
        whole_glu_one,
        whole_qkv,
        whole_attn,
        whole_glu_two,
        whole_inner,
        whole_middle,
        whole_glu_three,
        whole_quant,
        whole_table,
    ) = lax.psum(
        (
            grad_lstm,
            grad_glu_one,
            grad_qkv,
            grad_attn,
            grad_glu_two,
            grad_inner,
            grad_middle,
            grad_glu_three,
            level_slope,
            grad_table,
        ),
        "tm",
    )
    summed = (
        lax.psum_scatter(
            whole_lstm.astype(jnp.bfloat16), "dp", scatter_dimension=0, tiled=True
        ).astype(jnp.float32),
        lax.psum_scatter(
            whole_glu_one.astype(jnp.bfloat16), "dp", scatter_dimension=0, tiled=True
        ).astype(jnp.float32),
        lax.psum_scatter(
            whole_qkv.astype(jnp.bfloat16), "dp", scatter_dimension=0, tiled=True
        ).astype(jnp.float32),
        lax.psum_scatter(
            whole_attn.astype(jnp.bfloat16), "dp", scatter_dimension=0, tiled=True
        ).astype(jnp.float32),
        lax.psum_scatter(
            whole_glu_two.astype(jnp.bfloat16), "dp", scatter_dimension=0, tiled=True
        ).astype(jnp.float32),
        lax.psum_scatter(
            whole_inner.astype(jnp.bfloat16), "dp", scatter_dimension=0, tiled=True
        ).astype(jnp.float32),
        lax.psum_scatter(
            whole_middle.astype(jnp.bfloat16), "dp", scatter_dimension=0, tiled=True
        ).astype(jnp.float32),
        lax.psum_scatter(
            whole_glu_three.astype(jnp.bfloat16), "dp", scatter_dimension=0, tiled=True
        ).astype(jnp.float32),
        lax.psum_scatter(
            whole_quant.astype(jnp.bfloat16), "dp", scatter_dimension=0, tiled=True
        ).astype(jnp.float32),
        lax.psum_scatter(
            whole_table.astype(jnp.bfloat16), "dp", scatter_dimension=0, tiled=True
        ).astype(jnp.float32),
    )
    final_out = second_block_emit.astype(jnp.bfloat16).reshape(
        series_per_device, steps_per_device, model_width
    )
    input_out = input_grad.astype(jnp.bfloat16).reshape(
        series_per_device, steps_per_device, model_width
    )
    return (
        final_out,
        predicted_levels,
        input_out,
        summed[0],
        summed[1],
        summed[2],
        summed[3],
        summed[4],
        summed[5],
        summed[6],
        summed[7],
        summed[8],
        summed[9],
    )


def lane_head(shape, head_width, head):
    lane = lax.broadcasted_iota(jnp.int32, shape, len(shape) - 1)
    return (lane >= head * head_width) & (lane < (head + 1) * head_width)


FORGET, ENTER, CANDIDATE, EXIT = 0, 256, 512, 768
GLU_ONE_A, GLU_ONE_B = 1024, 1280
QUERY, KEY, VALUE = 1536, 1792, 2048
GLU_TWO_A, GLU_TWO_B = 2176, 2432
INNER, MIDDLE = 2688, 2944
GLU_THREE_A, GLU_THREE_B = 3200, 3456
ATTN_OUT = 3712
PACKED = 3968
VECTORS = 24
LANES = 128
SUBLANES = 8
CHUNKS = 64
TILE = 256


def nn(left, right):
    return jnp.dot(left, right, preferred_element_type=jnp.float32)


def nt(left, right):
    return lax.dot_general(
        left, right, (((1,), (1,)), ((), ())), preferred_element_type=jnp.float32
    )


def tn(left, right):
    return lax.dot_general(
        left, right, (((0,), (0,)), ((), ())), preferred_element_type=jnp.float32
    )


def low(values):
    return values.astype(jnp.bfloat16)


def sigmoid(values):
    return 0.5 * jnp.tanh(0.5 * values) + 0.5


def normalise(values, gain, shift):
    centred = values - jnp.mean(values, axis=-1, keepdims=True)
    spread = jnp.mean(centred * centred, axis=-1, keepdims=True)
    inverse = lax.rsqrt(spread + EPSILON)
    unit = centred * inverse
    return unit * gain + shift, unit, inverse


def normalise_back(grad, unit, inverse, gain):
    scaled = grad * gain
    return inverse * (
        scaled
        - jnp.mean(scaled, axis=-1, keepdims=True)
        - unit * jnp.mean(scaled * unit, axis=-1, keepdims=True)
    )


def rows_of(tile, size):
    return pl.ds(pl.multiple_of(tile * size, size), size)


def put_halves(ref, rows, values):
    ref[0, rows, :] = values[:, :LANES]
    ref[1, rows, : values.shape[1] - LANES] = values[:, LANES:]


def get_halves(ref, rows, width):
    return jnp.concatenate([ref[0, rows, :], ref[1, rows, : width - LANES]], axis=1)


def row_sum(ref, column, values):
    ref[column : column + 1, :] = jnp.sum(values, axis=0, keepdims=True)


def series_scratch(span, width, head_width):
    full = pltpu.VMEM((span, width), jnp.float32)
    half = pltpu.VMEM((span, width), jnp.bfloat16)
    flat = pltpu.VMEM((width, span), jnp.bfloat16)
    scan = pltpu.VMEM((2, span, LANES), jnp.float32)
    scan_more = pltpu.VMEM((2, span + 8, LANES), jnp.float32)
    narrow = pltpu.VMEM((span, head_width), jnp.bfloat16)
    column = pltpu.VMEM((span, 1), jnp.float32)
    tiles = span // TILE
    return dict(
        forget=scan_more,
        local=scan,
        mult=scan,
        cell=scan_more,
        carry=pltpu.VMEM((2, CHUNKS, LANES), jnp.float32),
        enter_gate=full,
        candidate=full,
        exit_gate=full,
        cell_tanh=full,
        hidden=half,
        glu_one=full,
        gate_one=full,
        unit_one=full,
        inverse_one=column,
        first_low=half,
        keys=half,
        values=narrow,
        head_queries=pltpu.VMEM((HEADS, span, width), jnp.bfloat16),
        head_keys=pltpu.VMEM((HEADS, span, width), jnp.bfloat16),
        **{
            "chances%d" % tile: pltpu.VMEM((HEADS, TILE, (tile + 1) * TILE), jnp.float32)
            for tile in range(tiles)
        },
        chance_sum=pltpu.VMEM((span, span), jnp.bfloat16),
        **{
            "score_grads%d" % tile: pltpu.VMEM((HEADS, span - tile * TILE, TILE), jnp.bfloat16)
            for tile in range(tiles)
        },
        block=pltpu.VMEM((TILE, span), jnp.float32),
        mixed=narrow,
        mixed_grad=narrow,
        sum_two_grad=full,
        query_grad=half,
        key_grad=half,
        value_grad=narrow,
        gate_grads=pltpu.VMEM((4, span, width), jnp.bfloat16),
        x=half,
        x_flat=flat,
        adjoint=flat,
        out=flat,
        input_grad=flat,
        w=pltpu.VMEM((width, PACKED), jnp.bfloat16),
        vec=pltpu.VMEM((VECTORS, width), jnp.float32),
        level=pltpu.VMEM((8, width), jnp.bfloat16),
        gv=pltpu.VMEM((VECTORS + 8, width), jnp.float32),
        slope=pltpu.VMEM((8, LANES), jnp.float32),
        predicted=pltpu.VMEM((8, LANES), jnp.float32),
        attn_flat=pltpu.VMEM((width, 2 * width // 5), jnp.float32),
        lstm_flat=pltpu.VMEM((width, 4 * LANES), jnp.float32),
        middle_send=pltpu.VMEM((2, width, GROUP_LANES["middle"]), jnp.bfloat16),
        first_send=pltpu.VMEM((2, width, GROUP_LANES["first"]), jnp.bfloat16),
        lstm_send=pltpu.VMEM((2, width, GROUP_LANES["lstm"]), jnp.bfloat16),
    )


def series_turn(r, chunk, steps):
    rows = rows_of(chunk, steps)
    r.x[rows, :] = r.x_flat[:, rows].T


def series_gates(r, begin):
    w, vec = r.w, r.vec
    span, width = r.x.shape
    rows = slice(0, span)
    x = r.x[...]

    def pre(block, column):
        return nn(x, w[:, block : block + width]) + vec[column : column + 1, :]

    time = lax.broadcasted_iota(jnp.int32, (span, width), 0)
    put_halves(r.forget, rows, jnp.where(time != begin, sigmoid(pre(FORGET, 0)), 0.0))
    enter = sigmoid(pre(ENTER, 1))
    candidate = jnp.tanh(pre(CANDIDATE, 2))
    r.enter_gate[...] = enter
    r.candidate[...] = candidate
    put_halves(r.local, rows, enter * candidate)
    r.exit_gate[...] = sigmoid(pre(EXIT, 3))


def scan_state():
    zeros = jnp.zeros((SUBLANES, LANES), jnp.float32)
    return ((zeros, zeros + 1.0),) * (2 * CHUNKS // SUBLANES)


def scan_step(r, steps, t, after, state):
    out = []
    for index, (value, mult) in enumerate(state):
        half, start = index % 2, index // 2 * SUBLANES * steps
        at = pl.ds(start + t, SUBLANES, stride=steps)
        forget = r.forget[half, pl.ds(start + t + after, SUBLANES, stride=steps), :]
        value = forget * value + r.local[half, at, :]
        mult = mult * forget
        r.local[half, at, :] = value
        r.mult[half, at, :] = mult
        out.append((value, mult))
    return tuple(out)


def scan_carry(r, ends, order):
    for half in range(2):
        state = jnp.zeros((1, LANES), jnp.float32)
        for chunk in order:
            r.carry[half, chunk : chunk + 1, :] = state
            value, mult = ends[chunk // SUBLANES * 2 + half]
            at = chunk % SUBLANES
            state = value[at : at + 1] + mult[at : at + 1] * state


def series_forward_scan(r):
    steps = r.x.shape[0] // CHUNKS
    ends = scan_state()
    for t in range(steps):
        ends = scan_step(r, steps, t, 0, ends)
    scan_carry(r, ends, range(CHUNKS))
    for half in range(2):
        r.cell[half, 0:8, :] = jnp.zeros((8, LANES), jnp.float32)


def series_forward_first(r):
    w, vec = r.w, r.vec
    span, width = r.x.shape
    head_width = width // HEADS
    steps = span // CHUNKS
    for chunk in range(CHUNKS):
        rows = slice(chunk * steps, (chunk + 1) * steps)
        later = slice(chunk * steps + 8, (chunk + 1) * steps + 8)
        for half in range(2):
            r.cell[half, later, :] = (
                r.local[half, rows, :]
                + r.mult[half, rows, :] * r.carry[half, chunk : chunk + 1, :]
            )
    tanh = jnp.tanh(get_halves(r.cell, slice(8, 8 + span), width))
    r.cell_tanh[...] = tanh
    hidden = low(r.exit_gate[...] * tanh)
    r.hidden[...] = hidden
    value = nn(hidden, w[:, GLU_ONE_A : GLU_ONE_A + width]) + vec[4:5, :]
    gate = sigmoid(nn(hidden, w[:, GLU_ONE_B : GLU_ONE_B + width]) + vec[5:6, :])
    r.glu_one[...] = value
    r.gate_one[...] = gate
    out, unit, inverse = normalise(
        r.x[...].astype(jnp.float32) + value * gate, vec[6:7, :], vec[7:8, :]
    )
    r.unit_one[...] = unit
    r.inverse_one[...] = inverse
    out = low(out)
    r.first_low[...] = out
    query = low(nn(out, w[:, QUERY : QUERY + width]))
    key = low(nn(out, w[:, KEY : KEY + width]))
    r.keys[...] = key
    r.values[...] = low(nn(out, w[:, VALUE : VALUE + head_width]))
    for head in range(HEADS):
        mine = lane_head((span, width), head_width, head)
        r.head_queries[head] = jnp.where(mine, query, jnp.zeros_like(query))
        r.head_keys[head] = jnp.where(mine, key, jnp.zeros_like(key))


def series_forward_attention(r, begin):
    span, head_width = r.values.shape
    scale = head_width ** (-0.5) * LOG2_E
    for tile in range(span // TILE):
        rows = slice(tile * TILE, (tile + 1) * TILE)
        seen = (tile + 1) * TILE
        row = tile * TILE + lax.broadcasted_iota(jnp.int32, (TILE, seen), 0)
        col = lax.broadcasted_iota(jnp.int32, (TILE, seen), 1)
        chances = getattr(r, "chances%d" % tile)
        r.block[:, :seen] = jnp.where(
            (col <= row) & (col >= jnp.minimum(begin, row)), 0.0, NEG_BIG
        )
        for head in range(HEADS):
            scores = (
                nt(r.head_queries[head, rows, :], r.keys[:seen, :]) * scale + r.block[:, :seen]
            )
            top = jnp.max(scores, axis=-1, keepdims=True)
            raised = jnp.exp2(scores - top)
            total = jnp.sum(raised, axis=-1, keepdims=True)
            chances[head] = raised * (1.0 / total)
        weights = chances[0]
        for head in range(1, HEADS):
            weights = weights + chances[head]
        weights = low(weights)
        r.chance_sum[rows, :seen] = weights
        r.mixed[rows, :] = low(nn(weights, r.values[:seen, :]) * (1.0 / HEADS))


def series_middle(r, horizon, after_forward):
    w, vec, gv = r.w, r.vec, r.gv
    span, width = r.x.shape
    head_width = width // HEADS
    first = r.unit_one[...] * vec[6:7, :] + vec[7:8, :]
    mixed = r.mixed[...]
    attn = low(nn(mixed, w[:head_width, ATTN_OUT : ATTN_OUT + width]))
    value_two = nn(attn, w[:, GLU_TWO_A : GLU_TWO_A + width]) + vec[8:9, :]
    gate_two = sigmoid(nn(attn, w[:, GLU_TWO_B : GLU_TWO_B + width]) + vec[9:10, :])
    second, unit_two, inverse_two = normalise(
        first + value_two * gate_two, vec[10:11, :], vec[11:12, :]
    )
    second_low = low(second)
    inner_pre = nn(second_low, w[:, INNER : INNER + width]) + vec[12:13, :]
    inner_exp = jnp.exp(jnp.minimum(inner_pre, 0.0))
    inner_low = low(jnp.where(inner_pre > 0, inner_pre, inner_exp - 1.0))
    middle_low = low(nn(inner_low, w[:, MIDDLE : MIDDLE + width]) + vec[13:14, :])
    value_three = nn(middle_low, w[:, GLU_THREE_A : GLU_THREE_A + width]) + vec[14:15, :]
    gate_three = sigmoid(nn(middle_low, w[:, GLU_THREE_B : GLU_THREE_B + width]) + vec[15:16, :])
    final, unit_three, inverse_three = normalise(
        second + value_three * gate_three, vec[16:17, :], vec[17:18, :]
    )
    final_low = low(final)
    r.out[...] = final_low.T
    steps = r.slope.shape[1]
    time = span - steps + lax.broadcasted_iota(jnp.int32, (8, steps), 1)
    ahead = jnp.where((time >= span - DEC) & (time < span - DEC + horizon), 1.0, 0.0)
    r.predicted[...] = nt(r.level[...], final_low[span - steps :]) * ahead
    after_forward()
    slope = low(r.slope[...] * ahead)
    gv[VECTORS : VECTORS + 8, :] = nn(slope, final_low[span - steps :])
    grad = r.adjoint[...].T.astype(jnp.float32)
    grad = jnp.concatenate(
        [grad[: span - steps], grad[span - steps :] + tn(slope, r.level[...])], axis=0
    )
    row_sum(gv, 16, grad * unit_three)
    row_sum(gv, 17, grad)
    sum_three = normalise_back(grad, unit_three, inverse_three, vec[16:17, :])
    grad_a = sum_three * gate_three
    grad_b = grad_a * value_three * (1.0 - gate_three)
    row_sum(gv, 14, grad_a)
    row_sum(gv, 15, grad_b)
    low_a, low_b = low(grad_a), low(grad_b)
    send = r.middle_send
    send[1, :, :width] = low(tn(middle_low, low_a))
    send[1, :, width : 2 * width] = low(tn(middle_low, low_b))
    middle_grad = nt(low_a, w[:, GLU_THREE_A : GLU_THREE_A + width]) + nt(
        low_b, w[:, GLU_THREE_B : GLU_THREE_B + width]
    )
    row_sum(gv, 13, middle_grad)
    middle_grad = low(middle_grad)
    send[1, :, 2 * width : 3 * width] = low(tn(inner_low, middle_grad))
    inner_grad = nt(middle_grad, w[:, MIDDLE : MIDDLE + width]) * jnp.where(
        inner_pre > 0, 1.0, inner_exp
    )
    row_sum(gv, 12, inner_grad)
    inner_grad = low(inner_grad)
    send[0, :, 2 * width : 3 * width] = low(tn(second_low, inner_grad))
    grad = sum_three + nt(inner_grad, w[:, INNER : INNER + width])
    row_sum(gv, 10, grad * unit_two)
    row_sum(gv, 11, grad)
    sum_two = normalise_back(grad, unit_two, inverse_two, vec[10:11, :])
    r.sum_two_grad[...] = sum_two
    grad_a = sum_two * gate_two
    grad_b = grad_a * value_two * (1.0 - gate_two)
    row_sum(gv, 8, grad_a)
    row_sum(gv, 9, grad_b)
    low_a, low_b = low(grad_a), low(grad_b)
    attn_grad = low(
        nt(low_a, w[:, GLU_TWO_A : GLU_TWO_A + width])
        + nt(low_b, w[:, GLU_TWO_B : GLU_TWO_B + width])
    )
    r.mixed_grad[...] = low(nt(attn_grad, w[:head_width, ATTN_OUT : ATTN_OUT + width]))
    send[0, :, :width] = low(tn(attn, low_a))
    send[0, :, width : 2 * width] = low(tn(attn, low_b))
    attn_weight = tn(mixed, attn_grad)
    rows, small = head_width, head_width // HEADS
    spare = width // 5
    r.attn_flat[...] = jnp.zeros_like(r.attn_flat)
    for group in range(HEADS):
        for piece in range(5):
            at = group * rows + small * (piece % 4)
            half = piece // 4
            r.attn_flat[at : at + small, half * spare : (half + 1) * spare] = attn_weight[
                group * small : (group + 1) * small, piece * spare : (piece + 1) * spare
            ]
    for half in range(2):
        send[half, :, 3 * width :] = low(r.attn_flat[:, half * spare : (half + 1) * spare])


def series_backward_attention(r, between):
    span, head_width = r.values.shape
    width = head_width * HEADS
    scale = head_width ** (-0.5)
    for tile in range(span // TILE):
        rows = slice(tile * TILE, (tile + 1) * TILE)
        seen = (tile + 1) * TILE
        held = getattr(r, "chances%d" % tile)
        head_grad = r.mixed_grad[rows, :] * (1.0 / HEADS)
        r.block[:, :seen] = nt(head_grad, r.values[:seen, :]) * scale
        total = jnp.zeros((TILE, width), jnp.float32)
        for head in range(HEADS):
            chances = held[head]
            slope = r.block[:, :seen]
            delta = jnp.sum(chances * slope, axis=-1, keepdims=True)
            grads = low(chances * (slope - delta))
            for part in range(tile + 1):
                getattr(r, "score_grads%d" % part)[
                    head, (tile - part) * TILE : (tile - part + 1) * TILE, :
                ] = grads[:, part * TILE : (part + 1) * TILE]
            total = total + nn(grads, r.head_keys[head, :seen, :])
        r.query_grad[rows, :] = low(total)
        between(tile)
    for tile in range(span // TILE):
        cols = slice(tile * TILE, (tile + 1) * TILE)
        start = tile * TILE
        total = jnp.zeros((TILE, width), jnp.float32)
        for head in range(HEADS):
            total = total + tn(
                getattr(r, "score_grads%d" % tile)[head], r.head_queries[head, start:, :]
            )
        r.key_grad[cols, :] = low(total)
        r.value_grad[cols, :] = low(
            tn(r.chance_sum[start:, cols], r.mixed_grad[start:, :] * (1.0 / HEADS))
        )


def series_backward_first(r):
    w, vec, gv = r.w, r.vec, r.gv
    span, width = r.hidden.shape
    head_width = width // HEADS
    rows = slice(0, span)
    send = r.first_send
    query, key, value = r.query_grad[...], r.key_grad[...], r.value_grad[...]
    grad = (
        r.sum_two_grad[...]
        + nt(query, w[:, QUERY : QUERY + width])
        + nt(key, w[:, KEY : KEY + width])
        + nt(value, w[:, VALUE : VALUE + head_width])
    )
    first = r.first_low[...]
    send[1, :, :width] = low(tn(first, query))
    send[1, :, width : 2 * width] = low(tn(first, key))
    send[1, :, 2 * width : 2 * width + head_width] = low(tn(first, value))
    unit = r.unit_one[...]
    row_sum(gv, 6, grad * unit)
    row_sum(gv, 7, grad)
    sum_one = normalise_back(grad, unit, r.inverse_one[...], vec[6:7, :])
    r.sum_two_grad[...] = sum_one
    gate = r.gate_one[...]
    grad_a = sum_one * gate
    grad_b = grad_a * r.glu_one[...] * (1.0 - gate)
    row_sum(gv, 4, grad_a)
    row_sum(gv, 5, grad_b)
    low_a, low_b = low(grad_a), low(grad_b)
    hidden_grad = nt(low_a, w[:, GLU_ONE_A : GLU_ONE_A + width]) + nt(
        low_b, w[:, GLU_ONE_B : GLU_ONE_B + width]
    )
    tanh, gate = r.cell_tanh[...], r.exit_gate[...]
    put_halves(r.local, rows, hidden_grad * gate * (1.0 - tanh * tanh))
    exit_grad = hidden_grad * tanh * gate * (1.0 - gate)
    row_sum(gv, 3, exit_grad)
    exit_grad = low(exit_grad)
    r.gate_grads[3] = exit_grad
    hidden = r.hidden[...]
    send[0, :, :width] = low(tn(hidden, low_a))
    send[0, :, width : 2 * width] = low(tn(hidden, low_b))
    send[0, :, 2 * width : 3 * width] = low(nn(r.x_flat[...], exit_grad))


def series_backward_scan(r):
    span = r.x.shape[0]
    steps = span // CHUNKS
    for half in range(2):
        r.forget[half, span:, :] = jnp.zeros((8, LANES), jnp.float32)

    ends = scan_state()
    for t in range(steps - 1, -1, -1):
        ends = scan_step(r, steps, t, 1, ends)
    scan_carry(r, ends, range(CHUNKS - 1, -1, -1))


def series_gate_grads(r):
    gv = r.gv
    span, width = r.x.shape
    steps = span // CHUNKS
    for half in range(2):
        for chunk in range(CHUNKS):
            rows = slice(chunk * steps, (chunk + 1) * steps)
            r.local[half, rows, :] += r.mult[half, rows, :] * r.carry[half, chunk : chunk + 1, :]
    grad = get_halves(r.local, slice(0, span), width)
    forget = get_halves(r.forget, slice(0, span), width)
    before = get_halves(r.cell, slice(7, 7 + span), width)
    enter, candidate = r.enter_gate[...], r.candidate[...]
    for gate, one in enumerate(
        (
            grad * before * forget * (1.0 - forget),
            grad * candidate * enter * (1.0 - enter),
            grad * enter * (1.0 - candidate * candidate),
        )
    ):
        row_sum(gv, gate, one)
        one = low(one)
        r.gate_grads[gate] = one
        r.lstm_flat[:, gate * width : (gate + 1) * width] = nn(r.x_flat[...], one)
    r.lstm_flat[:, 3 * width :] = gv[...].T
    lanes = r.lstm_send.shape[2]
    for half in range(2):
        r.lstm_send[half] = low(r.lstm_flat[:, half * lanes : (half + 1) * lanes])


def series_input_grad(r):
    width = r.x.shape[1]
    out = r.sum_two_grad[...].T
    for gate, block in enumerate((FORGET, ENTER, CANDIDATE, EXIT)):
        out = out + nt(r.w[:, block : block + width], r.gate_grads[gate])
    r.input_grad[...] = low(out)


class Exchange:
    def __init__(self, sems, devices, source, target, sources, targets):
        self.sems, self.source, self.target = sems, source, target
        self.sources, self.targets = sources, targets
        self.count, self.me, self.device = devices

    def other(self, step):
        return lax.rem(self.me + step, self.count)

    def copy(self, to, source, target):
        return pltpu.make_async_remote_copy(
            src_ref=source,
            dst_ref=target,
            send_sem=self.sems.at[0],
            recv_sem=self.sems.at[1],
            device_id=self.device(to),
            device_id_type=pl.DeviceIdType.MESH,
        )

    def one(self, to):
        return self.copy(to, self.source(to), self.target(self.me))

    def start(self):
        for step in range(1, self.count):
            self.one(self.other(step)).start()

    def all(self):
        return self.copy(self.other(1), self.sources, self.targets)

    def arrive(self):
        self.all().wait_recv()

    def sent(self):
        self.all().wait_send()


def over_time():
    return lax.axis_size("tm"), lax.axis_index("tm"), lambda to: {"tm": to}


def over_series():
    return lax.axis_size("dp"), lax.axis_index("dp"), lambda to: {"dp": to}


def over_chips():
    core = my_core()
    return (
        lax.axis_size("tm") // 2,
        lax.div(lax.axis_index("tm"), 2),
        lambda to: {"tm": 2 * to + core},
    )


def my_core():
    return lax.rem(lax.axis_index("tm"), 2)


def to_other_core(source, target, sems, index):
    return pltpu.make_async_remote_copy(
        src_ref=source,
        dst_ref=target,
        send_sem=sems.at[0, index],
        recv_sem=sems.at[1, index],
        device_id={"tm": lax.axis_index("tm") + 1 - 2 * my_core()},
        device_id_type=pl.DeviceIdType.MESH,
    )


GROUP_COLUMNS = (384, 384, 640)
GROUP_LANES = {"middle": 512, "first": 512, "lstm": 256}
DIRECT = ("lstm",)


def fold(values):
    lanes = values.shape[1] // 2
    return low(jnp.concatenate([values[:, :lanes], values[:, lanes:]], axis=0))


def unfold(values):
    rows = values.shape[0] // 2
    return jnp.concatenate([values[:rows], values[rows:]], axis=1)


def travel_scratch(count, groups, steps, width, params):
    rows = params[0].shape[0]
    out = dict(
        slopes=pltpu.VMEM((count, 8, steps), jnp.float32),
        levels=pltpu.VMEM((count, 8, steps), jnp.float32),
        stage=pltpu.VMEM((width, 2 * GROUP_COLUMNS[2]), jnp.float32),
        attn_stage=pltpu.VMEM((width, width), jnp.float32),
        table_stage=pltpu.VMEM((rows, LANES), jnp.float32),
        pack_stage=pltpu.VMEM((rows, GROUP_COLUMNS[2]), jnp.float32),
    )
    for index, param in enumerate(params):
        out["param%d" % index] = pltpu.VMEM(param.shape, jnp.float32)
    out["load_sems"] = pltpu.SemaphoreType.DMA((len(params) + 3,))
    out["begins"] = pltpu.SMEM((count,), jnp.int32)
    out["reaches"] = pltpu.SMEM((count,), jnp.int32)
    out["slope_in"] = pltpu.VMEM((LEVEL_TALLY, count, steps), jnp.bfloat16)
    for group, columns in enumerate(GROUP_COLUMNS):
        slab = -(-rows * columns // LANES // 16) * 16
        out["params%d" % group] = pltpu.VMEM((2, groups, slab, LANES), jnp.bfloat16)
        out["params%d_sems" % group] = pltpu.SemaphoreType.DMA((3 + groups,))
    for name, lanes in GROUP_LANES.items():
        out[name + "_near"] = pltpu.VMEM((width, lanes), jnp.bfloat16)
        folded = (2 * rows, lanes // 2)
        out[name + "_part"] = pltpu.VMEM((groups,) + folded, jnp.bfloat16)
        out[name + "_parts"] = pltpu.VMEM((groups,) + folded, jnp.bfloat16)
        places = count if name in DIRECT else count // 2
        out[name + "_chips"] = pltpu.VMEM((places,) + folded, jnp.bfloat16)
        out[name + "_core_sems"] = pltpu.SemaphoreType.DMA((2, 2))
        out[name + "_dp_sems"] = pltpu.SemaphoreType.DMA((2,))
        out[name + "_chip_sems"] = pltpu.SemaphoreType.DMA((2,))
    for name in ("x", "adjoint", "out", "input", "slope", "predicted"):
        out[name + "_sems"] = pltpu.SemaphoreType.DMA((2,))
    out["own_sems"] = pltpu.SemaphoreType.DMA((4,))
    return out


class Parameters:
    def __init__(self, r, group):
        self.buffer = getattr(r, "params%d" % group)
        self.sems = getattr(r, "params%d_sems" % group)
        self.core, self.mine, self.count = my_core(), lax.axis_index("dp"), lax.axis_size("dp")

    def other(self, step):
        return lax.rem(self.mine + step, self.count)

    def move(self, blocks, device, send, arrive):
        return pltpu.make_async_remote_copy(
            src_ref=blocks,
            dst_ref=blocks,
            send_sem=self.sems.at[send],
            recv_sem=self.sems.at[arrive],
            device_id=device,
            device_id_type=pl.DeviceIdType.MESH,
        )

    def over(self, to, origin):
        return self.move(self.buffer.at[self.core, origin], {"dp": to}, 0, 3 + origin)

    def hand(self, blocks):
        return self.move(blocks, {"tm": lax.axis_index("tm") + 1 - 2 * self.core}, 1, 2)

    def others(self, core):
        return self.buffer.at[core, pl.ds(0, self.count - 1)]

    def start(self):
        for step in range(1, self.count):
            self.over(self.other(step), self.mine).start()

    def pass_on(self):
        for step in range(1, self.count):
            origin = self.other(step)
            self.over(origin, origin).wait_recv()
            self.hand(self.buffer.at[self.core, origin]).start()

    def arrive(self):
        self.hand(self.others(1 - self.core)).wait_recv()

    def sent(self):
        self.move(self.others(self.core), {"dp": self.other(1)}, 0, 3).wait_send()
        self.hand(self.others(self.core)).wait_send()


class Reduction:
    def __init__(self, r, name, final):
        self.send, self.near = getattr(r, name + "_send"), getattr(r, name + "_near")
        self.part, self.parts = getattr(r, name + "_part"), getattr(r, name + "_parts")
        self.chips, self.final = getattr(r, name + "_chips"), final
        self.core, self.rows = my_core(), final.shape[1]
        self.core_sems = getattr(r, name + "_core_sems")
        part, parts, chips = self.part, self.parts, self.chips
        self.to_series = Exchange(
            getattr(r, name + "_dp_sems"),
            over_series(),
            lambda to: part.at[to],
            lambda origin: parts.at[origin],
            part.at[pl.ds(0, part.shape[0] - 1)],
            parts.at[pl.ds(0, part.shape[0] - 1)],
        )
        self.direct = name in DIRECT
        devices = over_time() if self.direct else over_chips()
        place = devices[1]
        self.to_chips = Exchange(
            getattr(r, name + "_chip_sems"),
            devices,
            lambda to: chips.at[place],
            lambda origin: chips.at[origin],
            chips.at[pl.ds(0, chips.shape[0] - 1)],
            chips.at[pl.ds(0, chips.shape[0] - 1)],
        )

    def out(self):
        return to_other_core(self.send.at[1 - self.core], self.near, self.core_sems, 0)

    def back(self, core):
        return to_other_core(self.final.at[core], self.final.at[core], self.core_sems, 1)

    def sum_of(self, ref, first=0, stride=1):
        total = ref[first].astype(jnp.float32)
        for index in range(first + stride, ref.shape[0], stride):
            total = total + ref[index].astype(jnp.float32)
        return total

    def start(self):
        self.out().start()

    def across_series(self):
        self.out().wait_recv()
        total = self.send[self.core].astype(jnp.float32) + self.near[...].astype(jnp.float32)
        for group in range(self.to_series.count):
            self.part[group] = fold(total[group * self.rows : (group + 1) * self.rows])
        self.to_series.start()

    def across_chips(self):
        self.to_series.arrive()
        self.parts[self.to_series.me] = self.part[self.to_series.me]
        self.chips[self.to_chips.me] = low(self.sum_of(self.parts))
        self.to_chips.start()

    def to_both(self):
        self.to_chips.arrive()
        if self.direct:
            for core in range(2):
                self.final[core] = unfold(self.sum_of(self.chips, core, 2))
        else:
            self.final[self.core] = unfold(self.sum_of(self.chips))
            self.back(self.core).start()

    def finish(self):
        if not self.direct:
            self.back(1 - self.core).wait_recv()
            self.back(self.core).wait_send()
        self.out().wait_send()
        self.to_series.sent()
        self.to_chips.sent()


def greet():
    barrier = pltpu.get_barrier_semaphore()
    total = 0
    for count, me, device in (over_time(), over_series()):
        for step in range(1, count):
            pl.semaphore_signal(
                barrier,
                inc=1,
                device_id=device(lax.rem(me + step, count)),
                device_id_type=pl.DeviceIdType.MESH,
            )
            total += 1
    return lambda: pl.semaphore_wait(barrier, total)


def pack_params(r, group, params):
    mine = lax.axis_index("dp")
    buffer, stage = getattr(r, "params%d" % group), r.pack_stage
    columns = GROUP_COLUMNS[group]

    def put(half, *arrays):
        at = 0
        for array in arrays:
            rows, width = array.shape
            stage[:rows, at : at + width] = array[...]
            at += width
        tiles = [stage[:, tile : tile + LANES] for tile in range(0, columns, LANES)]
        spare = buffer.shape[2] - stage.shape[0] * len(tiles)
        tiles.append(jnp.zeros((spare, LANES), jnp.float32))
        buffer[half, mine] = low(jnp.concatenate(tiles, axis=0))

    if group == 0:
        lstm, table, level = params
        rows = lstm.shape[0]
        r.table_stage[...] = jnp.zeros_like(r.table_stage)
        r.table_stage[: table.shape[0], :rows] = table[...]
        r.table_stage[VECTORS : VECTORS + LEVEL_TALLY, :rows] = level[...]
        put(0, lstm[:, :columns])
        put(1, lstm[:, columns:], r.table_stage)
    elif group == 1:
        for half, array in enumerate(params):
            put(half, array)
    else:
        glu_two, glu_three, inner, middle, attn = params
        put(0, glu_two, glu_three)
        put(1, inner, middle, attn)


def unpack_params(r, group, rows, attn_rows):
    width = r.w.shape[0]
    head_width = width // HEADS
    buffer, stage = getattr(r, "params%d" % group), r.stage
    columns = GROUP_COLUMNS[group]
    for half in range(2):
        for origin in range(buffer.shape[1]):
            tiles = buffer[half, origin].astype(jnp.float32)
            for tile in range(columns // LANES):
                at = half * columns + tile * LANES
                stage[origin * rows : (origin + 1) * rows, at : at + LANES] = tiles[
                    tile * rows : (tile + 1) * rows
                ]

    def place(block, column, size):
        r.w[:, block : block + size] = low(stage[:, column : column + size])

    if group == 0:
        for gate, block in enumerate((FORGET, ENTER, CANDIDATE, EXIT)):
            place(block, gate * width, width)
        vectors = jnp.concatenate(
            [
                stage[origin * rows : origin * rows + VECTORS + 8, 4 * width : 4 * width + rows]
                for origin in range(buffer.shape[1])
            ],
            axis=1,
        )
        r.vec[...] = vectors[:VECTORS]
        r.level[...] = low(vectors[VECTORS:])
    elif group == 1:
        place(GLU_ONE_A, 0, width)
        place(GLU_ONE_B, width, width)
        place(QUERY, columns, width)
        place(KEY, columns + width, width)
        place(VALUE, columns + 2 * width, head_width)
    else:
        place(GLU_TWO_A, 0, width)
        place(GLU_TWO_B, width, width)
        place(GLU_THREE_A, 2 * width, width)
        place(GLU_THREE_B, 3 * width, width)
        place(INNER, columns, width)
        place(MIDDLE, columns + width, width)
        for origin in range(buffer.shape[1]):
            r.attn_stage[origin * attn_rows : (origin + 1) * attn_rows, :] = stage[
                origin * rows : origin * rows + attn_rows,
                columns + 2 * width : columns + 3 * width,
            ]
        r.w[:head_width, ATTN_OUT : ATTN_OUT + width] = low(r.attn_stage[:head_width, :])


def series_kernel(begins_hbm, reaches_hbm, x_hbm, adjoint_hbm, slopes_hbm, *others):
    params, others = others[:10], others[10:]
    (out_hbm, predicted_out, input_hbm, final_middle, final_first, final_lstm), scratch = (
        others[:6],
        others[6:],
    )
    count, width, steps = x_hbm.shape
    span = count * steps
    groups = lax.axis_size("dp")
    names = series_scratch(span, width, width // HEADS)
    names.update(travel_scratch(count, groups, steps, width, params))
    r = types.SimpleNamespace(**dict(zip(names, scratch)))
    me = lax.axis_index("tm")
    last = count - 1

    def block(ref, index):
        return ref.at[:, rows_of(index, steps)]

    def whole(ref):
        return ref.at[:, pl.ds(0, (count - 1) * steps)]

    def rest(ref):
        return ref.at[pl.ds(0, count - 1)]

    def inward(sems, source, target):
        return Exchange(
            sems,
            over_time(),
            lambda to: source.at[to],
            lambda origin: block(target, origin),
            rest(source),
            whole(target),
        )

    def outward(sems, source, target):
        return Exchange(
            sems,
            over_time(),
            lambda to: block(source, to),
            lambda origin: target.at[origin],
            whole(source),
            rest(target),
        )

    x_over = inward(r.x_sems, x_hbm, r.x_flat)
    adjoint_over = inward(r.adjoint_sems, adjoint_hbm, r.adjoint)
    out_over = outward(r.out_sems, r.out, out_hbm)
    input_over = outward(r.input_sems, r.input_grad, input_hbm)
    slope_over = Exchange(
        r.slope_sems,
        over_time(),
        lambda to: r.slopes.at[to],
        lambda origin: r.slope,
        rest(r.slopes),
        r.slope,
    )
    predicted_over = Exchange(
        r.predicted_sems,
        over_time(),
        lambda to: r.predicted,
        lambda origin: r.levels.at[origin],
        r.predicted,
        rest(r.levels),
    )
    travelling = [Parameters(r, group) for group in range(3)]
    middle_sum = Reduction(r, "middle", final_middle)
    first_sum = Reduction(r, "first", final_first)
    lstm_sum = Reduction(r, "lstm", final_lstm)
    own_x = pltpu.make_async_copy(x_hbm.at[me], block(r.x_flat, me), r.own_sems.at[0])
    own_adjoint = pltpu.make_async_copy(adjoint_hbm.at[me], block(r.adjoint, me), r.own_sems.at[1])
    own_out = pltpu.make_async_copy(block(r.out, me), out_hbm.at[me], r.own_sems.at[2])
    own_input = pltpu.make_async_copy(block(r.input_grad, me), input_hbm.at[me], r.own_sems.at[3])
    held = [getattr(r, "param%d" % index) for index in range(len(params))]
    loads = [
        pltpu.make_async_copy(param, here, r.load_sems.at[index])
        for index, (param, here) in enumerate(
            zip(
                params + (begins_hbm, reaches_hbm, slopes_hbm),
                held + [r.begins, r.reaches, r.slope_in],
            )
        )
    ]
    begins, reaches, slopes = r.begins, r.reaches, r.slope_in

    def pack(group, *indices):
        for index in indices:
            loads[index].wait()
        pack_params(r, group, [held[index] for index in indices])

    everyone_here = greet()
    for load in loads:
        load.start()
    own_x.start()
    own_adjoint.start()
    pack(0, 0, 9, 8)
    everyone_here()
    travelling[0].start()
    x_over.start()
    pack(1, 1, 2)
    travelling[1].start()
    pack(2, 4, 7, 5, 6, 3)
    for load in loads[len(params) :]:
        load.wait()
    for track in range(count):
        r.slopes[track] = jnp.concatenate(
            [
                slopes[level_at].astype(jnp.float32)[track : track + 1]
                for level_at in range(LEVEL_TALLY)
            ]
            + [jnp.zeros((8 - LEVEL_TALLY, steps), jnp.float32)],
            axis=0,
        )
    begin = begins[me]
    choice = reaches[me]
    horizon = jnp.where(choice == 0, 1, jnp.where(choice == 1, 5, 24))
    rows, attn_rows = params[0].shape[0], params[3].shape[0]
    r.gv[...] = jnp.zeros_like(r.gv)
    own_x.wait()
    series_turn(r, me, steps)
    travelling[0].pass_on()

    x_over.arrive()
    for step in range(1, count):
        series_turn(r, x_over.other(step), steps)
    travelling[0].arrive()
    unpack_params(r, 0, rows, attn_rows)
    series_gates(r, begin)
    travelling[1].pass_on()
    travelling[2].start()
    adjoint_over.start()

    @pl.when(me == last)
    def _():
        slope_over.start()
        r.slope[...] = r.slopes[last]

    series_forward_scan(r)
    travelling[1].arrive()
    unpack_params(r, 1, rows, attn_rows)
    series_forward_first(r)
    series_forward_attention(r, begin)
    travelling[2].pass_on()
    travelling[2].arrive()
    unpack_params(r, 2, rows, attn_rows)
    own_adjoint.wait()
    adjoint_over.arrive()

    @pl.when(me != last)
    def _():
        slope_over.arrive()

    def forward_done():
        own_out.start()
        out_over.start()

        @pl.when(me != last)
        def _():
            predicted_over.one(last).start()

    series_middle(r, horizon, forward_done)
    middle_sum.start()

    def between(tile):
        if tile == 2:
            middle_sum.across_series()

    series_backward_attention(r, between)
    series_backward_first(r)
    first_sum.start()
    series_backward_scan(r)
    series_gate_grads(r)
    lstm_sum.start()
    first_sum.across_series()
    middle_sum.across_chips()
    series_input_grad(r)
    own_input.start()
    input_over.start()
    lstm_sum.across_series()
    first_sum.across_chips()
    middle_sum.to_both()

    @pl.when(me != last)
    def _():
        predicted_over.sent()
        predicted_out[...] = jnp.zeros_like(predicted_out)

    @pl.when(me == last)
    def _():
        slope_over.sent()
        predicted_over.arrive()
        r.levels[last] = r.predicted[...]
        for level_at in range(LEVEL_TALLY):
            predicted_out[level_at] = jnp.concatenate(
                [r.levels[track][level_at : level_at + 1] for track in range(count)], axis=0
            )

    lstm_sum.across_chips()
    first_sum.to_both()
    x_over.sent()
    adjoint_over.sent()
    for group in travelling:
        group.sent()
    own_out.wait()
    out_over.arrive()
    out_over.sent()
    middle_sum.finish()
    first_sum.finish()
    lstm_sum.to_both()
    own_input.wait()
    input_over.arrive()
    input_over.sent()
    lstm_sum.finish()


def unpack_kernel(final_middle, final_first, final_lstm, out_in, predicted_in, input_in, *others):
    (lstm, glu_one, qkv, attn, glu_two, inner, middle, glu_three, level, table) = others[:10]
    out, predicted, input_grad = others[10:]
    predicted[...] = predicted_in[...]
    rows, width = inner.shape
    lanes = final_lstm.shape[2]
    for ref, at in ((glu_two, 0), (glu_three, 1)):
        ref[...] = final_middle[at, :, : 2 * width]
    for ref, at in ((inner, 0), (middle, 1)):
        ref[...] = final_middle[at, :, 2 * width : 3 * width]
    small, spare = attn.shape[0], width // 5
    for piece in range(5):
        at = small * (piece % 4)
        attn[:, piece * spare : (piece + 1) * spare] = final_middle[
            piece // 4, at : at + small, 3 * width : 3 * width + spare
        ]
    glu_one[...] = final_first[0, :, : 2 * width]
    qkv[...] = final_first[1, :, : qkv.shape[1]]
    lstm[:, :lanes] = final_lstm[0]
    lstm[:, lanes : 3 * width] = final_lstm[1, :, : 3 * width - lanes]
    lstm[:, 3 * width :] = final_first[0, :, 2 * width : 3 * width]
    vectors = final_lstm[1, :, 3 * width - lanes :].T
    table[...] = vectors[: table.shape[0]]
    level[...] = vectors[VECTORS : VECTORS + LEVEL_TALLY]
    out[...] = out_in[...]
    input_grad[...] = input_in[...]


def whole_series(embedded_features, earliest_seen_moment, reach_choice, *others):
    count, steps, width = embedded_features.shape
    features = embedded_features.swapaxes(1, 2)
    adjoint = others[-2].swapaxes(1, 2)
    slopes = others[-1].swapaxes(0, 1)
    params = others[:-4] + (others[-4].T, others[-3].T)
    groups = lax.axis_size("dp")
    rows = params[0].shape[0]
    names = series_scratch(count * steps, width, width // HEADS)
    names.update(travel_scratch(count, groups, steps, width, params))
    smem, vmem, anywhere = (
        pl.BlockSpec(memory_space=space) for space in (pltpu.SMEM, pltpu.VMEM, pl.ANY)
    )
    moved = ((features.shape, jnp.bfloat16), (slopes.shape, jnp.float32))
    moved += moved[:1]
    out, predicted, input_grad, *finals = pl.pallas_call(
        series_kernel,
        out_shape=tuple(pltpu.VMEM(*one) for one in moved)
        + tuple(pltpu.VMEM((2, rows, lanes), jnp.float32) for lanes in GROUP_LANES.values()),
        in_specs=[anywhere] * (5 + len(params)),
        out_specs=(vmem,) * 6,
        scratch_shapes=list(names.values()),
        compiler_params=pltpu.CompilerParams(
            vmem_limit_bytes=VMEM_BYTES, collective_id=0, has_side_effects=True
        ),
    )(
        earliest_seen_moment,
        reach_choice,
        features,
        adjoint,
        slopes,
        *params,
    )
    *grads, level_grad, table_grad, out, predicted, input_grad = pl.pallas_call(
        unpack_kernel,
        out_shape=tuple(jax.ShapeDtypeStruct(param.shape, jnp.float32) for param in params)
        + tuple(jax.ShapeDtypeStruct(*one) for one in moved),
        in_specs=[vmem] * 6,
        out_specs=(vmem,) * (len(params) + 3),
        compiler_params=pltpu.CompilerParams(vmem_limit_bytes=VMEM_BYTES // 6),
    )(*finals, out, predicted, input_grad)
    return (
        out.swapaxes(1, 2),
        predicted.swapaxes(0, 1),
        input_grad.swapaxes(1, 2),
        *grads,
        level_grad.T,
        table_grad.T,
    )


def on_device(embedded_features, *others):
    count, steps, _ = embedded_features.shape
    one_each = count == lax.axis_size("tm") == SUBLANES and steps == LANES
    return (whole_series if one_each else shards)(embedded_features, *others)


def solution(mesh):
    placed = (
        P("dp", "tm", None),
        P("dp"),
        P("dp"),
        P("dp", None),
        P("dp", None),
        P("dp", None),
        P("dp", None),
        P("dp", None),
        P("dp", None),
        P("dp", None),
        P("dp", None),
        P("dp", None),
        P("dp", None),
        P("dp", "tm", None),
        P("dp", None, "tm"),
    )
    return jax.shard_map(
        on_device,
        mesh=mesh,
        in_specs=placed,
        out_specs=(
            P("dp", "tm", None),
            P("dp", None, "tm"),
            P("dp", "tm", None),
            P("dp", None),
            P("dp", None),
            P("dp", None),
            P("dp", None),
            P("dp", None),
            P("dp", None),
            P("dp", None),
            P("dp", None),
            P("dp", None),
            P("dp", None),
        ),
        check_vma=False,
    )
```

```python
import types

import jax
import jax.numpy as jnp
from jax import lax
from jax.experimental import pallas as pl
from jax.experimental.pallas import tpu as pltpu
from jax.sharding import PartitionSpec as P

HEADS = 4
LEVEL_TALLY = 3
DEC = 24
MICRO = 2


EPSILON = 1e-05
NEG_BIG = -1e30
attend_group = 2
LOG2_E = 1.4426950408889634
VMEM_BYTES = 60 * 2**20


def entering(value, axis, join, neutral, backward):
    count, mine = (lax.axis_size(axis), lax.axis_index(axis))
    pieces = jax.tree.map(lambda part: lax.all_gather(part, axis), value)
    if backward:
        pieces = jax.tree.map(lambda part: part[::-1], pieces)
        mine = count - 1 - mine
    so_far = jax.tree.map(
        lambda part, zero: jnp.full_like(part, 0) + jnp.asarray(zero, part.dtype), value, neutral
    )

    def turn(position, so_far):
        longer = join(so_far, jax.tree.map(lambda part: part[position], pieces))
        return jax.tree.map(lambda new, old: jnp.where(position < mine, new, old), longer, so_far)

    return lax.fori_loop(0, count - 1, turn, so_far)


def narrow_convert(values):
    return values.astype(jnp.bfloat16)


def tensor_dot_plain(left, right):
    return jnp.dot(left, right, preferred_element_type=jnp.float32)


def flipped_dot(left, right):
    return lax.dot_general(
        left, right, (((0,), (0,)), ((), ())), preferred_element_type=jnp.float32
    )


def dot_against_flipped(left, right):
    return lax.dot_general(
        left, right, (((1,), (1,)), ((), ())), preferred_element_type=jnp.float32
    )


def affine_join(earlier, later):
    return (later[0] * earlier[0], later[0] * earlier[1] + later[1])


def layer_norm(values, gains, offsets):
    centred = values - jnp.mean(values, axis=-1, keepdims=True)
    spread = jnp.mean(centred * centred, axis=-1, keepdims=True)
    return centred * lax.rsqrt(spread + EPSILON) * gains + offsets


def gated_unit(pre_act):
    half_width = pre_act.shape[-1] // 2
    return pre_act[..., :half_width] * jax.nn.sigmoid(pre_act[..., half_width:])


def lstm_gates(pre_act, keep_mask):
    quarter = pre_act.shape[-1] // 4
    forget = jax.nn.sigmoid(pre_act[..., :quarter]) * keep_mask
    inflow = jax.nn.sigmoid(pre_act[..., quarter : 2 * quarter]) * jnp.tanh(
        pre_act[..., 2 * quarter : 3 * quarter]
    )
    out_gate = jax.nn.sigmoid(pre_act[..., 3 * quarter :])
    return (forget, inflow, out_gate)


def masked_scores(query_block, key_block, query_pos, key_pos, begin_block, scale):
    raw = jnp.einsum("gqhd,gkhd->ghqk", query_block, key_block, preferred_element_type=jnp.float32)
    lowest = jnp.minimum(begin_block[:, None], query_pos[None, :])
    allowed = (key_pos[None, None, :] <= query_pos[None, :, None]) & (
        key_pos[None, None, :] >= lowest[:, :, None]
    )
    return jnp.where(allowed[:, None], raw * scale, NEG_BIG)


def score_grad(chances, dprob, row_delta, scale):
    return narrow_convert(chances * (dprob[:, None] - row_delta[..., None]) * scale)


def shards(
    embedded_features,
    earliest_seen_moment,
    reach_choice,
    lstm_valve_coeffs,
    lstm_unit_coeffs,
    asker_lookup_coeffs,
    attend_exit_coeffs,
    attend_unit_coeffs,
    skipnet_entry_coeffs,
    skipnet_inner_coeffs,
    skipnet_unit_coeffs,
    level_map_coeffs,
    bias_gain_table,
    block_emit_adjoint,
    predicted_adjoint,
):
    (
        mat_lstm,
        mat_glu_one,
        mat_qkv,
        mat_attn,
        mat_glu_two,
        mat_inner,
        mat_middle,
        mat_glu_three,
        level_dot,
        vec_table,
    ) = (
        lax.all_gather(narrow_convert(lstm_valve_coeffs), "dp", axis=0, tiled=True),
        lax.all_gather(narrow_convert(lstm_unit_coeffs), "dp", axis=0, tiled=True),
        lax.all_gather(narrow_convert(asker_lookup_coeffs), "dp", axis=0, tiled=True),
        lax.all_gather(narrow_convert(attend_exit_coeffs), "dp", axis=0, tiled=True),
        lax.all_gather(narrow_convert(attend_unit_coeffs), "dp", axis=0, tiled=True),
        lax.all_gather(narrow_convert(skipnet_entry_coeffs), "dp", axis=0, tiled=True),
        lax.all_gather(narrow_convert(skipnet_inner_coeffs), "dp", axis=0, tiled=True),
        lax.all_gather(narrow_convert(skipnet_unit_coeffs), "dp", axis=0, tiled=True),
        lax.all_gather(narrow_convert(level_map_coeffs), "dp", axis=0, tiled=True),
        lax.all_gather(narrow_convert(bias_gain_table), "dp", axis=0, tiled=True),
    )
    series_per_device, steps_per_device, model_width = embedded_features.shape
    seq_total = steps_per_device * lax.axis_size("tm")
    head_width = model_width // HEADS
    count_of_rows = series_per_device * steps_per_device
    scale = head_width ** (-0.5)
    vec_full = vec_table.astype(jnp.float32)
    time_local = lax.axis_index("tm") * steps_per_device + jnp.arange(
        steps_per_device, dtype=jnp.int32
    )
    time_all = jnp.arange(seq_total, dtype=jnp.int32)
    horizon_len = jnp.where(reach_choice == 0, 1, jnp.where(reach_choice == 1, 5, 24))
    ahead_moment_filter = (
        (
            (time_local[None, :] >= seq_total - DEC)
            & (time_local[None, :] < seq_total - DEC + horizon_len[:, None])
        )
        .astype(jnp.float32)
        .reshape(count_of_rows, 1)
    )
    keep_mask = (
        (time_local[None, :] != earliest_seen_moment[:, None])
        .astype(jnp.float32)
        .reshape(count_of_rows, 1)
    )
    group_size = series_per_device // MICRO
    group_total = series_per_device // attend_group
    state_ones = jnp.ones((group_size, model_width), jnp.float32)
    state_zeros = jnp.zeros((group_size, model_width), jnp.float32)

    def split_groups(array):
        return array.reshape((group_total, attend_group) + array.shape[1:])

    input_rows = embedded_features.reshape(count_of_rows, model_width)
    input_full = input_rows.astype(jnp.float32)
    lstm_pre = tensor_dot_plain(input_rows, mat_lstm) + vec_full[:, 0:4].T.reshape(-1)
    forget, inflow, out_gate = lstm_gates(lstm_pre, keep_mask)
    forget_seq = forget.reshape(series_per_device, steps_per_device, model_width)
    inflow_seq = inflow.reshape(series_per_device, steps_per_device, model_width)
    mult_seq, cell_local = lax.associative_scan(affine_join, (forget_seq, inflow_seq), axis=1)
    cell_parts = []
    for group in range(MICRO):
        lower_row = group * group_size
        upper_row = lower_row + group_size
        _, arriving = entering(
            (mult_seq[lower_row:upper_row, -1], cell_local[lower_row:upper_row, -1]),
            "tm",
            affine_join,
            (state_ones, state_zeros),
            False,
        )
        cell_parts.append(arriving)
    cell_in = jnp.concatenate(cell_parts, axis=0)
    cell_seq = cell_local + mult_seq * cell_in[:, None, :]
    cell_tanh = jnp.tanh(cell_seq.reshape(count_of_rows, model_width))
    hidden_low = narrow_convert(out_gate * cell_tanh)
    glu_one_pre = tensor_dot_plain(hidden_low, mat_glu_one) + vec_full[:, 4:6].T.reshape(-1)
    first_sum = input_full + gated_unit(glu_one_pre)
    first = layer_norm(first_sum, vec_full[:, 6], vec_full[:, 7])
    first_low = narrow_convert(first)
    qkv_low = narrow_convert(tensor_dot_plain(first_low, mat_qkv))
    query_low = qkv_low[:, :model_width].reshape(
        series_per_device, steps_per_device, HEADS, head_width
    )
    key_value = qkv_low[:, model_width:].reshape(
        series_per_device, steps_per_device, model_width + head_width
    )
    key_value_all = lax.all_gather(key_value, "tm", axis=1, tiled=True)
    keys_all = key_value_all[..., :model_width].reshape(
        series_per_device, seq_total, HEADS, head_width
    )
    values_all = key_value_all[..., model_width:]

    def attend_forward(block_args):
        query_block, key_block, value_block, begin_block = block_args
        scores = masked_scores(query_block, key_block, time_local, time_all, begin_block, scale)
        row_top = jnp.max(scores, axis=-1, keepdims=True)
        row_exp = jnp.exp(scores - row_top)
        row_total = jnp.sum(row_exp, axis=-1, keepdims=True)
        weights_low = narrow_convert(row_exp / row_total)
        mixed_block = jnp.einsum(
            "ghqk,gkd->gqd", weights_low, value_block, preferred_element_type=jnp.float32
        ) * (1.0 / HEADS)
        return (mixed_block, (row_top + jnp.log(row_total))[..., 0])

    mixed, log_total = lax.map(
        attend_forward,
        (
            split_groups(query_low),
            split_groups(keys_all),
            split_groups(values_all),
            split_groups(earliest_seen_moment),
        ),
    )
    mixed_low = narrow_convert(mixed.reshape(count_of_rows, head_width))
    attn_low = narrow_convert(tensor_dot_plain(mixed_low, mat_attn))
    glu_two_pre = tensor_dot_plain(attn_low, mat_glu_two) + vec_full[:, 8:10].T.reshape(-1)
    second_sum = first + gated_unit(glu_two_pre)
    second = layer_norm(second_sum, vec_full[:, 10], vec_full[:, 11])
    second_low = narrow_convert(second)
    inner_pre = tensor_dot_plain(second_low, mat_inner) + vec_full[:, 12]
    inner_low = narrow_convert(jax.nn.elu(inner_pre))
    middle_low = narrow_convert(tensor_dot_plain(inner_low, mat_middle) + vec_full[:, 13])
    glu_three_pre = tensor_dot_plain(middle_low, mat_glu_three) + vec_full[:, 14:16].T.reshape(-1)
    final_sum = second + gated_unit(glu_three_pre)
    second_block_emit = layer_norm(final_sum, vec_full[:, 16], vec_full[:, 17])
    closing_narrowed = narrow_convert(second_block_emit)
    predicted_entries = tensor_dot_plain(closing_narrowed, level_dot) * ahead_moment_filter
    predicted_levels = predicted_entries.reshape(
        series_per_device, steps_per_device, LEVEL_TALLY
    ).transpose(0, 2, 1)
    predicted_slope = narrow_convert(
        predicted_adjoint.astype(jnp.float32).transpose(0, 2, 1).reshape(count_of_rows, LEVEL_TALLY)
        * ahead_moment_filter
    )
    level_slope = flipped_dot(closing_narrowed, predicted_slope)
    final_grad = block_emit_adjoint.reshape(count_of_rows, model_width).astype(
        jnp.float32
    ) + dot_against_flipped(predicted_slope, level_dot)
    _, norm_pull = jax.vjp(layer_norm, final_sum, vec_full[:, 16], vec_full[:, 17])
    sum_three_grad, gain_three_grad, offset_three_grad = norm_pull(final_grad)
    _, glu_pull = jax.vjp(gated_unit, glu_three_pre)
    (glu_three_grad,) = glu_pull(sum_three_grad)
    glu_three_low = narrow_convert(glu_three_grad)
    grad_glu_three = flipped_dot(middle_low, glu_three_low)
    middle_grad = dot_against_flipped(glu_three_low, mat_glu_three)
    middle_grad_low = narrow_convert(middle_grad)
    grad_middle = flipped_dot(inner_low, middle_grad_low)
    inner_grad = dot_against_flipped(middle_grad_low, mat_middle)
    _, elu_pull = jax.vjp(jax.nn.elu, inner_pre)
    (inner_pre_grad,) = elu_pull(inner_grad)
    inner_pre_low = narrow_convert(inner_pre_grad)
    grad_inner = flipped_dot(second_low, inner_pre_low)
    second_grad = sum_three_grad + dot_against_flipped(inner_pre_low, mat_inner)
    _, norm_pull = jax.vjp(layer_norm, second_sum, vec_full[:, 10], vec_full[:, 11])
    sum_two_grad, gain_two_grad, offset_two_grad = norm_pull(second_grad)
    _, glu_pull = jax.vjp(gated_unit, glu_two_pre)
    (glu_two_grad,) = glu_pull(sum_two_grad)
    glu_two_low = narrow_convert(glu_two_grad)
    grad_glu_two = flipped_dot(attn_low, glu_two_low)
    attn_grad_low = narrow_convert(dot_against_flipped(glu_two_low, mat_glu_two))
    grad_attn = flipped_dot(mixed_low, attn_grad_low)
    mixed_grad_low = narrow_convert(dot_against_flipped(attn_grad_low, mat_attn))
    head_grad = (mixed_grad_low * (1.0 / HEADS)).reshape(
        series_per_device, steps_per_device, head_width
    )

    def attend_backward(block_args):
        query_block, key_block, value_block, begin_block, lse_block, dout_block = block_args
        scores = masked_scores(query_block, key_block, time_local, time_all, begin_block, scale)
        chances = jnp.exp(scores - lse_block[..., None])
        dprob = jnp.einsum(
            "gqd,gkd->gqk", dout_block, value_block, preferred_element_type=jnp.float32
        )
        row_delta = jnp.sum(chances * dprob[:, None], axis=-1)
        dscore = score_grad(chances, dprob, row_delta, scale)
        dquery = jnp.einsum(
            "ghqk,gkhd->gqhd", dscore, key_block, preferred_element_type=jnp.float32
        )
        dkey = jnp.einsum(
            "ghqk,gqhd->gkhd", dscore, query_block, preferred_element_type=jnp.float32
        )
        dvalue = jnp.einsum(
            "ghqk,gqd->gkd", narrow_convert(chances), dout_block, preferred_element_type=jnp.float32
        )
        key_terms = jnp.concatenate(
            [dkey.reshape(attend_group, seq_total, model_width), dvalue], axis=-1
        )
        return (dquery, key_terms)

    dquery, key_terms = lax.map(
        attend_backward,
        (
            split_groups(query_low),
            split_groups(keys_all),
            split_groups(values_all),
            split_groups(earliest_seen_moment),
            log_total,
            split_groups(head_grad),
        ),
    )
    own_keys = lax.psum_scatter(
        key_terms.reshape(series_per_device, seq_total, model_width + head_width),
        "tm",
        scatter_dimension=1,
        tiled=True,
    )
    qkv_grad = jnp.concatenate(
        [
            dquery.reshape(count_of_rows, model_width),
            own_keys.reshape(count_of_rows, model_width + head_width),
        ],
        axis=1,
    )
    qkv_grad_low = narrow_convert(qkv_grad)
    grad_qkv = flipped_dot(first_low, qkv_grad_low)
    first_grad = sum_two_grad + dot_against_flipped(qkv_grad_low, mat_qkv)
    _, norm_pull = jax.vjp(layer_norm, first_sum, vec_full[:, 6], vec_full[:, 7])
    sum_one_grad, gain_one_grad, offset_one_grad = norm_pull(first_grad)
    _, glu_pull = jax.vjp(gated_unit, glu_one_pre)
    (glu_one_grad,) = glu_pull(sum_one_grad)
    glu_one_low = narrow_convert(glu_one_grad)
    grad_glu_one = flipped_dot(hidden_low, glu_one_low)
    hidden_grad = dot_against_flipped(glu_one_low, mat_glu_one)
    out_gate_grad = hidden_grad * cell_tanh
    direct_grad = (hidden_grad * out_gate * (1.0 - cell_tanh * cell_tanh)).reshape(
        series_per_device, steps_per_device, model_width
    )
    next_forget = jnp.concatenate([forget_seq[:, 1:], jnp.ones_like(forget_seq[:, :1])], axis=1)
    rev_mult, rev_cell = lax.associative_scan(
        affine_join, (next_forget, direct_grad), axis=1, reverse=True
    )
    head_mult = forget_seq[:, 0] * rev_mult[:, 0]
    head_cell = forget_seq[:, 0] * rev_cell[:, 0]
    coming_parts = []
    for group in range(MICRO):
        lower_row = group * group_size
        upper_row = lower_row + group_size
        _, coming = entering(
            (head_mult[lower_row:upper_row], head_cell[lower_row:upper_row]),
            "tm",
            affine_join,
            (state_ones, state_zeros),
            True,
        )
        coming_parts.append(coming)
    coming_all = jnp.concatenate(coming_parts, axis=0)
    cell_grad = rev_cell + rev_mult * coming_all[:, None, :]
    cell_prev = jnp.concatenate([cell_in[:, None, :], cell_seq[:, :-1]], axis=1)
    forget_grad = (cell_grad * cell_prev).reshape(count_of_rows, model_width)
    _, gate_pull = jax.vjp(lambda pre_value: lstm_gates(pre_value, keep_mask), lstm_pre)
    (lstm_pre_grad,) = gate_pull(
        (forget_grad, cell_grad.reshape(count_of_rows, model_width), out_gate_grad)
    )
    lstm_low = narrow_convert(lstm_pre_grad)
    grad_lstm = flipped_dot(input_rows, lstm_low)
    input_grad = sum_one_grad + dot_against_flipped(lstm_low, mat_lstm)
    grad_table = jnp.concatenate(
        [
            jnp.sum(lstm_pre_grad, axis=0).reshape(4, model_width).T,
            jnp.sum(glu_one_grad, axis=0).reshape(2, model_width).T,
            gain_one_grad[:, None],
            offset_one_grad[:, None],
            jnp.sum(glu_two_grad, axis=0).reshape(2, model_width).T,
            gain_two_grad[:, None],
            offset_two_grad[:, None],
            jnp.sum(inner_pre_grad, axis=0)[:, None],
            jnp.sum(middle_grad, axis=0)[:, None],
            jnp.sum(glu_three_grad, axis=0).reshape(2, model_width).T,
            gain_three_grad[:, None],
            offset_three_grad[:, None],
        ],
        axis=1,
    )
    (
        whole_lstm,
        whole_glu_one,
        whole_qkv,
        whole_attn,
        whole_glu_two,
        whole_inner,
        whole_middle,
        whole_glu_three,
        whole_quant,
        whole_table,
    ) = lax.psum(
        (
            grad_lstm,
            grad_glu_one,
            grad_qkv,
            grad_attn,
            grad_glu_two,
            grad_inner,
            grad_middle,
            grad_glu_three,
            level_slope,
            grad_table,
        ),
        "tm",
    )
    summed = (
        lax.psum_scatter(
            whole_lstm.astype(jnp.bfloat16), "dp", scatter_dimension=0, tiled=True
        ).astype(jnp.float32),
        lax.psum_scatter(
            whole_glu_one.astype(jnp.bfloat16), "dp", scatter_dimension=0, tiled=True
        ).astype(jnp.float32),
        lax.psum_scatter(
            whole_qkv.astype(jnp.bfloat16), "dp", scatter_dimension=0, tiled=True
        ).astype(jnp.float32),
        lax.psum_scatter(
            whole_attn.astype(jnp.bfloat16), "dp", scatter_dimension=0, tiled=True
        ).astype(jnp.float32),
        lax.psum_scatter(
            whole_glu_two.astype(jnp.bfloat16), "dp", scatter_dimension=0, tiled=True
        ).astype(jnp.float32),
        lax.psum_scatter(
            whole_inner.astype(jnp.bfloat16), "dp", scatter_dimension=0, tiled=True
        ).astype(jnp.float32),
        lax.psum_scatter(
            whole_middle.astype(jnp.bfloat16), "dp", scatter_dimension=0, tiled=True
        ).astype(jnp.float32),
        lax.psum_scatter(
            whole_glu_three.astype(jnp.bfloat16), "dp", scatter_dimension=0, tiled=True
        ).astype(jnp.float32),
        lax.psum_scatter(
            whole_quant.astype(jnp.bfloat16), "dp", scatter_dimension=0, tiled=True
        ).astype(jnp.float32),
        lax.psum_scatter(
            whole_table.astype(jnp.bfloat16), "dp", scatter_dimension=0, tiled=True
        ).astype(jnp.float32),
    )
    final_out = second_block_emit.astype(jnp.bfloat16).reshape(
        series_per_device, steps_per_device, model_width
    )
    input_out = input_grad.astype(jnp.bfloat16).reshape(
        series_per_device, steps_per_device, model_width
    )
    return (
        final_out,
        predicted_levels,
        input_out,
        summed[0],
        summed[1],
        summed[2],
        summed[3],
        summed[4],
        summed[5],
        summed[6],
        summed[7],
        summed[8],
        summed[9],
    )


def lane_head(shape, head_width, head):
    lane = lax.broadcasted_iota(jnp.int32, shape, len(shape) - 1)
    return (lane >= head * head_width) & (lane < (head + 1) * head_width)


FORGET, ENTER, CANDIDATE, EXIT = 0, 256, 512, 768
GLU_ONE_A, GLU_ONE_B = 1024, 1280
QUERY, KEY, VALUE = 1536, 1792, 2048
GLU_TWO_A, GLU_TWO_B = 2176, 2432
INNER, MIDDLE = 2688, 2944
GLU_THREE_A, GLU_THREE_B = 3200, 3456
ATTN_OUT = 3712
PACKED = 3968
VECTORS = 24
LANES = 128
SUBLANES = 8
CHUNKS = 64
TILE = 256


def nn(left, right):
    return jnp.dot(left, right, preferred_element_type=jnp.float32)


def nt(left, right):
    return lax.dot_general(
        left, right, (((1,), (1,)), ((), ())), preferred_element_type=jnp.float32
    )


def tn(left, right):
    return lax.dot_general(
        left, right, (((0,), (0,)), ((), ())), preferred_element_type=jnp.float32
    )


def low(values):
    return values.astype(jnp.bfloat16)


def sigmoid(values):
    return 0.5 * jnp.tanh(0.5 * values) + 0.5


def normalise(values, gain, shift):
    centred = values - jnp.mean(values, axis=-1, keepdims=True)
    spread = jnp.mean(centred * centred, axis=-1, keepdims=True)
    inverse = lax.rsqrt(spread + EPSILON)
    unit = centred * inverse
    return unit * gain + shift, unit, inverse


def normalise_back(grad, unit, inverse, gain):
    scaled = grad * gain
    return inverse * (
        scaled
        - jnp.mean(scaled, axis=-1, keepdims=True)
        - unit * jnp.mean(scaled * unit, axis=-1, keepdims=True)
    )


def rows_of(tile, size):
    return pl.ds(pl.multiple_of(tile * size, size), size)


def put_halves(ref, rows, values):
    ref[0, rows, :] = values[:, :LANES]
    ref[1, rows, : values.shape[1] - LANES] = values[:, LANES:]


def get_halves(ref, rows, width):
    return jnp.concatenate([ref[0, rows, :], ref[1, rows, : width - LANES]], axis=1)


def row_sum(ref, column, values):
    ref[column : column + 1, :] = jnp.sum(values, axis=0, keepdims=True)


def series_scratch(span, width, head_width):
    full = pltpu.VMEM((span, width), jnp.float32)
    half = pltpu.VMEM((span, width), jnp.bfloat16)
    flat = pltpu.VMEM((width, span), jnp.bfloat16)
    scan = pltpu.VMEM((2, span, LANES), jnp.float32)
    scan_more = pltpu.VMEM((2, span + 8, LANES), jnp.float32)
    narrow = pltpu.VMEM((span, head_width), jnp.bfloat16)
    column = pltpu.VMEM((span, 1), jnp.float32)
    tiles = span // TILE
    return dict(
        forget=scan_more,
        local=scan,
        mult=scan,
        cell=scan_more,
        carry=pltpu.VMEM((2, CHUNKS, LANES), jnp.float32),
        enter_gate=full,
        candidate=full,
        exit_gate=full,
        cell_tanh=full,
        hidden=half,
        glu_one=full,
        gate_one=full,
        unit_one=full,
        inverse_one=column,
        first_low=half,
        keys=pltpu.VMEM((span, width + 1), jnp.bfloat16),
        values=narrow,
        head_queries=pltpu.VMEM((HEADS, span, width + 1), jnp.bfloat16),
        head_keys=pltpu.VMEM((HEADS, span, width), jnp.bfloat16),
        **{
            "chances%d" % tile: pltpu.VMEM((HEADS, TILE, (tile + 1) * TILE), jnp.float32)
            for tile in range(tiles)
        },
        chance_sum=pltpu.VMEM((span, span), jnp.bfloat16),
        **{
            "score_grads%d" % tile: pltpu.VMEM((HEADS, span - tile * TILE, TILE), jnp.bfloat16)
            for tile in range(tiles)
        },
        block=pltpu.VMEM((TILE, span), jnp.float32),
        mixed=narrow,
        mixed_grad=narrow,
        sum_two_grad=full,
        query_grad=half,
        key_grad=half,
        value_grad=narrow,
        gate_grads=pltpu.VMEM((4, span, width), jnp.bfloat16),
        x=half,
        x_flat=flat,
        adjoint=flat,
        out=flat,
        input_grad=flat,
        w=pltpu.VMEM((width, PACKED), jnp.bfloat16),
        vec=pltpu.VMEM((VECTORS, width), jnp.float32),
        level=pltpu.VMEM((8, width), jnp.bfloat16),
        gv=pltpu.VMEM((VECTORS + 8, width), jnp.float32),
        slope=pltpu.VMEM((8, LANES), jnp.float32),
        predicted=pltpu.VMEM((8, LANES), jnp.float32),
        attn_flat=pltpu.VMEM((width, 2 * width // 5), jnp.float32),
        lstm_flat=pltpu.VMEM((width, 4 * LANES), jnp.float32),
        middle_send=pltpu.VMEM((2, width, GROUP_LANES["middle"]), jnp.bfloat16),
        first_send=pltpu.VMEM((2, width, GROUP_LANES["first"]), jnp.bfloat16),
        lstm_send=pltpu.VMEM((2, width, GROUP_LANES["lstm"]), jnp.bfloat16),
    )


def series_turn(r, chunk, steps):
    rows = rows_of(chunk, steps)
    r.x[rows, :] = r.x_flat[:, rows].T


def series_gates(r, begin):
    w, vec = r.w, r.vec
    span, width = r.x.shape
    rows = slice(0, span)
    x = r.x[...]

    def pre(block, column):
        return nn(x, w[:, block : block + width]) + vec[column : column + 1, :]

    time = lax.broadcasted_iota(jnp.int32, (span, width), 0)
    put_halves(r.forget, rows, jnp.where(time != begin, sigmoid(pre(FORGET, 0)), 0.0))
    enter = sigmoid(pre(ENTER, 1))
    candidate = jnp.tanh(pre(CANDIDATE, 2))
    r.enter_gate[...] = enter
    r.candidate[...] = candidate
    put_halves(r.local, rows, enter * candidate)
    r.exit_gate[...] = sigmoid(pre(EXIT, 3))


def scan_state():
    zeros = jnp.zeros((SUBLANES, LANES), jnp.float32)
    return ((zeros, zeros + 1.0),) * (2 * CHUNKS // SUBLANES)


def scan_step(r, steps, t, after, state):
    out = []
    for index, (value, mult) in enumerate(state):
        half, start = index % 2, index // 2 * SUBLANES * steps
        at = pl.ds(start + t, SUBLANES, stride=steps)
        forget = r.forget[half, pl.ds(start + t + after, SUBLANES, stride=steps), :]
        value = forget * value + r.local[half, at, :]
        mult = mult * forget
        r.local[half, at, :] = value
        r.mult[half, at, :] = mult
        out.append((value, mult))
    return tuple(out)


def scan_carry(r, ends, order):
    for half in range(2):
        state = jnp.zeros((1, LANES), jnp.float32)
        for chunk in order:
            r.carry[half, chunk : chunk + 1, :] = state
            value, mult = ends[chunk // SUBLANES * 2 + half]
            at = chunk % SUBLANES
            state = value[at : at + 1] + mult[at : at + 1] * state


def series_forward_scan(r):
    steps = r.x.shape[0] // CHUNKS
    ends = scan_state()
    for t in range(steps):
        ends = scan_step(r, steps, t, 0, ends)
    scan_carry(r, ends, range(CHUNKS))
    for half in range(2):
        r.cell[half, 0:8, :] = jnp.zeros((8, LANES), jnp.float32)


def series_forward_first(r, begin):
    w, vec = r.w, r.vec
    span, width = r.x.shape
    head_width = width // HEADS
    steps = span // CHUNKS
    for chunk in range(CHUNKS):
        rows = slice(chunk * steps, (chunk + 1) * steps)
        later = slice(chunk * steps + 8, (chunk + 1) * steps + 8)
        for half in range(2):
            r.cell[half, later, :] = (
                r.local[half, rows, :]
                + r.mult[half, rows, :] * r.carry[half, chunk : chunk + 1, :]
            )
    tanh = jnp.tanh(get_halves(r.cell, slice(8, 8 + span), width))
    r.cell_tanh[...] = tanh
    hidden = low(r.exit_gate[...] * tanh)
    r.hidden[...] = hidden
    value = nn(hidden, w[:, GLU_ONE_A : GLU_ONE_A + width]) + vec[4:5, :]
    gate = sigmoid(nn(hidden, w[:, GLU_ONE_B : GLU_ONE_B + width]) + vec[5:6, :])
    r.glu_one[...] = value
    r.gate_one[...] = gate
    out, unit, inverse = normalise(
        r.x[...].astype(jnp.float32) + value * gate, vec[6:7, :], vec[7:8, :]
    )
    r.unit_one[...] = unit
    r.inverse_one[...] = inverse
    out = low(out)
    r.first_low[...] = out
    query = low(nn(out, w[:, QUERY : QUERY + width]))
    key = low(nn(out, w[:, KEY : KEY + width]))
    time = lax.broadcasted_iota(jnp.int32, (span, 1), 0)
    r.keys[...] = jnp.concatenate([key, low(jnp.where(time < begin, NEG_BIG, 0.0))], axis=1)
    one = jnp.ones((span, 1), jnp.bfloat16)
    r.values[...] = low(nn(out, w[:, VALUE : VALUE + head_width]))
    for head in range(HEADS):
        mine = lane_head((span, width), head_width, head)
        r.head_queries[head] = jnp.concatenate(
            [jnp.where(mine, query, jnp.zeros_like(query)), one], axis=1
        )
        r.head_keys[head] = jnp.where(mine, key, jnp.zeros_like(key))


def series_forward_attention(r, begin, between):
    span, head_width = r.values.shape
    width = head_width * HEADS
    scale = head_width ** (-0.5) * LOG2_E
    row = lax.broadcasted_iota(jnp.int32, (TILE, TILE), 0)
    col = lax.broadcasted_iota(jnp.int32, (TILE, TILE), 1)
    for tile in range(span // TILE):
        start, seen = tile * TILE, (tile + 1) * TILE
        rows = slice(start, seen)
        chances = getattr(r, "chances%d" % tile)
        r.block[:, :TILE] = jnp.where(
            (col <= row) & (col >= jnp.minimum(begin - start, row)), 0.0, NEG_BIG
        )
        for head in range(HEADS):
            near = (
                nt(r.head_queries[head, rows, :width], r.keys[rows, :width]) + r.block[:, :TILE]
            )
            top = jnp.max(near, axis=-1, keepdims=True)
            if tile:
                far = nt(r.head_queries[head, rows, :], r.keys[:start, :])
                top = jnp.maximum(top, jnp.max(far, axis=-1, keepdims=True))
                far = jnp.exp2((far - top) * scale)
            near = jnp.exp2((near - top) * scale)
            total = jnp.sum(near, axis=-1, keepdims=True)
            if tile:
                total = total + jnp.sum(far, axis=-1, keepdims=True)
            share = 1.0 / total
            chances[head, :, start:] = near * share
            if tile:
                chances[head, :, :start] = far * share
        weights = chances[0]
        for head in range(1, HEADS):
            weights = weights + chances[head]
        weights = low(weights)
        r.chance_sum[rows, :seen] = weights
        r.mixed[rows, :] = low(nn(weights, r.values[:seen, :]) * (1.0 / HEADS))
        between(tile)


def series_middle(r, horizon, after_forward):
    w, vec, gv = r.w, r.vec, r.gv
    span, width = r.x.shape
    head_width = width // HEADS
    first = r.unit_one[...] * vec[6:7, :] + vec[7:8, :]
    mixed = r.mixed[...]
    attn = low(nn(mixed, w[:head_width, ATTN_OUT : ATTN_OUT + width]))
    value_two = nn(attn, w[:, GLU_TWO_A : GLU_TWO_A + width]) + vec[8:9, :]
    gate_two = sigmoid(nn(attn, w[:, GLU_TWO_B : GLU_TWO_B + width]) + vec[9:10, :])
    second, unit_two, inverse_two = normalise(
        first + value_two * gate_two, vec[10:11, :], vec[11:12, :]
    )
    second_low = low(second)
    inner_pre = nn(second_low, w[:, INNER : INNER + width]) + vec[12:13, :]
    inner_exp = jnp.exp(jnp.minimum(inner_pre, 0.0))
    inner_low = low(jnp.where(inner_pre > 0, inner_pre, inner_exp - 1.0))
    middle_low = low(nn(inner_low, w[:, MIDDLE : MIDDLE + width]) + vec[13:14, :])
    value_three = nn(middle_low, w[:, GLU_THREE_A : GLU_THREE_A + width]) + vec[14:15, :]
    gate_three = sigmoid(nn(middle_low, w[:, GLU_THREE_B : GLU_THREE_B + width]) + vec[15:16, :])
    final, unit_three, inverse_three = normalise(
        second + value_three * gate_three, vec[16:17, :], vec[17:18, :]
    )
    final_low = low(final)
    r.out[...] = final_low.T
    steps = r.slope.shape[1]
    time = span - steps + lax.broadcasted_iota(jnp.int32, (8, steps), 1)
    ahead = jnp.where((time >= span - DEC) & (time < span - DEC + horizon), 1.0, 0.0)
    r.predicted[...] = nt(r.level[...], final_low[span - steps :]) * ahead
    after_forward()
    slope = low(r.slope[...] * ahead)
    gv[VECTORS : VECTORS + 8, :] = nn(slope, final_low[span - steps :])
    grad = r.adjoint[...].T.astype(jnp.float32)
    grad = jnp.concatenate(
        [grad[: span - steps], grad[span - steps :] + tn(slope, r.level[...])], axis=0
    )
    row_sum(gv, 16, grad * unit_three)
    row_sum(gv, 17, grad)
    sum_three = normalise_back(grad, unit_three, inverse_three, vec[16:17, :])
    grad_a = sum_three * gate_three
    grad_b = grad_a * value_three * (1.0 - gate_three)
    row_sum(gv, 14, grad_a)
    row_sum(gv, 15, grad_b)
    low_a, low_b = low(grad_a), low(grad_b)
    send = r.middle_send
    send[1, :, :width] = low(tn(middle_low, low_a))
    send[1, :, width : 2 * width] = low(tn(middle_low, low_b))
    middle_grad = nt(low_a, w[:, GLU_THREE_A : GLU_THREE_A + width]) + nt(
        low_b, w[:, GLU_THREE_B : GLU_THREE_B + width]
    )
    row_sum(gv, 13, middle_grad)
    middle_grad = low(middle_grad)
    send[1, :, 2 * width : 3 * width] = low(tn(inner_low, middle_grad))
    inner_grad = nt(middle_grad, w[:, MIDDLE : MIDDLE + width]) * jnp.where(
        inner_pre > 0, 1.0, inner_exp
    )
    row_sum(gv, 12, inner_grad)
    inner_grad = low(inner_grad)
    send[0, :, 2 * width : 3 * width] = low(tn(second_low, inner_grad))
    grad = sum_three + nt(inner_grad, w[:, INNER : INNER + width])
    row_sum(gv, 10, grad * unit_two)
    row_sum(gv, 11, grad)
    sum_two = normalise_back(grad, unit_two, inverse_two, vec[10:11, :])
    r.sum_two_grad[...] = sum_two
    grad_a = sum_two * gate_two
    grad_b = grad_a * value_two * (1.0 - gate_two)
    row_sum(gv, 8, grad_a)
    row_sum(gv, 9, grad_b)
    low_a, low_b = low(grad_a), low(grad_b)
    attn_grad = low(
        nt(low_a, w[:, GLU_TWO_A : GLU_TWO_A + width])
        + nt(low_b, w[:, GLU_TWO_B : GLU_TWO_B + width])
    )
    r.mixed_grad[...] = low(nt(attn_grad, w[:head_width, ATTN_OUT : ATTN_OUT + width]))
    send[0, :, :width] = low(tn(attn, low_a))
    send[0, :, width : 2 * width] = low(tn(attn, low_b))
    attn_weight = tn(mixed, attn_grad)
    rows, small = head_width, head_width // HEADS
    spare = width // 5
    r.attn_flat[...] = jnp.zeros_like(r.attn_flat)
    for group in range(HEADS):
        for piece in range(5):
            at = group * rows + small * (piece % 4)
            half = piece // 4
            r.attn_flat[at : at + small, half * spare : (half + 1) * spare] = attn_weight[
                group * small : (group + 1) * small, piece * spare : (piece + 1) * spare
            ]
    for half in range(2):
        send[half, :, 3 * width :] = low(r.attn_flat[:, half * spare : (half + 1) * spare])


def series_backward_attention(r, between):
    span, head_width = r.values.shape
    width = head_width * HEADS
    scale = head_width ** (-0.5)
    for tile in range(span // TILE):
        rows = slice(tile * TILE, (tile + 1) * TILE)
        seen = (tile + 1) * TILE
        held = getattr(r, "chances%d" % tile)
        head_grad = r.mixed_grad[rows, :] * (1.0 / HEADS)
        r.block[:, :seen] = nt(head_grad, r.values[:seen, :]) * scale
        total = jnp.zeros((TILE, width), jnp.float32)
        for head in range(HEADS):
            chances = held[head]
            slope = r.block[:, :seen]
            delta = jnp.sum(chances * slope, axis=-1, keepdims=True)
            grads = low(chances * (slope - delta))
            for part in range(tile + 1):
                getattr(r, "score_grads%d" % part)[
                    head, (tile - part) * TILE : (tile - part + 1) * TILE, :
                ] = grads[:, part * TILE : (part + 1) * TILE]
            total = total + nn(grads, r.head_keys[head, :seen, :])
        r.query_grad[rows, :] = low(total)
        between(tile)
    for tile in range(span // TILE):
        cols = slice(tile * TILE, (tile + 1) * TILE)
        start = tile * TILE
        total = jnp.zeros((TILE, width), jnp.float32)
        for head in range(HEADS):
            total = total + tn(
                getattr(r, "score_grads%d" % tile)[head],
                r.head_queries[head, start:, :width],
            )
        r.key_grad[cols, :] = low(total)
        r.value_grad[cols, :] = low(
            tn(r.chance_sum[start:, cols], r.mixed_grad[start:, :] * (1.0 / HEADS))
        )


def series_backward_first(r):
    w, vec, gv = r.w, r.vec, r.gv
    span, width = r.hidden.shape
    head_width = width // HEADS
    rows = slice(0, span)
    send = r.first_send
    query, key, value = r.query_grad[...], r.key_grad[...], r.value_grad[...]
    grad = (
        r.sum_two_grad[...]
        + nt(query, w[:, QUERY : QUERY + width])
        + nt(key, w[:, KEY : KEY + width])
        + nt(value, w[:, VALUE : VALUE + head_width])
    )
    first = r.first_low[...]
    send[1, :, :width] = low(tn(first, query))
    send[1, :, width : 2 * width] = low(tn(first, key))
    send[1, :, 2 * width : 2 * width + head_width] = low(tn(first, value))
    unit = r.unit_one[...]
    row_sum(gv, 6, grad * unit)
    row_sum(gv, 7, grad)
    sum_one = normalise_back(grad, unit, r.inverse_one[...], vec[6:7, :])
    r.sum_two_grad[...] = sum_one
    gate = r.gate_one[...]
    grad_a = sum_one * gate
    grad_b = grad_a * r.glu_one[...] * (1.0 - gate)
    row_sum(gv, 4, grad_a)
    row_sum(gv, 5, grad_b)
    low_a, low_b = low(grad_a), low(grad_b)
    hidden_grad = nt(low_a, w[:, GLU_ONE_A : GLU_ONE_A + width]) + nt(
        low_b, w[:, GLU_ONE_B : GLU_ONE_B + width]
    )
    tanh, gate = r.cell_tanh[...], r.exit_gate[...]
    put_halves(r.local, rows, hidden_grad * gate * (1.0 - tanh * tanh))
    exit_grad = hidden_grad * tanh * gate * (1.0 - gate)
    row_sum(gv, 3, exit_grad)
    exit_grad = low(exit_grad)
    r.gate_grads[3] = exit_grad
    hidden = r.hidden[...]
    send[0, :, :width] = low(tn(hidden, low_a))
    send[0, :, width : 2 * width] = low(tn(hidden, low_b))
    send[0, :, 2 * width : 3 * width] = low(nn(r.x_flat[...], exit_grad))


def series_backward_scan(r):
    span = r.x.shape[0]
    steps = span // CHUNKS
    for half in range(2):
        r.forget[half, span:, :] = jnp.zeros((8, LANES), jnp.float32)

    ends = scan_state()
    for t in range(steps - 1, -1, -1):
        ends = scan_step(r, steps, t, 1, ends)
    scan_carry(r, ends, range(CHUNKS - 1, -1, -1))


def series_gate_grads(r):
    gv = r.gv
    span, width = r.x.shape
    steps = span // CHUNKS
    for half in range(2):
        for chunk in range(CHUNKS):
            rows = slice(chunk * steps, (chunk + 1) * steps)
            r.local[half, rows, :] += r.mult[half, rows, :] * r.carry[half, chunk : chunk + 1, :]
    grad = get_halves(r.local, slice(0, span), width)
    forget = get_halves(r.forget, slice(0, span), width)
    before = get_halves(r.cell, slice(7, 7 + span), width)
    enter, candidate = r.enter_gate[...], r.candidate[...]
    for gate, one in enumerate(
        (
            grad * before * forget * (1.0 - forget),
            grad * candidate * enter * (1.0 - enter),
            grad * enter * (1.0 - candidate * candidate),
        )
    ):
        row_sum(gv, gate, one)
        one = low(one)
        r.gate_grads[gate] = one
        r.lstm_flat[:, gate * width : (gate + 1) * width] = nn(r.x_flat[...], one)
    r.lstm_flat[:, 3 * width :] = gv[...].T
    lanes = r.lstm_send.shape[2]
    for half in range(2):
        r.lstm_send[half] = low(r.lstm_flat[:, half * lanes : (half + 1) * lanes])


def series_input_grad(r):
    width = r.x.shape[1]
    out = r.sum_two_grad[...].T
    for gate, block in enumerate((FORGET, ENTER, CANDIDATE, EXIT)):
        out = out + nt(r.w[:, block : block + width], r.gate_grads[gate])
    r.input_grad[...] = low(out)


class Exchange:
    def __init__(self, sems, devices, source, target, sources, targets):
        self.sems, self.source, self.target = sems, source, target
        self.sources, self.targets = sources, targets
        self.count, self.me, self.device = devices

    def other(self, step):
        return lax.rem(self.me + step, self.count)

    def copy(self, to, source, target):
        return pltpu.make_async_remote_copy(
            src_ref=source,
            dst_ref=target,
            send_sem=self.sems.at[0],
            recv_sem=self.sems.at[1],
            device_id=self.device(to),
            device_id_type=pl.DeviceIdType.MESH,
        )

    def one(self, to):
        return self.copy(to, self.source(to), self.target(self.me))

    def start(self):
        for step in range(1, self.count):
            self.one(self.other(step)).start()

    def all(self):
        return self.copy(self.other(1), self.sources, self.targets)

    def arrive(self):
        self.all().wait_recv()

    def sent(self):
        self.all().wait_send()


def over_time():
    return lax.axis_size("tm"), lax.axis_index("tm"), lambda to: {"tm": to}


def over_series():
    return lax.axis_size("dp"), lax.axis_index("dp"), lambda to: {"dp": to}


def over_chips():
    core = my_core()
    return (
        lax.axis_size("tm") // 2,
        lax.div(lax.axis_index("tm"), 2),
        lambda to: {"tm": 2 * to + core},
    )


def my_core():
    return lax.rem(lax.axis_index("tm"), 2)


def to_other_core(source, target, sems, index):
    return pltpu.make_async_remote_copy(
        src_ref=source,
        dst_ref=target,
        send_sem=sems.at[0, index],
        recv_sem=sems.at[1, index],
        device_id={"tm": lax.axis_index("tm") + 1 - 2 * my_core()},
        device_id_type=pl.DeviceIdType.MESH,
    )


GROUP_COLUMNS = (384, 384, 640)
GROUP_LANES = {"middle": 512, "first": 512, "lstm": 256}
DIRECT = ("lstm",)


def fold(values):
    lanes = values.shape[1] // 2
    return low(jnp.concatenate([values[:, :lanes], values[:, lanes:]], axis=0))


def unfold(values):
    rows = values.shape[0] // 2
    return jnp.concatenate([values[:rows], values[rows:]], axis=1)


def travel_scratch(count, groups, steps, width, params):
    rows = params[0].shape[0]
    out = dict(
        slopes=pltpu.VMEM((count, 8, steps), jnp.float32),
        levels=pltpu.VMEM((count, 8, steps), jnp.float32),
        stage=pltpu.VMEM((width, 2 * GROUP_COLUMNS[2]), jnp.float32),
        attn_stage=pltpu.VMEM((width, width), jnp.float32),
        table_stage=pltpu.VMEM((rows, LANES), jnp.float32),
        pack_stage=pltpu.VMEM((rows, GROUP_COLUMNS[2]), jnp.float32),
    )
    for index, param in enumerate(params):
        out["param%d" % index] = pltpu.VMEM(param.shape, jnp.float32)
    out["load_sems"] = pltpu.SemaphoreType.DMA((len(params) + 3,))
    out["begins"] = pltpu.SMEM((count,), jnp.int32)
    out["reaches"] = pltpu.SMEM((count,), jnp.int32)
    out["slope_in"] = pltpu.VMEM((LEVEL_TALLY, count, steps), jnp.bfloat16)
    for group, columns in enumerate(GROUP_COLUMNS):
        slab = -(-rows * columns // LANES // 16) * 16
        out["params%d" % group] = pltpu.VMEM((2, groups, slab, LANES), jnp.bfloat16)
        out["params%d_sems" % group] = pltpu.SemaphoreType.DMA((3 + groups,))
    for name, lanes in GROUP_LANES.items():
        out[name + "_near"] = pltpu.VMEM((width, lanes), jnp.bfloat16)
        folded = (2 * rows, lanes // 2)
        out[name + "_part"] = pltpu.VMEM((groups,) + folded, jnp.bfloat16)
        out[name + "_parts"] = pltpu.VMEM((groups,) + folded, jnp.bfloat16)
        places = count if name in DIRECT else count // 2
        out[name + "_chips"] = pltpu.VMEM((places,) + folded, jnp.bfloat16)
        out[name + "_core_sems"] = pltpu.SemaphoreType.DMA((2, 2))
        out[name + "_dp_sems"] = pltpu.SemaphoreType.DMA((2,))
        out[name + "_chip_sems"] = pltpu.SemaphoreType.DMA((2,))
    for name in ("x", "adjoint", "out", "input", "slope", "predicted"):
        out[name + "_sems"] = pltpu.SemaphoreType.DMA((2,))
    out["own_sems"] = pltpu.SemaphoreType.DMA((4,))
    return out


class Parameters:
    def __init__(self, r, group):
        self.buffer = getattr(r, "params%d" % group)
        self.sems = getattr(r, "params%d_sems" % group)
        self.core, self.mine, self.count = my_core(), lax.axis_index("dp"), lax.axis_size("dp")

    def other(self, step):
        return lax.rem(self.mine + step, self.count)

    def move(self, blocks, device, send, arrive):
        return pltpu.make_async_remote_copy(
            src_ref=blocks,
            dst_ref=blocks,
            send_sem=self.sems.at[send],
            recv_sem=self.sems.at[arrive],
            device_id=device,
            device_id_type=pl.DeviceIdType.MESH,
        )

    def over(self, to, origin):
        return self.move(self.buffer.at[self.core, origin], {"dp": to}, 0, 3 + origin)

    def hand(self, blocks):
        return self.move(blocks, {"tm": lax.axis_index("tm") + 1 - 2 * self.core}, 1, 2)

    def others(self, core):
        return self.buffer.at[core, pl.ds(0, self.count - 1)]

    def start(self):
        for step in range(1, self.count):
            self.over(self.other(step), self.mine).start()

    def pass_on(self):
        for step in range(1, self.count):
            origin = self.other(step)
            self.over(origin, origin).wait_recv()
            self.hand(self.buffer.at[self.core, origin]).start()

    def arrive(self):
        self.hand(self.others(1 - self.core)).wait_recv()

    def sent(self):
        self.move(self.others(self.core), {"dp": self.other(1)}, 0, 3).wait_send()
        self.hand(self.others(self.core)).wait_send()


class Reduction:
    def __init__(self, r, name, final):
        self.send, self.near = getattr(r, name + "_send"), getattr(r, name + "_near")
        self.part, self.parts = getattr(r, name + "_part"), getattr(r, name + "_parts")
        self.chips, self.final = getattr(r, name + "_chips"), final
        self.core, self.rows = my_core(), final.shape[1]
        self.core_sems = getattr(r, name + "_core_sems")
        part, parts, chips = self.part, self.parts, self.chips
        self.to_series = Exchange(
            getattr(r, name + "_dp_sems"),
            over_series(),
            lambda to: part.at[to],
            lambda origin: parts.at[origin],
            part.at[pl.ds(0, part.shape[0] - 1)],
            parts.at[pl.ds(0, part.shape[0] - 1)],
        )
        self.direct = name in DIRECT
        devices = over_time() if self.direct else over_chips()
        place = devices[1]
        self.to_chips = Exchange(
            getattr(r, name + "_chip_sems"),
            devices,
            lambda to: chips.at[place],
            lambda origin: chips.at[origin],
            chips.at[pl.ds(0, chips.shape[0] - 1)],
            chips.at[pl.ds(0, chips.shape[0] - 1)],
        )

    def out(self):
        return to_other_core(self.send.at[1 - self.core], self.near, self.core_sems, 0)

    def back(self, core):
        return to_other_core(self.final.at[core], self.final.at[core], self.core_sems, 1)

    def sum_of(self, ref, first=0, stride=1):
        total = ref[first].astype(jnp.float32)
        for index in range(first + stride, ref.shape[0], stride):
            total = total + ref[index].astype(jnp.float32)
        return total

    def start(self):
        self.out().start()

    def across_series(self):
        self.out().wait_recv()
        total = self.send[self.core].astype(jnp.float32) + self.near[...].astype(jnp.float32)
        for group in range(self.to_series.count):
            self.part[group] = fold(total[group * self.rows : (group + 1) * self.rows])
        self.to_series.start()

    def across_chips(self):
        self.to_series.arrive()
        self.parts[self.to_series.me] = self.part[self.to_series.me]
        self.chips[self.to_chips.me] = low(self.sum_of(self.parts))
        self.to_chips.start()

    def to_both(self):
        self.to_chips.arrive()
        if self.direct:
            for core in range(2):
                self.final[core] = unfold(self.sum_of(self.chips, core, 2))
        else:
            self.final[self.core] = unfold(self.sum_of(self.chips))
            self.back(self.core).start()

    def finish(self):
        if not self.direct:
            self.back(1 - self.core).wait_recv()
            self.back(self.core).wait_send()
        self.out().wait_send()
        self.to_series.sent()
        self.to_chips.sent()


def greet():
    barrier = pltpu.get_barrier_semaphore()
    total = 0
    for count, me, device in (over_time(), over_series()):
        for step in range(1, count):
            pl.semaphore_signal(
                barrier,
                inc=1,
                device_id=device(lax.rem(me + step, count)),
                device_id_type=pl.DeviceIdType.MESH,
            )
            total += 1
    return lambda: pl.semaphore_wait(barrier, total)


def pack_params(r, group, params):
    mine = lax.axis_index("dp")
    buffer, stage = getattr(r, "params%d" % group), r.pack_stage
    columns = GROUP_COLUMNS[group]

    def put(half, *arrays):
        at = 0
        for array in arrays:
            rows, width = array.shape
            stage[:rows, at : at + width] = array[...]
            at += width
        tiles = [stage[:, tile : tile + LANES] for tile in range(0, columns, LANES)]
        spare = buffer.shape[2] - stage.shape[0] * len(tiles)
        tiles.append(jnp.zeros((spare, LANES), jnp.float32))
        buffer[half, mine] = low(jnp.concatenate(tiles, axis=0))

    if group == 0:
        lstm, table, level = params
        rows = lstm.shape[0]
        r.table_stage[...] = jnp.zeros_like(r.table_stage)
        r.table_stage[: table.shape[0], :rows] = table[...]
        r.table_stage[VECTORS : VECTORS + LEVEL_TALLY, :rows] = level[...]
        put(0, lstm[:, :columns])
        put(1, lstm[:, columns:], r.table_stage)
    elif group == 1:
        for half, array in enumerate(params):
            put(half, array)
    else:
        glu_two, glu_three, inner, middle, attn = params
        put(0, glu_two, glu_three)
        put(1, inner, middle, attn)


def unpack_params(r, group, rows, attn_rows):
    width = r.w.shape[0]
    head_width = width // HEADS
    buffer, stage = getattr(r, "params%d" % group), r.stage
    columns = GROUP_COLUMNS[group]
    for half in range(2):
        for origin in range(buffer.shape[1]):
            tiles = buffer[half, origin].astype(jnp.float32)
            for tile in range(columns // LANES):
                at = half * columns + tile * LANES
                stage[origin * rows : (origin + 1) * rows, at : at + LANES] = tiles[
                    tile * rows : (tile + 1) * rows
                ]

    def place(block, column, size):
        r.w[:, block : block + size] = low(stage[:, column : column + size])

    if group == 0:
        for gate, block in enumerate((FORGET, ENTER, CANDIDATE, EXIT)):
            place(block, gate * width, width)
        vectors = jnp.concatenate(
            [
                stage[origin * rows : origin * rows + VECTORS + 8, 4 * width : 4 * width + rows]
                for origin in range(buffer.shape[1])
            ],
            axis=1,
        )
        r.vec[...] = vectors[:VECTORS]
        r.level[...] = low(vectors[VECTORS:])
    elif group == 1:
        place(GLU_ONE_A, 0, width)
        place(GLU_ONE_B, width, width)
        place(QUERY, columns, width)
        place(KEY, columns + width, width)
        place(VALUE, columns + 2 * width, head_width)
    else:
        place(GLU_TWO_A, 0, width)
        place(GLU_TWO_B, width, width)
        place(GLU_THREE_A, 2 * width, width)
        place(GLU_THREE_B, 3 * width, width)
        place(INNER, columns, width)
        place(MIDDLE, columns + width, width)
        for origin in range(buffer.shape[1]):
            r.attn_stage[origin * attn_rows : (origin + 1) * attn_rows, :] = stage[
                origin * rows : origin * rows + attn_rows,
                columns + 2 * width : columns + 3 * width,
            ]
        r.w[:head_width, ATTN_OUT : ATTN_OUT + width] = low(r.attn_stage[:head_width, :])


def series_kernel(begins_hbm, reaches_hbm, x_hbm, adjoint_hbm, slopes_hbm, *others):
    params, others = others[:10], others[10:]
    (out_hbm, predicted_out, input_hbm, final_middle, final_first, final_lstm), scratch = (
        others[:6],
        others[6:],
    )
    count, width, steps = x_hbm.shape
    span = count * steps
    groups = lax.axis_size("dp")
    names = series_scratch(span, width, width // HEADS)
    names.update(travel_scratch(count, groups, steps, width, params))
    r = types.SimpleNamespace(**dict(zip(names, scratch)))
    me = lax.axis_index("tm")
    last = count - 1

    def block(ref, index):
        return ref.at[:, rows_of(index, steps)]

    def whole(ref):
        return ref.at[:, pl.ds(0, (count - 1) * steps)]

    def rest(ref):
        return ref.at[pl.ds(0, count - 1)]

    def inward(sems, source, target):
        return Exchange(
            sems,
            over_time(),
            lambda to: source.at[to],
            lambda origin: block(target, origin),
            rest(source),
            whole(target),
        )

    def outward(sems, source, target):
        return Exchange(
            sems,
            over_time(),
            lambda to: block(source, to),
            lambda origin: target.at[origin],
            whole(source),
            rest(target),
        )

    x_over = inward(r.x_sems, x_hbm, r.x_flat)
    adjoint_over = inward(r.adjoint_sems, adjoint_hbm, r.adjoint)
    out_over = outward(r.out_sems, r.out, out_hbm)
    input_over = outward(r.input_sems, r.input_grad, input_hbm)
    slope_over = Exchange(
        r.slope_sems,
        over_time(),
        lambda to: r.slopes.at[to],
        lambda origin: r.slope,
        rest(r.slopes),
        r.slope,
    )
    predicted_over = Exchange(
        r.predicted_sems,
        over_time(),
        lambda to: r.predicted,
        lambda origin: r.levels.at[origin],
        r.predicted,
        rest(r.levels),
    )
    travelling = [Parameters(r, group) for group in range(3)]
    middle_sum = Reduction(r, "middle", final_middle)
    first_sum = Reduction(r, "first", final_first)
    lstm_sum = Reduction(r, "lstm", final_lstm)
    own_x = pltpu.make_async_copy(x_hbm.at[me], block(r.x_flat, me), r.own_sems.at[0])
    own_adjoint = pltpu.make_async_copy(adjoint_hbm.at[me], block(r.adjoint, me), r.own_sems.at[1])
    own_out = pltpu.make_async_copy(block(r.out, me), out_hbm.at[me], r.own_sems.at[2])
    own_input = pltpu.make_async_copy(block(r.input_grad, me), input_hbm.at[me], r.own_sems.at[3])
    held = [getattr(r, "param%d" % index) for index in range(len(params))]
    loads = [
        pltpu.make_async_copy(param, here, r.load_sems.at[index])
        for index, (param, here) in enumerate(
            zip(
                params + (begins_hbm, reaches_hbm, slopes_hbm),
                held + [r.begins, r.reaches, r.slope_in],
            )
        )
    ]
    begins, reaches, slopes = r.begins, r.reaches, r.slope_in

    def pack(group, *indices):
        for index in indices:
            loads[index].wait()
        pack_params(r, group, [held[index] for index in indices])

    everyone_here = greet()
    for load in loads:
        load.start()
    own_x.start()
    own_adjoint.start()
    pack(0, 0, 9, 8)
    everyone_here()
    travelling[0].start()
    x_over.start()
    pack(1, 1, 2)
    travelling[1].start()
    pack(2, 4, 7, 5, 6, 3)
    for load in loads[len(params) :]:
        load.wait()
    for track in range(count):
        r.slopes[track] = jnp.concatenate(
            [
                slopes[level_at].astype(jnp.float32)[track : track + 1]
                for level_at in range(LEVEL_TALLY)
            ]
            + [jnp.zeros((8 - LEVEL_TALLY, steps), jnp.float32)],
            axis=0,
        )
    begin = begins[me]
    choice = reaches[me]
    horizon = jnp.where(choice == 0, 1, jnp.where(choice == 1, 5, 24))
    rows, attn_rows = params[0].shape[0], params[3].shape[0]
    r.gv[...] = jnp.zeros_like(r.gv)
    own_x.wait()
    series_turn(r, me, steps)
    travelling[0].pass_on()

    x_over.arrive()
    for step in range(1, count):
        series_turn(r, x_over.other(step), steps)
    travelling[0].arrive()
    unpack_params(r, 0, rows, attn_rows)
    series_gates(r, begin)
    travelling[1].pass_on()
    travelling[2].start()

    @pl.when(me == last)
    def _():
        slope_over.start()
        r.slope[...] = r.slopes[last]

    series_forward_scan(r)
    travelling[1].arrive()
    unpack_params(r, 1, rows, attn_rows)
    adjoint_over.start()
    series_forward_first(r, begin)

    def within(tile):
        if tile == 2:
            travelling[2].pass_on()

    series_forward_attention(r, begin, within)
    travelling[2].arrive()
    unpack_params(r, 2, rows, attn_rows)
    own_adjoint.wait()
    adjoint_over.arrive()

    @pl.when(me != last)
    def _():
        slope_over.arrive()

    def forward_done():
        own_out.start()
        out_over.start()

        @pl.when(me != last)
        def _():
            predicted_over.one(last).start()

    series_middle(r, horizon, forward_done)
    middle_sum.start()

    def between(tile):
        if tile == 2:
            middle_sum.across_series()

    series_backward_attention(r, between)
    series_backward_first(r)
    first_sum.start()
    series_backward_scan(r)
    series_gate_grads(r)
    lstm_sum.start()
    first_sum.across_series()
    middle_sum.across_chips()
    series_input_grad(r)
    own_input.start()
    input_over.start()
    lstm_sum.across_series()
    first_sum.across_chips()
    middle_sum.to_both()

    @pl.when(me != last)
    def _():
        predicted_over.sent()
        predicted_out[...] = jnp.zeros_like(predicted_out)

    @pl.when(me == last)
    def _():
        slope_over.sent()
        predicted_over.arrive()
        r.levels[last] = r.predicted[...]
        for level_at in range(LEVEL_TALLY):
            predicted_out[level_at] = jnp.concatenate(
                [r.levels[track][level_at : level_at + 1] for track in range(count)], axis=0
            )

    lstm_sum.across_chips()
    first_sum.to_both()
    x_over.sent()
    adjoint_over.sent()
    for group in travelling:
        group.sent()
    own_out.wait()
    out_over.arrive()
    out_over.sent()
    middle_sum.finish()
    first_sum.finish()
    lstm_sum.to_both()
    own_input.wait()
    input_over.arrive()
    input_over.sent()
    lstm_sum.finish()


def unpack_kernel(final_middle, final_first, final_lstm, out_in, predicted_in, input_in, *others):
    (lstm, glu_one, qkv, attn, glu_two, inner, middle, glu_three, level, table) = others[:10]
    out, predicted, input_grad = others[10:]
    predicted[...] = predicted_in[...]
    rows, width = inner.shape
    lanes = final_lstm.shape[2]
    for ref, at in ((glu_two, 0), (glu_three, 1)):
        ref[...] = final_middle[at, :, : 2 * width]
    for ref, at in ((inner, 0), (middle, 1)):
        ref[...] = final_middle[at, :, 2 * width : 3 * width]
    small, spare = attn.shape[0], width // 5
    for piece in range(5):
        at = small * (piece % 4)
        attn[:, piece * spare : (piece + 1) * spare] = final_middle[
            piece // 4, at : at + small, 3 * width : 3 * width + spare
        ]
    glu_one[...] = final_first[0, :, : 2 * width]
    qkv[...] = final_first[1, :, : qkv.shape[1]]
    lstm[:, :lanes] = final_lstm[0]
    lstm[:, lanes : 3 * width] = final_lstm[1, :, : 3 * width - lanes]
    lstm[:, 3 * width :] = final_first[0, :, 2 * width : 3 * width]
    vectors = final_lstm[1, :, 3 * width - lanes :].T
    table[...] = vectors[: table.shape[0]]
    level[...] = vectors[VECTORS : VECTORS + LEVEL_TALLY]
    out[...] = out_in[...]
    input_grad[...] = input_in[...]


def whole_series(embedded_features, earliest_seen_moment, reach_choice, *others):
    count, steps, width = embedded_features.shape
    features = embedded_features.swapaxes(1, 2)
    adjoint = others[-2].swapaxes(1, 2)
    slopes = others[-1].swapaxes(0, 1)
    params = others[:-4] + (others[-4].T, others[-3].T)
    groups = lax.axis_size("dp")
    rows = params[0].shape[0]
    names = series_scratch(count * steps, width, width // HEADS)
    names.update(travel_scratch(count, groups, steps, width, params))
    smem, vmem, anywhere = (
        pl.BlockSpec(memory_space=space) for space in (pltpu.SMEM, pltpu.VMEM, pl.ANY)
    )
    moved = ((features.shape, jnp.bfloat16), (slopes.shape, jnp.float32))
    moved += moved[:1]
    out, predicted, input_grad, *finals = pl.pallas_call(
        series_kernel,
        out_shape=tuple(pltpu.VMEM(*one) for one in moved)
        + tuple(pltpu.VMEM((2, rows, lanes), jnp.float32) for lanes in GROUP_LANES.values()),
        in_specs=[anywhere] * (5 + len(params)),
        out_specs=(vmem,) * 6,
        scratch_shapes=list(names.values()),
        compiler_params=pltpu.CompilerParams(
            vmem_limit_bytes=VMEM_BYTES, collective_id=0, has_side_effects=True
        ),
    )(
        earliest_seen_moment,
        reach_choice,
        features,
        adjoint,
        slopes,
        *params,
    )
    *grads, level_grad, table_grad, out, predicted, input_grad = pl.pallas_call(
        unpack_kernel,
        out_shape=tuple(jax.ShapeDtypeStruct(param.shape, jnp.float32) for param in params)
        + tuple(jax.ShapeDtypeStruct(*one) for one in moved),
        in_specs=[vmem] * 6,
        out_specs=(vmem,) * (len(params) + 3),
        compiler_params=pltpu.CompilerParams(vmem_limit_bytes=VMEM_BYTES // 6),
    )(*finals, out, predicted, input_grad)
    return (
        out.swapaxes(1, 2),
        predicted.swapaxes(0, 1),
        input_grad.swapaxes(1, 2),
        *grads,
        level_grad.T,
        table_grad.T,
    )


def on_device(embedded_features, *others):
    count, steps, _ = embedded_features.shape
    one_each = count == lax.axis_size("tm") == SUBLANES and steps == LANES
    return (whole_series if one_each else shards)(embedded_features, *others)


def solution(mesh):
    placed = (
        P("dp", "tm", None),
        P("dp"),
        P("dp"),
        P("dp", None),
        P("dp", None),
        P("dp", None),
        P("dp", None),
        P("dp", None),
        P("dp", None),
        P("dp", None),
        P("dp", None),
        P("dp", None),
        P("dp", None),
        P("dp", "tm", None),
        P("dp", None, "tm"),
    )
    return jax.shard_map(
        on_device,
        mesh=mesh,
        in_specs=placed,
        out_specs=(
            P("dp", "tm", None),
            P("dp", None, "tm"),
            P("dp", "tm", None),
            P("dp", None),
            P("dp", None),
            P("dp", None),
            P("dp", None),
            P("dp", None),
            P("dp", None),
            P("dp", None),
            P("dp", None),
            P("dp", None),
            P("dp", None),
        ),
        check_vma=False,
    )
```

```python
import types

import jax
import jax.numpy as jnp
from jax import lax
from jax.experimental import pallas as pl
from jax.experimental.pallas import tpu as pltpu
from jax.sharding import PartitionSpec as P

HEADS = 4
LEVEL_TALLY = 3
DEC = 24
MICRO = 2


EPSILON = 1e-05
NEG_BIG = -1e30
attend_group = 2
LOG2_E = 1.4426950408889634
VMEM_BYTES = 60 * 2**20


def entering(value, axis, join, neutral, backward):
    count, mine = (lax.axis_size(axis), lax.axis_index(axis))
    pieces = jax.tree.map(lambda part: lax.all_gather(part, axis), value)
    if backward:
        pieces = jax.tree.map(lambda part: part[::-1], pieces)
        mine = count - 1 - mine
    so_far = jax.tree.map(
        lambda part, zero: jnp.full_like(part, 0) + jnp.asarray(zero, part.dtype), value, neutral
    )

    def turn(position, so_far):
        longer = join(so_far, jax.tree.map(lambda part: part[position], pieces))
        return jax.tree.map(lambda new, old: jnp.where(position < mine, new, old), longer, so_far)

    return lax.fori_loop(0, count - 1, turn, so_far)


def narrow_convert(values):
    return values.astype(jnp.bfloat16)


def tensor_dot_plain(left, right):
    return jnp.dot(left, right, preferred_element_type=jnp.float32)


def flipped_dot(left, right):
    return lax.dot_general(
        left, right, (((0,), (0,)), ((), ())), preferred_element_type=jnp.float32
    )


def dot_against_flipped(left, right):
    return lax.dot_general(
        left, right, (((1,), (1,)), ((), ())), preferred_element_type=jnp.float32
    )


def affine_join(earlier, later):
    return (later[0] * earlier[0], later[0] * earlier[1] + later[1])


def layer_norm(values, gains, offsets):
    centred = values - jnp.mean(values, axis=-1, keepdims=True)
    spread = jnp.mean(centred * centred, axis=-1, keepdims=True)
    return centred * lax.rsqrt(spread + EPSILON) * gains + offsets


def gated_unit(pre_act):
    half_width = pre_act.shape[-1] // 2
    return pre_act[..., :half_width] * jax.nn.sigmoid(pre_act[..., half_width:])


def lstm_gates(pre_act, keep_mask):
    quarter = pre_act.shape[-1] // 4
    forget = jax.nn.sigmoid(pre_act[..., :quarter]) * keep_mask
    inflow = jax.nn.sigmoid(pre_act[..., quarter : 2 * quarter]) * jnp.tanh(
        pre_act[..., 2 * quarter : 3 * quarter]
    )
    out_gate = jax.nn.sigmoid(pre_act[..., 3 * quarter :])
    return (forget, inflow, out_gate)


def masked_scores(query_block, key_block, query_pos, key_pos, begin_block, scale):
    raw = jnp.einsum("gqhd,gkhd->ghqk", query_block, key_block, preferred_element_type=jnp.float32)
    lowest = jnp.minimum(begin_block[:, None], query_pos[None, :])
    allowed = (key_pos[None, None, :] <= query_pos[None, :, None]) & (
        key_pos[None, None, :] >= lowest[:, :, None]
    )
    return jnp.where(allowed[:, None], raw * scale, NEG_BIG)


def score_grad(chances, dprob, row_delta, scale):
    return narrow_convert(chances * (dprob[:, None] - row_delta[..., None]) * scale)


def shards(
    embedded_features,
    earliest_seen_moment,
    reach_choice,
    lstm_valve_coeffs,
    lstm_unit_coeffs,
    asker_lookup_coeffs,
    attend_exit_coeffs,
    attend_unit_coeffs,
    skipnet_entry_coeffs,
    skipnet_inner_coeffs,
    skipnet_unit_coeffs,
    level_map_coeffs,
    bias_gain_table,
    block_emit_adjoint,
    predicted_adjoint,
):
    (
        mat_lstm,
        mat_glu_one,
        mat_qkv,
        mat_attn,
        mat_glu_two,
        mat_inner,
        mat_middle,
        mat_glu_three,
        level_dot,
        vec_table,
    ) = (
        lax.all_gather(narrow_convert(lstm_valve_coeffs), "dp", axis=0, tiled=True),
        lax.all_gather(narrow_convert(lstm_unit_coeffs), "dp", axis=0, tiled=True),
        lax.all_gather(narrow_convert(asker_lookup_coeffs), "dp", axis=0, tiled=True),
        lax.all_gather(narrow_convert(attend_exit_coeffs), "dp", axis=0, tiled=True),
        lax.all_gather(narrow_convert(attend_unit_coeffs), "dp", axis=0, tiled=True),
        lax.all_gather(narrow_convert(skipnet_entry_coeffs), "dp", axis=0, tiled=True),
        lax.all_gather(narrow_convert(skipnet_inner_coeffs), "dp", axis=0, tiled=True),
        lax.all_gather(narrow_convert(skipnet_unit_coeffs), "dp", axis=0, tiled=True),
        lax.all_gather(narrow_convert(level_map_coeffs), "dp", axis=0, tiled=True),
        lax.all_gather(narrow_convert(bias_gain_table), "dp", axis=0, tiled=True),
    )
    series_per_device, steps_per_device, model_width = embedded_features.shape
    seq_total = steps_per_device * lax.axis_size("tm")
    head_width = model_width // HEADS
    count_of_rows = series_per_device * steps_per_device
    scale = head_width ** (-0.5)
    vec_full = vec_table.astype(jnp.float32)
    time_local = lax.axis_index("tm") * steps_per_device + jnp.arange(
        steps_per_device, dtype=jnp.int32
    )
    time_all = jnp.arange(seq_total, dtype=jnp.int32)
    horizon_len = jnp.where(reach_choice == 0, 1, jnp.where(reach_choice == 1, 5, 24))
    ahead_moment_filter = (
        (
            (time_local[None, :] >= seq_total - DEC)
            & (time_local[None, :] < seq_total - DEC + horizon_len[:, None])
        )
        .astype(jnp.float32)
        .reshape(count_of_rows, 1)
    )
    keep_mask = (
        (time_local[None, :] != earliest_seen_moment[:, None])
        .astype(jnp.float32)
        .reshape(count_of_rows, 1)
    )
    group_size = series_per_device // MICRO
    group_total = series_per_device // attend_group
    state_ones = jnp.ones((group_size, model_width), jnp.float32)
    state_zeros = jnp.zeros((group_size, model_width), jnp.float32)

    def split_groups(array):
        return array.reshape((group_total, attend_group) + array.shape[1:])

    input_rows = embedded_features.reshape(count_of_rows, model_width)
    input_full = input_rows.astype(jnp.float32)
    lstm_pre = tensor_dot_plain(input_rows, mat_lstm) + vec_full[:, 0:4].T.reshape(-1)
    forget, inflow, out_gate = lstm_gates(lstm_pre, keep_mask)
    forget_seq = forget.reshape(series_per_device, steps_per_device, model_width)
    inflow_seq = inflow.reshape(series_per_device, steps_per_device, model_width)
    mult_seq, cell_local = lax.associative_scan(affine_join, (forget_seq, inflow_seq), axis=1)
    cell_parts = []
    for group in range(MICRO):
        lower_row = group * group_size
        upper_row = lower_row + group_size
        _, arriving = entering(
            (mult_seq[lower_row:upper_row, -1], cell_local[lower_row:upper_row, -1]),
            "tm",
            affine_join,
            (state_ones, state_zeros),
            False,
        )
        cell_parts.append(arriving)
    cell_in = jnp.concatenate(cell_parts, axis=0)
    cell_seq = cell_local + mult_seq * cell_in[:, None, :]
    cell_tanh = jnp.tanh(cell_seq.reshape(count_of_rows, model_width))
    hidden_low = narrow_convert(out_gate * cell_tanh)
    glu_one_pre = tensor_dot_plain(hidden_low, mat_glu_one) + vec_full[:, 4:6].T.reshape(-1)
    first_sum = input_full + gated_unit(glu_one_pre)
    first = layer_norm(first_sum, vec_full[:, 6], vec_full[:, 7])
    first_low = narrow_convert(first)
    qkv_low = narrow_convert(tensor_dot_plain(first_low, mat_qkv))
    query_low = qkv_low[:, :model_width].reshape(
        series_per_device, steps_per_device, HEADS, head_width
    )
    key_value = qkv_low[:, model_width:].reshape(
        series_per_device, steps_per_device, model_width + head_width
    )
    key_value_all = lax.all_gather(key_value, "tm", axis=1, tiled=True)
    keys_all = key_value_all[..., :model_width].reshape(
        series_per_device, seq_total, HEADS, head_width
    )
    values_all = key_value_all[..., model_width:]

    def attend_forward(block_args):
        query_block, key_block, value_block, begin_block = block_args
        scores = masked_scores(query_block, key_block, time_local, time_all, begin_block, scale)
        row_top = jnp.max(scores, axis=-1, keepdims=True)
        row_exp = jnp.exp(scores - row_top)
        row_total = jnp.sum(row_exp, axis=-1, keepdims=True)
        weights_low = narrow_convert(row_exp / row_total)
        mixed_block = jnp.einsum(
            "ghqk,gkd->gqd", weights_low, value_block, preferred_element_type=jnp.float32
        ) * (1.0 / HEADS)
        return (mixed_block, (row_top + jnp.log(row_total))[..., 0])

    mixed, log_total = lax.map(
        attend_forward,
        (
            split_groups(query_low),
            split_groups(keys_all),
            split_groups(values_all),
            split_groups(earliest_seen_moment),
        ),
    )
    mixed_low = narrow_convert(mixed.reshape(count_of_rows, head_width))
    attn_low = narrow_convert(tensor_dot_plain(mixed_low, mat_attn))
    glu_two_pre = tensor_dot_plain(attn_low, mat_glu_two) + vec_full[:, 8:10].T.reshape(-1)
    second_sum = first + gated_unit(glu_two_pre)
    second = layer_norm(second_sum, vec_full[:, 10], vec_full[:, 11])
    second_low = narrow_convert(second)
    inner_pre = tensor_dot_plain(second_low, mat_inner) + vec_full[:, 12]
    inner_low = narrow_convert(jax.nn.elu(inner_pre))
    middle_low = narrow_convert(tensor_dot_plain(inner_low, mat_middle) + vec_full[:, 13])
    glu_three_pre = tensor_dot_plain(middle_low, mat_glu_three) + vec_full[:, 14:16].T.reshape(-1)
    final_sum = second + gated_unit(glu_three_pre)
    second_block_emit = layer_norm(final_sum, vec_full[:, 16], vec_full[:, 17])
    closing_narrowed = narrow_convert(second_block_emit)
    predicted_entries = tensor_dot_plain(closing_narrowed, level_dot) * ahead_moment_filter
    predicted_levels = predicted_entries.reshape(
        series_per_device, steps_per_device, LEVEL_TALLY
    ).transpose(0, 2, 1)
    predicted_slope = narrow_convert(
        predicted_adjoint.astype(jnp.float32).transpose(0, 2, 1).reshape(count_of_rows, LEVEL_TALLY)
        * ahead_moment_filter
    )
    level_slope = flipped_dot(closing_narrowed, predicted_slope)
    final_grad = block_emit_adjoint.reshape(count_of_rows, model_width).astype(
        jnp.float32
    ) + dot_against_flipped(predicted_slope, level_dot)
    _, norm_pull = jax.vjp(layer_norm, final_sum, vec_full[:, 16], vec_full[:, 17])
    sum_three_grad, gain_three_grad, offset_three_grad = norm_pull(final_grad)
    _, glu_pull = jax.vjp(gated_unit, glu_three_pre)
    (glu_three_grad,) = glu_pull(sum_three_grad)
    glu_three_low = narrow_convert(glu_three_grad)
    grad_glu_three = flipped_dot(middle_low, glu_three_low)
    middle_grad = dot_against_flipped(glu_three_low, mat_glu_three)
    middle_grad_low = narrow_convert(middle_grad)
    grad_middle = flipped_dot(inner_low, middle_grad_low)
    inner_grad = dot_against_flipped(middle_grad_low, mat_middle)
    _, elu_pull = jax.vjp(jax.nn.elu, inner_pre)
    (inner_pre_grad,) = elu_pull(inner_grad)
    inner_pre_low = narrow_convert(inner_pre_grad)
    grad_inner = flipped_dot(second_low, inner_pre_low)
    second_grad = sum_three_grad + dot_against_flipped(inner_pre_low, mat_inner)
    _, norm_pull = jax.vjp(layer_norm, second_sum, vec_full[:, 10], vec_full[:, 11])
    sum_two_grad, gain_two_grad, offset_two_grad = norm_pull(second_grad)
    _, glu_pull = jax.vjp(gated_unit, glu_two_pre)
    (glu_two_grad,) = glu_pull(sum_two_grad)
    glu_two_low = narrow_convert(glu_two_grad)
    grad_glu_two = flipped_dot(attn_low, glu_two_low)
    attn_grad_low = narrow_convert(dot_against_flipped(glu_two_low, mat_glu_two))
    grad_attn = flipped_dot(mixed_low, attn_grad_low)
    mixed_grad_low = narrow_convert(dot_against_flipped(attn_grad_low, mat_attn))
    head_grad = (mixed_grad_low * (1.0 / HEADS)).reshape(
        series_per_device, steps_per_device, head_width
    )

    def attend_backward(block_args):
        query_block, key_block, value_block, begin_block, lse_block, dout_block = block_args
        scores = masked_scores(query_block, key_block, time_local, time_all, begin_block, scale)
        chances = jnp.exp(scores - lse_block[..., None])
        dprob = jnp.einsum(
            "gqd,gkd->gqk", dout_block, value_block, preferred_element_type=jnp.float32
        )
        row_delta = jnp.sum(chances * dprob[:, None], axis=-1)
        dscore = score_grad(chances, dprob, row_delta, scale)
        dquery = jnp.einsum(
            "ghqk,gkhd->gqhd", dscore, key_block, preferred_element_type=jnp.float32
        )
        dkey = jnp.einsum(
            "ghqk,gqhd->gkhd", dscore, query_block, preferred_element_type=jnp.float32
        )
        dvalue = jnp.einsum(
            "ghqk,gqd->gkd", narrow_convert(chances), dout_block, preferred_element_type=jnp.float32
        )
        key_terms = jnp.concatenate(
            [dkey.reshape(attend_group, seq_total, model_width), dvalue], axis=-1
        )
        return (dquery, key_terms)

    dquery, key_terms = lax.map(
        attend_backward,
        (
            split_groups(query_low),
            split_groups(keys_all),
            split_groups(values_all),
            split_groups(earliest_seen_moment),
            log_total,
            split_groups(head_grad),
        ),
    )
    own_keys = lax.psum_scatter(
        key_terms.reshape(series_per_device, seq_total, model_width + head_width),
        "tm",
        scatter_dimension=1,
        tiled=True,
    )
    qkv_grad = jnp.concatenate(
        [
            dquery.reshape(count_of_rows, model_width),
            own_keys.reshape(count_of_rows, model_width + head_width),
        ],
        axis=1,
    )
    qkv_grad_low = narrow_convert(qkv_grad)
    grad_qkv = flipped_dot(first_low, qkv_grad_low)
    first_grad = sum_two_grad + dot_against_flipped(qkv_grad_low, mat_qkv)
    _, norm_pull = jax.vjp(layer_norm, first_sum, vec_full[:, 6], vec_full[:, 7])
    sum_one_grad, gain_one_grad, offset_one_grad = norm_pull(first_grad)
    _, glu_pull = jax.vjp(gated_unit, glu_one_pre)
    (glu_one_grad,) = glu_pull(sum_one_grad)
    glu_one_low = narrow_convert(glu_one_grad)
    grad_glu_one = flipped_dot(hidden_low, glu_one_low)
    hidden_grad = dot_against_flipped(glu_one_low, mat_glu_one)
    out_gate_grad = hidden_grad * cell_tanh
    direct_grad = (hidden_grad * out_gate * (1.0 - cell_tanh * cell_tanh)).reshape(
        series_per_device, steps_per_device, model_width
    )
    next_forget = jnp.concatenate([forget_seq[:, 1:], jnp.ones_like(forget_seq[:, :1])], axis=1)
    rev_mult, rev_cell = lax.associative_scan(
        affine_join, (next_forget, direct_grad), axis=1, reverse=True
    )
    head_mult = forget_seq[:, 0] * rev_mult[:, 0]
    head_cell = forget_seq[:, 0] * rev_cell[:, 0]
    coming_parts = []
    for group in range(MICRO):
        lower_row = group * group_size
        upper_row = lower_row + group_size
        _, coming = entering(
            (head_mult[lower_row:upper_row], head_cell[lower_row:upper_row]),
            "tm",
            affine_join,
            (state_ones, state_zeros),
            True,
        )
        coming_parts.append(coming)
    coming_all = jnp.concatenate(coming_parts, axis=0)
    cell_grad = rev_cell + rev_mult * coming_all[:, None, :]
    cell_prev = jnp.concatenate([cell_in[:, None, :], cell_seq[:, :-1]], axis=1)
    forget_grad = (cell_grad * cell_prev).reshape(count_of_rows, model_width)
    _, gate_pull = jax.vjp(lambda pre_value: lstm_gates(pre_value, keep_mask), lstm_pre)
    (lstm_pre_grad,) = gate_pull(
        (forget_grad, cell_grad.reshape(count_of_rows, model_width), out_gate_grad)
    )
    lstm_low = narrow_convert(lstm_pre_grad)
    grad_lstm = flipped_dot(input_rows, lstm_low)
    input_grad = sum_one_grad + dot_against_flipped(lstm_low, mat_lstm)
    grad_table = jnp.concatenate(
        [
            jnp.sum(lstm_pre_grad, axis=0).reshape(4, model_width).T,
            jnp.sum(glu_one_grad, axis=0).reshape(2, model_width).T,
            gain_one_grad[:, None],
            offset_one_grad[:, None],
            jnp.sum(glu_two_grad, axis=0).reshape(2, model_width).T,
            gain_two_grad[:, None],
            offset_two_grad[:, None],
            jnp.sum(inner_pre_grad, axis=0)[:, None],
            jnp.sum(middle_grad, axis=0)[:, None],
            jnp.sum(glu_three_grad, axis=0).reshape(2, model_width).T,
            gain_three_grad[:, None],
            offset_three_grad[:, None],
        ],
        axis=1,
    )
    (
        whole_lstm,
        whole_glu_one,
        whole_qkv,
        whole_attn,
        whole_glu_two,
        whole_inner,
        whole_middle,
        whole_glu_three,
        whole_quant,
        whole_table,
    ) = lax.psum(
        (
            grad_lstm,
            grad_glu_one,
            grad_qkv,
            grad_attn,
            grad_glu_two,
            grad_inner,
            grad_middle,
            grad_glu_three,
            level_slope,
            grad_table,
        ),
        "tm",
    )
    summed = (
        lax.psum_scatter(
            whole_lstm.astype(jnp.bfloat16), "dp", scatter_dimension=0, tiled=True
        ).astype(jnp.float32),
        lax.psum_scatter(
            whole_glu_one.astype(jnp.bfloat16), "dp", scatter_dimension=0, tiled=True
        ).astype(jnp.float32),
        lax.psum_scatter(
            whole_qkv.astype(jnp.bfloat16), "dp", scatter_dimension=0, tiled=True
        ).astype(jnp.float32),
        lax.psum_scatter(
            whole_attn.astype(jnp.bfloat16), "dp", scatter_dimension=0, tiled=True
        ).astype(jnp.float32),
        lax.psum_scatter(
            whole_glu_two.astype(jnp.bfloat16), "dp", scatter_dimension=0, tiled=True
        ).astype(jnp.float32),
        lax.psum_scatter(
            whole_inner.astype(jnp.bfloat16), "dp", scatter_dimension=0, tiled=True
        ).astype(jnp.float32),
        lax.psum_scatter(
            whole_middle.astype(jnp.bfloat16), "dp", scatter_dimension=0, tiled=True
        ).astype(jnp.float32),
        lax.psum_scatter(
            whole_glu_three.astype(jnp.bfloat16), "dp", scatter_dimension=0, tiled=True
        ).astype(jnp.float32),
        lax.psum_scatter(
            whole_quant.astype(jnp.bfloat16), "dp", scatter_dimension=0, tiled=True
        ).astype(jnp.float32),
        lax.psum_scatter(
            whole_table.astype(jnp.bfloat16), "dp", scatter_dimension=0, tiled=True
        ).astype(jnp.float32),
    )
    final_out = second_block_emit.astype(jnp.bfloat16).reshape(
        series_per_device, steps_per_device, model_width
    )
    input_out = input_grad.astype(jnp.bfloat16).reshape(
        series_per_device, steps_per_device, model_width
    )
    return (
        final_out,
        predicted_levels,
        input_out,
        summed[0],
        summed[1],
        summed[2],
        summed[3],
        summed[4],
        summed[5],
        summed[6],
        summed[7],
        summed[8],
        summed[9],
    )


def lane_head(shape, head_width, head):
    lane = lax.broadcasted_iota(jnp.int32, shape, len(shape) - 1)
    return (lane >= head * head_width) & (lane < (head + 1) * head_width)


FORGET, ENTER, CANDIDATE, EXIT = 0, 256, 512, 768
GLU_ONE_A, GLU_ONE_B = 1024, 1280
QUERY, KEY, VALUE = 1536, 1792, 2048
GLU_TWO_A, GLU_TWO_B = 2176, 2432
INNER, MIDDLE = 2688, 2944
GLU_THREE_A, GLU_THREE_B = 3200, 3456
ATTN_OUT = 3712
PACKED = 3968
VECTORS = 24
LANES = 128
SUBLANES = 8
CHUNKS = 64
TILE = 256


def nn(left, right):
    return jnp.dot(left, right, preferred_element_type=jnp.float32)


def nt(left, right):
    return lax.dot_general(
        left, right, (((1,), (1,)), ((), ())), preferred_element_type=jnp.float32
    )


def tn(left, right):
    return lax.dot_general(
        left, right, (((0,), (0,)), ((), ())), preferred_element_type=jnp.float32
    )


def low(values):
    return values.astype(jnp.bfloat16)


def sigmoid(values):
    return 0.5 * jnp.tanh(0.5 * values) + 0.5


def normalise(values, gain, shift):
    centred = values - jnp.mean(values, axis=-1, keepdims=True)
    spread = jnp.mean(centred * centred, axis=-1, keepdims=True)
    inverse = lax.rsqrt(spread + EPSILON)
    unit = centred * inverse
    return unit * gain + shift, unit, inverse


def normalise_back(grad, unit, inverse, gain):
    scaled = grad * gain
    return inverse * (
        scaled
        - jnp.mean(scaled, axis=-1, keepdims=True)
        - unit * jnp.mean(scaled * unit, axis=-1, keepdims=True)
    )


def rows_of(tile, size):
    return pl.ds(pl.multiple_of(tile * size, size), size)


def put_halves(ref, rows, values):
    ref[0, rows, :] = values[:, :LANES]
    ref[1, rows, : values.shape[1] - LANES] = values[:, LANES:]


def get_halves(ref, rows, width):
    return jnp.concatenate([ref[0, rows, :], ref[1, rows, : width - LANES]], axis=1)


def row_sum(ref, column, values):
    ref[column : column + 1, :] = jnp.sum(values, axis=0, keepdims=True)


def series_scratch(span, width, head_width):
    full = pltpu.VMEM((span, width), jnp.float32)
    half = pltpu.VMEM((span, width), jnp.bfloat16)
    flat = pltpu.VMEM((width, span), jnp.bfloat16)
    scan = pltpu.VMEM((2, span, LANES), jnp.float32)
    scan_more = pltpu.VMEM((2, span + 8, LANES), jnp.float32)
    narrow = pltpu.VMEM((span, head_width), jnp.bfloat16)
    column = pltpu.VMEM((span, 1), jnp.float32)
    tiles = span // TILE
    return dict(
        forget=scan_more,
        local=scan,
        mult=scan,
        cell=scan_more,
        carry=pltpu.VMEM((2, CHUNKS, LANES), jnp.float32),
        enter_gate=full,
        candidate=full,
        exit_gate=full,
        cell_tanh=full,
        hidden=half,
        glu_one=full,
        gate_one=full,
        unit_one=full,
        inverse_one=column,
        first_low=half,
        keys=pltpu.VMEM((span, width + 1), jnp.bfloat16),
        values=narrow,
        head_queries=pltpu.VMEM((HEADS, span, width + 1), jnp.bfloat16),
        head_keys=pltpu.VMEM((HEADS, span, width), jnp.bfloat16),
        **{
            "chances%d" % tile: pltpu.VMEM((HEADS, TILE, (tile + 1) * TILE), jnp.float32)
            for tile in range(tiles)
        },
        chance_sum=pltpu.VMEM((span, span), jnp.bfloat16),
        **{
            "score_grads%d" % tile: pltpu.VMEM((HEADS, span - tile * TILE, TILE), jnp.bfloat16)
            for tile in range(tiles)
        },
        block=pltpu.VMEM((TILE, span), jnp.float32),
        mixed=narrow,
        mixed_grad=narrow,
        sum_two_grad=full,
        query_grad=half,
        key_grad=half,
        value_grad=narrow,
        gate_grads=pltpu.VMEM((4, span, width), jnp.bfloat16),
        x=half,
        x_flat=flat,
        adjoint=flat,
        out=flat,
        input_grad=flat,
        w=pltpu.VMEM((width, PACKED), jnp.bfloat16),
        vec=pltpu.VMEM((VECTORS, width), jnp.float32),
        level=pltpu.VMEM((8, width), jnp.bfloat16),
        gv=pltpu.VMEM((VECTORS + 8, width), jnp.float32),
        slope=pltpu.VMEM((8, LANES), jnp.float32),
        predicted=pltpu.VMEM((8, LANES), jnp.float32),
        attn_flat=pltpu.VMEM((width, 2 * width // 5), jnp.float32),
        lstm_flat=pltpu.VMEM((width, 4 * LANES), jnp.float32),
        middle_send=pltpu.VMEM((2, width, GROUP_LANES["middle"]), jnp.bfloat16),
        first_send=pltpu.VMEM((2, width, GROUP_LANES["first"]), jnp.bfloat16),
        lstm_send=pltpu.VMEM((2, width, GROUP_LANES["lstm"]), jnp.bfloat16),
    )


def series_turn(r, chunk, steps):
    rows = rows_of(chunk, steps)
    r.x[rows, :] = r.x_flat[:, rows].T


def series_gates(r, begin):
    w, vec = r.w, r.vec
    span, width = r.x.shape
    rows = slice(0, span)
    x = r.x[...]

    def pre(block, column):
        return nn(x, w[:, block : block + width]) + vec[column : column + 1, :]

    time = lax.broadcasted_iota(jnp.int32, (span, width), 0)
    put_halves(r.forget, rows, jnp.where(time != begin, sigmoid(pre(FORGET, 0)), 0.0))
    enter = sigmoid(pre(ENTER, 1))
    candidate = jnp.tanh(pre(CANDIDATE, 2))
    r.enter_gate[...] = enter
    r.candidate[...] = candidate
    put_halves(r.local, rows, enter * candidate)
    r.exit_gate[...] = sigmoid(pre(EXIT, 3))


def scan_state():
    zeros = jnp.zeros((SUBLANES, LANES), jnp.float32)
    return ((zeros, zeros + 1.0),) * (2 * CHUNKS // SUBLANES)


def scan_step(r, steps, t, after, state):
    out = []
    for index, (value, mult) in enumerate(state):
        half, start = index % 2, index // 2 * SUBLANES * steps
        at = pl.ds(start + t, SUBLANES, stride=steps)
        forget = r.forget[half, pl.ds(start + t + after, SUBLANES, stride=steps), :]
        value = forget * value + r.local[half, at, :]
        mult = mult * forget
        r.local[half, at, :] = value
        r.mult[half, at, :] = mult
        out.append((value, mult))
    return tuple(out)


def scan_carry(r, ends, order):
    for half in range(2):
        state = jnp.zeros((1, LANES), jnp.float32)
        for chunk in order:
            r.carry[half, chunk : chunk + 1, :] = state
            value, mult = ends[chunk // SUBLANES * 2 + half]
            at = chunk % SUBLANES
            state = value[at : at + 1] + mult[at : at + 1] * state


def series_forward_scan(r):
    steps = r.x.shape[0] // CHUNKS
    ends = scan_state()
    for t in range(steps):
        ends = scan_step(r, steps, t, 0, ends)
    scan_carry(r, ends, range(CHUNKS))
    for half in range(2):
        r.cell[half, 0:8, :] = jnp.zeros((8, LANES), jnp.float32)


def series_forward_first(r, begin):
    w, vec = r.w, r.vec
    span, width = r.x.shape
    head_width = width // HEADS
    steps = span // CHUNKS
    for chunk in range(CHUNKS):
        rows = slice(chunk * steps, (chunk + 1) * steps)
        later = slice(chunk * steps + 8, (chunk + 1) * steps + 8)
        for half in range(2):
            r.cell[half, later, :] = (
                r.local[half, rows, :]
                + r.mult[half, rows, :] * r.carry[half, chunk : chunk + 1, :]
            )
    tanh = jnp.tanh(get_halves(r.cell, slice(8, 8 + span), width))
    r.cell_tanh[...] = tanh
    hidden = low(r.exit_gate[...] * tanh)
    r.hidden[...] = hidden
    value = nn(hidden, w[:, GLU_ONE_A : GLU_ONE_A + width]) + vec[4:5, :]
    gate = sigmoid(nn(hidden, w[:, GLU_ONE_B : GLU_ONE_B + width]) + vec[5:6, :])
    r.glu_one[...] = value
    r.gate_one[...] = gate
    out, unit, inverse = normalise(
        r.x[...].astype(jnp.float32) + value * gate, vec[6:7, :], vec[7:8, :]
    )
    r.unit_one[...] = unit
    r.inverse_one[...] = inverse
    out = low(out)
    r.first_low[...] = out
    query = low(nn(out, w[:, QUERY : QUERY + width]))
    key = low(nn(out, w[:, KEY : KEY + width]))
    time = lax.broadcasted_iota(jnp.int32, (span, 1), 0)
    r.keys[...] = jnp.concatenate([key, low(jnp.where(time < begin, NEG_BIG, 0.0))], axis=1)
    one = jnp.ones((span, 1), jnp.bfloat16)
    r.values[...] = low(nn(out, w[:, VALUE : VALUE + head_width]))
    for head in range(HEADS):
        mine = lane_head((span, width), head_width, head)
        r.head_queries[head] = jnp.concatenate(
            [jnp.where(mine, query, jnp.zeros_like(query)), one], axis=1
        )
        r.head_keys[head] = jnp.where(mine, key, jnp.zeros_like(key))


def series_forward_attention(r, begin, between):
    span, head_width = r.values.shape
    width = head_width * HEADS
    scale = head_width ** (-0.5) * LOG2_E
    row = lax.broadcasted_iota(jnp.int32, (TILE, TILE), 0)
    col = lax.broadcasted_iota(jnp.int32, (TILE, TILE), 1)
    for tile in range(span // TILE):
        start, seen = tile * TILE, (tile + 1) * TILE
        rows = slice(start, seen)
        chances = getattr(r, "chances%d" % tile)
        r.block[:, :TILE] = jnp.where(
            (col <= row) & (col >= jnp.minimum(begin - start, row)), 0.0, NEG_BIG
        )
        for head in range(HEADS):
            near = (
                nt(r.head_queries[head, rows, :width], r.keys[rows, :width]) + r.block[:, :TILE]
            )
            top = jnp.max(near, axis=-1, keepdims=True)
            if tile:
                far = nt(r.head_queries[head, rows, :], r.keys[:start, :])
                top = jnp.maximum(top, jnp.max(far, axis=-1, keepdims=True))
                far = jnp.exp2((far - top) * scale)
            near = jnp.exp2((near - top) * scale)
            total = jnp.sum(near, axis=-1, keepdims=True)
            if tile:
                total = total + jnp.sum(far, axis=-1, keepdims=True)
            share = 1.0 / total
            chances[head, :, start:] = near * share
            if tile:
                chances[head, :, :start] = far * share
        weights = chances[0]
        for head in range(1, HEADS):
            weights = weights + chances[head]
        weights = low(weights)
        r.chance_sum[rows, :seen] = weights
        r.mixed[rows, :] = low(nn(weights, r.values[:seen, :]) * (1.0 / HEADS))
        between(tile)


def series_middle(r, horizon, after_forward):
    w, vec, gv = r.w, r.vec, r.gv
    span, width = r.x.shape
    head_width = width // HEADS
    first = r.unit_one[...] * vec[6:7, :] + vec[7:8, :]
    mixed = r.mixed[...]
    attn = low(nn(mixed, w[:head_width, ATTN_OUT : ATTN_OUT + width]))
    value_two = nn(attn, w[:, GLU_TWO_A : GLU_TWO_A + width]) + vec[8:9, :]
    gate_two = sigmoid(nn(attn, w[:, GLU_TWO_B : GLU_TWO_B + width]) + vec[9:10, :])
    second, unit_two, inverse_two = normalise(
        first + value_two * gate_two, vec[10:11, :], vec[11:12, :]
    )
    second_low = low(second)
    inner_pre = nn(second_low, w[:, INNER : INNER + width]) + vec[12:13, :]
    inner_exp = jnp.exp(jnp.minimum(inner_pre, 0.0))
    inner_low = low(jnp.where(inner_pre > 0, inner_pre, inner_exp - 1.0))
    middle_low = low(nn(inner_low, w[:, MIDDLE : MIDDLE + width]) + vec[13:14, :])
    value_three = nn(middle_low, w[:, GLU_THREE_A : GLU_THREE_A + width]) + vec[14:15, :]
    gate_three = sigmoid(nn(middle_low, w[:, GLU_THREE_B : GLU_THREE_B + width]) + vec[15:16, :])
    final, unit_three, inverse_three = normalise(
        second + value_three * gate_three, vec[16:17, :], vec[17:18, :]
    )
    final_low = low(final)
    r.out[...] = final_low.T
    steps = r.slope.shape[1]
    time = span - steps + lax.broadcasted_iota(jnp.int32, (8, steps), 1)
    ahead = jnp.where((time >= span - DEC) & (time < span - DEC + horizon), 1.0, 0.0)
    r.predicted[...] = nt(r.level[...], final_low[span - steps :]) * ahead
    after_forward()
    slope = low(r.slope[...] * ahead)
    gv[VECTORS : VECTORS + 8, :] = nn(slope, final_low[span - steps :])
    grad = r.adjoint[...].T.astype(jnp.float32)
    grad = jnp.concatenate(
        [grad[: span - steps], grad[span - steps :] + tn(slope, r.level[...])], axis=0
    )
    row_sum(gv, 16, grad * unit_three)
    row_sum(gv, 17, grad)
    sum_three = normalise_back(grad, unit_three, inverse_three, vec[16:17, :])
    grad_a = sum_three * gate_three
    grad_b = grad_a * value_three * (1.0 - gate_three)
    row_sum(gv, 14, grad_a)
    row_sum(gv, 15, grad_b)
    low_a, low_b = low(grad_a), low(grad_b)
    send = r.middle_send
    send[1, :, :width] = low(tn(middle_low, low_a))
    send[1, :, width : 2 * width] = low(tn(middle_low, low_b))
    middle_grad = nt(low_a, w[:, GLU_THREE_A : GLU_THREE_A + width]) + nt(
        low_b, w[:, GLU_THREE_B : GLU_THREE_B + width]
    )
    row_sum(gv, 13, middle_grad)
    middle_grad = low(middle_grad)
    send[1, :, 2 * width : 3 * width] = low(tn(inner_low, middle_grad))
    inner_grad = nt(middle_grad, w[:, MIDDLE : MIDDLE + width]) * jnp.where(
        inner_pre > 0, 1.0, inner_exp
    )
    row_sum(gv, 12, inner_grad)
    inner_grad = low(inner_grad)
    send[0, :, 2 * width : 3 * width] = low(tn(second_low, inner_grad))
    grad = sum_three + nt(inner_grad, w[:, INNER : INNER + width])
    row_sum(gv, 10, grad * unit_two)
    row_sum(gv, 11, grad)
    sum_two = normalise_back(grad, unit_two, inverse_two, vec[10:11, :])
    r.sum_two_grad[...] = sum_two
    grad_a = sum_two * gate_two
    grad_b = grad_a * value_two * (1.0 - gate_two)
    row_sum(gv, 8, grad_a)
    row_sum(gv, 9, grad_b)
    low_a, low_b = low(grad_a), low(grad_b)
    attn_grad = low(
        nt(low_a, w[:, GLU_TWO_A : GLU_TWO_A + width])
        + nt(low_b, w[:, GLU_TWO_B : GLU_TWO_B + width])
    )
    r.mixed_grad[...] = low(nt(attn_grad, w[:head_width, ATTN_OUT : ATTN_OUT + width]))
    send[0, :, :width] = low(tn(attn, low_a))
    send[0, :, width : 2 * width] = low(tn(attn, low_b))
    attn_weight = tn(mixed, attn_grad)
    rows, small = head_width, head_width // HEADS
    spare = width // 5
    r.attn_flat[...] = jnp.zeros_like(r.attn_flat)
    for group in range(HEADS):
        for piece in range(5):
            at = group * rows + small * (piece % 4)
            half = piece // 4
            r.attn_flat[at : at + small, half * spare : (half + 1) * spare] = attn_weight[
                group * small : (group + 1) * small, piece * spare : (piece + 1) * spare
            ]
    for half in range(2):
        send[half, :, 3 * width :] = low(r.attn_flat[:, half * spare : (half + 1) * spare])


def series_backward_attention(r, between):
    span, head_width = r.values.shape
    width = head_width * HEADS
    scale = head_width ** (-0.5)
    for tile in range(span // TILE):
        rows = slice(tile * TILE, (tile + 1) * TILE)
        seen = (tile + 1) * TILE
        held = getattr(r, "chances%d" % tile)
        head_grad = r.mixed_grad[rows, :] * (1.0 / HEADS)
        r.block[:, :seen] = nt(head_grad, r.values[:seen, :]) * scale
        total = jnp.zeros((TILE, width), jnp.float32)
        for head in range(HEADS):
            chances = held[head]
            slope = r.block[:, :seen]
            delta = jnp.sum(chances * slope, axis=-1, keepdims=True)
            grads = low(chances * (slope - delta))
            for part in range(tile + 1):
                getattr(r, "score_grads%d" % part)[
                    head, (tile - part) * TILE : (tile - part + 1) * TILE, :
                ] = grads[:, part * TILE : (part + 1) * TILE]
            total = total + nn(grads, r.head_keys[head, :seen, :])
        r.query_grad[rows, :] = low(total)
        between(tile)
    for tile in range(span // TILE):
        cols = slice(tile * TILE, (tile + 1) * TILE)
        start = tile * TILE
        total = jnp.zeros((TILE, width), jnp.float32)
        for head in range(HEADS):
            total = total + tn(
                getattr(r, "score_grads%d" % tile)[head],
                r.head_queries[head, start:, :width],
            )
        r.key_grad[cols, :] = low(total)
        r.value_grad[cols, :] = low(
            tn(r.chance_sum[start:, cols], r.mixed_grad[start:, :] * (1.0 / HEADS))
        )


def series_backward_first(r):
    w, vec, gv = r.w, r.vec, r.gv
    span, width = r.hidden.shape
    head_width = width // HEADS
    rows = slice(0, span)
    send = r.first_send
    query, key, value = r.query_grad[...], r.key_grad[...], r.value_grad[...]
    grad = (
        r.sum_two_grad[...]
        + nt(query, w[:, QUERY : QUERY + width])
        + nt(key, w[:, KEY : KEY + width])
        + nt(value, w[:, VALUE : VALUE + head_width])
    )
    first = r.first_low[...]
    send[1, :, :width] = low(tn(first, query))
    send[1, :, width : 2 * width] = low(tn(first, key))
    send[1, :, 2 * width : 2 * width + head_width] = low(tn(first, value))
    unit = r.unit_one[...]
    row_sum(gv, 6, grad * unit)
    row_sum(gv, 7, grad)
    sum_one = normalise_back(grad, unit, r.inverse_one[...], vec[6:7, :])
    r.sum_two_grad[...] = sum_one
    gate = r.gate_one[...]
    grad_a = sum_one * gate
    grad_b = grad_a * r.glu_one[...] * (1.0 - gate)
    row_sum(gv, 4, grad_a)
    row_sum(gv, 5, grad_b)
    low_a, low_b = low(grad_a), low(grad_b)
    hidden_grad = nt(low_a, w[:, GLU_ONE_A : GLU_ONE_A + width]) + nt(
        low_b, w[:, GLU_ONE_B : GLU_ONE_B + width]
    )
    tanh, gate = r.cell_tanh[...], r.exit_gate[...]
    put_halves(r.local, rows, hidden_grad * gate * (1.0 - tanh * tanh))
    exit_grad = hidden_grad * tanh * gate * (1.0 - gate)
    row_sum(gv, 3, exit_grad)
    exit_grad = low(exit_grad)
    r.gate_grads[3] = exit_grad
    hidden = r.hidden[...]
    send[0, :, :width] = low(tn(hidden, low_a))
    send[0, :, width : 2 * width] = low(tn(hidden, low_b))
    send[0, :, 2 * width : 3 * width] = low(nn(r.x_flat[...], exit_grad))


def series_backward_scan(r):
    span = r.x.shape[0]
    steps = span // CHUNKS
    for half in range(2):
        r.forget[half, span:, :] = jnp.zeros((8, LANES), jnp.float32)

    ends = scan_state()
    for t in range(steps - 1, -1, -1):
        ends = scan_step(r, steps, t, 1, ends)
    scan_carry(r, ends, range(CHUNKS - 1, -1, -1))


def series_gate_grads(r):
    gv = r.gv
    span, width = r.x.shape
    steps = span // CHUNKS
    for half in range(2):
        for chunk in range(CHUNKS):
            rows = slice(chunk * steps, (chunk + 1) * steps)
            r.local[half, rows, :] += r.mult[half, rows, :] * r.carry[half, chunk : chunk + 1, :]
    grad = get_halves(r.local, slice(0, span), width)
    forget = get_halves(r.forget, slice(0, span), width)
    before = get_halves(r.cell, slice(7, 7 + span), width)
    enter, candidate = r.enter_gate[...], r.candidate[...]
    for gate, one in enumerate(
        (
            grad * before * forget * (1.0 - forget),
            grad * candidate * enter * (1.0 - enter),
            grad * enter * (1.0 - candidate * candidate),
        )
    ):
        row_sum(gv, gate, one)
        one = low(one)
        r.gate_grads[gate] = one
        r.lstm_flat[:, gate * width : (gate + 1) * width] = nn(r.x_flat[...], one)
    r.lstm_flat[:, 3 * width :] = gv[...].T
    lanes = r.lstm_send.shape[2]
    for half in range(2):
        r.lstm_send[half] = low(r.lstm_flat[:, half * lanes : (half + 1) * lanes])


def series_input_grad(r):
    width = r.x.shape[1]
    out = r.sum_two_grad[...].T
    for gate, block in enumerate((FORGET, ENTER, CANDIDATE, EXIT)):
        out = out + nt(r.w[:, block : block + width], r.gate_grads[gate])
    r.input_grad[...] = low(out)


class Exchange:
    def __init__(self, sems, devices, source, target, sources, targets):
        self.sems, self.source, self.target = sems, source, target
        self.sources, self.targets = sources, targets
        self.count, self.me, self.device = devices

    def other(self, step):
        return lax.rem(self.me + step, self.count)

    def copy(self, to, source, target):
        return pltpu.make_async_remote_copy(
            src_ref=source,
            dst_ref=target,
            send_sem=self.sems.at[0],
            recv_sem=self.sems.at[1],
            device_id=self.device(to),
            device_id_type=pl.DeviceIdType.MESH,
        )

    def one(self, to):
        return self.copy(to, self.source(to), self.target(self.me))

    def start(self):
        for step in range(1, self.count):
            self.one(self.other(step)).start()

    def all(self):
        return self.copy(self.other(1), self.sources, self.targets)

    def arrive(self):
        self.all().wait_recv()

    def sent(self):
        self.all().wait_send()


def over_time():
    return lax.axis_size("tm"), lax.axis_index("tm"), lambda to: {"tm": to}


def over_series():
    return lax.axis_size("dp"), lax.axis_index("dp"), lambda to: {"dp": to}


def over_chips():
    core = my_core()
    return (
        lax.axis_size("tm") // 2,
        lax.div(lax.axis_index("tm"), 2),
        lambda to: {"tm": 2 * to + core},
    )


def my_core():
    return lax.rem(lax.axis_index("tm"), 2)


def to_other_core(source, target, sems, index):
    return pltpu.make_async_remote_copy(
        src_ref=source,
        dst_ref=target,
        send_sem=sems.at[0, index],
        recv_sem=sems.at[1, index],
        device_id={"tm": lax.axis_index("tm") + 1 - 2 * my_core()},
        device_id_type=pl.DeviceIdType.MESH,
    )


GROUP_COLUMNS = (384, 384, 640)
GROUP_LANES = {"middle": 512, "first": 512, "lstm": 256}
DIRECT = ("lstm",)


def fold(values):
    lanes = values.shape[1] // 2
    return low(jnp.concatenate([values[:, :lanes], values[:, lanes:]], axis=0))


def unfold(values):
    rows = values.shape[0] // 2
    return jnp.concatenate([values[:rows], values[rows:]], axis=1)


def travel_scratch(count, groups, steps, width, params):
    rows = params[0].shape[0]
    out = dict(
        slopes=pltpu.VMEM((count, 8, steps), jnp.float32),
        levels=pltpu.VMEM((count, 8, steps), jnp.float32),
        stage=pltpu.VMEM((width, 2 * GROUP_COLUMNS[2]), jnp.float32),
        attn_stage=pltpu.VMEM((width, width), jnp.float32),
        table_stage=pltpu.VMEM((rows, LANES), jnp.float32),
        pack_stage=pltpu.VMEM((rows, GROUP_COLUMNS[2]), jnp.float32),
    )
    for index, param in enumerate(params):
        out["param%d" % index] = pltpu.VMEM(param.shape, jnp.float32)
    out["load_sems"] = pltpu.SemaphoreType.DMA((len(params) + 3,))
    out["begins"] = pltpu.SMEM((count,), jnp.int32)
    out["reaches"] = pltpu.SMEM((count,), jnp.int32)
    out["slope_in"] = pltpu.VMEM((LEVEL_TALLY, count, steps), jnp.bfloat16)
    for group, columns in enumerate(GROUP_COLUMNS):
        slab = -(-rows * columns // LANES // 16) * 16
        out["params%d" % group] = pltpu.VMEM((2, groups, slab, LANES), jnp.bfloat16)
        out["params%d_sems" % group] = pltpu.SemaphoreType.DMA((4,))
    for name, lanes in GROUP_LANES.items():
        out[name + "_near"] = pltpu.VMEM((width, lanes), jnp.bfloat16)
        folded = (2 * rows, lanes // 2)
        out[name + "_part"] = pltpu.VMEM((groups,) + folded, jnp.bfloat16)
        out[name + "_parts"] = pltpu.VMEM((groups,) + folded, jnp.bfloat16)
        places = count if name in DIRECT else count // 2
        out[name + "_chips"] = pltpu.VMEM((places,) + folded, jnp.bfloat16)
        out[name + "_core_sems"] = pltpu.SemaphoreType.DMA((2, 2))
        out[name + "_dp_sems"] = pltpu.SemaphoreType.DMA((2,))
        out[name + "_chip_sems"] = pltpu.SemaphoreType.DMA((2,))
    for name in ("x", "adjoint", "out", "input", "slope", "predicted"):
        out[name + "_sems"] = pltpu.SemaphoreType.DMA((2,))
    out["own_sems"] = pltpu.SemaphoreType.DMA((4,))
    return out


class Parameters:
    def __init__(self, r, group):
        self.buffer = getattr(r, "params%d" % group)
        self.sems = getattr(r, "params%d_sems" % group)
        self.core, self.mine, self.count = my_core(), lax.axis_index("dp"), lax.axis_size("dp")

    def other(self, step):
        return lax.rem(self.mine + step, self.count)

    def move(self, blocks, device, send, arrive):
        return pltpu.make_async_remote_copy(
            src_ref=blocks,
            dst_ref=blocks,
            send_sem=self.sems.at[send],
            recv_sem=self.sems.at[arrive],
            device_id=device,
            device_id_type=pl.DeviceIdType.MESH,
        )

    def over(self, to, origin):
        return self.move(self.buffer.at[self.core, origin], {"dp": to}, 0, 3)

    def hand(self, blocks):
        return self.move(blocks, {"tm": lax.axis_index("tm") + 1 - 2 * self.core}, 1, 2)

    def others(self, core):
        return self.buffer.at[core, pl.ds(0, self.count - 1)]

    def start(self):
        for step in range(1, self.count):
            self.over(self.other(step), self.mine).start()

    def pass_on(self):
        self.move(self.others(self.core), {"dp": self.other(1)}, 0, 3).wait_recv()
        for step in range(1, self.count):
            self.hand(self.buffer.at[self.core, self.other(step)]).start()

    def arrive(self):
        self.hand(self.others(1 - self.core)).wait_recv()

    def sent(self):
        self.move(self.others(self.core), {"dp": self.other(1)}, 0, 3).wait_send()
        self.hand(self.others(self.core)).wait_send()


class Reduction:
    def __init__(self, r, name, final):
        self.send, self.near = getattr(r, name + "_send"), getattr(r, name + "_near")
        self.part, self.parts = getattr(r, name + "_part"), getattr(r, name + "_parts")
        self.chips, self.final = getattr(r, name + "_chips"), final
        self.core, self.rows = my_core(), final.shape[1]
        self.core_sems = getattr(r, name + "_core_sems")
        part, parts, chips = self.part, self.parts, self.chips
        self.to_series = Exchange(
            getattr(r, name + "_dp_sems"),
            over_series(),
            lambda to: part.at[to],
            lambda origin: parts.at[origin],
            part.at[pl.ds(0, part.shape[0] - 1)],
            parts.at[pl.ds(0, part.shape[0] - 1)],
        )
        self.direct = name in DIRECT
        devices = over_time() if self.direct else over_chips()
        place = devices[1]
        self.to_chips = Exchange(
            getattr(r, name + "_chip_sems"),
            devices,
            lambda to: chips.at[place],
            lambda origin: chips.at[origin],
            chips.at[pl.ds(0, chips.shape[0] - 1)],
            chips.at[pl.ds(0, chips.shape[0] - 1)],
        )

    def out(self):
        return to_other_core(self.send.at[1 - self.core], self.near, self.core_sems, 0)

    def back(self, core):
        return to_other_core(self.final.at[core], self.final.at[core], self.core_sems, 1)

    def sum_of(self, ref, first=0, stride=1):
        total = ref[first].astype(jnp.float32)
        for index in range(first + stride, ref.shape[0], stride):
            total = total + ref[index].astype(jnp.float32)
        return total

    def start(self):
        self.out().start()

    def across_series(self):
        self.out().wait_recv()
        total = self.send[self.core].astype(jnp.float32) + self.near[...].astype(jnp.float32)
        for group in range(self.to_series.count):
            self.part[group] = fold(total[group * self.rows : (group + 1) * self.rows])
        self.to_series.start()

    def across_chips(self):
        self.to_series.arrive()
        self.parts[self.to_series.me] = self.part[self.to_series.me]
        self.chips[self.to_chips.me] = low(self.sum_of(self.parts))
        self.to_chips.start()

    def to_both(self):
        self.to_chips.arrive()
        if self.direct:
            for core in range(2):
                self.final[core] = unfold(self.sum_of(self.chips, core, 2))
        else:
            self.final[self.core] = unfold(self.sum_of(self.chips))
            self.back(self.core).start()

    def finish(self):
        if not self.direct:
            self.back(1 - self.core).wait_recv()
            self.back(self.core).wait_send()
        self.out().wait_send()
        self.to_series.sent()
        self.to_chips.sent()


def greet():
    barrier = pltpu.get_barrier_semaphore()
    total = 0
    for count, me, device in (over_time(), over_series()):
        for step in range(1, count):
            pl.semaphore_signal(
                barrier,
                inc=1,
                device_id=device(lax.rem(me + step, count)),
                device_id_type=pl.DeviceIdType.MESH,
            )
            total += 1
    return lambda: pl.semaphore_wait(barrier, total)


def pack_params(r, group, params):
    mine = lax.axis_index("dp")
    buffer, stage = getattr(r, "params%d" % group), r.pack_stage
    columns = GROUP_COLUMNS[group]

    def put(half, *arrays):
        at = 0
        for array in arrays:
            rows, width = array.shape
            stage[:rows, at : at + width] = array[...]
            at += width
        tiles = [stage[:, tile : tile + LANES] for tile in range(0, columns, LANES)]
        spare = buffer.shape[2] - stage.shape[0] * len(tiles)
        tiles.append(jnp.zeros((spare, LANES), jnp.float32))
        buffer[half, mine] = low(jnp.concatenate(tiles, axis=0))

    if group == 0:
        lstm, table, level = params
        rows = lstm.shape[0]
        r.table_stage[...] = jnp.zeros_like(r.table_stage)
        r.table_stage[: table.shape[0], :rows] = table[...]
        r.table_stage[VECTORS : VECTORS + LEVEL_TALLY, :rows] = level[...]
        put(0, lstm[:, :columns])
        put(1, lstm[:, columns:], r.table_stage)
    elif group == 1:
        for half, array in enumerate(params):
            put(half, array)
    else:
        glu_two, glu_three, inner, middle, attn = params
        put(0, glu_two, glu_three)
        put(1, inner, middle, attn)


def unpack_params(r, group, rows, attn_rows):
    width = r.w.shape[0]
    head_width = width // HEADS
    buffer, stage = getattr(r, "params%d" % group), r.stage
    columns = GROUP_COLUMNS[group]
    for half in range(2):
        for origin in range(buffer.shape[1]):
            tiles = buffer[half, origin].astype(jnp.float32)
            for tile in range(columns // LANES):
                at = half * columns + tile * LANES
                stage[origin * rows : (origin + 1) * rows, at : at + LANES] = tiles[
                    tile * rows : (tile + 1) * rows
                ]

    def place(block, column, size):
        r.w[:, block : block + size] = low(stage[:, column : column + size])

    if group == 0:
        for gate, block in enumerate((FORGET, ENTER, CANDIDATE, EXIT)):
            place(block, gate * width, width)
        vectors = jnp.concatenate(
            [
                stage[origin * rows : origin * rows + VECTORS + 8, 4 * width : 4 * width + rows]
                for origin in range(buffer.shape[1])
            ],
            axis=1,
        )
        r.vec[...] = vectors[:VECTORS]
        r.level[...] = low(vectors[VECTORS:])
    elif group == 1:
        place(GLU_ONE_A, 0, width)
        place(GLU_ONE_B, width, width)
        place(QUERY, columns, width)
        place(KEY, columns + width, width)
        place(VALUE, columns + 2 * width, head_width)
    else:
        place(GLU_TWO_A, 0, width)
        place(GLU_TWO_B, width, width)
        place(GLU_THREE_A, 2 * width, width)
        place(GLU_THREE_B, 3 * width, width)
        place(INNER, columns, width)
        place(MIDDLE, columns + width, width)
        for origin in range(buffer.shape[1]):
            r.attn_stage[origin * attn_rows : (origin + 1) * attn_rows, :] = stage[
                origin * rows : origin * rows + attn_rows,
                columns + 2 * width : columns + 3 * width,
            ]
        r.w[:head_width, ATTN_OUT : ATTN_OUT + width] = low(r.attn_stage[:head_width, :])


def series_kernel(begins_hbm, reaches_hbm, x_hbm, adjoint_hbm, slopes_hbm, *others):
    params, others = others[:10], others[10:]
    (out_hbm, predicted_out, input_hbm, final_middle, final_first, final_lstm), scratch = (
        others[:6],
        others[6:],
    )
    count, width, steps = x_hbm.shape
    span = count * steps
    groups = lax.axis_size("dp")
    names = series_scratch(span, width, width // HEADS)
    names.update(travel_scratch(count, groups, steps, width, params))
    r = types.SimpleNamespace(**dict(zip(names, scratch)))
    me = lax.axis_index("tm")
    last = count - 1

    def block(ref, index):
        return ref.at[:, rows_of(index, steps)]

    def whole(ref):
        return ref.at[:, pl.ds(0, (count - 1) * steps)]

    def rest(ref):
        return ref.at[pl.ds(0, count - 1)]

    def inward(sems, source, target):
        return Exchange(
            sems,
            over_time(),
            lambda to: source.at[to],
            lambda origin: block(target, origin),
            rest(source),
            whole(target),
        )

    def outward(sems, source, target):
        return Exchange(
            sems,
            over_time(),
            lambda to: block(source, to),
            lambda origin: target.at[origin],
            whole(source),
            rest(target),
        )

    x_over = inward(r.x_sems, x_hbm, r.x_flat)
    adjoint_over = inward(r.adjoint_sems, adjoint_hbm, r.adjoint)
    out_over = outward(r.out_sems, r.out, out_hbm)
    input_over = outward(r.input_sems, r.input_grad, input_hbm)
    slope_over = Exchange(
        r.slope_sems,
        over_time(),
        lambda to: r.slopes.at[to],
        lambda origin: r.slope,
        rest(r.slopes),
        r.slope,
    )
    predicted_over = Exchange(
        r.predicted_sems,
        over_time(),
        lambda to: r.predicted,
        lambda origin: r.levels.at[origin],
        r.predicted,
        rest(r.levels),
    )
    travelling = [Parameters(r, group) for group in range(3)]
    middle_sum = Reduction(r, "middle", final_middle)
    first_sum = Reduction(r, "first", final_first)
    lstm_sum = Reduction(r, "lstm", final_lstm)
    own_x = pltpu.make_async_copy(x_hbm.at[me], block(r.x_flat, me), r.own_sems.at[0])
    own_adjoint = pltpu.make_async_copy(adjoint_hbm.at[me], block(r.adjoint, me), r.own_sems.at[1])
    own_out = pltpu.make_async_copy(block(r.out, me), out_hbm.at[me], r.own_sems.at[2])
    own_input = pltpu.make_async_copy(block(r.input_grad, me), input_hbm.at[me], r.own_sems.at[3])
    held = [getattr(r, "param%d" % index) for index in range(len(params))]
    loads = [
        pltpu.make_async_copy(param, here, r.load_sems.at[index])
        for index, (param, here) in enumerate(
            zip(
                params + (begins_hbm, reaches_hbm, slopes_hbm),
                held + [r.begins, r.reaches, r.slope_in],
            )
        )
    ]
    begins, reaches, slopes = r.begins, r.reaches, r.slope_in

    def pack(group, *indices):
        for index in indices:
            loads[index].wait()
        pack_params(r, group, [held[index] for index in indices])

    everyone_here = greet()
    for load in loads:
        load.start()
    own_x.start()
    own_adjoint.start()
    pack(0, 0, 9, 8)
    everyone_here()
    travelling[0].start()
    x_over.start()
    pack(1, 1, 2)
    travelling[1].start()
    pack(2, 4, 7, 5, 6, 3)
    for load in loads[len(params) :]:
        load.wait()
    for track in range(count):
        r.slopes[track] = jnp.concatenate(
            [
                slopes[level_at].astype(jnp.float32)[track : track + 1]
                for level_at in range(LEVEL_TALLY)
            ]
            + [jnp.zeros((8 - LEVEL_TALLY, steps), jnp.float32)],
            axis=0,
        )
    begin = begins[me]
    choice = reaches[me]
    horizon = jnp.where(choice == 0, 1, jnp.where(choice == 1, 5, 24))
    rows, attn_rows = params[0].shape[0], params[3].shape[0]
    r.gv[...] = jnp.zeros_like(r.gv)
    own_x.wait()
    series_turn(r, me, steps)
    travelling[0].pass_on()

    x_over.arrive()
    for step in range(1, count):
        series_turn(r, x_over.other(step), steps)
    travelling[0].arrive()
    unpack_params(r, 0, rows, attn_rows)
    series_gates(r, begin)
    travelling[1].pass_on()
    travelling[2].start()

    @pl.when(me == last)
    def _():
        slope_over.start()
        r.slope[...] = r.slopes[last]

    series_forward_scan(r)
    travelling[1].arrive()
    unpack_params(r, 1, rows, attn_rows)
    adjoint_over.start()
    series_forward_first(r, begin)

    def within(tile):
        if tile == 2:
            travelling[2].pass_on()

    series_forward_attention(r, begin, within)
    travelling[2].arrive()
    unpack_params(r, 2, rows, attn_rows)
    own_adjoint.wait()
    adjoint_over.arrive()

    @pl.when(me != last)
    def _():
        slope_over.arrive()

    def forward_done():
        own_out.start()
        out_over.start()

        @pl.when(me != last)
        def _():
            predicted_over.one(last).start()

    series_middle(r, horizon, forward_done)
    middle_sum.start()

    def between(tile):
        if tile == 2:
            middle_sum.across_series()

    series_backward_attention(r, between)
    series_backward_first(r)
    first_sum.start()
    series_backward_scan(r)
    series_gate_grads(r)
    lstm_sum.start()
    first_sum.across_series()
    middle_sum.across_chips()
    series_input_grad(r)
    own_input.start()
    input_over.start()
    lstm_sum.across_series()
    first_sum.across_chips()
    middle_sum.to_both()

    @pl.when(me != last)
    def _():
        predicted_over.sent()
        predicted_out[...] = jnp.zeros_like(predicted_out)

    @pl.when(me == last)
    def _():
        slope_over.sent()
        predicted_over.arrive()
        r.levels[last] = r.predicted[...]
        for level_at in range(LEVEL_TALLY):
            predicted_out[level_at] = jnp.concatenate(
                [r.levels[track][level_at : level_at + 1] for track in range(count)], axis=0
            )

    lstm_sum.across_chips()
    first_sum.to_both()
    x_over.sent()
    adjoint_over.sent()
    for group in travelling:
        group.sent()
    own_out.wait()
    out_over.arrive()
    out_over.sent()
    middle_sum.finish()
    first_sum.finish()
    lstm_sum.to_both()
    own_input.wait()
    input_over.arrive()
    input_over.sent()
    lstm_sum.finish()


def unpack_kernel(final_middle, final_first, final_lstm, out_in, predicted_in, input_in, *others):
    (lstm, glu_one, qkv, attn, glu_two, inner, middle, glu_three, level, table) = others[:10]
    out, predicted, input_grad = others[10:]
    predicted[...] = predicted_in[...]
    rows, width = inner.shape
    lanes = final_lstm.shape[2]
    for ref, at in ((glu_two, 0), (glu_three, 1)):
        ref[...] = final_middle[at, :, : 2 * width]
    for ref, at in ((inner, 0), (middle, 1)):
        ref[...] = final_middle[at, :, 2 * width : 3 * width]
    small, spare = attn.shape[0], width // 5
    for piece in range(5):
        at = small * (piece % 4)
        attn[:, piece * spare : (piece + 1) * spare] = final_middle[
            piece // 4, at : at + small, 3 * width : 3 * width + spare
        ]
    glu_one[...] = final_first[0, :, : 2 * width]
    qkv[...] = final_first[1, :, : qkv.shape[1]]
    lstm[:, :lanes] = final_lstm[0]
    lstm[:, lanes : 3 * width] = final_lstm[1, :, : 3 * width - lanes]
    lstm[:, 3 * width :] = final_first[0, :, 2 * width : 3 * width]
    vectors = final_lstm[1, :, 3 * width - lanes :].T
    table[...] = vectors[: table.shape[0]]
    level[...] = vectors[VECTORS : VECTORS + LEVEL_TALLY]
    out[...] = out_in[...]
    input_grad[...] = input_in[...]


def whole_series(embedded_features, earliest_seen_moment, reach_choice, *others):
    count, steps, width = embedded_features.shape
    features = embedded_features.swapaxes(1, 2)
    adjoint = others[-2].swapaxes(1, 2)
    slopes = others[-1].swapaxes(0, 1)
    params = others[:-4] + (others[-4].T, others[-3].T)
    groups = lax.axis_size("dp")
    rows = params[0].shape[0]
    names = series_scratch(count * steps, width, width // HEADS)
    names.update(travel_scratch(count, groups, steps, width, params))
    smem, vmem, anywhere = (
        pl.BlockSpec(memory_space=space) for space in (pltpu.SMEM, pltpu.VMEM, pl.ANY)
    )
    moved = ((features.shape, jnp.bfloat16), (slopes.shape, jnp.float32))
    moved += moved[:1]
    out, predicted, input_grad, *finals = pl.pallas_call(
        series_kernel,
        out_shape=tuple(pltpu.VMEM(*one) for one in moved)
        + tuple(pltpu.VMEM((2, rows, lanes), jnp.float32) for lanes in GROUP_LANES.values()),
        in_specs=[anywhere] * (5 + len(params)),
        out_specs=(vmem,) * 6,
        scratch_shapes=list(names.values()),
        compiler_params=pltpu.CompilerParams(
            vmem_limit_bytes=VMEM_BYTES, collective_id=0, has_side_effects=True
        ),
    )(
        earliest_seen_moment,
        reach_choice,
        features,
        adjoint,
        slopes,
        *params,
    )
    *grads, level_grad, table_grad, out, predicted, input_grad = pl.pallas_call(
        unpack_kernel,
        out_shape=tuple(jax.ShapeDtypeStruct(param.shape, jnp.float32) for param in params)
        + tuple(jax.ShapeDtypeStruct(*one) for one in moved),
        in_specs=[vmem] * 6,
        out_specs=(vmem,) * (len(params) + 3),
        compiler_params=pltpu.CompilerParams(vmem_limit_bytes=VMEM_BYTES // 6),
    )(*finals, out, predicted, input_grad)
    return (
        out.swapaxes(1, 2),
        predicted.swapaxes(0, 1),
        input_grad.swapaxes(1, 2),
        *grads,
        level_grad.T,
        table_grad.T,
    )


def on_device(embedded_features, *others):
    count, steps, _ = embedded_features.shape
    one_each = count == lax.axis_size("tm") == SUBLANES and steps == LANES
    return (whole_series if one_each else shards)(embedded_features, *others)


def solution(mesh):
    placed = (
        P("dp", "tm", None),
        P("dp"),
        P("dp"),
        P("dp", None),
        P("dp", None),
        P("dp", None),
        P("dp", None),
        P("dp", None),
        P("dp", None),
        P("dp", None),
        P("dp", None),
        P("dp", None),
        P("dp", None),
        P("dp", "tm", None),
        P("dp", None, "tm"),
    )
    return jax.shard_map(
        on_device,
        mesh=mesh,
        in_specs=placed,
        out_specs=(
            P("dp", "tm", None),
            P("dp", None, "tm"),
            P("dp", "tm", None),
            P("dp", None),
            P("dp", None),
            P("dp", None),
            P("dp", None),
            P("dp", None),
            P("dp", None),
            P("dp", None),
            P("dp", None),
            P("dp", None),
            P("dp", None),
        ),
        check_vma=False,
    )
```
